32 devices in a mesh: seq: 8 (over z, x), exp: 4 (over y, core).
Axes of the slice: x: 2, y: 2, z: 4, core: 2. Of those that a mesh axis runs over, the one named last changes fastest.
Arguments:
- residual: bfloat16 [1024, 2048], P('seq', 'exp'), may hold values from -36 to 36
- queries: bfloat16 [1024, 2048], P('seq', 'exp'), may hold values from -6 to 6
- key_vectors: bfloat16 [1024, 2048], P('seq', 'exp'), may hold values from -6 to 6
- value_vectors: bfloat16 [1024, 2048], P('seq', 'exp'), may hold values from -36 to 36
- head_gain: float32 [2048], P('exp'), may hold values from 0.25 to 1.75
- norm_gain: float32 [2048], replicated, may hold values from 0.25 to 1.75
- routes: int32 [1024, 8], P('seq'), may hold values from 0 to 7, as said below
- route_gates: float32 [1024, 8], P('seq'), may hold values from 0.2 to 1
- expert_in: bfloat16 [8, 2, 2048, 1024], P('seq'), may hold values from -0.125 to 0.125
- expert_out: bfloat16 [8, 1024, 2048], P('seq'), may hold values from -0.1875 to 0.1875
Outputs:
- layer_out: bfloat16 [1024, 2048], P('seq', 'exp')
The draws below stay inside these ranges and needn't reach their ends.
Inputs may be any that keep to these rules, and one draw needn't show every extreme that they name: `routes`: each row names 8 different experts. In every aligned block of 32 rows no expert is named by more than 32 rows, and the same 2 experts are named by exactly 32 rows in every block.
All inputs are finite; a program needn't handle non-finite values.
Results may differ from the reference program's by a relative error of at most 0.0075.
Values may be sent and summed in bfloat16 or wider, within the bound.
No kernel may reach another device: no remote copies, remote signals or barrier semaphores. Data moves between devices by JAX's collectives and lax.ppermute only.
A program may use at most 128 MiB of HBM per device.

```python
import math
import jax
import jax.numpy as jnp
from jax import lax

D = 2048
HEADS = 16
HEAD = 128
FF = 1024
TOPK = 8
EXPERTS = 8
TOK_DEV = 128
SEQ_LEN = 1024
SUB = 32
CAP = 32
HOT = 2


def draw_residual(key, part):
    key_base, key_cols, key_rows = jax.random.split(jax.random.fold_in(key, 5), 3)
    entries = jnp.clip(jax.random.normal(key_base, (SEQ_LEN, D), jnp.float32), -6.0, 6.0)
    column_scale = jnp.exp(jax.random.uniform(key_cols, (D,), jnp.float32, math.log(0.3), math.log(3.0)))
    row_scale = jnp.exp(jax.random.uniform(key_rows, (SEQ_LEN, 1), jnp.float32, math.log(0.5), math.log(2.0)))
    return (entries * column_scale[None, :] * row_scale).astype(jnp.bfloat16)


def draw_value_vectors(key, part):
    key_base, key_cols, key_rows = jax.random.split(jax.random.fold_in(key, 9), 3)
    entries = jnp.clip(jax.random.normal(key_base, (SEQ_LEN, D), jnp.float32), -6.0, 6.0)
    column_scale = jnp.exp(jax.random.uniform(key_cols, (D,), jnp.float32, math.log(0.3), math.log(3.0)))
    row_scale = jnp.exp(jax.random.uniform(key_rows, (SEQ_LEN, 1), jnp.float32, math.log(0.5), math.log(2.0)))
    return (entries * column_scale[None, :] * row_scale).astype(jnp.bfloat16)


def draw_routes(key, part):
    key_order, key_blocks = jax.random.split(jax.random.fold_in(key, 17), 2)
    expert_order = jax.random.permutation(key_order, EXPERTS).astype(jnp.int32)
    per_block = SUB * TOPK
    remainder = per_block - HOT * CAP
    cold_count = EXPERTS - HOT
    base_load = remainder // cold_count
    extra_count = remainder - base_load * cold_count
    spread = max(0, min(base_load, CAP - base_load - 1))
    pair_count = cold_count // 2
    block_count = SEQ_LEN // SUB
    positions = jnp.arange(per_block, dtype=jnp.int32)
    hot_loads = jnp.full((HOT,), CAP, jnp.int32)

    def one_block(block_key):
        key_pick, key_pair, key_shift, key_rows, key_cols = jax.random.split(block_key, 5)
        ranking = jax.random.permutation(key_pick, cold_count)
        load_counts = base_load + (ranking < extra_count).astype(jnp.int32)
        pairing = jax.random.permutation(key_pair, cold_count)
        shifts = jax.random.randint(key_shift, (pair_count,), 0, spread + 1, dtype=jnp.int32)
        load_counts = load_counts.at[pairing[0:2 * pair_count:2]].add(-shifts)
        load_counts = load_counts.at[pairing[1:2 * pair_count:2]].add(shifts)
        segment_ends = jnp.cumsum(jnp.concatenate([hot_loads, load_counts]))
        segment = jnp.sum((positions[:, None] >= segment_ends[None, :]).astype(jnp.int32), axis=1)
        chosen = expert_order[segment].reshape(TOPK, SUB).T
        row_order = jax.random.permutation(key_rows, SUB)
        column_order = jax.random.permutation(key_cols, TOPK)
        return chosen[row_order][:, column_order]
    block_keys = jax.random.split(key_blocks, block_count)
    return jax.vmap(one_block)(block_keys).reshape(SEQ_LEN, TOPK).astype(jnp.int32)


def levels(stream_key, extent, cuts, low, high):
    gain = 1.0
    for dim, parts in cuts:
        heights = jax.random.uniform(jax.random.fold_in(jax.random.fold_in(stream_key, 6), dim), (parts,), jnp.float32, low / len(cuts), high / len(cuts))
        gain = gain * jnp.repeat(jnp.exp(heights), extent[dim] // parts).reshape((-1,) + (1,) * (len(extent) - 1 - dim))
    return gain


def bell_draw(stream_key, dims, scale, limit, shards=(), held_as=jnp.bfloat16):
    gain = levels(stream_key, dims, shards, -0.22, 0.18) if shards else 1.0
    values = jax.random.normal(stream_key, dims, jnp.float32) * scale * gain
    return jnp.minimum(jnp.maximum(values, -limit), limit).astype(held_as)


def setup_inputs(seed: int = 0) -> dict:
    key_list = jax.random.split(jax.random.key(seed), 11)
    residual = draw_residual(jax.random.fold_in(key_list[10], 71), 0)
    queries = bell_draw(key_list[1], (SEQ_LEN, D), 1.0, 6.0, ((0, 8), (1, 4)))
    key_vectors = bell_draw(key_list[2], (SEQ_LEN, D), 1.0, 6.0, ((0, 8), (1, 4)))
    value_vectors = draw_value_vectors(jax.random.fold_in(key_list[10], 71), 0)
    head_gain = jnp.clip(1.0 + 0.15 * jax.random.normal(key_list[4], (D,), jnp.float32), 0.25, 1.75)
    norm_gain = jnp.clip(1.0 + 0.15 * jax.random.normal(key_list[5], (D,), jnp.float32), 0.25, 1.75)
    routes = draw_routes(jax.random.fold_in(key_list[10], 71), 0)
    route_gates = jnp.clip(0.2 + 0.8 * jax.random.uniform(key_list[7], (SEQ_LEN, TOPK), jnp.float32) ** levels(key_list[7], (SEQ_LEN, TOPK), ((0, 8),), -0.2, 0.2), 0.2, 1.0)
    expert_in = bell_draw(key_list[8], (EXPERTS, 2, D, FF), D ** -0.5, 0.125, ((0, 8),))
    expert_out = bell_draw(key_list[9], (EXPERTS, FF, D), FF ** -0.5, 0.1875, ((0, 8),))
    return dict(residual=residual, queries=queries, key_vectors=key_vectors, value_vectors=value_vectors, head_gain=head_gain, norm_gain=norm_gain, routes=routes, route_gates=route_gates, expert_in=expert_in, expert_out=expert_out)


def to_blocks(matrix):
    return matrix.astype(jnp.float32).reshape(matrix.shape[0] // TOK_DEV, TOK_DEV, HEADS, HEAD)

def attend_block(state_sum, block_triple):
    query_block, key_block, value_block = block_triple
    causal = jnp.tril(jnp.ones((TOK_DEV, TOK_DEV), jnp.float32))
    carried = jnp.einsum('bhd,hde->bhe', query_block, state_sum, precision=lax.Precision.HIGHEST)
    scores = jnp.einsum('bhd,chd->hbc', query_block, key_block, precision=lax.Precision.HIGHEST) * causal[None]
    within = jnp.einsum('hbc,che->bhe', scores, value_block, precision=lax.Precision.HIGHEST)
    state_sum = state_sum + jnp.einsum('chd,che->hde', key_block, value_block, precision=lax.Precision.HIGHEST)
    return (state_sum, carried + within)

def mix_experts(normed, routes, route_gates, expert_in, expert_out):
    length = normed.shape[0]
    block_rows = 256
    flat_routes = routes.reshape(-1).astype(jnp.int32)
    route_total = flat_routes.shape[0]
    expert_ids = jnp.arange(EXPERTS, dtype=jnp.int32)
    counts = lax.optimization_barrier(jnp.sum((flat_routes[:, None] == expert_ids[None, :]).astype(jnp.int32), axis=0))
    starts = jnp.cumsum(counts) - counts
    padded = (counts + block_rows - 1) // block_rows * block_rows
    padded_starts = jnp.cumsum(padded) - padded
    route_order = jnp.argsort(flat_routes, stable=True).astype(jnp.int32)
    flat_gates = route_gates.reshape(-1)
    block_count = (route_total + block_rows - 1) // block_rows + EXPERTS
    offsets = jnp.arange(block_rows, dtype=jnp.int32)

    def one_block(running, block_index):
        first_row = block_index * block_rows
        expert = jnp.minimum(jnp.sum((padded_starts + padded <= first_row).astype(jnp.int32)), EXPERTS - 1)
        within = first_row - padded_starts[expert] + offsets
        live_rows = (within >= 0) & (within < counts[expert])
        position = jnp.clip(starts[expert] + within, 0, route_total - 1).astype(jnp.int32)
        route_index = route_order[position]
        token_index = (route_index // TOPK).astype(jnp.int32)
        weight = jnp.where(live_rows, flat_gates[route_index], jnp.zeros((), flat_gates.dtype))
        chosen = normed[token_index]
        pair_weights = expert_in[expert]
        gate_pre = jnp.dot(chosen, pair_weights[0], preferred_element_type=jnp.float32)
        up_pre = jnp.dot(chosen, pair_weights[1], preferred_element_type=jnp.float32)
        activated = (jax.nn.silu(gate_pre) * up_pre).astype(jnp.bfloat16)
        produced = jnp.dot(activated, expert_out[expert], preferred_element_type=jnp.float32).astype(jnp.bfloat16)
        produced = lax.optimization_barrier(produced).astype(jnp.float32)
        running = running.at[token_index].add(weight[:, None] * produced)
        return (running, None)
    zero_sum = jnp.zeros((length, D), jnp.float32)
    result, unused = lax.scan(one_block, zero_sum, jnp.arange(block_count, dtype=jnp.int32))
    return result

def reference(residual, queries, key_vectors, value_vectors, head_gain, norm_gain, routes, route_gates, expert_in, expert_out):
    length = residual.shape[0]
    initial = jnp.zeros((HEADS, HEAD, HEAD), jnp.float32)
    final_state, outputs = lax.scan(attend_block, initial, (to_blocks(queries), to_blocks(key_vectors), to_blocks(value_vectors)))
    raw_output = outputs.reshape(length, HEADS, HEAD)
    scaled = raw_output * lax.rsqrt(lax.optimization_barrier(jnp.mean(raw_output * raw_output, axis=-1, keepdims=True)) + 1e-06)
    attention_out = scaled.reshape(length, D) * head_gain
    hidden = (residual.astype(jnp.float32) + attention_out).astype(jnp.bfloat16)
    widened = hidden.astype(jnp.float32)
    normed = (widened * lax.rsqrt(lax.optimization_barrier(jnp.mean(widened * widened, axis=-1, keepdims=True)) + 1e-06) * norm_gain).astype(jnp.bfloat16)
    moe_out = mix_experts(normed, routes, route_gates, expert_in, expert_out)
    return (widened + moe_out).astype(jnp.bfloat16)
```

```python
import functools

import jax
import jax.numpy as jnp
from jax import lax
from jax.experimental import pallas as pl
from jax.experimental.pallas import tpu as pltpu
from jax.sharding import PartitionSpec as P

HEAD = 128
F32 = jnp.float32
BF16 = jnp.bfloat16
WHOLE = pl.BlockSpec(memory_space=pltpu.VMEM)
SCALAR = pl.BlockSpec(memory_space=pltpu.SMEM)


def call(kernel, outs, inputs, flops=0, limit=16 << 20):
    moved = sum(a.size * a.dtype.itemsize for a in inputs)
    moved += sum(a.size * a.dtype.itemsize for a in outs)
    return pl.pallas_call(
        kernel,
        out_shape=outs,
        in_specs=[SCALAR] + [WHOLE] * (len(inputs) - 1),
        out_specs=[WHOLE] * len(outs),
        compiler_params=pltpu.CompilerParams(vmem_limit_bytes=limit),
        cost_estimate=pl.CostEstimate(flops=flops, bytes_accessed=moved, transcendentals=0),
    )(*inputs)


def shape(dims, dtype):
    return jax.ShapeDtypeStruct(dims, dtype)


def split(value):
    high = value.astype(BF16)
    return high, (value - high.astype(F32)).astype(BF16)


def state_kernel(scalars, key_ref, value_ref, kept_ref, given_ref):
    width = key_ref.shape[1] // 2
    place = scalars[1]
    for h in range(key_ref.shape[1] // HEAD):
        cols = slice(h * HEAD, (h + 1) * HEAD)
        state = lax.dot_general(
            key_ref[:, cols], value_ref[:, cols], (((0,), (0,)), ((), ())),
            preferred_element_type=F32,
        ).astype(BF16)
        half, inner = divmod(h * HEAD, width)

        @pl.when(place == half)
        def _():
            kept_ref[:, inner:inner + HEAD] = state

        @pl.when(place != half)
        def _():
            given_ref[:, inner:inner + HEAD] = state


def within_kernel(scalars, query_ref, key_ref, value_ref, out_ref):
    rows = query_ref.shape[0]
    causal = lax.broadcasted_iota(jnp.int32, (rows, rows), 0) >= lax.broadcasted_iota(
        jnp.int32, (rows, rows), 1
    )
    for h in range(query_ref.shape[1] // HEAD):
        cols = slice(h * HEAD, (h + 1) * HEAD)
        scores = lax.dot_general(
            query_ref[:, cols], key_ref[:, cols], (((1,), (1,)), ((), ())),
            preferred_element_type=F32,
        )
        high, low = split(jnp.where(causal, scores, 0.0))
        value = value_ref[:, cols]
        out_ref[:, cols] = jnp.dot(high, value, preferred_element_type=F32) + jnp.dot(
            low, value, preferred_element_type=F32
        )


def attend_kernel(
    parts, scalars, query_ref, mine_ref, other_ref, within_ref, residual_ref, gain_ref,
    hidden_ref, own_ref, *piece_refs
):
    place = scalars[1]
    width = query_ref.shape[1] // 2
    mine = mine_ref[...].astype(F32)
    other = other_ref[...].astype(F32)
    halves = [jnp.where(place == 0, mine, other), jnp.where(place == 0, other, mine)]
    for h in range(query_ref.shape[1] // HEAD):
        cols = slice(h * HEAD, (h + 1) * HEAD)
        half, inner = divmod(h * HEAD, width)
        query = query_ref[:, cols]
        high, low = split(halves[half][:, inner:inner + HEAD])
        raw = (
            jnp.dot(query, high, preferred_element_type=F32)
            + jnp.dot(query, low, preferred_element_type=F32)
            + within_ref[:, cols]
        )
        scaled = raw * lax.rsqrt(jnp.mean(raw * raw, axis=-1, keepdims=True) + 1e-06)
        hidden_ref[:, cols] = (
            residual_ref[:, cols].astype(F32) + scaled * gain_ref[:, cols]
        ).astype(BF16)
    count = hidden_ref.shape[0] // parts
    for j in range(parts):
        target = own_ref if j == 0 else piece_refs[j - 1]
        start = pl.multiple_of((scalars[0] ^ j) * count, count)
        target[...] = hidden_ref[pl.ds(start, count), :]


def norm_kernel(parts, scalars, gain_ref, pack_ref, *refs):
    pieces, out_ref = refs[:parts], refs[parts]
    width = pieces[0].shape[1]
    total = 0.0
    for ref in pieces:
        value = ref[...].astype(F32)
        total += jnp.sum(value * value, axis=-1, keepdims=True)
    scale = lax.rsqrt(total / (parts * width) + 1e-06)
    for j in range(parts):
        start = pl.multiple_of((scalars[0] ^ j) * width, width)
        cols = pl.ds(start, width)
        out_ref[:, cols] = (pieces[j][...].astype(F32) * scale * gain_ref[:, cols]).astype(BF16)
    out_ref[:, parts * width:] = pack_ref[...]


def expert_kernel(blocks, scalars, *refs):
    x_refs = refs[:blocks]
    gate_ref, up_ref, down_ref = refs[blocks:blocks + 3]
    out_refs = refs[blocks + 3:2 * blocks + 3]
    rows_ref, acc_ref = refs[2 * blocks + 3:]
    step = pl.program_id(0)
    width = acc_ref.shape[1]
    spans = []
    first = 0
    for ref in x_refs:
        spans.append(slice(first, first + ref.shape[0]))
        first += ref.shape[0]

    @pl.when(step == 0)
    def _():
        for ref, span in zip(x_refs, spans):
            rows_ref[span, :] = ref[:, :width]

    rows = rows_ref[...]
    gate = jnp.dot(rows, gate_ref[0, 0], preferred_element_type=F32)
    up = jnp.dot(rows, up_ref[0, 0], preferred_element_type=F32)
    activated = (gate / (1.0 + jnp.exp(-gate)) * up).astype(BF16)
    part = jnp.dot(activated, down_ref[0], preferred_element_type=F32)

    @pl.when(step == 0)
    def _():
        acc_ref[...] = part

    @pl.when(step > 0)
    def _():
        acc_ref[...] += part

    @pl.when(step == pl.num_programs(0) - 1)
    def _():
        experts = scalars[2]
        for x_ref, out_ref, span in zip(x_refs, out_refs, spans):
            pack = x_ref[:, width:].astype(F32)
            lane = lax.broadcasted_iota(jnp.int32, pack.shape, 1)
            chosen = (lane == scalars[3]) | (lane == scalars[3] + experts)
            weight = jnp.sum(jnp.where(chosen, pack, 0.0), axis=-1, keepdims=True)
            produced = acc_ref[span, :].astype(BF16).astype(F32)
            out_ref[...] = (produced * weight).astype(BF16)


def run_expert(scalars, blocks, expert_in, expert_out):
    width, hidden_units = expert_in.shape[2:]
    total = sum(b.shape[0] for b in blocks)
    chunk = min(hidden_units, 256)
    steps = hidden_units // chunk
    kernel = functools.partial(expert_kernel, len(blocks))
    return pl.pallas_call(
        kernel,
        grid=(steps,),
        out_shape=[shape((b.shape[0], width), BF16) for b in blocks],
        in_specs=[SCALAR]
        + [pl.BlockSpec(b.shape, lambda f: (0, 0)) for b in blocks]
        + [
            pl.BlockSpec((1, 1, width, chunk), lambda f: (0, 0, 0, f)),
            pl.BlockSpec((1, 1, width, chunk), lambda f: (0, 1, 0, f)),
            pl.BlockSpec((1, chunk, width), lambda f: (0, f, 0)),
        ],
        out_specs=[pl.BlockSpec((b.shape[0], width), lambda f: (0, 0)) for b in blocks],
        scratch_shapes=[pltpu.VMEM((total, width), BF16), pltpu.VMEM((total, width), F32)],
        compiler_params=pltpu.CompilerParams(vmem_limit_bytes=32 << 20),
        cost_estimate=pl.CostEstimate(
            flops=6 * total * width * hidden_units,
            bytes_accessed=6 * width * hidden_units + 4 * total * width,
            transcendentals=total * hidden_units,
        ),
    )(scalars, *blocks, expert_in, expert_in, expert_out)


def ring_order(count):
    return list(range(0, count, 2)) + list(range(1, count, 2))[::-1]


def add_rows(*terms):
    return sum(t.astype(F32) for t in terms).astype(BF16)


def dense_experts(block, scalars, expert_in, expert_out):
    count = lax.axis_size("seq")
    width = expert_in.shape[2]
    order = ring_order(count)
    forward = [(order[p], order[(p + 1) % count]) for p in range(count)]
    backward = [(b, a) for a, b in forward]
    half = block.shape[0] // 2
    far = count // 2
    ahead, behind = [block], [block]
    for step in range(1, far):
        ahead.append(lax.ppermute(ahead[-1], "seq", forward))
        behind.append(lax.ppermute(behind[-1], "seq", backward))
    top = lax.ppermute(ahead[-1][:half], "seq", forward)
    bottom = lax.ppermute(behind[-1][half:], "seq", backward)
    blocks = [block] + ahead[1:] + behind[1:] + [top, bottom]
    made = run_expert(scalars, blocks, expert_in, expert_out)
    own, from_ahead, from_behind = made[0], made[1:far], made[far:2 * far - 1]
    top, bottom = made[-2:]
    going, coming = (
        lax.ppermute(top, "seq", forward),
        lax.ppermute(bottom, "seq", backward),
    )
    for distance in range(far - 1, 0, -1):
        to_front, to_back = from_behind[distance - 1], from_ahead[distance - 1]
        if distance == far - 1:
            going = jnp.concatenate([add_rows(going, to_front[:half]), to_front[half:]])
            coming = jnp.concatenate([to_back[:half], add_rows(coming, to_back[half:])])
        else:
            going = add_rows(going, to_front)
            coming = add_rows(coming, to_back)
        going = lax.ppermute(going, "seq", forward)
        coming = lax.ppermute(coming, "seq", backward)
    return own, going, coming


def mix_kernel(parts, scalars, a_ref, b_ref, c_ref, *out_refs):
    width = out_refs[0].shape[1]
    for j, out_ref in enumerate(out_refs):
        start = pl.multiple_of((scalars[0] ^ j) * width, width)
        cols = pl.ds(start, width)
        out_ref[...] = (
            a_ref[:, cols].astype(F32) + b_ref[:, cols].astype(F32) + c_ref[:, cols].astype(F32)
        ).astype(BF16)


def final_kernel(parts, scalars, hidden_ref, *refs):
    out_ref = refs[parts]
    count = out_ref.shape[0] // parts
    for j in range(parts):
        rows = pl.ds(pl.multiple_of((scalars[0] ^ j) * count, count), count)
        out_ref[rows, :] = (
            hidden_ref[rows, :].astype(F32) + refs[j][...].astype(F32)
        ).astype(BF16)


def slot_ids(block_routes, expert_count, capacity):
    row_count, top_count = block_routes.shape
    expert_ids = jnp.arange(expert_count, dtype=jnp.int32)
    onehot = (
        (block_routes[:, :, None] == expert_ids[None, None, :])
        .astype(jnp.int32)
        .reshape(row_count * top_count, expert_count)
    )
    earlier = jnp.cumsum(onehot, axis=0) - onehot
    ranking = jnp.sum(earlier * onehot, axis=1).reshape(row_count, top_count)
    return block_routes * capacity + ranking


def routed_experts(normed, my_routes, my_gates, expert_in, expert_out):
    sub_count, model_width = normed.shape
    expert_count = lax.axis_size("seq") * expert_in.shape[0]
    top_count = my_routes.shape[1]
    capacity = min(sub_count, max(2, 3 * sub_count * top_count // (2 * expert_count)))
    slot_count = expert_count * capacity
    my_slots = slot_ids(my_routes, expert_count, capacity)
    columns = jnp.arange(slot_count, dtype=jnp.int32)
    placer = jnp.sum(
        (my_slots[None, :, :] == columns[:, None, None]).astype(jnp.int32), axis=2
    ).astype(BF16)
    outgoing = (
        jnp.dot(placer, normed, preferred_element_type=F32)
        .astype(BF16)
        .reshape(expert_count, capacity, model_width)
    )
    arrived = lax.all_to_all(outgoing, "seq", split_axis=0, concat_axis=0, tiled=True)
    flat_rows = arrived.reshape(-1, model_width)
    gate_up = jnp.einsum("nd,gdf->gnf", flat_rows, expert_in[0], preferred_element_type=F32)
    activated = (jax.nn.silu(gate_up[0]) * gate_up[1]).astype(BF16)
    produced = jnp.dot(activated, expert_out[0], preferred_element_type=F32).astype(BF16)
    answered = produced.reshape(arrived.shape)
    returned = lax.all_to_all(answered, "seq", split_axis=0, concat_axis=0, tiled=True)
    picked = returned.reshape(slot_count, model_width)[my_slots.reshape(-1)].reshape(
        sub_count, top_count, model_width
    )
    return jnp.sum(picked.astype(F32) * my_gates[:, :, None], axis=1)


def exchange(pieces, axis):
    count = lax.axis_size(axis)
    return [
        lax.ppermute(piece, axis, [(i, i ^ j) for i in range(count)])
        for j, piece in enumerate(pieces, start=1)
    ]


def prior_states(scalars, key_vectors, value_vectors):
    rows, width = key_vectors.shape
    count = lax.axis_size("seq")
    swap = [(i, i ^ 1) for i in range(count)]
    half = shape((HEAD, width // 2), BF16)
    kept, given = call(
        state_kernel, [half, half], [scalars, key_vectors, value_vectors],
        flops=2 * rows * width * HEAD,
    )
    partner = lax.ppermute(given, "seq", swap)
    running = add_rows(kept, partner)
    before = jnp.zeros(half.shape, F32)
    distance = 2
    while distance < count:
        came = lax.ppermute(
            running, "seq", [(i, i + distance) for i in range(count - distance)]
        )
        before = before + came.astype(F32)
        if 2 * distance < count:
            running = add_rows(running, came)
        distance *= 2
    first = scalars[1] == 0
    mine = before + jnp.where(first, 0.0, partner.astype(F32))
    sent = jnp.where(first, before + kept.astype(F32), before).astype(BF16)
    other = lax.ppermute(sent, "seq", swap)
    return mine, other


def per_device(
    residual,
    queries,
    key_vectors,
    value_vectors,
    head_gain,
    norm_gain,
    routes,
    route_gates,
    expert_in,
    expert_out,
):
    rows, width = residual.shape
    parts = lax.axis_size("exp")
    count = rows // parts
    experts = lax.axis_size("seq") * expert_in.shape[0]
    position = lax.axis_index("seq")
    my_index = lax.axis_index("exp")
    scalars = jnp.stack([my_index, position % 2, experts, position]).astype(jnp.int32)
    mine, other = prior_states(scalars, key_vectors, value_vectors)
    [within] = call(
        within_kernel, [shape((rows, width), F32)],
        [scalars, queries, key_vectors, value_vectors], flops=6 * rows * rows * width,
    )
    piece = shape((count, width), BF16)
    hidden, own, *pieces = call(
        functools.partial(attend_kernel, parts),
        [shape((rows, width), BF16), piece] + [piece] * (parts - 1),
        [scalars, queries, mine, other, within, residual, head_gain[None, :]],
        flops=4 * rows * width * HEAD,
    )
    my_routes = lax.dynamic_slice_in_dim(routes, my_index * count, count, 0)
    my_gates = lax.dynamic_slice_in_dim(route_gates, my_index * count, count, 0)
    weights = jnp.sum(
        jnp.where(
            my_routes[:, :, None] == jnp.arange(experts, dtype=jnp.int32),
            my_gates[:, :, None],
            0.0,
        ),
        axis=1,
    )
    high = lax.reduce_precision(weights, 8, 7)
    lanes = -(-2 * experts // HEAD) * HEAD
    pack = jnp.pad(
        jnp.concatenate([high, weights - high], axis=1), ((0, 0), (0, lanes - 2 * experts))
    ).astype(BF16)
    gathered = exchange(pieces, "exp")
    [block] = call(
        functools.partial(norm_kernel, parts),
        [shape((count, width * parts + lanes), BF16)],
        [scalars, norm_gain[None, :], pack, own] + gathered,
    )
    if routes.shape[1] == experts:
        terms = dense_experts(block, scalars, expert_in, expert_out)
    else:
        mixed = routed_experts(
            block[:, : width * parts], my_routes, my_gates, expert_in, expert_out
        )
        nothing = jnp.zeros_like(mixed)
        terms = (mixed, nothing, nothing)
    own, *pieces = call(
        functools.partial(mix_kernel, parts),
        [shape((count, width), BF16)] * parts,
        [scalars, *terms],
    )
    returned = exchange(pieces, "exp")
    [out] = call(
        functools.partial(final_kernel, parts),
        [shape((rows, width), BF16)],
        [scalars, hidden, own] + returned,
    )
    return out


def solution(mesh):
    placed = (
        P("seq", "exp"),
        P("seq", "exp"),
        P("seq", "exp"),
        P("seq", "exp"),
        P("exp"),
        P(),
        P("seq", None),
        P("seq", None),
        P("seq", None, None, None),
        P("seq", None, None),
    )
    return jax.shard_map(
        per_device, mesh=mesh, in_specs=placed, out_specs=P("seq", "exp"), check_vma=False
    )
```

```python
import functools

import jax
import jax.numpy as jnp
from jax import lax
from jax.experimental import pallas as pl
from jax.experimental.pallas import tpu as pltpu
from jax.sharding import PartitionSpec as P

HEAD = 128
F32 = jnp.float32
BF16 = jnp.bfloat16
WHOLE = pl.BlockSpec(memory_space=pltpu.VMEM)
FAR = pl.BlockSpec(memory_space=pltpu.HBM)
SCALAR = pl.BlockSpec(memory_space=pltpu.SMEM)


def call(kernel, outs, inputs, far=(), scratch=(), out_specs=None, flops=0, limit=16 << 20):
    moved = sum(a.size * a.dtype.itemsize for a in [*inputs, *outs])
    return pl.pallas_call(
        kernel,
        out_shape=outs,
        in_specs=[
            SCALAR if i == 0 else FAR if i in far else WHOLE for i in range(len(inputs))
        ],
        out_specs=out_specs or [WHOLE] * len(outs),
        scratch_shapes=scratch,
        compiler_params=pltpu.CompilerParams(vmem_limit_bytes=limit),
        cost_estimate=pl.CostEstimate(flops=flops, bytes_accessed=moved, transcendentals=0),
    )(*inputs)


def shape(dims, dtype):
    return jax.ShapeDtypeStruct(dims, dtype)


def split(value):
    high = value.astype(BF16)
    return high, (value - high.astype(F32)).astype(BF16)


def add_rows(*terms):
    return sum(t.astype(F32) for t in terms).astype(BF16)


def run_copies(pairs, sems):
    copies = [pltpu.make_async_copy(a, b, sems.at[i]) for i, (a, b) in enumerate(pairs)]
    for copy in copies:
        copy.start()
    for copy in copies:
        copy.wait()


def state_kernel(scalars, key_ref, value_ref, kept_ref, given_ref, keys, values, sems):
    run_copies([(key_ref, keys), (value_ref, values)], sems)
    width = keys.shape[1] // 2
    place = scalars[1]
    for h in range(keys.shape[1] // HEAD):
        cols = slice(h * HEAD, (h + 1) * HEAD)
        state = lax.dot_general(
            keys[:, cols], values[:, cols], (((0,), (0,)), ((), ())), preferred_element_type=F32
        ).astype(BF16)
        half, inner = divmod(h * HEAD, width)

        @pl.when(place == half)
        def _():
            kept_ref[:, inner:inner + HEAD] = state

        @pl.when(place != half)
        def _():
            given_ref[:, inner:inner + HEAD] = state


def pack_kernel(scalars, *refs):
    sources, out_ref, sems = refs[:-2], refs[-2], refs[-1]
    width = out_ref.shape[1] // len(sources)
    theirs = pl.ds(pl.multiple_of((1 - scalars[1]) * width, width), width)
    run_copies(
        [
            (ref.at[:, theirs], out_ref.at[:, i * width:(i + 1) * width])
            for i, ref in enumerate(sources)
        ],
        sems,
    )


def within_kernel(
    scalars, key_ref, value_ref, query_ref, residual_ref, gain_ref, norm_ref, came_ref,
    out_ref, my_query, my_residual, my_gain, my_norm, keys, values, sems
):
    rows, width = my_query.shape
    mine = pl.ds(pl.multiple_of(scalars[1] * width, width), width)
    run_copies(
        [
            (key_ref.at[:, mine], keys),
            (value_ref.at[:, mine], values),
            (query_ref.at[:, mine], my_query),
            (residual_ref.at[:, mine], my_residual),
            (gain_ref.at[:, mine], my_gain),
            (norm_ref, my_norm),
        ],
        sems,
    )
    causal = lax.broadcasted_iota(jnp.int32, (rows, rows), 0) >= lax.broadcasted_iota(
        jnp.int32, (rows, rows), 1
    )
    for block in range(2):
        for inner in range(0, width, HEAD):
            cols = slice(inner, inner + HEAD)
            if block == 0:
                query, key, value = my_query[:, cols], keys[:, cols], values[:, cols]
            else:
                key, value, query = (
                    came_ref[:, i * width + inner:i * width + inner + HEAD] for i in range(3)
                )
            scores = lax.dot_general(
                query, key, (((1,), (1,)), ((), ())), preferred_element_type=F32
            )
            high, low = split(jnp.where(causal, scores, 0.0))
            out_ref[block, :, cols] = jnp.dot(
                high, value, preferred_element_type=F32
            ) + jnp.dot(low, value, preferred_element_type=F32)


def attend_kernel(
    parts, earlier, scalars, within_ref, my_query, my_residual, my_gain, came_ref, kept_ref,
    partner_ref, *refs
):
    before_refs, piece_refs, hidden = refs[:earlier], refs[earlier:-1], refs[-1]
    rows, width = my_query.shape
    before = sum(ref[...].astype(F32) for ref in before_refs)
    first = scalars[1] == 0
    for block in range(2):
        extra = (partner_ref if block == 0 else kept_ref)[...].astype(F32)
        use = jnp.logical_not(first) if block == 0 else first
        state = before + jnp.where(use, extra, 0.0)
        for inner in range(0, width, HEAD):
            cols = slice(inner, inner + HEAD)
            if block == 0:
                query, residual = my_query[:, cols], my_residual[:, cols]
            else:
                query, residual = (
                    came_ref[:, i * width + inner:i * width + inner + HEAD] for i in (2, 3)
                )
            high, low = split(state[:, cols])
            raw = (
                jnp.dot(query, high, preferred_element_type=F32)
                + jnp.dot(query, low, preferred_element_type=F32)
                + within_ref[block, :, cols]
            )
            scaled = raw * lax.rsqrt(jnp.mean(raw * raw, axis=-1, keepdims=True) + 1e-06)
            hidden[block, :, cols] = (
                residual.astype(F32) + scaled * my_gain[:, cols]
            ).astype(BF16)
    count = rows // parts
    for j, piece in enumerate(piece_refs):
        block, other = divmod(j, parts)
        start = pl.multiple_of((scalars[0] ^ other) * count, count)
        piece[...] = hidden[block, pl.ds(start, count), :]


def norm_kernel(parts, scalars, gain_ref, pack_ref, *refs):
    pieces, hidden_ref, out_ref = refs[:-2], refs[-2], refs[-1]
    width = pieces[0].shape[1]
    model = hidden_ref.shape[1]
    total = 0.0
    for ref in pieces:
        value = ref[...].astype(F32)
        total += jnp.sum(value * value, axis=-1, keepdims=True)
    scale = lax.rsqrt(total / model + 1e-06)
    for j, ref in enumerate(pieces):
        block, other = divmod(j, parts)
        slot = (scalars[0] ^ other) * 2 + (scalars[1] ^ block)
        cols = pl.ds(pl.multiple_of(slot * width, width), width)
        hidden_ref[:, cols] = ref[...]
        out_ref[:, cols] = (ref[...].astype(F32) * scale * gain_ref[:, cols]).astype(BF16)
    out_ref[:, model:] = pack_ref[...]


def load_kernel(scalars, in_ref, out_ref, in_kept, out_kept, sems):
    pairs = []
    for source, target in ((in_ref, in_kept), (out_ref, out_kept)):
        pieces = 4
        step = source.shape[-2] // pieces
        for lead in range(source.shape[0]):
            for i in range(pieces):
                cut = pl.ds(i * step, step)
                pairs.append((source.at[lead, cut], target.at[lead, cut]))
    run_copies(pairs, sems)


def load_weights(scalars, expert_in, expert_out):
    return call(
        load_kernel,
        [shape(expert_in.shape, BF16), shape(expert_out.shape, BF16)],
        [scalars, expert_in, expert_out],
        far=(1, 2),
        scratch=[pltpu.SemaphoreType.DMA((4 * (expert_in.shape[0] + expert_out.shape[0]),))],
    )


def expert_kernel(blocks, scalars, in_ref, down_ref, *refs):
    x_refs = refs[:blocks]
    out_refs = refs[blocks:2 * blocks]
    rows_ref, acc_ref = refs[2 * blocks:]
    width = acc_ref.shape[1]
    units = in_ref.shape[2]
    chunk = min(units, 256)
    spans = []
    first = 0
    for ref in x_refs:
        span = slice(first, first + ref.shape[0])
        rows_ref[span, :] = ref[:, :width]
        spans.append(span)
        first += ref.shape[0]
    acc_ref[...] = jnp.zeros_like(acc_ref)

    @pl.loop(0, units // chunk)
    def _(step):
        cut = pl.ds(pl.multiple_of(step * chunk, chunk), chunk)
        gate = jnp.dot(rows_ref[...], in_ref[0, :, cut], preferred_element_type=F32)
        up = jnp.dot(rows_ref[...], in_ref[1, :, cut], preferred_element_type=F32)
        activated = (gate / (1.0 + jnp.exp(-gate)) * up).astype(BF16)
        acc_ref[...] += jnp.dot(activated, down_ref[0, cut, :], preferred_element_type=F32)

    experts = scalars[2]
    for x_ref, out_ref, span in zip(x_refs, out_refs, spans):
        pack = x_ref[:, width:].astype(F32)
        lane = lax.broadcasted_iota(jnp.int32, pack.shape, 1)
        chosen = (lane == scalars[3]) | (lane == scalars[3] + experts)
        weight = jnp.sum(jnp.where(chosen, pack, 0.0), axis=-1, keepdims=True)
        produced = acc_ref[span, :].astype(BF16).astype(F32)
        out_ref[...] = (produced * weight).astype(BF16)


def run_expert(scalars, blocks, weights_in, weights_out):
    width, units = weights_in.shape[1:]
    total = sum(b.shape[0] for b in blocks)
    return call(
        functools.partial(expert_kernel, len(blocks)),
        [shape((b.shape[0], width), BF16) for b in blocks],
        [scalars, weights_in, weights_out, *blocks],
        scratch=[pltpu.VMEM((total, width), BF16), pltpu.VMEM((total, width), F32)],
        flops=6 * total * width * units,
        limit=24 << 20,
    )


def ring_order(count):
    return list(range(0, count, 2)) + list(range(1, count, 2))[::-1]


def dense_experts(block, scalars, expert_in, expert_out):
    count = lax.axis_size("seq")
    order = ring_order(count)
    half = block.shape[0] // 2
    far = count // 2

    def hop(rows, steps):
        return lax.ppermute(
            rows, "seq", [(order[p], order[(p + steps) % count]) for p in range(count)]
        )

    ahead, behind = [block], [block]
    for distance in range(1, far):
        ahead.append(hop(ahead[-1], 1))
        behind.append(hop(behind[-1], -1))
    top = hop(ahead[-2][:half], 2)
    bottom = hop(behind[-2][half:], -2)
    weights = load_weights(scalars, expert_in[0], expert_out)
    blocks = [block] + ahead[1:] + behind[1:] + [top, bottom]
    made = run_expert(scalars, blocks, *weights)
    own, from_ahead, from_behind = made[0], made[1:far], made[far:2 * far - 1]
    top, bottom = made[-2:]
    early_going, early_coming = hop(bottom, 2), hop(top, -2)
    going, coming = hop(from_behind[-1], 1), hop(from_ahead[-1], -1)
    for distance in range(far - 2, 0, -1):
        to_front, to_back = from_behind[distance - 1], from_ahead[distance - 1]
        if distance == far - 2:
            going = jnp.concatenate(
                [
                    add_rows(going[:half], to_front[:half]),
                    add_rows(going[half:], to_front[half:], early_going),
                ]
            )
            coming = jnp.concatenate(
                [
                    add_rows(coming[:half], to_back[:half], early_coming),
                    add_rows(coming[half:], to_back[half:]),
                ]
            )
        else:
            going = add_rows(going, to_front)
            coming = add_rows(coming, to_back)
        going, coming = hop(going, 1), hop(coming, -1)
    return own, going, coming


def mix_kernel(scalars, hidden_ref, a_ref, b_ref, c_ref, *out_refs):
    width = out_refs[0].shape[1]
    for j, out_ref in enumerate(out_refs):
        cols = pl.ds(pl.multiple_of((scalars[0] ^ j) * width, width), width)
        mixed = a_ref[:, cols].astype(F32) + b_ref[:, cols].astype(F32)
        mixed += c_ref[:, cols].astype(F32)
        out_ref[...] = (hidden_ref[:, cols].astype(F32) + mixed).astype(BF16)


def join_kernel(scalars, *refs):
    pieces, out_ref, sems = refs[:-2], refs[-2], refs[-1]
    count = pieces[0].shape[0]
    pairs = []
    for j, piece in enumerate(pieces):
        rows = pl.ds(pl.multiple_of((scalars[0] ^ j) * count, count), count)
        pairs.append((piece, out_ref.at[rows, :]))
    run_copies(pairs, sems)


def slot_ids(block_routes, expert_count, capacity):
    row_count, top_count = block_routes.shape
    expert_ids = jnp.arange(expert_count, dtype=jnp.int32)
    onehot = (
        (block_routes[:, :, None] == expert_ids[None, None, :])
        .astype(jnp.int32)
        .reshape(row_count * top_count, expert_count)
    )
    earlier = jnp.cumsum(onehot, axis=0) - onehot
    ranking = jnp.sum(earlier * onehot, axis=1).reshape(row_count, top_count)
    return block_routes * capacity + ranking


def routed_experts(normed, my_routes, my_gates, expert_in, expert_out):
    sub_count, model_width = normed.shape
    expert_count = lax.axis_size("seq") * expert_in.shape[0]
    top_count = my_routes.shape[1]
    capacity = min(sub_count, max(2, 3 * sub_count * top_count // (2 * expert_count)))
    slot_count = expert_count * capacity
    my_slots = slot_ids(my_routes, expert_count, capacity)
    columns = jnp.arange(slot_count, dtype=jnp.int32)
    placer = jnp.sum(
        (my_slots[None, :, :] == columns[:, None, None]).astype(jnp.int32), axis=2
    ).astype(BF16)
    outgoing = (
        jnp.dot(placer, normed, preferred_element_type=F32)
        .astype(BF16)
        .reshape(expert_count, capacity, model_width)
    )
    arrived = lax.all_to_all(outgoing, "seq", split_axis=0, concat_axis=0, tiled=True)
    flat_rows = arrived.reshape(-1, model_width)
    gate_up = jnp.einsum("nd,gdf->gnf", flat_rows, expert_in[0], preferred_element_type=F32)
    activated = (jax.nn.silu(gate_up[0]) * gate_up[1]).astype(BF16)
    produced = jnp.dot(activated, expert_out[0], preferred_element_type=F32).astype(BF16)
    answered = produced.reshape(arrived.shape)
    returned = lax.all_to_all(answered, "seq", split_axis=0, concat_axis=0, tiled=True)
    picked = returned.reshape(slot_count, model_width)[my_slots.reshape(-1)].reshape(
        sub_count, top_count, model_width
    )
    return jnp.sum(picked.astype(F32) * my_gates[:, :, None], axis=1)


def prior_states(kept, partner):
    count = lax.axis_size("seq")

    def pass_on(state, distance):
        return lax.ppermute(
            state, "seq", [(i, i + 2 * distance) for i in range(count - 2 * distance)]
        )

    pairs = count // 2
    running = add_rows(kept, partner)
    if pairs <= 4:
        return [pass_on(running, distance) for distance in range(1, pairs)]
    terms = []
    distance = 1
    while distance < pairs:
        terms.append(pass_on(running, distance))
        running = add_rows(running, terms[-1])
        distance *= 2
    return terms


def per_device(
    residual,
    queries,
    key_vectors,
    value_vectors,
    head_gain,
    norm_gain,
    routes,
    route_gates,
    expert_in,
    expert_out,
):
    rows, width = residual.shape
    seq, parts = lax.axis_size("seq"), lax.axis_size("exp")
    count, half, model = rows // parts, width // 2, width * parts
    experts = seq * expert_in.shape[0]
    position = lax.axis_index("seq")
    my_index = lax.axis_index("exp")
    scalars = jnp.stack([my_index, position % 2, experts, position]).astype(jnp.int32)
    swap = [(i, i ^ 1) for i in range(seq)]

    state = shape((HEAD, half), BF16)
    kept, given = call(
        state_kernel, [state, state], [scalars, key_vectors, value_vectors], far=(1, 2),
        scratch=[pltpu.VMEM((rows, width), BF16)] * 2 + [pltpu.SemaphoreType.DMA((2,))],
        flops=2 * rows * width * HEAD,
    )
    partner = lax.ppermute(given, "seq", swap)
    [packed] = call(
        pack_kernel, [shape((rows, 4 * half), BF16)],
        [scalars, key_vectors, value_vectors, queries, residual], far=(1, 2, 3, 4),
        scratch=[pltpu.SemaphoreType.DMA((4,))],
    )
    came = lax.ppermute(packed, "seq", swap)
    before = prior_states(kept, partner)
    within, my_query, my_residual, my_gain, my_norm = call(
        within_kernel,
        [
            shape((2, rows, half), F32),
            shape((rows, half), BF16),
            shape((rows, half), BF16),
            shape((1, half), F32),
            shape((1, model), F32),
        ],
        [
            scalars, key_vectors, value_vectors, queries, residual, head_gain[None, :],
            norm_gain[None, :], came,
        ],
        far=(1, 2, 3, 4, 5, 6),
        scratch=[pltpu.VMEM((rows, half), BF16)] * 2 + [pltpu.SemaphoreType.DMA((6,))],
        flops=6 * rows * rows * width,
    )
    pieces = call(
        functools.partial(attend_kernel, parts, len(before)),
        [shape((count, half), BF16)] * (2 * parts),
        [scalars, within, my_query, my_residual, my_gain, came, kept, partner, *before],
        scratch=[pltpu.VMEM((2, rows, half), BF16)],
        flops=4 * rows * width * HEAD,
    )
    gathered = [pieces[0]]
    for j in range(1, 2 * parts):
        block, other = divmod(j, parts)
        gathered.append(
            lax.ppermute(
                pieces[j],
                ("seq", "exp"),
                [
                    (s * parts + e, (s ^ block) * parts + (e ^ other))
                    for s in range(seq)
                    for e in range(parts)
                ],
            )
        )

    my_routes = lax.dynamic_slice_in_dim(routes, my_index * count, count, 0)
    my_gates = lax.dynamic_slice_in_dim(route_gates, my_index * count, count, 0)
    weights = jnp.sum(
        jnp.where(
            my_routes[:, :, None] == jnp.arange(experts, dtype=jnp.int32),
            my_gates[:, :, None],
            0.0,
        ),
        axis=1,
    )
    high = lax.reduce_precision(weights, 8, 7)
    lanes = -(-2 * experts // HEAD) * HEAD
    pack = jnp.pad(
        jnp.concatenate([high, weights - high], axis=1), ((0, 0), (0, lanes - 2 * experts))
    ).astype(BF16)
    hidden, block = call(
        functools.partial(norm_kernel, parts),
        [shape((count, model), BF16), shape((count, model + lanes), BF16)],
        [scalars, my_norm, pack] + gathered,
    )
    if routes.shape[1] == experts:
        terms = dense_experts(block, scalars, expert_in, expert_out)
    else:
        mixed = routed_experts(block[:, :model], my_routes, my_gates, expert_in, expert_out)
        nothing = jnp.zeros_like(mixed)
        terms = (mixed, nothing, nothing)
    ready = call(
        mix_kernel, [shape((count, width), BF16)] * parts, [scalars, hidden, *terms]
    )
    returned = [ready[0]] + [
        lax.ppermute(ready[j], "exp", [(i, i ^ j) for i in range(parts)])
        for j in range(1, parts)
    ]
    [out] = call(
        join_kernel, [shape((rows, width), BF16)], [scalars] + returned, out_specs=[FAR],
        scratch=[pltpu.SemaphoreType.DMA((parts,))],
    )
    return out


def solution(mesh):
    placed = (
        P("seq", "exp"),
        P("seq", "exp"),
        P("seq", "exp"),
        P("seq", "exp"),
        P("exp"),
        P(),
        P("seq", None),
        P("seq", None),
        P("seq", None, None, None),
        P("seq", None, None),
    )
    return jax.shard_map(
        per_device, mesh=mesh, in_specs=placed, out_specs=P("seq", "exp"), check_vma=False
    )
```

```python
import functools

import jax
import jax.numpy as jnp
from jax import lax
from jax.experimental import pallas as pl
from jax.experimental.pallas import tpu as pltpu
from jax.sharding import PartitionSpec as P

HEAD = 128
F32 = jnp.float32
BF16 = jnp.bfloat16
WHOLE = pl.BlockSpec(memory_space=pltpu.VMEM)
FAR = pl.BlockSpec(memory_space=pltpu.HBM)
SCALAR = pl.BlockSpec(memory_space=pltpu.SMEM)


def call(kernel, outs, inputs, far=(), scratch=(), out_specs=None, flops=0, limit=16 << 20):
    moved = sum(a.size * a.dtype.itemsize for a in [*inputs, *outs])
    inputs = [
        pltpu.with_memory_space_constraint(a, pltpu.HBM) if i in far else a
        for i, a in enumerate(inputs)
    ]
    return pl.pallas_call(
        kernel,
        out_shape=outs,
        in_specs=[
            SCALAR if i == 0 else FAR if i in far else WHOLE for i in range(len(inputs))
        ],
        out_specs=out_specs or [WHOLE] * len(outs),
        scratch_shapes=scratch,
        compiler_params=pltpu.CompilerParams(vmem_limit_bytes=limit),
        cost_estimate=pl.CostEstimate(flops=flops, bytes_accessed=moved, transcendentals=0),
    )(*inputs)


def shape(dims, dtype):
    return jax.ShapeDtypeStruct(dims, dtype)


def split(value):
    high = value.astype(BF16)
    return high, (value - high.astype(F32)).astype(BF16)


def add_rows(*terms):
    return sum(t.astype(F32) for t in terms).astype(BF16)


def run_copies(pairs, sems):
    copies = [pltpu.make_async_copy(a, b, sems.at[i]) for i, (a, b) in enumerate(pairs)]
    for copy in copies:
        copy.start()
    for copy in copies:
        copy.wait()


def state_kernel(scalars, key_ref, value_ref, kept_ref, given_ref, keys, values, sems):
    run_copies([(key_ref, keys), (value_ref, values)], sems)
    width = keys.shape[1] // 2
    place = scalars[1]
    for h in range(keys.shape[1] // HEAD):
        cols = slice(h * HEAD, (h + 1) * HEAD)
        state = lax.dot_general(
            keys[:, cols], values[:, cols], (((0,), (0,)), ((), ())), preferred_element_type=F32
        ).astype(BF16)
        half, inner = divmod(h * HEAD, width)

        @pl.when(place == half)
        def _():
            kept_ref[:, inner:inner + HEAD] = state

        @pl.when(place != half)
        def _():
            given_ref[:, inner:inner + HEAD] = state


def pack_kernel(scalars, *refs):
    sources, out_ref, sems = refs[:-2], refs[-2], refs[-1]
    width = out_ref.shape[1] // len(sources)
    theirs = pl.ds(pl.multiple_of((1 - scalars[1]) * width, width), width)
    run_copies(
        [
            (ref.at[:, theirs], out_ref.at[:, i * width:(i + 1) * width])
            for i, ref in enumerate(sources)
        ],
        sems,
    )


def within_kernel(
    scalars, key_ref, value_ref, query_ref, residual_ref, gain_ref, norm_ref, came_ref,
    out_ref, my_query, my_residual, my_gain, my_norm, keys, values, sems
):
    rows, width = my_query.shape
    mine = pl.ds(pl.multiple_of(scalars[1] * width, width), width)
    run_copies(
        [
            (key_ref.at[:, mine], keys),
            (value_ref.at[:, mine], values),
            (query_ref.at[:, mine], my_query),
            (residual_ref.at[:, mine], my_residual),
            (gain_ref.at[:, mine], my_gain),
            (norm_ref, my_norm),
        ],
        sems,
    )
    causal = lax.broadcasted_iota(jnp.int32, (rows, rows), 0) >= lax.broadcasted_iota(
        jnp.int32, (rows, rows), 1
    )
    for block in range(2):
        for inner in range(0, width, HEAD):
            cols = slice(inner, inner + HEAD)
            if block == 0:
                query, key, value = my_query[:, cols], keys[:, cols], values[:, cols]
            else:
                key, value, query = (
                    came_ref[:, i * width + inner:i * width + inner + HEAD] for i in range(3)
                )
            scores = lax.dot_general(
                query, key, (((1,), (1,)), ((), ())), preferred_element_type=F32
            )
            high, low = split(jnp.where(causal, scores, 0.0))
            out_ref[block, :, cols] = jnp.dot(
                high, value, preferred_element_type=F32
            ) + jnp.dot(low, value, preferred_element_type=F32)


def attend_kernel(
    parts, earlier, scalars, loaded_ref, within_ref, my_query, my_residual, my_gain, came_ref, kept_ref,
    partner_ref, *refs
):
    before_refs, piece_refs, hidden = refs[:earlier], refs[earlier:-1], refs[-1]
    rows, width = my_query.shape
    before = sum(ref[...].astype(F32) for ref in before_refs)
    first = scalars[1] == 0
    for block in range(2):
        extra = (partner_ref if block == 0 else kept_ref)[...].astype(F32)
        use = jnp.logical_not(first) if block == 0 else first
        state = before + jnp.where(use, extra, 0.0)
        for inner in range(0, width, HEAD):
            cols = slice(inner, inner + HEAD)
            if block == 0:
                query, residual = my_query[:, cols], my_residual[:, cols]
            else:
                query, residual = (
                    came_ref[:, i * width + inner:i * width + inner + HEAD] for i in (2, 3)
                )
            high, low = split(state[:, cols])
            raw = (
                jnp.dot(query, high, preferred_element_type=F32)
                + jnp.dot(query, low, preferred_element_type=F32)
                + within_ref[block, :, cols]
            )
            scaled = raw * lax.rsqrt(jnp.mean(raw * raw, axis=-1, keepdims=True) + 1e-06)
            hidden[block, :, cols] = (
                residual.astype(F32) + scaled * my_gain[:, cols]
            ).astype(BF16)
    count = rows // parts
    for j, piece in enumerate(piece_refs):
        block, other = divmod(j, parts)
        start = pl.multiple_of((scalars[0] ^ other) * count, count)
        piece[...] = hidden[block, pl.ds(start, count), :]


def norm_kernel(parts, scalars, gain_ref, pack_ref, *refs):
    pieces, hidden_ref, out_ref = refs[:-2], refs[-2], refs[-1]
    width = pieces[0].shape[1]
    model = hidden_ref.shape[1]
    total = 0.0
    for ref in pieces:
        value = ref[...].astype(F32)
        total += jnp.sum(value * value, axis=-1, keepdims=True)
    scale = lax.rsqrt(total / model + 1e-06)
    for j, ref in enumerate(pieces):
        block, other = divmod(j, parts)
        slot = (scalars[0] ^ other) * 2 + (scalars[1] ^ block)
        cols = pl.ds(pl.multiple_of(slot * width, width), width)
        hidden_ref[:, cols] = ref[...]
        out_ref[:, cols] = (ref[...].astype(F32) * scale * gain_ref[:, cols]).astype(BF16)
    out_ref[:, model:] = pack_ref[...]


def load_kernel(scalars, in_ref, out_ref, after_ref, in_kept, out_kept, done_ref, sems):
    done_ref[...] = jnp.zeros_like(done_ref)
    pairs = []
    for source, target in ((in_ref, in_kept), (out_ref, out_kept)):
        pieces = 4
        step = source.shape[-2] // pieces
        for lead in range(source.shape[0]):
            for i in range(pieces):
                cut = pl.ds(i * step, step)
                pairs.append((source.at[lead, cut], target.at[lead, cut]))
    run_copies(pairs, sems)


def load_weights(scalars, expert_in, expert_out, after):
    return call(
        load_kernel,
        [shape(expert_in.shape, BF16), shape(expert_out.shape, BF16), shape((8, HEAD), F32)],
        [scalars, expert_in, expert_out, after],
        far=(1, 2),
        scratch=[pltpu.SemaphoreType.DMA((4 * (expert_in.shape[0] + expert_out.shape[0]),))],
    )


def expert_kernel(blocks, scalars, in_ref, down_ref, *refs):
    x_refs = refs[:blocks]
    out_refs = refs[blocks:2 * blocks]
    rows_ref, acc_ref = refs[2 * blocks:]
    width = acc_ref.shape[1]
    units = in_ref.shape[2]
    chunk = min(units, 256)
    spans = []
    first = 0
    for ref in x_refs:
        span = slice(first, first + ref.shape[0])
        rows_ref[span, :] = ref[:, :width]
        spans.append(span)
        first += ref.shape[0]
    acc_ref[...] = jnp.zeros_like(acc_ref)

    @pl.loop(0, units // chunk)
    def _(step):
        cut = pl.ds(pl.multiple_of(step * chunk, chunk), chunk)
        gate = jnp.dot(rows_ref[...], in_ref[0, :, cut], preferred_element_type=F32)
        up = jnp.dot(rows_ref[...], in_ref[1, :, cut], preferred_element_type=F32)
        activated = (gate / (1.0 + jnp.exp(-gate)) * up).astype(BF16)
        acc_ref[...] += jnp.dot(activated, down_ref[0, cut, :], preferred_element_type=F32)

    experts = scalars[2]
    for x_ref, out_ref, span in zip(x_refs, out_refs, spans):
        pack = x_ref[:, width:].astype(F32)
        lane = lax.broadcasted_iota(jnp.int32, pack.shape, 1)
        chosen = (lane == scalars[3]) | (lane == scalars[3] + experts)
        weight = jnp.sum(jnp.where(chosen, pack, 0.0), axis=-1, keepdims=True)
        produced = acc_ref[span, :].astype(BF16).astype(F32)
        out_ref[...] = (produced * weight).astype(BF16)


def run_expert(scalars, blocks, weights_in, weights_out):
    width, units = weights_in.shape[1:]
    total = sum(b.shape[0] for b in blocks)
    return call(
        functools.partial(expert_kernel, len(blocks)),
        [shape((b.shape[0], width), BF16) for b in blocks],
        [scalars, weights_in, weights_out, *blocks],
        scratch=[pltpu.VMEM((total, width), BF16), pltpu.VMEM((total, width), F32)],
        flops=6 * total * width * units,
        limit=24 << 20,
    )


def ring_order(count):
    return list(range(0, count, 2)) + list(range(1, count, 2))[::-1]


def dense_experts(block, scalars, weights):
    count = lax.axis_size("seq")
    order = ring_order(count)
    half = block.shape[0] // 2
    far = count // 2

    def hop(rows, steps):
        return lax.ppermute(
            rows, "seq", [(order[p], order[(p + steps) % count]) for p in range(count)]
        )

    ahead, behind = [block], [block]
    for distance in range(1, far):
        ahead.append(hop(ahead[-1], 1))
        behind.append(hop(behind[-1], -1))
    top = hop(ahead[-2][:half], 2)
    bottom = hop(behind[-2][half:], -2)
    blocks = [block] + ahead[1:] + behind[1:] + [top, bottom]
    made = run_expert(scalars, blocks, *weights)
    own, from_ahead, from_behind = made[0], made[1:far], made[far:2 * far - 1]
    top, bottom = made[-2:]
    early_going, early_coming = hop(bottom, 2), hop(top, -2)
    going, coming = hop(from_behind[-1], 1), hop(from_ahead[-1], -1)
    for distance in range(far - 2, 0, -1):
        to_front, to_back = from_behind[distance - 1], from_ahead[distance - 1]
        if distance == far - 2:
            going = jnp.concatenate(
                [
                    add_rows(going[:half], to_front[:half]),
                    add_rows(going[half:], to_front[half:], early_going),
                ]
            )
            coming = jnp.concatenate(
                [
                    add_rows(coming[:half], to_back[:half], early_coming),
                    add_rows(coming[half:], to_back[half:]),
                ]
            )
        else:
            going = add_rows(going, to_front)
            coming = add_rows(coming, to_back)
        going, coming = hop(going, 1), hop(coming, -1)
    return own, going, coming


def mix_kernel(scalars, hidden_ref, a_ref, b_ref, c_ref, *out_refs):
    width = out_refs[0].shape[1]
    for j, out_ref in enumerate(out_refs):
        cols = pl.ds(pl.multiple_of((scalars[0] ^ j) * width, width), width)
        mixed = a_ref[:, cols].astype(F32) + b_ref[:, cols].astype(F32)
        mixed += c_ref[:, cols].astype(F32)
        out_ref[...] = (hidden_ref[:, cols].astype(F32) + mixed).astype(BF16)


def join_kernel(scalars, *refs):
    pieces, out_ref, sems = refs[:-2], refs[-2], refs[-1]
    count = pieces[0].shape[0]
    pairs = []
    for j, piece in enumerate(pieces):
        rows = pl.ds(pl.multiple_of((scalars[0] ^ j) * count, count), count)
        pairs.append((piece, out_ref.at[rows, :]))
    run_copies(pairs, sems)


def slot_ids(block_routes, expert_count, capacity):
    row_count, top_count = block_routes.shape
    expert_ids = jnp.arange(expert_count, dtype=jnp.int32)
    onehot = (
        (block_routes[:, :, None] == expert_ids[None, None, :])
        .astype(jnp.int32)
        .reshape(row_count * top_count, expert_count)
    )
    earlier = jnp.cumsum(onehot, axis=0) - onehot
    ranking = jnp.sum(earlier * onehot, axis=1).reshape(row_count, top_count)
    return block_routes * capacity + ranking


def routed_experts(normed, my_routes, my_gates, expert_in, expert_out):
    sub_count, model_width = normed.shape
    expert_count = lax.axis_size("seq") * expert_in.shape[0]
    top_count = my_routes.shape[1]
    capacity = min(sub_count, max(2, 3 * sub_count * top_count // (2 * expert_count)))
    slot_count = expert_count * capacity
    my_slots = slot_ids(my_routes, expert_count, capacity)
    columns = jnp.arange(slot_count, dtype=jnp.int32)
    placer = jnp.sum(
        (my_slots[None, :, :] == columns[:, None, None]).astype(jnp.int32), axis=2
    ).astype(BF16)
    outgoing = (
        jnp.dot(placer, normed, preferred_element_type=F32)
        .astype(BF16)
        .reshape(expert_count, capacity, model_width)
    )
    arrived = lax.all_to_all(outgoing, "seq", split_axis=0, concat_axis=0, tiled=True)
    flat_rows = arrived.reshape(-1, model_width)
    gate_up = jnp.einsum("nd,gdf->gnf", flat_rows, expert_in[0], preferred_element_type=F32)
    activated = (jax.nn.silu(gate_up[0]) * gate_up[1]).astype(BF16)
    produced = jnp.dot(activated, expert_out[0], preferred_element_type=F32).astype(BF16)
    answered = produced.reshape(arrived.shape)
    returned = lax.all_to_all(answered, "seq", split_axis=0, concat_axis=0, tiled=True)
    picked = returned.reshape(slot_count, model_width)[my_slots.reshape(-1)].reshape(
        sub_count, top_count, model_width
    )
    return jnp.sum(picked.astype(F32) * my_gates[:, :, None], axis=1)


def prior_states(kept, partner):
    count = lax.axis_size("seq")

    def pass_on(state, distance):
        return lax.ppermute(
            state, "seq", [(i, i + 2 * distance) for i in range(count - 2 * distance)]
        )

    pairs = count // 2
    running = add_rows(kept, partner)
    if pairs <= 4:
        return [pass_on(running, distance) for distance in range(1, pairs)]
    terms = []
    distance = 1
    while distance < pairs:
        terms.append(pass_on(running, distance))
        running = add_rows(running, terms[-1])
        distance *= 2
    return terms


def per_device(
    residual,
    queries,
    key_vectors,
    value_vectors,
    head_gain,
    norm_gain,
    routes,
    route_gates,
    expert_in,
    expert_out,
):
    rows, width = residual.shape
    seq, parts = lax.axis_size("seq"), lax.axis_size("exp")
    count, half, model = rows // parts, width // 2, width * parts
    experts = seq * expert_in.shape[0]
    position = lax.axis_index("seq")
    my_index = lax.axis_index("exp")
    scalars = jnp.stack([my_index, position % 2, experts, position]).astype(jnp.int32)
    swap = [(i, i ^ 1) for i in range(seq)]

    state = shape((HEAD, half), BF16)
    kept, given = call(
        state_kernel, [state, state], [scalars, key_vectors, value_vectors], far=(1, 2),
        scratch=[pltpu.VMEM((rows, width), BF16)] * 2 + [pltpu.SemaphoreType.DMA((2,))],
        flops=2 * rows * width * HEAD,
    )
    partner = lax.ppermute(given, "seq", swap)
    [packed] = call(
        pack_kernel, [shape((rows, 4 * half), BF16)],
        [scalars, key_vectors, value_vectors, queries, residual], far=(1, 2, 3, 4),
        scratch=[pltpu.SemaphoreType.DMA((4,))],
    )
    came = lax.ppermute(packed, "seq", swap)
    before = prior_states(kept, partner)
    within, my_query, my_residual, my_gain, my_norm = call(
        within_kernel,
        [
            shape((2, rows, half), F32),
            shape((rows, half), BF16),
            shape((rows, half), BF16),
            shape((1, half), F32),
            shape((1, model), F32),
        ],
        [
            scalars, key_vectors, value_vectors, queries, residual, head_gain[None, :],
            norm_gain[None, :], came,
        ],
        far=(1, 2, 3, 4, 5, 6),
        scratch=[pltpu.VMEM((rows, half), BF16)] * 2 + [pltpu.SemaphoreType.DMA((6,))],
        flops=6 * rows * rows * width,
    )
    dense = routes.shape[1] == experts
    if dense:
        *weights, loaded = load_weights(scalars, expert_in[0], expert_out, partner)
    else:
        loaded = jnp.zeros((8, HEAD), F32)
    pieces = call(
        functools.partial(attend_kernel, parts, len(before)),
        [shape((count, half), BF16)] * (2 * parts),
        [scalars, loaded, within, my_query, my_residual, my_gain, came, kept, partner, *before],
        scratch=[pltpu.VMEM((2, rows, half), BF16)],
        flops=4 * rows * width * HEAD,
    )
    gathered = [pieces[0]]
    for j in range(1, 2 * parts):
        block, other = divmod(j, parts)
        gathered.append(
            lax.ppermute(
                pieces[j],
                ("seq", "exp"),
                [
                    (s * parts + e, (s ^ block) * parts + (e ^ other))
                    for s in range(seq)
                    for e in range(parts)
                ],
            )
        )

    my_routes = lax.dynamic_slice_in_dim(routes, my_index * count, count, 0)
    my_gates = lax.dynamic_slice_in_dim(route_gates, my_index * count, count, 0)
    mixing = jnp.sum(
        jnp.where(
            my_routes[:, :, None] == jnp.arange(experts, dtype=jnp.int32),
            my_gates[:, :, None],
            0.0,
        ),
        axis=1,
    )
    high = lax.reduce_precision(mixing, 8, 7)
    lanes = -(-2 * experts // HEAD) * HEAD
    pack = jnp.pad(
        jnp.concatenate([high, mixing - high], axis=1), ((0, 0), (0, lanes - 2 * experts))
    ).astype(BF16)
    hidden, block = call(
        functools.partial(norm_kernel, parts),
        [shape((count, model), BF16), shape((count, model + lanes), BF16)],
        [scalars, my_norm, pack] + gathered,
    )
    if dense:
        terms = dense_experts(block, scalars, weights)
    else:
        mixed = routed_experts(block[:, :model], my_routes, my_gates, expert_in, expert_out)
        nothing = jnp.zeros_like(mixed)
        terms = (mixed, nothing, nothing)
    ready = call(
        mix_kernel, [shape((count, width), BF16)] * parts, [scalars, hidden, *terms]
    )
    returned = [ready[0]] + [
        lax.ppermute(ready[j], "exp", [(i, i ^ j) for i in range(parts)])
        for j in range(1, parts)
    ]
    [out] = call(
        join_kernel, [shape((rows, width), BF16)], [scalars] + returned, out_specs=[FAR],
        scratch=[pltpu.SemaphoreType.DMA((parts,))],
    )
    return out


def solution(mesh):
    placed = (
        P("seq", "exp"),
        P("seq", "exp"),
        P("seq", "exp"),
        P("seq", "exp"),
        P("exp"),
        P(),
        P("seq", None),
        P("seq", None),
        P("seq", None, None, None),
        P("seq", None, None),
    )
    return jax.shard_map(
        per_device, mesh=mesh, in_specs=placed, out_specs=P("seq", "exp"), check_vma=False
    )
```

```python
import functools

import jax
import jax.numpy as jnp
from jax import lax
from jax.experimental import pallas as pl
from jax.experimental.pallas import tpu as pltpu
from jax.sharding import PartitionSpec as P

HEAD = 128
F32 = jnp.float32
BF16 = jnp.bfloat16
WHOLE = pl.BlockSpec(memory_space=pltpu.VMEM)
FAR = pl.BlockSpec(memory_space=pltpu.HBM)
SCALAR = pl.BlockSpec(memory_space=pltpu.SMEM)


def call(kernel, outs, inputs, far=(), small=(), scratch=(), out_specs=None, flops=0, limit=16 << 20):
    moved = sum(a.size * a.dtype.itemsize for a in [*inputs, *outs])
    inputs = [
        pltpu.with_memory_space_constraint(a, pltpu.HBM) if i in far else a
        for i, a in enumerate(inputs)
    ]
    return pl.pallas_call(
        kernel,
        out_shape=outs,
        in_specs=[
            SCALAR if i == 0 or i in small else FAR if i in far else WHOLE
            for i in range(len(inputs))
        ],
        out_specs=out_specs or [WHOLE] * len(outs),
        scratch_shapes=scratch,
        compiler_params=pltpu.CompilerParams(vmem_limit_bytes=limit),
        cost_estimate=pl.CostEstimate(flops=flops, bytes_accessed=moved, transcendentals=0),
    )(*inputs)


def shape(dims, dtype):
    return jax.ShapeDtypeStruct(dims, dtype)


def split(value):
    high = value.astype(BF16)
    return high, (value - high.astype(F32)).astype(BF16)


def add_rows(*terms):
    return sum(t.astype(F32) for t in terms).astype(BF16)


def run_copies(pairs, sems):
    copies = [pltpu.make_async_copy(a, b, sems.at[i]) for i, (a, b) in enumerate(pairs)]
    for copy in copies:
        copy.start()
    for copy in copies:
        copy.wait()


def open_kernel(
    scalars, key_ref, value_ref, query_ref, residual_ref, gain_ref, norm_ref,
    kept_ref, given_ref, theirs_ref, mine_ref, my_gain, my_norm, keys, values, sems
):
    rows, full = keys.shape
    width = full // 2
    place = scalars[1]
    my_cols = pl.ds(pl.multiple_of(place * width, width), width)
    their_cols = pl.ds(pl.multiple_of((1 - place) * width, width), width)
    pairs = [(key_ref, keys), (value_ref, values)]
    for i, ref in enumerate((key_ref, value_ref, query_ref, residual_ref)):
        spot = slice(i * width, (i + 1) * width)
        pairs.append((ref.at[:, their_cols], theirs_ref.at[:, spot]))
        pairs.append((ref.at[:, my_cols], mine_ref.at[:, spot]))
    pairs += [(gain_ref.at[:, my_cols], my_gain), (norm_ref, my_norm)]
    copies = [pltpu.make_async_copy(a, b, sems.at[i]) for i, (a, b) in enumerate(pairs)]
    for copy in copies:
        copy.start()
    for copy in copies[:2]:
        copy.wait()
    for h in range(full // HEAD):
        cols = slice(h * HEAD, (h + 1) * HEAD)
        state = lax.dot_general(
            keys[:, cols], values[:, cols], (((0,), (0,)), ((), ())), preferred_element_type=F32
        ).astype(BF16)
        half, inner = divmod(h * HEAD, width)

        @pl.when(place == half)
        def _():
            kept_ref[:, inner:inner + HEAD] = state

        @pl.when(place != half)
        def _():
            given_ref[:, inner:inner + HEAD] = state

    for copy in copies[2:]:
        copy.wait()


def within_kernel(scalars, mine_ref, came_ref, out_ref):
    rows, width = out_ref.shape[1:]
    causal = lax.broadcasted_iota(jnp.int32, (rows, rows), 0) >= lax.broadcasted_iota(
        jnp.int32, (rows, rows), 1
    )
    for block, ref in enumerate((mine_ref, came_ref)):
        for inner in range(0, width, HEAD):
            key, value, query = (
                ref[:, i * width + inner:i * width + inner + HEAD] for i in range(3)
            )
            scores = lax.dot_general(
                query, key, (((1,), (1,)), ((), ())), preferred_element_type=F32
            )
            high, low = split(jnp.where(causal, scores, 0.0))
            out_ref[block, :, inner:inner + HEAD] = jnp.dot(
                high, value, preferred_element_type=F32
            ) + jnp.dot(low, value, preferred_element_type=F32)


def attend_kernel(
    parts, earlier, scalars, within_ref, mine_ref, came_ref, my_gain, kept_ref, partner_ref, *refs
):
    before_refs, piece_refs, hidden = refs[:earlier], refs[earlier:-1], refs[-1]
    rows, width = hidden.shape[1:]
    before = sum(ref[...].astype(F32) for ref in before_refs)
    first = scalars[1] == 0
    for block, ref in enumerate((mine_ref, came_ref)):
        extra = (partner_ref if block == 0 else kept_ref)[...].astype(F32)
        use = jnp.logical_not(first) if block == 0 else first
        state = before + jnp.where(use, extra, 0.0)
        for inner in range(0, width, HEAD):
            cols = slice(inner, inner + HEAD)
            query, residual = (
                ref[:, i * width + inner:i * width + inner + HEAD] for i in (2, 3)
            )
            high, low = split(state[:, cols])
            raw = (
                jnp.dot(query, high, preferred_element_type=F32)
                + jnp.dot(query, low, preferred_element_type=F32)
                + within_ref[block, :, cols]
            )
            scaled = raw * lax.rsqrt(jnp.mean(raw * raw, axis=-1, keepdims=True) + 1e-06)
            hidden[block, :, cols] = (
                residual.astype(F32) + scaled * my_gain[:, cols]
            ).astype(BF16)
    count = rows // parts
    for j, piece in enumerate(piece_refs):
        rows_j = pl.ds(pl.multiple_of((scalars[0] ^ j) * count, count), count)
        for block in range(2):
            side = first if block == 0 else jnp.logical_not(first)

            @pl.when(side)
            def _():
                piece[:count, :] = hidden[block, rows_j, :]

            @pl.when(jnp.logical_not(side))
            def _():
                piece[count:, :] = hidden[block, rows_j, :]


def load_kernel(scalars, source, after_ref, target, done_ref, sems):
    done_ref[...] = jnp.zeros_like(done_ref)
    pieces = sems.shape[0]
    step = source.shape[0] // pieces
    run_copies(
        [
            (source.at[pl.ds(i * step, step)], target.at[pl.ds(i * step, step)])
            for i in range(pieces)
        ],
        sems,
    )


def load_near(scalars, source, after):
    return call(
        load_kernel, [shape(source.shape, source.dtype), shape((8, HEAD), F32)],
        [scalars, source, after], far=(1,), scratch=[pltpu.SemaphoreType.DMA((8,))],
    )


def expert_kernel(
    parts, far, scalars, sources, in_ref, down_ref, gain_ref, *refs
):
    count = 2 * far
    messages = refs[:count + 1]
    hidden_ref = refs[count + 1]
    out_refs = refs[count + 2:2 * count + 3]
    rows_ref, gates_ref, act_ref, made_ref = refs[2 * count + 3:]
    model = rows_ref.shape[1]
    width = model // (2 * parts)
    pair = messages[0].shape[0]
    half = pair // 2
    gates_ref[...] = jnp.zeros_like(gates_ref)
    for i, ref in enumerate(messages):
        source = sources[i]
        base = (source // 2) * pair + (half if i == count else 0)
        rows = pl.ds(pl.multiple_of(base, half), ref.shape[0])
        for j in range(parts):
            start = ((scalars[0] ^ j) * 2 + source % 2) * width
            cols = pl.ds(pl.multiple_of(start, width), width)
            rows_ref[rows, cols] = ref[:, j * width:(j + 1) * width]
        gates_ref[rows, :] += ref[:, parts * width:].astype(F32)
    hidden_ref[...] = rows_ref[pl.ds(pl.multiple_of(sources[0] * half, half), half), :]
    for s in range(count):
        rows = slice(s * half, (s + 1) * half)
        value = rows_ref[rows, :].astype(F32)
        scale = lax.rsqrt(jnp.mean(value * value, axis=-1, keepdims=True) + 1e-06)
        rows_ref[rows, :] = (value * scale * gain_ref[...]).astype(BF16)
    lane = lax.broadcasted_iota(jnp.int32, gates_ref.shape, 1)
    chosen = (lane == scalars[3]) | (lane == scalars[3] + scalars[2])
    weight = jnp.sum(jnp.where(chosen, gates_ref[...], 0.0), axis=-1, keepdims=True)

    units = in_ref.shape[1]
    chunk = min(units, 256)

    @pl.loop(0, units // chunk)
    def _(step):
        cut = pl.ds(pl.multiple_of(step * chunk, chunk), chunk)
        gate = jnp.dot(rows_ref[...], in_ref[:model, cut], preferred_element_type=F32)
        up = jnp.dot(rows_ref[...], in_ref[model:, cut], preferred_element_type=F32)
        act_ref[:, cut] = (gate / (1.0 + jnp.exp(-gate)) * up).astype(BF16)

    chunk = min(model, 512)

    @pl.loop(0, model // chunk)
    def _(step):
        cut = pl.ds(pl.multiple_of(step * chunk, chunk), chunk)
        produced = jnp.dot(act_ref[...], down_ref[:, cut], preferred_element_type=F32)
        made_ref[:, cut] = (produced.astype(BF16).astype(F32) * weight).astype(BF16)

    quarter = half // 2
    for i, out_ref in enumerate(out_refs):
        base = sources[i] * half + (quarter if i == count else 0)
        out_ref[...] = made_ref[pl.ds(pl.multiple_of(base, quarter), out_ref.shape[0]), :]


def run_expert(scalars, sources, messages, weights_in, weights_out, norm_gain):
    parts, far = lax.axis_size("exp"), lax.axis_size("seq") // 2
    units, model = weights_out.shape
    half = messages[0].shape[0] // 2
    total = 2 * far * half
    block, part = shape((half, model), BF16), shape((half // 2, model), BF16)
    return call(
        functools.partial(expert_kernel, parts, far),
        [block] + [block] * (2 * far - 1) + [part] * 2,
        [scalars, sources, weights_in, weights_out, norm_gain, *messages],
        small=(1,),
        scratch=[
            pltpu.VMEM((total, model), BF16),
            pltpu.VMEM((total, messages[0].shape[1] - model // 2), F32),
            pltpu.VMEM((total, units), BF16),
            pltpu.VMEM((total, model), BF16),
        ],
        flops=6 * total * model * units,
        limit=24 << 20,
    )


def ring_order(count):
    return list(range(0, count, 2)) + list(range(1, count, 2))[::-1]


def dense_experts(message, scalars, expert_in, expert_out, norm_gain):
    count = lax.axis_size("seq")
    order = ring_order(count)
    far = count // 2
    half = message.shape[0] // 2

    def hop(rows, steps):
        return lax.ppermute(
            rows, "seq", [(order[p], order[(p + steps) % count]) for p in range(count)]
        )

    reach = [0] + [-d for d in range(1, far)] + [d for d in range(1, far)] + [far, far]
    table = [[order[(order.index(s) + d) % count] for d in reach] for s in range(count)]
    sources = jnp.asarray(table, jnp.int32)[scalars[3]]

    weights = [expert_in.reshape(-1, expert_in.shape[-1]), expert_out]
    near, after = [], message
    forward, backward = [message], [message]
    for distance in range(1, far):
        ahead, behind = hop(forward[-1], 1), hop(backward[-1], -1)
        if weights:
            loaded, sign = load_near(scalars, weights.pop(0), after)
            near.append(loaded)
            ahead, behind, after = lax.optimization_barrier((ahead, behind, sign))
        forward.append(ahead)
        backward.append(behind)
    top = hop(forward[-2][:half], 2)
    bottom = hop(backward[-2][half:], -2)
    messages = [message] + forward[1:] + backward[1:] + [top, bottom]
    hidden, *made = run_expert(scalars, sources, messages, *near, norm_gain)
    own, to_back, to_front = made[0], made[1:far], made[far:2 * far - 1]
    top, bottom = made[-2:]
    half = half // 2
    early_going, early_coming = hop(bottom, 2), hop(top, -2)
    going, coming = hop(to_front[-1], 1), hop(to_back[-1], -1)
    for distance in range(far - 2, 0, -1):
        front, back = to_front[distance - 1], to_back[distance - 1]
        if distance == far - 2:
            going = jnp.concatenate(
                [
                    add_rows(going[:half], front[:half]),
                    add_rows(going[half:], front[half:], early_going),
                ]
            )
            coming = jnp.concatenate(
                [
                    add_rows(coming[:half], back[:half], early_coming),
                    add_rows(coming[half:], back[half:]),
                ]
            )
        else:
            going = add_rows(going, front)
            coming = add_rows(coming, back)
        going, coming = lax.optimization_barrier((going, coming))
        going, coming = hop(going, 1), hop(coming, -1)
    return hidden, own, going, coming


def mix_kernel(scalars, hidden_ref, a_ref, b_ref, c_ref, *out_refs):
    width = out_refs[0].shape[1]
    for j, out_ref in enumerate(out_refs):
        cols = pl.ds(pl.multiple_of((scalars[0] ^ j) * width, width), width)
        mixed = a_ref[:, cols].astype(F32) + b_ref[:, cols].astype(F32)
        mixed += c_ref[:, cols].astype(F32)
        out_ref[...] = (hidden_ref[:, cols].astype(F32) + mixed).astype(BF16)


def join_kernel(scalars, *refs):
    pieces, out_ref, sems = refs[:-2], refs[-2], refs[-1]
    count = pieces[0].shape[0]
    pairs = []
    for j, piece in enumerate(pieces):
        rows = pl.ds(pl.multiple_of((scalars[0] ^ j) * count, count), count)
        pairs.append((piece, out_ref.at[rows, :]))
    run_copies(pairs, sems)


def slot_ids(block_routes, expert_count, capacity):
    row_count, top_count = block_routes.shape
    expert_ids = jnp.arange(expert_count, dtype=jnp.int32)
    onehot = (
        (block_routes[:, :, None] == expert_ids[None, None, :])
        .astype(jnp.int32)
        .reshape(row_count * top_count, expert_count)
    )
    earlier = jnp.cumsum(onehot, axis=0) - onehot
    ranking = jnp.sum(earlier * onehot, axis=1).reshape(row_count, top_count)
    return block_routes * capacity + ranking


def routed_experts(normed, my_routes, my_gates, expert_in, expert_out):
    sub_count, model_width = normed.shape
    expert_count = lax.axis_size("seq") * expert_in.shape[0]
    top_count = my_routes.shape[1]
    capacity = min(sub_count, max(2, 3 * sub_count * top_count // (2 * expert_count)))
    slot_count = expert_count * capacity
    my_slots = slot_ids(my_routes, expert_count, capacity)
    columns = jnp.arange(slot_count, dtype=jnp.int32)
    placer = jnp.sum(
        (my_slots[None, :, :] == columns[:, None, None]).astype(jnp.int32), axis=2
    ).astype(BF16)
    outgoing = (
        jnp.dot(placer, normed, preferred_element_type=F32)
        .astype(BF16)
        .reshape(expert_count, capacity, model_width)
    )
    arrived = lax.all_to_all(outgoing, "seq", split_axis=0, concat_axis=0, tiled=True)
    flat_rows = arrived.reshape(-1, model_width)
    gate_up = jnp.einsum("nd,gdf->gnf", flat_rows, expert_in[0], preferred_element_type=F32)
    activated = (jax.nn.silu(gate_up[0]) * gate_up[1]).astype(BF16)
    produced = jnp.dot(activated, expert_out[0], preferred_element_type=F32).astype(BF16)
    answered = produced.reshape(arrived.shape)
    returned = lax.all_to_all(answered, "seq", split_axis=0, concat_axis=0, tiled=True)
    picked = returned.reshape(slot_count, model_width)[my_slots.reshape(-1)].reshape(
        sub_count, top_count, model_width
    )
    return jnp.sum(picked.astype(F32) * my_gates[:, :, None], axis=1)


def prior_states(kept, partner):
    count = lax.axis_size("seq")

    def pass_on(state, distance):
        return lax.ppermute(
            state, "seq", [(i, i + 2 * distance) for i in range(count - 2 * distance)]
        )

    pairs = count // 2
    running = add_rows(kept, partner)
    if pairs <= 4:
        return [pass_on(running, distance) for distance in reversed(range(1, pairs))]
    terms = []
    distance = 1
    while distance < pairs:
        terms.append(pass_on(running, distance))
        running = add_rows(running, terms[-1])
        distance *= 2
    return terms


def spread_rows(pieces):
    parts = len(pieces)
    bit = parts // 2
    held = {(j, 0): piece for j, piece in enumerate(pieces)}
    while bit:
        for (target, source), piece in list(held.items()):
            if target & bit:
                came = lax.ppermute(piece, "exp", [(i, i ^ bit) for i in range(parts)])
                held[(target ^ bit, source ^ bit)] = came
                del held[(target, source)]
        bit //= 2
    return [held[(0, j)] for j in range(parts)]


def own_rows(gathered, place, my_index, swap):
    parts = len(gathered)
    count, width = gathered[0].shape[0] // 2, gathered[0].shape[1]
    stacked = jnp.stack(gathered, axis=1).reshape(2, count, parts, width)
    mine = lax.dynamic_index_in_dim(stacked, place, 0, keepdims=False)
    other = lax.dynamic_index_in_dim(stacked, 1 - place, 0, keepdims=False)
    came = lax.ppermute(other, "seq", swap)
    both = jnp.where(
        place == 0, jnp.stack([mine, came], axis=2), jnp.stack([came, mine], axis=2)
    )
    index = my_index ^ jnp.arange(parts, dtype=jnp.int32)
    return jnp.take(both, index, axis=1).reshape(count, 2 * parts * width)


def per_device(
    residual,
    queries,
    key_vectors,
    value_vectors,
    head_gain,
    norm_gain,
    routes,
    route_gates,
    expert_in,
    expert_out,
):
    rows, width = residual.shape
    seq, parts = lax.axis_size("seq"), lax.axis_size("exp")
    count, half, model = rows // parts, width // 2, width * parts
    experts = seq * expert_in.shape[0]
    position = lax.axis_index("seq")
    my_index = lax.axis_index("exp")
    place = position % 2
    scalars = jnp.stack([my_index, place, experts, position]).astype(jnp.int32)
    swap = [(i, i ^ 1) for i in range(seq)]

    state, packed = shape((HEAD, half), BF16), shape((rows, 4 * half), BF16)
    kept, given, theirs, mine, my_gain, my_norm = call(
        open_kernel,
        [state, state, packed, packed, shape((1, half), F32), shape((1, model), F32)],
        [
            scalars, key_vectors, value_vectors, queries, residual, head_gain[None, :],
            norm_gain[None, :],
        ],
        far=(1, 2, 3, 4, 5, 6),
        scratch=[pltpu.VMEM((rows, width), BF16)] * 2 + [pltpu.SemaphoreType.DMA((12,))],
        flops=2 * rows * width * HEAD,
    )
    partner = lax.ppermute(given, "seq", swap)
    came = lax.ppermute(theirs, "seq", swap)
    before = prior_states(kept, partner)
    [within] = call(
        within_kernel, [shape((2, rows, half), F32)], [scalars, mine, came],
        flops=6 * rows * rows * width,
    )
    pieces = call(
        functools.partial(attend_kernel, parts, len(before)),
        [shape((2 * count, half), BF16)] * parts,
        [scalars, within, mine, came, my_gain, kept, partner, *before],
        scratch=[pltpu.VMEM((2, rows, half), BF16)],
        flops=4 * rows * width * HEAD,
    )
    gathered = spread_rows(pieces)

    my_routes = lax.dynamic_slice_in_dim(routes, my_index * count, count, 0)
    my_gates = lax.dynamic_slice_in_dim(route_gates, my_index * count, count, 0)
    if routes.shape[1] == experts:
        mixing = jnp.sum(
            jnp.where(
                my_routes[:, :, None] == jnp.arange(experts, dtype=jnp.int32),
                my_gates[:, :, None],
                0.0,
            ),
            axis=1,
        )
        mixing = jnp.concatenate(
            [jnp.where(place == 0, mixing, 0.0), jnp.where(place == 0, 0.0, mixing)]
        )
        high = lax.reduce_precision(mixing, 8, 7)
        lanes = -(-2 * experts // HEAD) * HEAD
        pack = jnp.pad(
            jnp.concatenate([high, mixing - high], axis=1), ((0, 0), (0, lanes - 2 * experts))
        ).astype(BF16)
        message = jnp.concatenate(gathered + [pack], axis=1)
        hidden, *terms = dense_experts(message, scalars, expert_in[0], expert_out[0], my_norm)
    else:
        hidden = own_rows(gathered, place, my_index, swap)
        widened = hidden.astype(F32)
        normed = (
            widened
            * lax.rsqrt(jnp.mean(widened * widened, axis=-1, keepdims=True) + 1e-06)
            * norm_gain
        ).astype(BF16)
        mixed = routed_experts(normed, my_routes, my_gates, expert_in, expert_out)
        nothing = jnp.zeros_like(mixed)
        terms = (mixed, nothing, nothing)
    ready = call(
        mix_kernel, [shape((count, width), BF16)] * parts, [scalars, hidden, *terms]
    )
    returned = [ready[0]] + [
        lax.ppermute(ready[j], "exp", [(i, i ^ j) for i in range(parts)])
        for j in range(1, parts)
    ]
    [out] = call(
        join_kernel, [shape((rows, width), BF16)], [scalars] + returned, out_specs=[FAR],
        scratch=[pltpu.SemaphoreType.DMA((parts,))],
    )
    return out


def solution(mesh):
    placed = (
        P("seq", "exp"),
        P("seq", "exp"),
        P("seq", "exp"),
        P("seq", "exp"),
        P("exp"),
        P(),
        P("seq", None),
        P("seq", None),
        P("seq", None, None, None),
        P("seq", None, None),
    )
    return jax.shard_map(
        per_device, mesh=mesh, in_specs=placed, out_specs=P("seq", "exp"), check_vma=False
    )
```

```python
import functools

import jax
import jax.numpy as jnp
from jax import lax
from jax.experimental import pallas as pl
from jax.experimental.pallas import tpu as pltpu
from jax.sharding import PartitionSpec as P

HEAD = 128
F32 = jnp.float32
BF16 = jnp.bfloat16
WHOLE = pl.BlockSpec(memory_space=pltpu.VMEM)
FAR = pl.BlockSpec(memory_space=pltpu.HBM)
SCALAR = pl.BlockSpec(memory_space=pltpu.SMEM)


def call(kernel, outs, inputs, far=(), small=(), scratch=(), out_specs=None, flops=0, limit=16 << 20):
    moved = sum(a.size * a.dtype.itemsize for a in [*inputs, *outs])
    inputs = [
        pltpu.with_memory_space_constraint(a, pltpu.HBM) if i in far else a
        for i, a in enumerate(inputs)
    ]
    return pl.pallas_call(
        kernel,
        out_shape=outs,
        in_specs=[
            SCALAR if i == 0 or i in small else FAR if i in far else WHOLE
            for i in range(len(inputs))
        ],
        out_specs=out_specs or [WHOLE] * len(outs),
        scratch_shapes=scratch,
        compiler_params=pltpu.CompilerParams(vmem_limit_bytes=limit),
        cost_estimate=pl.CostEstimate(flops=flops, bytes_accessed=moved, transcendentals=0),
    )(*inputs)


def shape(dims, dtype):
    return jax.ShapeDtypeStruct(dims, dtype)


def split(value):
    high = value.astype(BF16)
    return high, (value - high.astype(F32)).astype(BF16)


def add_rows(*terms):
    return sum(t.astype(F32) for t in terms).astype(BF16)


def run_copies(pairs, sems):
    copies = [pltpu.make_async_copy(a, b, sems.at[i]) for i, (a, b) in enumerate(pairs)]
    for copy in copies:
        copy.start()
    for copy in copies:
        copy.wait()


def open_kernel(
    scalars, key_ref, value_ref, query_ref, residual_ref, gain_ref, norm_ref,
    kept_ref, given_ref, keys, values, query, residual, gain, norm, sems
):
    pairs = [
        (key_ref, keys), (value_ref, values), (query_ref, query), (residual_ref, residual),
        (gain_ref, gain), (norm_ref, norm),
    ]
    copies = [pltpu.make_async_copy(a, b, sems.at[i]) for i, (a, b) in enumerate(pairs)]
    for copy in copies:
        copy.start()
    for copy in copies[:2]:
        copy.wait()
    width = keys.shape[1] // 2
    place = scalars[1]
    for h in range(keys.shape[1] // HEAD):
        cols = slice(h * HEAD, (h + 1) * HEAD)
        state = lax.dot_general(
            keys[:, cols], values[:, cols], (((0,), (0,)), ((), ())), preferred_element_type=F32
        ).astype(BF16)
        half, inner = divmod(h * HEAD, width)

        @pl.when(place == half)
        def _():
            kept_ref[:, inner:inner + HEAD] = state

        @pl.when(place != half)
        def _():
            given_ref[:, inner:inner + HEAD] = state

    for copy in copies[2:]:
        copy.wait()


def within_kernel(scalars, keys, values, queries, out_ref):
    rows, width = out_ref.shape
    causal = lax.broadcasted_iota(jnp.int32, (rows, rows), 0) >= lax.broadcasted_iota(
        jnp.int32, (rows, rows), 1
    )
    for start in range(0, width, HEAD):
        cols = slice(start, start + HEAD)
        scores = lax.dot_general(
            queries[:, cols], keys[:, cols], (((1,), (1,)), ((), ())), preferred_element_type=F32
        )
        high, low = split(jnp.where(causal, scores, 0.0))
        out_ref[:, cols] = jnp.dot(
            high, values[:, cols], preferred_element_type=F32
        ) + jnp.dot(low, values[:, cols], preferred_element_type=F32)


def back_kernel(earlier, scalars, kept_ref, *refs):
    before_refs, out_ref = refs[:earlier], refs[earlier]
    before = sum(ref[...].astype(F32) for ref in before_refs)
    extra = jnp.where(scalars[1] == 0, kept_ref[...].astype(F32), 0.0)
    out_ref[...] = (before + extra).astype(BF16)


def attend_kernel(
    parts, earlier, scalars, within_ref, queries, residuals, gain_ref, partner_ref, other_ref, *refs
):
    before_refs, piece_refs, hidden = refs[:earlier], refs[earlier:-1], refs[-1]
    rows, full = hidden.shape
    width = full // 2
    first = scalars[1] == 0
    mine = sum(ref[...].astype(F32) for ref in before_refs)
    mine = mine + jnp.where(first, 0.0, partner_ref[...].astype(F32))
    other = other_ref[...].astype(F32)
    halves = [jnp.where(first, mine, other), jnp.where(first, other, mine)]
    for start in range(0, full, HEAD):
        cols = slice(start, start + HEAD)
        half, inner = divmod(start, width)
        high, low = split(halves[half][:, inner:inner + HEAD])
        raw = (
            jnp.dot(queries[:, cols], high, preferred_element_type=F32)
            + jnp.dot(queries[:, cols], low, preferred_element_type=F32)
            + within_ref[:, cols]
        )
        scaled = raw * lax.rsqrt(jnp.mean(raw * raw, axis=-1, keepdims=True) + 1e-06)
        hidden[:, cols] = (residuals[:, cols].astype(F32) + scaled * gain_ref[:, cols]).astype(BF16)
    count = rows // parts
    for j, piece in enumerate(piece_refs):
        piece[...] = hidden[pl.ds(pl.multiple_of((scalars[0] ^ j) * count, count), count), :]


def norm_kernel(scalars, gain_ref, pack_ref, *refs):
    pieces, hidden_ref, out_ref = refs[:-2], refs[-2], refs[-1]
    width = pieces[0].shape[1]
    model = hidden_ref.shape[1]
    total = 0.0
    for ref in pieces:
        value = ref[...].astype(F32)
        total += jnp.sum(value * value, axis=-1, keepdims=True)
    scale = lax.rsqrt(total / model + 1e-06)
    for j, ref in enumerate(pieces):
        cols = pl.ds(pl.multiple_of((scalars[0] ^ j) * width, width), width)
        hidden_ref[:, cols] = ref[...]
        out_ref[:, cols] = (ref[...].astype(F32) * scale * gain_ref[:, cols]).astype(BF16)
    out_ref[:, model:] = pack_ref[...]


def load_kernel(scalars, source, after_ref, target, done_ref, sems):
    done_ref[...] = jnp.zeros_like(done_ref)
    pieces = sems.shape[0]
    step = source.shape[0] // pieces
    run_copies(
        [
            (source.at[pl.ds(i * step, step)], target.at[pl.ds(i * step, step)])
            for i in range(pieces)
        ],
        sems,
    )


def load_near(scalars, source, after):
    return call(
        load_kernel, [shape(source.shape, source.dtype), shape((8, HEAD), F32)],
        [scalars, source, after], far=(1,), scratch=[pltpu.SemaphoreType.DMA((8,))],
    )


def expert_kernel(blocks, scalars, in_ref, down_ref, *refs):
    x_refs, out_refs, done_ref = refs[:blocks], refs[blocks:2 * blocks], refs[2 * blocks]
    rows_ref, act_ref, made_ref = refs[2 * blocks + 1:]
    done_ref[...] = jnp.zeros_like(done_ref)
    model, units = rows_ref.shape[1], in_ref.shape[1]
    spans, packs = [], []
    first = 0
    for ref in x_refs:
        spans.append(slice(first, first + ref.shape[0]))
        rows_ref[spans[-1], :] = ref[:, :model]
        packs.append(ref[:, model:].astype(F32))
        first += ref.shape[0]
    pack = jnp.concatenate(packs)
    lane = lax.broadcasted_iota(jnp.int32, pack.shape, 1)
    chosen = (lane == scalars[3]) | (lane == scalars[3] + scalars[2])
    weight = jnp.sum(jnp.where(chosen, pack, 0.0), axis=-1, keepdims=True)
    chunk = min(units, 256)

    @pl.loop(0, units // chunk)
    def _(step):
        cut = pl.ds(pl.multiple_of(step * chunk, chunk), chunk)
        gate = jnp.dot(rows_ref[...], in_ref[:model, cut], preferred_element_type=F32)
        up = jnp.dot(rows_ref[...], in_ref[model:, cut], preferred_element_type=F32)
        act_ref[:, cut] = (gate / (1.0 + jnp.exp(-gate)) * up).astype(BF16)

    wide = min(model, 512)

    @pl.loop(0, model // wide)
    def _(step):
        cut = pl.ds(pl.multiple_of(step * wide, wide), wide)
        produced = jnp.dot(act_ref[...], down_ref[:, cut], preferred_element_type=F32)
        made_ref[:, cut] = (produced.astype(BF16).astype(F32) * weight).astype(BF16)

    for out_ref, span in zip(out_refs, spans):
        out_ref[...] = made_ref[span, :]


def run_expert(scalars, blocks, weights_in, weights_out):
    units, model = weights_out.shape
    total = sum(b.shape[0] for b in blocks)
    *made, sign = call(
        functools.partial(expert_kernel, len(blocks)),
        [shape((b.shape[0], model), BF16) for b in blocks] + [shape((8, HEAD), F32)],
        [scalars, weights_in, weights_out, *blocks],
        scratch=[
            pltpu.VMEM((total, model), BF16),
            pltpu.VMEM((total, units), BF16),
            pltpu.VMEM((total, model), BF16),
        ],
        flops=6 * total * model * units,
    )
    return made, sign


def ring_order(count):
    return list(range(0, count, 2)) + list(range(1, count, 2))[::-1]


def dense_experts(block, scalars, expert_in, expert_out):
    count = lax.axis_size("seq")
    order = ring_order(count)
    half = block.shape[0] // 2
    far = count // 2

    def hop(rows, steps):
        return lax.ppermute(
            rows, "seq", [(order[p], order[(p + steps) % count]) for p in range(count)]
        )

    weights = [expert_in.reshape(-1, expert_in.shape[-1]), expert_out]
    near, after = [], block
    ahead, behind = [block], [block]
    for distance in range(1, far):
        came, went = hop(ahead[-1], 1), hop(behind[-1], -1)
        if weights:
            loaded, sign = load_near(scalars, weights.pop(0), after)
            near.append(loaded)
            came, went, after = lax.optimization_barrier((came, went, sign))
        ahead.append(came)
        behind.append(went)
    top = hop(ahead[-2][:half], 2)
    bottom = hop(behind[-2][half:], -2)
    (own, *close), sign = run_expert(scalars, ahead[:-1] + behind[1:-1], *near)
    last, first, top, bottom, _ = lax.optimization_barrier(
        (ahead[-1], behind[-1], top, bottom, sign)
    )
    (last, first, top, bottom), _ = run_expert(scalars, [last, first, top, bottom], *near)
    to_back, to_front = close[:far - 2] + [last], close[far - 2:] + [first]
    early_going, early_coming = hop(bottom, 2), hop(top, -2)
    going, coming = hop(to_front[-1], 1), hop(to_back[-1], -1)
    for distance in range(far - 2, 0, -1):
        front, back = to_front[distance - 1], to_back[distance - 1]
        if distance == far - 2:
            going = jnp.concatenate(
                [
                    add_rows(going[:half], front[:half]),
                    add_rows(going[half:], front[half:], early_going),
                ]
            )
            coming = jnp.concatenate(
                [
                    add_rows(coming[:half], back[:half], early_coming),
                    add_rows(coming[half:], back[half:]),
                ]
            )
        else:
            going = add_rows(going, front)
            coming = add_rows(coming, back)
        going, coming = hop(going, 1), hop(coming, -1)
    return own, going, coming


def mix_kernel(scalars, hidden_ref, a_ref, b_ref, c_ref, *out_refs):
    width = out_refs[0].shape[1]
    for j, out_ref in enumerate(out_refs):
        cols = pl.ds(pl.multiple_of((scalars[0] ^ j) * width, width), width)
        mixed = a_ref[:, cols].astype(F32) + b_ref[:, cols].astype(F32)
        mixed += c_ref[:, cols].astype(F32)
        out_ref[...] = (hidden_ref[:, cols].astype(F32) + mixed).astype(BF16)


def join_kernel(scalars, *refs):
    pieces, out_ref, sems = refs[:-2], refs[-2], refs[-1]
    count = pieces[0].shape[0]
    pairs = []
    for j, piece in enumerate(pieces):
        rows = pl.ds(pl.multiple_of((scalars[0] ^ j) * count, count), count)
        pairs.append((piece, out_ref.at[rows, :]))
    run_copies(pairs, sems)


def slot_ids(block_routes, expert_count, capacity):
    row_count, top_count = block_routes.shape
    expert_ids = jnp.arange(expert_count, dtype=jnp.int32)
    onehot = (
        (block_routes[:, :, None] == expert_ids[None, None, :])
        .astype(jnp.int32)
        .reshape(row_count * top_count, expert_count)
    )
    earlier = jnp.cumsum(onehot, axis=0) - onehot
    ranking = jnp.sum(earlier * onehot, axis=1).reshape(row_count, top_count)
    return block_routes * capacity + ranking


def routed_experts(normed, my_routes, my_gates, expert_in, expert_out):
    sub_count, model_width = normed.shape
    expert_count = lax.axis_size("seq") * expert_in.shape[0]
    top_count = my_routes.shape[1]
    capacity = min(sub_count, max(2, 3 * sub_count * top_count // (2 * expert_count)))
    slot_count = expert_count * capacity
    my_slots = slot_ids(my_routes, expert_count, capacity)
    columns = jnp.arange(slot_count, dtype=jnp.int32)
    placer = jnp.sum(
        (my_slots[None, :, :] == columns[:, None, None]).astype(jnp.int32), axis=2
    ).astype(BF16)
    outgoing = (
        jnp.dot(placer, normed, preferred_element_type=F32)
        .astype(BF16)
        .reshape(expert_count, capacity, model_width)
    )
    arrived = lax.all_to_all(outgoing, "seq", split_axis=0, concat_axis=0, tiled=True)
    flat_rows = arrived.reshape(-1, model_width)
    gate_up = jnp.einsum("nd,gdf->gnf", flat_rows, expert_in[0], preferred_element_type=F32)
    activated = (jax.nn.silu(gate_up[0]) * gate_up[1]).astype(BF16)
    produced = jnp.dot(activated, expert_out[0], preferred_element_type=F32).astype(BF16)
    answered = produced.reshape(arrived.shape)
    returned = lax.all_to_all(answered, "seq", split_axis=0, concat_axis=0, tiled=True)
    picked = returned.reshape(slot_count, model_width)[my_slots.reshape(-1)].reshape(
        sub_count, top_count, model_width
    )
    return jnp.sum(picked.astype(F32) * my_gates[:, :, None], axis=1)


def prior_states(kept, partner):
    count = lax.axis_size("seq")

    def pass_on(state, distance):
        return lax.ppermute(
            state, "seq", [(i, i + 2 * distance) for i in range(count - 2 * distance)]
        )

    pairs = count // 2
    running = add_rows(kept, partner)
    if pairs <= 4:
        return [pass_on(running, distance) for distance in reversed(range(1, pairs))]
    terms = []
    distance = 1
    while distance < pairs:
        terms.append(pass_on(running, distance))
        running = add_rows(running, terms[-1])
        distance *= 2
    return terms


def spread_rows(pieces):
    parts = len(pieces)
    bit = parts // 2
    held = {(j, 0): piece for j, piece in enumerate(pieces)}
    while bit:
        for (target, source), piece in list(held.items()):
            if target & bit:
                came = lax.ppermute(piece, "exp", [(i, i ^ bit) for i in range(parts)])
                held[(target ^ bit, source ^ bit)] = came
                del held[(target, source)]
        bit //= 2
    return [held[(0, j)] for j in range(parts)]


def per_device(
    residual,
    queries,
    key_vectors,
    value_vectors,
    head_gain,
    norm_gain,
    routes,
    route_gates,
    expert_in,
    expert_out,
):
    rows, width = residual.shape
    seq, parts = lax.axis_size("seq"), lax.axis_size("exp")
    count, half, model = rows // parts, width // 2, width * parts
    experts = seq * expert_in.shape[0]
    position = lax.axis_index("seq")
    my_index = lax.axis_index("exp")
    place = position % 2
    scalars = jnp.stack([my_index, place, experts, position]).astype(jnp.int32)
    swap = [(i, i ^ 1) for i in range(seq)]

    state, heads = shape((HEAD, half), BF16), shape((rows, width), BF16)
    kept, given, keys, values, query, rest, my_gain, my_norm = call(
        open_kernel,
        [state] * 2 + [heads] * 4 + [shape((1, width), F32), shape((1, model), F32)],
        [
            scalars, key_vectors, value_vectors, queries, residual, head_gain[None, :],
            norm_gain[None, :],
        ],
        far=(1, 2, 3, 4, 5, 6),
        scratch=[pltpu.SemaphoreType.DMA((6,))],
        flops=2 * rows * width * HEAD,
    )
    partner = lax.ppermute(given, "seq", swap)
    [within] = call(
        within_kernel, [shape((rows, width), F32)], [scalars, keys, values, query],
        flops=6 * rows * rows * width,
    )
    before = prior_states(kept, partner)
    [lacked] = call(
        functools.partial(back_kernel, len(before)), [state], [scalars, kept, *before]
    )
    other = lax.ppermute(lacked, "seq", swap)
    pieces = call(
        functools.partial(attend_kernel, parts, len(before)),
        [shape((count, width), BF16)] * parts,
        [scalars, within, query, rest, my_gain, partner, other, *before],
        scratch=[pltpu.VMEM((rows, width), BF16)],
        flops=4 * rows * width * HEAD,
    )
    gathered = spread_rows(pieces)

    my_routes = lax.dynamic_slice_in_dim(routes, my_index * count, count, 0)
    my_gates = lax.dynamic_slice_in_dim(route_gates, my_index * count, count, 0)
    mixing = jnp.sum(
        jnp.where(
            my_routes[:, :, None] == jnp.arange(experts, dtype=jnp.int32),
            my_gates[:, :, None],
            0.0,
        ),
        axis=1,
    )
    high = lax.reduce_precision(mixing, 8, 7)
    lanes = -(-2 * experts // HEAD) * HEAD
    pack = jnp.pad(
        jnp.concatenate([high, mixing - high], axis=1), ((0, 0), (0, lanes - 2 * experts))
    ).astype(BF16)
    hidden, block = call(
        norm_kernel,
        [shape((count, model), BF16), shape((count, model + lanes), BF16)],
        [scalars, my_norm, pack] + gathered,
    )
    if routes.shape[1] == experts:
        terms = dense_experts(block, scalars, expert_in[0], expert_out[0])
    else:
        mixed = routed_experts(block[:, :model], my_routes, my_gates, expert_in, expert_out)
        nothing = jnp.zeros_like(mixed)
        terms = (mixed, nothing, nothing)
    ready = call(
        mix_kernel, [shape((count, width), BF16)] * parts, [scalars, hidden, *terms]
    )
    returned = [ready[0]] + [
        lax.ppermute(ready[j], "exp", [(i, i ^ j) for i in range(parts)])
        for j in range(1, parts)
    ]
    [out] = call(
        join_kernel, [shape((rows, width), BF16)], [scalars] + returned, out_specs=[FAR],
        scratch=[pltpu.SemaphoreType.DMA((parts,))],
    )
    return out


def solution(mesh):
    placed = (
        P("seq", "exp"),
        P("seq", "exp"),
        P("seq", "exp"),
        P("seq", "exp"),
        P("exp"),
        P(),
        P("seq", None),
        P("seq", None),
        P("seq", None, None, None),
        P("seq", None, None),
    )
    return jax.shard_map(
        per_device, mesh=mesh, in_specs=placed, out_specs=P("seq", "exp"), check_vma=False
    )
```

```python
import functools

import jax
import jax.numpy as jnp
from jax import lax
from jax.experimental import pallas as pl
from jax.experimental.pallas import tpu as pltpu
from jax.sharding import PartitionSpec as P

HEAD = 128
F32 = jnp.float32
BF16 = jnp.bfloat16
WHOLE = pl.BlockSpec(memory_space=pltpu.VMEM)
FAR = pl.BlockSpec(memory_space=pltpu.HBM)
SCALAR = pl.BlockSpec(memory_space=pltpu.SMEM)


def call(kernel, outs, inputs, far=(), small=(), scratch=(), out_specs=None, flops=0, limit=16 << 20):
    moved = sum(a.size * a.dtype.itemsize for a in [*inputs, *outs])
    inputs = [
        pltpu.with_memory_space_constraint(a, pltpu.HBM) if i in far else a
        for i, a in enumerate(inputs)
    ]
    return pl.pallas_call(
        kernel,
        out_shape=outs,
        in_specs=[
            SCALAR if i == 0 or i in small else FAR if i in far else WHOLE
            for i in range(len(inputs))
        ],
        out_specs=out_specs or [WHOLE] * len(outs),
        scratch_shapes=scratch,
        compiler_params=pltpu.CompilerParams(vmem_limit_bytes=limit),
        cost_estimate=pl.CostEstimate(flops=flops, bytes_accessed=moved, transcendentals=0),
    )(*inputs)


def shape(dims, dtype):
    return jax.ShapeDtypeStruct(dims, dtype)


def split(value):
    high = value.astype(BF16)
    return high, (value - high.astype(F32)).astype(BF16)


def add_rows(*terms):
    return sum(t.astype(F32) for t in terms).astype(BF16)


def run_copies(pairs, sems):
    copies = [pltpu.make_async_copy(a, b, sems.at[i]) for i, (a, b) in enumerate(pairs)]
    for copy in copies:
        copy.start()
    for copy in copies:
        copy.wait()


def open_kernel(
    scalars, key_ref, value_ref, query_ref, residual_ref, gain_ref, norm_ref,
    kept_ref, given_ref, keys, values, query, residual, gain, norm, sems
):
    pairs = [
        (key_ref, keys), (value_ref, values), (query_ref, query), (residual_ref, residual),
        (gain_ref, gain), (norm_ref, norm),
    ]
    copies = [pltpu.make_async_copy(a, b, sems.at[i]) for i, (a, b) in enumerate(pairs)]
    for copy in copies:
        copy.start()
    for copy in copies[:2]:
        copy.wait()
    width = keys.shape[1] // 2
    place = scalars[1]
    for h in range(keys.shape[1] // HEAD):
        cols = slice(h * HEAD, (h + 1) * HEAD)
        state = lax.dot_general(
            keys[:, cols], values[:, cols], (((0,), (0,)), ((), ())), preferred_element_type=F32
        ).astype(BF16)
        half, inner = divmod(h * HEAD, width)

        @pl.when(place == half)
        def _():
            kept_ref[:, inner:inner + HEAD] = state

        @pl.when(place != half)
        def _():
            given_ref[:, inner:inner + HEAD] = state

    for copy in copies[2:]:
        copy.wait()


def within_kernel(scalars, keys, values, queries, out_ref):
    rows, width = out_ref.shape
    causal = lax.broadcasted_iota(jnp.int32, (rows, rows), 0) >= lax.broadcasted_iota(
        jnp.int32, (rows, rows), 1
    )
    for start in range(0, width, HEAD):
        cols = slice(start, start + HEAD)
        scores = lax.dot_general(
            queries[:, cols], keys[:, cols], (((1,), (1,)), ((), ())), preferred_element_type=F32
        )
        high, low = split(jnp.where(causal, scores, 0.0))
        out_ref[:, cols] = jnp.dot(
            high, values[:, cols], preferred_element_type=F32
        ) + jnp.dot(low, values[:, cols], preferred_element_type=F32)


def back_kernel(earlier, scalars, sign_ref, kept_ref, *refs):
    before_refs, out_ref = refs[:earlier], refs[earlier]
    before = sum(ref[...].astype(F32) for ref in before_refs)
    extra = jnp.where(scalars[1] == 0, kept_ref[...].astype(F32), 0.0)
    out_ref[...] = (before + extra).astype(BF16)


def attend_kernel(
    parts, earlier, scalars, within_ref, queries, residuals, gain_ref, partner_ref, other_ref, *refs
):
    before_refs, piece_refs, hidden = refs[:earlier], refs[earlier:-1], refs[-1]
    rows, full = hidden.shape
    width = full // 2
    first = scalars[1] == 0
    mine = sum(ref[...].astype(F32) for ref in before_refs)
    mine = mine + jnp.where(first, 0.0, partner_ref[...].astype(F32))
    other = other_ref[...].astype(F32)
    halves = [jnp.where(first, mine, other), jnp.where(first, other, mine)]
    for start in range(0, full, HEAD):
        cols = slice(start, start + HEAD)
        half, inner = divmod(start, width)
        high, low = split(halves[half][:, inner:inner + HEAD])
        raw = (
            jnp.dot(queries[:, cols], high, preferred_element_type=F32)
            + jnp.dot(queries[:, cols], low, preferred_element_type=F32)
            + within_ref[:, cols]
        )
        scaled = raw * lax.rsqrt(jnp.mean(raw * raw, axis=-1, keepdims=True) + 1e-06)
        hidden[:, cols] = (residuals[:, cols].astype(F32) + scaled * gain_ref[:, cols]).astype(BF16)
    count = rows // parts
    for j, piece in enumerate(piece_refs):
        piece[...] = hidden[pl.ds(pl.multiple_of((scalars[0] ^ j) * count, count), count), :]


def norm_kernel(scalars, gain_ref, pack_ref, *refs):
    pieces, hidden_ref, out_ref = refs[:-2], refs[-2], refs[-1]
    width = pieces[0].shape[1]
    model = hidden_ref.shape[1]
    total = 0.0
    for ref in pieces:
        value = ref[...].astype(F32)
        total += jnp.sum(value * value, axis=-1, keepdims=True)
    scale = lax.rsqrt(total / model + 1e-06)
    for j, ref in enumerate(pieces):
        cols = pl.ds(pl.multiple_of((scalars[0] ^ j) * width, width), width)
        hidden_ref[:, cols] = ref[...]
        out_ref[:, cols] = (ref[...].astype(F32) * scale * gain_ref[:, cols]).astype(BF16)
    out_ref[:, model:] = pack_ref[...]


def load_kernel(scalars, source, after_ref, target, done_ref, sems):
    done_ref[...] = jnp.zeros_like(done_ref)
    pieces = sems.shape[0]
    step = source.shape[0] // pieces
    run_copies(
        [
            (source.at[pl.ds(i * step, step)], target.at[pl.ds(i * step, step)])
            for i in range(pieces)
        ],
        sems,
    )


def load_near(scalars, source, after):
    return call(
        load_kernel, [shape(source.shape, source.dtype), shape((8, HEAD), F32)],
        [scalars, source, after], far=(1,), scratch=[pltpu.SemaphoreType.DMA((8,))],
    )


def expert_kernel(blocks, scalars, in_ref, down_ref, *refs):
    x_refs, out_refs = refs[:blocks], refs[blocks:2 * blocks]
    rows_ref, act_ref, made_ref = refs[2 * blocks:]
    model, units = rows_ref.shape[1], in_ref.shape[1]
    spans, packs = [], []
    first = 0
    for ref in x_refs:
        spans.append(slice(first, first + ref.shape[0]))
        rows_ref[spans[-1], :] = ref[:, :model]
        packs.append(ref[:, model:].astype(F32))
        first += ref.shape[0]
    pack = jnp.concatenate(packs)
    lane = lax.broadcasted_iota(jnp.int32, pack.shape, 1)
    chosen = (lane == scalars[3]) | (lane == scalars[3] + scalars[2])
    weight = jnp.sum(jnp.where(chosen, pack, 0.0), axis=-1, keepdims=True)
    chunk = min(units, 512)

    @pl.loop(0, units // chunk)
    def _(step):
        cut = pl.ds(pl.multiple_of(step * chunk, chunk), chunk)
        gate = jnp.dot(rows_ref[...], in_ref[:model, cut], preferred_element_type=F32)
        up = jnp.dot(rows_ref[...], in_ref[model:, cut], preferred_element_type=F32)
        act_ref[:, cut] = (gate / (1.0 + jnp.exp(-gate)) * up).astype(BF16)

    wide = min(model, 1024)

    @pl.loop(0, model // wide)
    def _(step):
        cut = pl.ds(pl.multiple_of(step * wide, wide), wide)
        produced = jnp.dot(act_ref[...], down_ref[:, cut], preferred_element_type=F32)
        made_ref[:, cut] = (produced.astype(BF16).astype(F32) * weight).astype(BF16)

    for out_ref, span in zip(out_refs, spans):
        out_ref[...] = made_ref[span, :]


def run_expert(scalars, blocks, weights_in, weights_out):
    units, model = weights_out.shape
    total = sum(b.shape[0] for b in blocks)
    return call(
        functools.partial(expert_kernel, len(blocks)),
        [shape((b.shape[0], model), BF16) for b in blocks],
        [scalars, weights_in, weights_out, *blocks],
        scratch=[
            pltpu.VMEM((total, model), BF16),
            pltpu.VMEM((total, units), BF16),
            pltpu.VMEM((total, model), BF16),
        ],
        flops=6 * total * model * units,
        limit=24 << 20,
    )


def ring_order(count):
    return list(range(0, count, 2)) + list(range(1, count, 2))[::-1]


def dense_experts(block, scalars, weights_in, expert_out):
    count = lax.axis_size("seq")
    order = ring_order(count)
    half = block.shape[0] // 2
    far = count // 2

    def hop(rows, steps):
        return lax.ppermute(
            rows, "seq", [(order[p], order[(p + steps) % count]) for p in range(count)]
        )

    ahead, behind = [block], [block]
    for distance in range(1, far):
        came, went = hop(ahead[-1], 1), hop(behind[-1], -1)
        if distance == 1:
            weights_out, sign = load_near(scalars, expert_out, block)
            came, went, sign = lax.optimization_barrier((came, went, sign))
        ahead.append(came)
        behind.append(went)
    top = hop(ahead[-2][:half], 2)
    bottom = hop(behind[-2][half:], -2)
    made = run_expert(scalars, ahead + behind[1:] + [top, bottom], weights_in, weights_out)
    own, to_back, to_front = made[0], made[1:far], made[far:2 * far - 1]
    top, bottom = made[-2:]
    early_going, early_coming = hop(bottom, 2), hop(top, -2)
    going, coming = hop(to_front[-1], 1), hop(to_back[-1], -1)
    for distance in range(far - 2, 0, -1):
        front, back = to_front[distance - 1], to_back[distance - 1]
        if distance == far - 2:
            going = jnp.concatenate(
                [
                    add_rows(going[:half], front[:half]),
                    add_rows(going[half:], front[half:], early_going),
                ]
            )
            coming = jnp.concatenate(
                [
                    add_rows(coming[:half], back[:half], early_coming),
                    add_rows(coming[half:], back[half:]),
                ]
            )
        else:
            going = add_rows(going, front)
            coming = add_rows(coming, back)
        going, coming = hop(going, 1), hop(coming, -1)
    return own, going, coming


def mix_kernel(scalars, hidden_ref, a_ref, b_ref, c_ref, *out_refs):
    width = out_refs[0].shape[1]
    for j, out_ref in enumerate(out_refs):
        cols = pl.ds(pl.multiple_of((scalars[0] ^ j) * width, width), width)
        mixed = a_ref[:, cols].astype(F32) + b_ref[:, cols].astype(F32)
        mixed += c_ref[:, cols].astype(F32)
        out_ref[...] = (hidden_ref[:, cols].astype(F32) + mixed).astype(BF16)


def slot_ids(block_routes, expert_count, capacity):
    row_count, top_count = block_routes.shape
    expert_ids = jnp.arange(expert_count, dtype=jnp.int32)
    onehot = (
        (block_routes[:, :, None] == expert_ids[None, None, :])
        .astype(jnp.int32)
        .reshape(row_count * top_count, expert_count)
    )
    earlier = jnp.cumsum(onehot, axis=0) - onehot
    ranking = jnp.sum(earlier * onehot, axis=1).reshape(row_count, top_count)
    return block_routes * capacity + ranking


def routed_experts(normed, my_routes, my_gates, expert_in, expert_out):
    sub_count, model_width = normed.shape
    expert_count = lax.axis_size("seq") * expert_in.shape[0]
    top_count = my_routes.shape[1]
    capacity = min(sub_count, max(2, 3 * sub_count * top_count // (2 * expert_count)))
    slot_count = expert_count * capacity
    my_slots = slot_ids(my_routes, expert_count, capacity)
    columns = jnp.arange(slot_count, dtype=jnp.int32)
    placer = jnp.sum(
        (my_slots[None, :, :] == columns[:, None, None]).astype(jnp.int32), axis=2
    ).astype(BF16)
    outgoing = (
        jnp.dot(placer, normed, preferred_element_type=F32)
        .astype(BF16)
        .reshape(expert_count, capacity, model_width)
    )
    arrived = lax.all_to_all(outgoing, "seq", split_axis=0, concat_axis=0, tiled=True)
    flat_rows = arrived.reshape(-1, model_width)
    gate_up = jnp.einsum("nd,gdf->gnf", flat_rows, expert_in[0], preferred_element_type=F32)
    activated = (jax.nn.silu(gate_up[0]) * gate_up[1]).astype(BF16)
    produced = jnp.dot(activated, expert_out[0], preferred_element_type=F32).astype(BF16)
    answered = produced.reshape(arrived.shape)
    returned = lax.all_to_all(answered, "seq", split_axis=0, concat_axis=0, tiled=True)
    picked = returned.reshape(slot_count, model_width)[my_slots.reshape(-1)].reshape(
        sub_count, top_count, model_width
    )
    return jnp.sum(picked.astype(F32) * my_gates[:, :, None], axis=1)


def prior_states(kept, partner):
    count = lax.axis_size("seq")

    def pass_on(state, distance):
        return lax.ppermute(
            state, "seq", [(i, i + 2 * distance) for i in range(count - 2 * distance)]
        )

    pairs = count // 2
    running = add_rows(kept, partner)
    if pairs <= 4:
        return [pass_on(running, distance) for distance in range(1, pairs)]
    terms = []
    distance = 1
    while distance < pairs:
        terms.append(pass_on(running, distance))
        running = add_rows(running, terms[-1])
        distance *= 2
    return terms


def exchange(pieces):
    parts = len(pieces)
    return [pieces[0]] + [
        lax.ppermute(pieces[j], "exp", [(i, i ^ j) for i in range(parts)])
        for j in range(1, parts)
    ]


def per_device(
    residual,
    queries,
    key_vectors,
    value_vectors,
    head_gain,
    norm_gain,
    routes,
    route_gates,
    expert_in,
    expert_out,
):
    rows, width = residual.shape
    seq, parts = lax.axis_size("seq"), lax.axis_size("exp")
    count, half, model = rows // parts, width // 2, width * parts
    experts = seq * expert_in.shape[0]
    position = lax.axis_index("seq")
    my_index = lax.axis_index("exp")
    place = position % 2
    scalars = jnp.stack([my_index, place, experts, position]).astype(jnp.int32)
    swap = [(i, i ^ 1) for i in range(seq)]

    state, heads = shape((HEAD, half), BF16), shape((rows, width), BF16)
    kept, given, keys, values, query, rest, my_gain, my_norm = call(
        open_kernel,
        [state] * 2 + [heads] * 4 + [shape((1, width), F32), shape((1, model), F32)],
        [
            scalars, key_vectors, value_vectors, queries, residual, head_gain[None, :],
            norm_gain[None, :],
        ],
        far=(1, 2, 3, 4, 5, 6),
        scratch=[pltpu.SemaphoreType.DMA((6,))],
        flops=2 * rows * width * HEAD,
    )
    partner = lax.ppermute(given, "seq", swap)
    [within] = call(
        within_kernel, [shape((rows, width), F32)], [scalars, keys, values, query],
        flops=6 * rows * rows * width,
    )
    before = prior_states(kept, partner)
    dense = routes.shape[1] == experts
    sign = jnp.zeros((8, HEAD), F32)
    if dense:
        weights_in, sign = load_near(
            scalars, expert_in.reshape(-1, expert_in.shape[-1]), partner
        )
    [lacked] = call(
        functools.partial(back_kernel, len(before)), [state], [scalars, sign, kept, *before]
    )
    other = lax.ppermute(lacked, "seq", swap)
    pieces = call(
        functools.partial(attend_kernel, parts, len(before)),
        [shape((count, width), BF16)] * parts,
        [scalars, within, query, rest, my_gain, partner, other, *before],
        scratch=[pltpu.VMEM((rows, width), BF16)],
        flops=4 * rows * width * HEAD,
    )
    gathered = exchange(pieces)

    my_routes = lax.dynamic_slice_in_dim(routes, my_index * count, count, 0)
    my_gates = lax.dynamic_slice_in_dim(route_gates, my_index * count, count, 0)
    mixing = jnp.sum(
        jnp.where(
            my_routes[:, :, None] == jnp.arange(experts, dtype=jnp.int32),
            my_gates[:, :, None],
            0.0,
        ),
        axis=1,
    )
    high = lax.reduce_precision(mixing, 8, 7)
    lanes = -(-2 * experts // HEAD) * HEAD
    pack = jnp.pad(
        jnp.concatenate([high, mixing - high], axis=1), ((0, 0), (0, lanes - 2 * experts))
    ).astype(BF16)
    hidden, block = call(
        norm_kernel,
        [shape((count, model), BF16), shape((count, model + lanes), BF16)],
        [scalars, my_norm, pack] + gathered,
    )
    if dense:
        terms = dense_experts(block, scalars, weights_in, expert_out[0])
    else:
        mixed = routed_experts(block[:, :model], my_routes, my_gates, expert_in, expert_out)
        nothing = jnp.zeros_like(mixed)
        terms = (mixed, nothing, nothing)
    ready = call(
        mix_kernel, [shape((count, width), BF16)] * parts, [scalars, hidden, *terms]
    )
    returned = exchange(ready)
    order = list(range(parts))
    bit = 1
    while bit < parts:
        turn = (my_index & bit) != 0
        returned = [jnp.where(turn, returned[i ^ bit], returned[i]) for i in order]
        bit *= 2
    return jnp.concatenate(returned)


def solution(mesh):
    placed = (
        P("seq", "exp"),
        P("seq", "exp"),
        P("seq", "exp"),
        P("seq", "exp"),
        P("exp"),
        P(),
        P("seq", None),
        P("seq", None),
        P("seq", None, None, None),
        P("seq", None, None),
    )
    return jax.shard_map(
        per_device, mesh=mesh, in_specs=placed, out_specs=P("seq", "exp"), check_vma=False
    )
```

```python
import functools

import jax
import jax.numpy as jnp
from jax import lax
from jax.experimental import pallas as pl
from jax.experimental.pallas import tpu as pltpu
from jax.sharding import PartitionSpec as P

HEAD = 128
F32 = jnp.float32
BF16 = jnp.bfloat16
WHOLE = pl.BlockSpec(memory_space=pltpu.VMEM)
FAR = pl.BlockSpec(memory_space=pltpu.HBM)
SCALAR = pl.BlockSpec(memory_space=pltpu.SMEM)


def call(kernel, outs, inputs, far=(), small=(), scratch=(), out_specs=None, flops=0, limit=16 << 20):
    moved = sum(a.size * a.dtype.itemsize for a in [*inputs, *outs])
    inputs = [
        pltpu.with_memory_space_constraint(a, pltpu.HBM) if i in far else a
        for i, a in enumerate(inputs)
    ]
    return pl.pallas_call(
        kernel,
        out_shape=outs,
        in_specs=[
            SCALAR if i == 0 or i in small else FAR if i in far else WHOLE
            for i in range(len(inputs))
        ],
        out_specs=out_specs or [WHOLE] * len(outs),
        scratch_shapes=scratch,
        compiler_params=pltpu.CompilerParams(vmem_limit_bytes=limit),
        cost_estimate=pl.CostEstimate(flops=flops, bytes_accessed=moved, transcendentals=0),
    )(*inputs)


def shape(dims, dtype):
    return jax.ShapeDtypeStruct(dims, dtype)


def split(value):
    high = value.astype(BF16)
    return high, (value - high.astype(F32)).astype(BF16)


def add_rows(*terms):
    return sum(t.astype(F32) for t in terms).astype(BF16)


def run_copies(pairs, sems):
    copies = [pltpu.make_async_copy(a, b, sems.at[i]) for i, (a, b) in enumerate(pairs)]
    for copy in copies:
        copy.start()
    for copy in copies:
        copy.wait()


def open_kernel(
    scalars, key_ref, value_ref, query_ref, residual_ref, gain_ref, norm_ref,
    kept_ref, given_ref, keys, values, query, residual, gain, norm, sems
):
    pairs = [
        (key_ref, keys), (value_ref, values), (query_ref, query), (residual_ref, residual),
        (gain_ref, gain), (norm_ref, norm),
    ]
    copies = [pltpu.make_async_copy(a, b, sems.at[i]) for i, (a, b) in enumerate(pairs)]
    for copy in copies:
        copy.start()
    for copy in copies[:2]:
        copy.wait()
    width = keys.shape[1] // 2
    place = scalars[1]
    sides = []
    for side in range(2):
        cols = slice(side * width, (side + 1) * width)
        square = lax.dot_general(
            keys[:, cols], values[:, cols], (((0,), (0,)), ((), ())), preferred_element_type=F32
        )
        sides.append(
            jnp.concatenate(
                [square[h:h + HEAD, h:h + HEAD] for h in range(0, width, HEAD)], axis=1
            ).astype(BF16)
        )
    kept_ref[...] = jnp.where(place == 0, sides[0], sides[1])
    given_ref[...] = jnp.where(place == 0, sides[1], sides[0])
    for copy in copies[2:]:
        copy.wait()


def within_kernel(scalars, keys, values, queries, out_ref):
    rows, width = out_ref.shape
    causal = lax.broadcasted_iota(jnp.int32, (rows, rows), 0) >= lax.broadcasted_iota(
        jnp.int32, (rows, rows), 1
    )
    for start in range(0, width, HEAD):
        cols = slice(start, start + HEAD)
        scores = lax.dot_general(
            queries[:, cols], keys[:, cols], (((1,), (1,)), ((), ())), preferred_element_type=F32
        )
        high, low = split(jnp.where(causal, scores, 0.0))
        out_ref[:, cols] = jnp.dot(
            high, values[:, cols], preferred_element_type=F32
        ) + jnp.dot(low, values[:, cols], preferred_element_type=F32)


def attend_kernel(
    parts, scalars, sign_ref, within_ref, queries, residuals, gain_ref, mine_ref, other_ref, *refs
):
    piece_refs, hidden = refs[:-1], refs[-1]
    rows, full = hidden.shape
    width = full // 2
    first = scalars[1] == 0
    mine, other = mine_ref[...], other_ref[...].astype(F32)
    halves = [jnp.where(first, mine, other), jnp.where(first, other, mine)]
    for start in range(0, full, HEAD):
        cols = slice(start, start + HEAD)
        half, inner = divmod(start, width)
        high, low = split(halves[half][:, inner:inner + HEAD])
        raw = (
            jnp.dot(queries[:, cols], high, preferred_element_type=F32)
            + jnp.dot(queries[:, cols], low, preferred_element_type=F32)
            + within_ref[:, cols]
        )
        scaled = raw * lax.rsqrt(jnp.mean(raw * raw, axis=-1, keepdims=True) + 1e-06)
        hidden[:, cols] = (residuals[:, cols].astype(F32) + scaled * gain_ref[:, cols]).astype(BF16)
    count = rows // parts
    for j, piece in enumerate(piece_refs):
        piece[...] = hidden[pl.ds(pl.multiple_of((scalars[0] ^ j) * count, count), count), :]


def norm_kernel(scalars, gain_ref, pack_ref, *refs):
    pieces, hidden_ref, out_ref = refs[:-2], refs[-2], refs[-1]
    width = pieces[0].shape[1]
    model = hidden_ref.shape[1]
    total = 0.0
    for ref in pieces:
        value = ref[...].astype(F32)
        total += jnp.sum(value * value, axis=-1, keepdims=True)
    scale = lax.rsqrt(total / model + 1e-06)
    for j, ref in enumerate(pieces):
        cols = pl.ds(pl.multiple_of((scalars[0] ^ j) * width, width), width)
        hidden_ref[:, cols] = ref[...]
        out_ref[:, cols] = (ref[...].astype(F32) * scale * gain_ref[:, cols]).astype(BF16)
    out_ref[:, model:] = pack_ref[...]


def load_kernel(lead, scalars, source, after_ref, target, done_ref, sems):
    done_ref[...] = jnp.zeros_like(done_ref)
    pieces = sems.shape[0]
    step = target.shape[0] // pieces
    cuts = [pl.ds(i * step, step) for i in range(pieces)]
    run_copies([(source.at[lead, cut], target.at[cut]) for cut in cuts], sems)


def load_near(scalars, source, lead, after):
    return call(
        functools.partial(load_kernel, lead),
        [shape(source.shape[1:], source.dtype), shape((8, HEAD), F32)],
        [scalars, source, after], far=(1,), scratch=[pltpu.SemaphoreType.DMA((8,))],
    )


def expert_kernel(blocks, scalars, gate_ref, up_ref, down_ref, *refs):
    x_refs, out_refs = refs[:blocks], refs[blocks:2 * blocks]
    rows_ref, act_ref, made_ref = refs[2 * blocks:]
    model, units = gate_ref.shape
    spans, packs = [], []
    first = 0
    for ref in x_refs:
        spans.append(slice(first, first + ref.shape[0]))
        rows_ref[spans[-1], :] = ref[:, :model]
        packs.append(ref[:, model:].astype(F32))
        first += ref.shape[0]
    pack = jnp.concatenate(packs)
    lane = lax.broadcasted_iota(jnp.int32, pack.shape, 1)
    chosen = (lane == scalars[3]) | (lane == scalars[3] + scalars[2])
    weight = jnp.sum(jnp.where(chosen, pack, 0.0), axis=-1, keepdims=True)
    chunk = min(units, 512)

    @pl.loop(0, units // chunk)
    def _(step):
        cut = pl.ds(pl.multiple_of(step * chunk, chunk), chunk)
        gate = jnp.dot(rows_ref[...], gate_ref[:, cut], preferred_element_type=F32)
        up = jnp.dot(rows_ref[...], up_ref[:, cut], preferred_element_type=F32)
        act_ref[:, cut] = (gate / (1.0 + jnp.exp(-gate)) * up).astype(BF16)

    wide = min(model, 1024)

    @pl.loop(0, model // wide)
    def _(step):
        cut = pl.ds(pl.multiple_of(step * wide, wide), wide)
        produced = jnp.dot(act_ref[...], down_ref[:, cut], preferred_element_type=F32)
        made_ref[:, cut] = (produced.astype(BF16).astype(F32) * weight).astype(BF16)

    for out_ref, span in zip(out_refs, spans):
        out_ref[...] = made_ref[span, :]


def run_expert(scalars, blocks, weights_gate, weights_up, weights_out):
    units, model = weights_out.shape
    total = sum(b.shape[0] for b in blocks)
    return call(
        functools.partial(expert_kernel, len(blocks)),
        [shape((b.shape[0], model), BF16) for b in blocks],
        [scalars, weights_gate, weights_up, weights_out, *blocks],
        scratch=[
            pltpu.VMEM((total, model), BF16),
            pltpu.VMEM((total, units), BF16),
            pltpu.VMEM((total, model), BF16),
        ],
        flops=6 * total * model * units,
        limit=24 << 20,
    )


def ring_order(count):
    return list(range(0, count, 2)) + list(range(1, count, 2))[::-1]


def dense_experts(block, scalars, turns, weights_gate, weights_up, expert_out):
    count = lax.axis_size("seq")
    order = ring_order(count)
    far = count // 2
    parts = lax.axis_size("exp")

    def hop(rows, steps):
        return lax.ppermute(
            rows, "seq", [(order[p], order[(p + steps) % count]) for p in range(count)]
        )

    def far_hop(rows):
        pairs = []
        for p in range(count):
            for e in range(parts):
                target = order[(p + (2 if e % 2 == 0 else -2)) % count]
                pairs.append((order[p] * parts + e, target * parts + e))
        return lax.ppermute(rows, ("seq", "exp"), pairs)

    ahead, behind = [block], [block]
    for distance in range(1, far):
        came, went = hop(ahead[-1], 1), hop(behind[-1], -1)
        if distance == 1:
            weights_out, _ = load_near(scalars, expert_out, 0, came)
        ahead.append(came)
        behind.append(went)
    turned = turns[0]
    farthest = far_hop(jnp.where(turned, behind[-2], ahead[-2]))
    made = run_expert(
        scalars, ahead + behind[1:] + [farthest], weights_gate, weights_up, weights_out
    )
    own, to_back, to_front, farthest = made[0], made[1:far], made[far:-1], made[-1]
    going, coming = hop(to_front[-1], 1), hop(to_back[-1], -1)
    early = far_hop(farthest)
    for distance in range(far - 2, 0, -1):
        front, back = to_front[distance - 1], to_back[distance - 1]
        if distance == far - 2:
            nothing = jnp.zeros_like(early)
            going = add_rows(going, front, jnp.where(turned, nothing, early))
            coming = add_rows(coming, back, jnp.where(turned, early, nothing))
        else:
            going = add_rows(going, front)
            coming = add_rows(coming, back)
        going, coming = hop(going, 1), hop(coming, -1)
    return own, going, coming


def slot_ids(block_routes, expert_count, capacity):
    row_count, top_count = block_routes.shape
    expert_ids = jnp.arange(expert_count, dtype=jnp.int32)
    onehot = (
        (block_routes[:, :, None] == expert_ids[None, None, :])
        .astype(jnp.int32)
        .reshape(row_count * top_count, expert_count)
    )
    earlier = jnp.cumsum(onehot, axis=0) - onehot
    ranking = jnp.sum(earlier * onehot, axis=1).reshape(row_count, top_count)
    return block_routes * capacity + ranking


def routed_experts(normed, my_routes, my_gates, expert_in, expert_out):
    sub_count, model_width = normed.shape
    expert_count = lax.axis_size("seq") * expert_in.shape[0]
    top_count = my_routes.shape[1]
    capacity = min(sub_count, max(2, 3 * sub_count * top_count // (2 * expert_count)))
    slot_count = expert_count * capacity
    my_slots = slot_ids(my_routes, expert_count, capacity)
    columns = jnp.arange(slot_count, dtype=jnp.int32)
    placer = jnp.sum(
        (my_slots[None, :, :] == columns[:, None, None]).astype(jnp.int32), axis=2
    ).astype(BF16)
    outgoing = (
        jnp.dot(placer, normed, preferred_element_type=F32)
        .astype(BF16)
        .reshape(expert_count, capacity, model_width)
    )
    arrived = lax.all_to_all(outgoing, "seq", split_axis=0, concat_axis=0, tiled=True)
    flat_rows = arrived.reshape(-1, model_width)
    gate_up = jnp.einsum("nd,gdf->gnf", flat_rows, expert_in[0], preferred_element_type=F32)
    activated = (jax.nn.silu(gate_up[0]) * gate_up[1]).astype(BF16)
    produced = jnp.dot(activated, expert_out[0], preferred_element_type=F32).astype(BF16)
    answered = produced.reshape(arrived.shape)
    returned = lax.all_to_all(answered, "seq", split_axis=0, concat_axis=0, tiled=True)
    picked = returned.reshape(slot_count, model_width)[my_slots.reshape(-1)].reshape(
        sub_count, top_count, model_width
    )
    return jnp.sum(picked.astype(F32) * my_gates[:, :, None], axis=1)


def swap_pairs(rows, distance):
    count = lax.axis_size("seq")
    return lax.ppermute(rows, "seq", [(i, i ^ (2 * distance)) for i in range(count)])


def prior_states(total, later):
    pairs = lax.axis_size("seq") // 2
    bits = len(later)
    if pairs <= 4:
        terms = [
            swap_pairs(total, distance).astype(F32) * later[distance.bit_length() - 1]
            for distance in range(1, pairs)
        ]
        return sum(terms)
    before = jnp.zeros(total.shape, F32)
    for b in range(bits):
        came = swap_pairs(total, 1 << b)
        before = before + came.astype(F32) * later[b]
        total = add_rows(total, came)
    return before


def exchange(pieces):
    parts = len(pieces)
    return [pieces[0]] + [
        lax.ppermute(pieces[j], "exp", [(i, i ^ j) for i in range(parts)])
        for j in range(1, parts)
    ]


def turn_order(items, turns):
    for b, turn in enumerate(turns):
        items = [jnp.where(turn, items[i ^ (1 << b)], items[i]) for i in range(len(items))]
    return items


def per_device(
    residual,
    queries,
    key_vectors,
    value_vectors,
    head_gain,
    norm_gain,
    routes,
    route_gates,
    expert_in,
    expert_out,
):
    rows, width = residual.shape
    seq, parts = lax.axis_size("seq"), lax.axis_size("exp")
    count, half, model = rows // parts, width // 2, width * parts
    experts = seq * expert_in.shape[0]
    position = lax.axis_index("seq")
    my_index = lax.axis_index("exp")
    place = position % 2
    scalars = jnp.stack([my_index, place, experts, position]).astype(jnp.int32)
    swap = [(i, i ^ 1) for i in range(seq)]
    pair_bits, part_bits = (seq // 2).bit_length() - 1, parts.bit_length() - 1
    first, second, *later = [
        flag.astype(F32).reshape(1, 1)
        for flag in [1 - place, place] + [(position >> (b + 1)) & 1 for b in range(pair_bits)]
    ]
    turns = [((my_index >> b) & 1 != 0).reshape(1, 1) for b in range(part_bits)]
    scalars, first, second, later, turns = lax.optimization_barrier(
        (scalars, first, second, later, turns)
    )
    state, heads = shape((HEAD, half), BF16), shape((rows, width), BF16)
    kept, given, keys, values, query, rest, my_gain, my_norm = call(
        open_kernel,
        [state] * 2 + [heads] * 4 + [shape((1, width), F32), shape((1, model), F32)],
        [
            scalars, key_vectors, value_vectors, queries, residual, head_gain[None, :],
            norm_gain[None, :],
        ],
        far=(1, 2, 3, 4, 5, 6),
        scratch=[pltpu.SemaphoreType.DMA((6,))],
        flops=2 * rows * width * HEAD,
    )
    partner = lax.ppermute(given, "seq", swap)
    [within] = call(
        within_kernel, [shape((rows, width), F32)], [scalars, keys, values, query],
        flops=6 * rows * rows * width,
    )
    dense = routes.shape[1] == experts
    total, within = lax.optimization_barrier((add_rows(kept, partner), within))
    before = prior_states(total, later)
    sign = jnp.zeros((8, HEAD), F32)
    if dense:
        weights_gate, sign = load_near(scalars, expert_in[0], 0, total)
    lacked = (before + kept.astype(F32) * first + sign[:1, :1]).astype(BF16)
    mine = before + partner.astype(F32) * second
    if dense:
        weights_up, sign = load_near(scalars, expert_in[0], 1, lacked)
    other = lax.ppermute(lacked, "seq", swap)
    pieces = call(
        functools.partial(attend_kernel, parts),
        [shape((count, width), BF16)] * parts,
        [scalars, sign, within, query, rest, my_gain, mine, other],
        scratch=[pltpu.VMEM((rows, width), BF16)],
        flops=4 * rows * width * HEAD,
    )
    gathered = exchange(pieces)

    my_routes = lax.dynamic_slice_in_dim(routes, my_index * count, count, 0)
    my_gates = lax.dynamic_slice_in_dim(route_gates, my_index * count, count, 0)
    mixing = jnp.sum(
        jnp.where(
            my_routes[:, :, None] == jnp.arange(experts, dtype=jnp.int32),
            my_gates[:, :, None],
            0.0,
        ),
        axis=1,
    )
    high = lax.reduce_precision(mixing, 8, 7)
    lanes = -(-2 * experts // HEAD) * HEAD
    pack = jnp.pad(
        jnp.concatenate([high, mixing - high], axis=1), ((0, 0), (0, lanes - 2 * experts))
    ).astype(BF16)
    hidden, block = call(
        norm_kernel,
        [shape((count, model), BF16), shape((count, model + lanes), BF16)],
        [scalars, my_norm, pack] + gathered,
    )
    if dense:
        terms = dense_experts(
            block, scalars, turns, weights_gate, weights_up, expert_out
        )
    else:
        mixed = routed_experts(block[:, :model], my_routes, my_gates, expert_in, expert_out)
        terms = [mixed]
    own, *others = terms
    mixed = own.astype(F32) + sum(t.astype(F32) for t in others)
    ready = (hidden.astype(F32) + mixed).astype(BF16)
    columns = [ready[:, i * width:(i + 1) * width] for i in range(parts)]
    return jnp.concatenate(turn_order(exchange(turn_order(columns, turns)), turns))


def solution(mesh):
    placed = (
        P("seq", "exp"),
        P("seq", "exp"),
        P("seq", "exp"),
        P("seq", "exp"),
        P("exp"),
        P(),
        P("seq", None),
        P("seq", None),
        P("seq", None, None, None),
        P("seq", None, None),
    )
    return jax.shard_map(
        per_device, mesh=mesh, in_specs=placed, out_specs=P("seq", "exp"), check_vma=False
    )
```

```python
import functools

import jax
import jax.numpy as jnp
from jax import lax
from jax.experimental import pallas as pl
from jax.experimental.pallas import tpu as pltpu
from jax.sharding import PartitionSpec as P

HEAD = 128
F32 = jnp.float32
BF16 = jnp.bfloat16
WHOLE = pl.BlockSpec(memory_space=pltpu.VMEM)
FAR = pl.BlockSpec(memory_space=pltpu.HBM)
SCALAR = pl.BlockSpec(memory_space=pltpu.SMEM)


def call(kernel, outs, inputs, far=(), small=(), scratch=(), out_specs=None, flops=0, limit=16 << 20):
    moved = sum(a.size * a.dtype.itemsize for a in [*inputs, *outs])
    inputs = [
        pltpu.with_memory_space_constraint(a, pltpu.HBM) if i in far else a
        for i, a in enumerate(inputs)
    ]
    return pl.pallas_call(
        kernel,
        out_shape=outs,
        in_specs=[
            SCALAR if i == 0 or i in small else FAR if i in far else WHOLE
            for i in range(len(inputs))
        ],
        out_specs=out_specs or [WHOLE] * len(outs),
        scratch_shapes=scratch,
        compiler_params=pltpu.CompilerParams(vmem_limit_bytes=limit),
        cost_estimate=pl.CostEstimate(flops=flops, bytes_accessed=moved, transcendentals=0),
    )(*inputs)


def shape(dims, dtype):
    return jax.ShapeDtypeStruct(dims, dtype)


def split(value):
    high = value.astype(BF16)
    return high, (value - high.astype(F32)).astype(BF16)


def add_rows(*terms):
    return sum(t.astype(F32) for t in terms).astype(BF16)


def run_copies(pairs, sems):
    copies = [pltpu.make_async_copy(a, b, sems.at[i]) for i, (a, b) in enumerate(pairs)]
    for copy in copies:
        copy.start()
    for copy in copies:
        copy.wait()


def open_kernel(
    scalars, key_ref, value_ref, query_ref, residual_ref, gain_ref, norm_ref,
    kept_ref, given_ref, keys, values, query, residual, gain, norm, sems
):
    pairs = [
        (key_ref, keys), (value_ref, values), (query_ref, query), (residual_ref, residual),
        (gain_ref, gain), (norm_ref, norm),
    ]
    copies = [pltpu.make_async_copy(a, b, sems.at[i]) for i, (a, b) in enumerate(pairs)]
    for copy in copies:
        copy.start()
    for copy in copies[:2]:
        copy.wait()
    width = keys.shape[1] // 2
    place = scalars[1]
    sides = []
    for side in range(2):
        cols = slice(side * width, (side + 1) * width)
        square = lax.dot_general(
            keys[:, cols], values[:, cols], (((0,), (0,)), ((), ())), preferred_element_type=F32
        )
        sides.append(
            jnp.concatenate(
                [square[h:h + HEAD, h:h + HEAD] for h in range(0, width, HEAD)], axis=1
            ).astype(BF16)
        )
    kept_ref[...] = jnp.where(place == 0, sides[0], sides[1])
    given_ref[...] = jnp.where(place == 0, sides[1], sides[0])
    for copy in copies[2:]:
        copy.wait()


def within_kernel(scalars, keys, values, queries, out_ref):
    rows, width = out_ref.shape
    causal = lax.broadcasted_iota(jnp.int32, (rows, rows), 0) >= lax.broadcasted_iota(
        jnp.int32, (rows, rows), 1
    )
    for start in range(0, width, HEAD):
        cols = slice(start, start + HEAD)
        scores = lax.dot_general(
            queries[:, cols], keys[:, cols], (((1,), (1,)), ((), ())), preferred_element_type=F32
        )
        high, low = split(jnp.where(causal, scores, 0.0))
        out_ref[:, cols] = jnp.dot(
            high, values[:, cols], preferred_element_type=F32
        ) + jnp.dot(low, values[:, cols], preferred_element_type=F32)


def back_kernel(earlier, scalars, sign_ref, kept_ref, partner_ref, *refs):
    came_refs, mine_ref, lacked_ref = refs[:earlier], refs[earlier], refs[earlier + 1]
    before = jnp.zeros(mine_ref.shape, F32)
    for i, ref in enumerate(came_refs):
        before += jnp.where(scalars[4 + i] == 1, ref[...].astype(F32), 0.0)
    first = scalars[1] == 0
    mine_ref[...] = before + jnp.where(first, 0.0, partner_ref[...].astype(F32))
    lacked_ref[...] = (before + jnp.where(first, kept_ref[...].astype(F32), 0.0)).astype(BF16)


def attend_kernel(
    parts, scalars, within_ref, queries, residuals, gain_ref, mine_ref, other_ref, *refs
):
    piece_refs, hidden = refs[:-1], refs[-1]
    rows, full = hidden.shape
    width = full // 2
    first = scalars[1] == 0
    mine, other = mine_ref[...], other_ref[...].astype(F32)
    halves = [jnp.where(first, mine, other), jnp.where(first, other, mine)]
    for start in range(0, full, HEAD):
        cols = slice(start, start + HEAD)
        half, inner = divmod(start, width)
        high, low = split(halves[half][:, inner:inner + HEAD])
        raw = (
            jnp.dot(queries[:, cols], high, preferred_element_type=F32)
            + jnp.dot(queries[:, cols], low, preferred_element_type=F32)
            + within_ref[:, cols]
        )
        scaled = raw * lax.rsqrt(jnp.mean(raw * raw, axis=-1, keepdims=True) + 1e-06)
        hidden[:, cols] = (residuals[:, cols].astype(F32) + scaled * gain_ref[:, cols]).astype(BF16)
    count = rows // parts
    for j, piece in enumerate(piece_refs):
        piece[...] = hidden[pl.ds(pl.multiple_of((scalars[0] ^ j) * count, count), count), :]


def norm_kernel(scalars, sign_ref, gain_ref, pack_ref, *refs):
    pieces, hidden_ref, out_ref = refs[:-2], refs[-2], refs[-1]
    width = pieces[0].shape[1]
    model = hidden_ref.shape[1]
    total = 0.0
    for ref in pieces:
        value = ref[...].astype(F32)
        total += jnp.sum(value * value, axis=-1, keepdims=True)
    scale = lax.rsqrt(total / model + 1e-06)
    for j, ref in enumerate(pieces):
        cols = pl.ds(pl.multiple_of((scalars[0] ^ j) * width, width), width)
        hidden_ref[:, cols] = ref[...]
        out_ref[:, cols] = (ref[...].astype(F32) * scale * gain_ref[:, cols]).astype(BF16)
    out_ref[:, model:] = pack_ref[...]


def load_kernel(lead, scalars, source, after_ref, target, done_ref, sems):
    done_ref[...] = jnp.zeros_like(done_ref)
    pieces = sems.shape[0]
    step = target.shape[0] // pieces
    cuts = [pl.ds(i * step, step) for i in range(pieces)]
    run_copies([(source.at[lead, cut], target.at[cut]) for cut in cuts], sems)


def load_near(scalars, source, lead, after):
    return call(
        functools.partial(load_kernel, lead),
        [shape(source.shape[1:], source.dtype), shape((8, HEAD), F32)],
        [scalars, source, after], far=(1,), scratch=[pltpu.SemaphoreType.DMA((8,))],
    )


def expert_kernel(blocks, scalars, gate_ref, up_ref, down_ref, *refs):
    x_refs, out_refs = refs[:blocks], refs[blocks:2 * blocks]
    rows_ref, act_ref, made_ref = refs[2 * blocks:]
    model, units = gate_ref.shape
    spans, packs = [], []
    first = 0
    for ref in x_refs:
        spans.append(slice(first, first + ref.shape[0]))
        rows_ref[spans[-1], :] = ref[:, :model]
        packs.append(ref[:, model:].astype(F32))
        first += ref.shape[0]
    pack = jnp.concatenate(packs)
    lane = lax.broadcasted_iota(jnp.int32, pack.shape, 1)
    chosen = (lane == scalars[3]) | (lane == scalars[3] + scalars[2])
    weight = jnp.sum(jnp.where(chosen, pack, 0.0), axis=-1, keepdims=True)
    chunk = min(units, 512)

    @pl.loop(0, units // chunk)
    def _(step):
        cut = pl.ds(pl.multiple_of(step * chunk, chunk), chunk)
        gate = jnp.dot(rows_ref[...], gate_ref[:, cut], preferred_element_type=F32)
        up = jnp.dot(rows_ref[...], up_ref[:, cut], preferred_element_type=F32)
        act_ref[:, cut] = (gate / (1.0 + jnp.exp(-gate)) * up).astype(BF16)

    wide = min(model, 1024)

    @pl.loop(0, model // wide)
    def _(step):
        cut = pl.ds(pl.multiple_of(step * wide, wide), wide)
        produced = jnp.dot(act_ref[...], down_ref[:, cut], preferred_element_type=F32)
        made_ref[:, cut] = (produced.astype(BF16).astype(F32) * weight).astype(BF16)

    for out_ref, span in zip(out_refs, spans):
        out_ref[...] = made_ref[span, :]


def run_expert(scalars, blocks, weights_gate, weights_up, weights_out):
    units, model = weights_out.shape
    total = sum(b.shape[0] for b in blocks)
    return call(
        functools.partial(expert_kernel, len(blocks)),
        [shape((b.shape[0], model), BF16) for b in blocks],
        [scalars, weights_gate, weights_up, weights_out, *blocks],
        scratch=[
            pltpu.VMEM((total, model), BF16),
            pltpu.VMEM((total, units), BF16),
            pltpu.VMEM((total, model), BF16),
        ],
        flops=6 * total * model * units,
        limit=24 << 20,
    )


def ring_order(count):
    return list(range(0, count, 2)) + list(range(1, count, 2))[::-1]


def far_sides(position, my_index, count):
    place = jnp.where(position % 2 == 0, position // 2, count - 1 - position // 2)
    onward = ((place // 2) % 2 == 0) != (my_index % 2 == 1)
    return onward == (place % 2 == 1)


def dense_experts(block, scalars, pick, weights_gate, weights_up, expert_out):
    count, parts = lax.axis_size("seq"), lax.axis_size("exp")
    order = ring_order(count)
    far = count // 2

    def trade(rows, pairs):
        both = [(order[a], order[b]) for a, b in pairs]
        return lax.ppermute(rows, "seq", both + [(b, a) for a, b in both])

    def trade_first(rows):
        return trade(rows, [(p, p + 1) for p in range(0, count, 2)])

    def trade_second(rows):
        return trade(rows, [(p, (p + 1) % count) for p in range(1, count, 2)])

    def trade_far(rows):
        pairs = []
        for e in range(parts):
            for p in range(count):
                ahead = (p // 2) % 2 == e % 2
                other = order[(p + (2 if ahead else -2)) % count]
                pairs.append((order[p] * parts + e, other * parts + e))
        return lax.ppermute(rows, ("seq", "exp"), pairs)

    first, second = [block], [block]
    for distance in range(1, far):
        came = trade_first(second[-1]), trade_second(first[-1])
        if distance == 1:
            weights_out, _ = load_near(scalars, expert_out, 0, came[0])
        first.append(came[0])
        second.append(came[1])
    farthest = trade_far(jnp.where(pick, first[-2], second[-2]))
    own, *made, farthest = run_expert(
        scalars, first + second[1:] + [farthest], weights_gate, weights_up, weights_out
    )
    made_first, made_second = made[:far - 1], made[far - 1:]
    back_first, back_second = made_first[-1], made_second[-1]
    early = trade_far(farthest)
    for distance in range(far - 2, -1, -1):
        to_second, to_first = trade_first(back_first), trade_second(back_second)
        if distance == 0:
            return own, to_second, to_first
        terms_first = [made_first[distance - 1], to_first]
        terms_second = [made_second[distance - 1], to_second]
        if distance == far - 2:
            nothing = jnp.zeros_like(early)
            terms_first.append(jnp.where(pick, early, nothing))
            terms_second.append(jnp.where(pick, nothing, early))
        back_first, back_second = add_rows(*terms_first), add_rows(*terms_second)


def slot_ids(block_routes, expert_count, capacity):
    row_count, top_count = block_routes.shape
    expert_ids = jnp.arange(expert_count, dtype=jnp.int32)
    onehot = (
        (block_routes[:, :, None] == expert_ids[None, None, :])
        .astype(jnp.int32)
        .reshape(row_count * top_count, expert_count)
    )
    earlier = jnp.cumsum(onehot, axis=0) - onehot
    ranking = jnp.sum(earlier * onehot, axis=1).reshape(row_count, top_count)
    return block_routes * capacity + ranking


def routed_experts(normed, my_routes, my_gates, expert_in, expert_out):
    sub_count, model_width = normed.shape
    expert_count = lax.axis_size("seq") * expert_in.shape[0]
    top_count = my_routes.shape[1]
    capacity = min(sub_count, max(2, 3 * sub_count * top_count // (2 * expert_count)))
    slot_count = expert_count * capacity
    my_slots = slot_ids(my_routes, expert_count, capacity)
    columns = jnp.arange(slot_count, dtype=jnp.int32)
    placer = jnp.sum(
        (my_slots[None, :, :] == columns[:, None, None]).astype(jnp.int32), axis=2
    ).astype(BF16)
    outgoing = (
        jnp.dot(placer, normed, preferred_element_type=F32)
        .astype(BF16)
        .reshape(expert_count, capacity, model_width)
    )
    arrived = lax.all_to_all(outgoing, "seq", split_axis=0, concat_axis=0, tiled=True)
    flat_rows = arrived.reshape(-1, model_width)
    gate_up = jnp.einsum("nd,gdf->gnf", flat_rows, expert_in[0], preferred_element_type=F32)
    activated = (jax.nn.silu(gate_up[0]) * gate_up[1]).astype(BF16)
    produced = jnp.dot(activated, expert_out[0], preferred_element_type=F32).astype(BF16)
    answered = produced.reshape(arrived.shape)
    returned = lax.all_to_all(answered, "seq", split_axis=0, concat_axis=0, tiled=True)
    picked = returned.reshape(slot_count, model_width)[my_slots.reshape(-1)].reshape(
        sub_count, top_count, model_width
    )
    return jnp.sum(picked.astype(F32) * my_gates[:, :, None], axis=1)


def swap_pairs(rows, distance):
    count = lax.axis_size("seq")
    return lax.ppermute(rows, "seq", [(i, i ^ (2 * distance)) for i in range(count)])


def pair_steps(pairs):
    bits = pairs.bit_length() - 1
    direct = pairs <= 4
    steps = range(1, pairs) if direct else [1 << b for b in range(bits)]
    return direct, [(d, d.bit_length() - 1) for d in steps]


def prior_states(total):
    count = lax.axis_size("seq")
    direct, steps = pair_steps(count // 2)
    terms = []
    for distance, _ in steps:
        terms.append(
            lax.ppermute(total, "seq", [(i, i ^ (2 * distance)) for i in range(count)])
        )
        if not direct:
            total = add_rows(total, terms[-1])
    return terms


def exchange(pieces):
    parts = len(pieces)
    return [pieces[0]] + [
        lax.ppermute(pieces[j], "exp", [(i, i ^ j) for i in range(parts)])
        for j in range(1, parts)
    ]


def turn_order(items, turns):
    for b, turn in enumerate(turns):
        items = [jnp.where(turn, items[i ^ (1 << b)], items[i]) for i in range(len(items))]
    return items


def per_device(
    residual,
    queries,
    key_vectors,
    value_vectors,
    head_gain,
    norm_gain,
    routes,
    route_gates,
    expert_in,
    expert_out,
):
    rows, width = residual.shape
    seq, parts = lax.axis_size("seq"), lax.axis_size("exp")
    count, half, model = rows // parts, width // 2, width * parts
    experts = seq * expert_in.shape[0]
    position = lax.axis_index("seq")
    my_index = lax.axis_index("exp")
    place = position % 2
    _, steps = pair_steps(seq // 2)
    scalars = jnp.stack(
        [my_index, place, experts, position] + [(position >> (bit + 1)) & 1 for _, bit in steps]
    ).astype(jnp.int32)
    swap = [(i, i ^ 1) for i in range(seq)]
    turns = [
        ((my_index >> b) & 1 != 0).reshape(1, 1) for b in range(parts.bit_length() - 1)
    ]
    pick = far_sides(position, my_index, seq).reshape(1, 1)
    my_rows = (my_index * count).astype(jnp.uint32)
    scalars, turns, pick, my_rows = lax.optimization_barrier((scalars, turns, pick, my_rows))
    state, heads = shape((HEAD, half), BF16), shape((rows, width), BF16)
    kept, given, keys, values, query, rest, my_gain, my_norm = call(
        open_kernel,
        [state] * 2 + [heads] * 4 + [shape((1, width), F32), shape((1, model), F32)],
        [
            scalars, key_vectors, value_vectors, queries, residual, head_gain[None, :],
            norm_gain[None, :],
        ],
        far=(1, 2, 3, 4, 5, 6),
        scratch=[pltpu.SemaphoreType.DMA((6,))],
        flops=2 * rows * width * HEAD,
    )
    partner = lax.ppermute(given, "seq", swap)
    [within] = call(
        within_kernel, [shape((rows, width), F32)], [scalars, keys, values, query],
        flops=6 * rows * rows * width,
    )
    dense = routes.shape[1] == experts
    total, sign = add_rows(kept, partner), jnp.zeros((8, HEAD), F32)
    if dense:
        weights_gate, sign = load_near(scalars, expert_in[0], 0, given)
        total, sign = lax.optimization_barrier((total, sign))
    before = prior_states(total)
    mine, lacked = call(
        functools.partial(back_kernel, len(before)), [shape(state.shape, F32), state],
        [scalars, sign, kept, partner, *before],
    )
    other = lax.ppermute(lacked, "seq", swap)
    pieces = call(
        functools.partial(attend_kernel, parts),
        [shape((count, width), BF16)] * parts,
        [scalars, within, query, rest, my_gain, mine, other],
        scratch=[pltpu.VMEM((rows, width), BF16)],
        flops=4 * rows * width * HEAD,
    )
    gathered = exchange(pieces)
    if dense:
        weights_up, sign = load_near(scalars, expert_in[0], 1, pieces[0])

    my_routes = lax.dynamic_slice_in_dim(routes, my_rows, count, 0)
    my_gates = lax.dynamic_slice_in_dim(route_gates, my_rows, count, 0)
    mixing = jnp.sum(
        jnp.where(
            my_routes[:, :, None] == jnp.arange(experts, dtype=jnp.int32),
            my_gates[:, :, None],
            0.0,
        ),
        axis=1,
    )
    high = lax.reduce_precision(mixing, 8, 7)
    lanes = -(-2 * experts // HEAD) * HEAD
    pack = jnp.pad(
        jnp.concatenate([high, mixing - high], axis=1), ((0, 0), (0, lanes - 2 * experts))
    ).astype(BF16)
    hidden, block = call(
        norm_kernel,
        [shape((count, model), BF16), shape((count, model + lanes), BF16)],
        [scalars, sign, my_norm, pack] + gathered,
    )
    if dense:
        terms = dense_experts(
            block, scalars, pick, weights_gate, weights_up, expert_out
        )
    else:
        mixed = routed_experts(block[:, :model], my_routes, my_gates, expert_in, expert_out)
        terms = [mixed]
    own, *others = terms
    mixed = own.astype(F32) + sum(t.astype(F32) for t in others)
    ready = (hidden.astype(F32) + mixed).astype(BF16)
    columns = [ready[:, i * width:(i + 1) * width] for i in range(parts)]
    return jnp.concatenate(turn_order(exchange(turn_order(columns, turns)), turns))


def solution(mesh):
    placed = (
        P("seq", "exp"),
        P("seq", "exp"),
        P("seq", "exp"),
        P("seq", "exp"),
        P("exp"),
        P(),
        P("seq", None),
        P("seq", None),
        P("seq", None, None, None),
        P("seq", None, None),
    )
    return jax.shard_map(
        per_device, mesh=mesh, in_specs=placed, out_specs=P("seq", "exp"), check_vma=False
    )
```

```python
import functools

import jax
import jax.numpy as jnp
from jax import lax
from jax.experimental import pallas as pl
from jax.experimental.pallas import tpu as pltpu
from jax.sharding import PartitionSpec as P

HEAD = 128
F32 = jnp.float32
BF16 = jnp.bfloat16
WHOLE = pl.BlockSpec(memory_space=pltpu.VMEM)
FAR = pl.BlockSpec(memory_space=pltpu.HBM)
SCALAR = pl.BlockSpec(memory_space=pltpu.SMEM)


def call(kernel, outs, inputs, far=(), small=(), scratch=(), out_specs=None, flops=0, limit=16 << 20):
    moved = sum(a.size * a.dtype.itemsize for a in [*inputs, *outs])
    inputs = [
        pltpu.with_memory_space_constraint(a, pltpu.HBM) if i in far else a
        for i, a in enumerate(inputs)
    ]
    return pl.pallas_call(
        kernel,
        out_shape=outs,
        in_specs=[
            SCALAR if i == 0 or i in small else FAR if i in far else WHOLE
            for i in range(len(inputs))
        ],
        out_specs=out_specs or [WHOLE] * len(outs),
        scratch_shapes=scratch,
        compiler_params=pltpu.CompilerParams(vmem_limit_bytes=limit),
        cost_estimate=pl.CostEstimate(flops=flops, bytes_accessed=moved, transcendentals=0),
    )(*inputs)


def shape(dims, dtype):
    return jax.ShapeDtypeStruct(dims, dtype)


def split(value):
    high = value.astype(BF16)
    return high, (value - high.astype(F32)).astype(BF16)


def add_rows(*terms):
    return sum(t.astype(F32) for t in terms).astype(BF16)


def run_copies(pairs, sems):
    copies = [pltpu.make_async_copy(a, b, sems.at[i]) for i, (a, b) in enumerate(pairs)]
    for copy in copies:
        copy.start()
    for copy in copies:
        copy.wait()


def open_kernel(
    scalars, key_ref, value_ref, query_ref, residual_ref, gain_ref, norm_ref,
    kept_ref, given_ref, keys, values, query, residual, gain, norm, sems
):
    pairs = [
        (key_ref, keys), (value_ref, values), (query_ref, query), (residual_ref, residual),
        (gain_ref, gain), (norm_ref, norm),
    ]
    copies = [pltpu.make_async_copy(a, b, sems.at[i]) for i, (a, b) in enumerate(pairs)]
    for copy in copies:
        copy.start()
    for copy in copies[:2]:
        copy.wait()
    width = keys.shape[1] // 2
    place = scalars[1]
    sides = []
    for side in range(2):
        cols = slice(side * width, (side + 1) * width)
        square = lax.dot_general(
            keys[:, cols], values[:, cols], (((0,), (0,)), ((), ())), preferred_element_type=F32
        )
        sides.append(
            jnp.concatenate(
                [square[h:h + HEAD, h:h + HEAD] for h in range(0, width, HEAD)], axis=1
            ).astype(BF16)
        )
    kept_ref[...] = jnp.where(place == 0, sides[0], sides[1])
    given_ref[...] = jnp.where(place == 0, sides[1], sides[0])
    for copy in copies[2:]:
        copy.wait()


def within_kernel(scalars, keys, values, queries, out_ref):
    rows, width = out_ref.shape
    causal = lax.broadcasted_iota(jnp.int32, (rows, rows), 0) >= lax.broadcasted_iota(
        jnp.int32, (rows, rows), 1
    )
    for start in range(0, width, HEAD):
        cols = slice(start, start + HEAD)
        scores = lax.dot_general(
            queries[:, cols], keys[:, cols], (((1,), (1,)), ((), ())), preferred_element_type=F32
        )
        high, low = split(jnp.where(causal, scores, 0.0))
        out_ref[:, cols] = jnp.dot(
            high, values[:, cols], preferred_element_type=F32
        ) + jnp.dot(low, values[:, cols], preferred_element_type=F32)


def back_kernel(earlier, scalars, sign_ref, kept_ref, partner_ref, *refs):
    came_refs, mine_ref, lacked_ref = refs[:earlier], refs[earlier], refs[earlier + 1]
    before = jnp.zeros(mine_ref.shape, F32)
    for i, ref in enumerate(came_refs):
        before += jnp.where(scalars[4 + i] == 1, ref[...].astype(F32), 0.0)
    first = scalars[1] == 0
    mine_ref[...] = before + jnp.where(first, 0.0, partner_ref[...].astype(F32))
    lacked_ref[...] = (before + jnp.where(first, kept_ref[...].astype(F32), 0.0)).astype(BF16)


def attend_kernel(
    parts, scalars, sign_ref, within_ref, queries, residuals, gain_ref, mine_ref, other_ref, *refs
):
    piece_refs, hidden = refs[:-1], refs[-1]
    rows, full = hidden.shape
    width = full // 2
    first = scalars[1] == 0
    mine, other = mine_ref[...], other_ref[...].astype(F32)
    halves = [jnp.where(first, mine, other), jnp.where(first, other, mine)]
    for start in range(0, full, HEAD):
        cols = slice(start, start + HEAD)
        half, inner = divmod(start, width)
        high, low = split(halves[half][:, inner:inner + HEAD])
        raw = (
            jnp.dot(queries[:, cols], high, preferred_element_type=F32)
            + jnp.dot(queries[:, cols], low, preferred_element_type=F32)
            + within_ref[:, cols]
        )
        scaled = raw * lax.rsqrt(jnp.mean(raw * raw, axis=-1, keepdims=True) + 1e-06)
        hidden[:, cols] = (residuals[:, cols].astype(F32) + scaled * gain_ref[:, cols]).astype(BF16)
    count = rows // parts
    for j, piece in enumerate(piece_refs):
        piece[...] = hidden[pl.ds(pl.multiple_of((scalars[0] ^ j) * count, count), count), :]


def norm_kernel(scalars, gain_ref, pack_ref, *refs):
    pieces, hidden_ref, out_ref = refs[:-2], refs[-2], refs[-1]
    width = pieces[0].shape[1]
    model = hidden_ref.shape[1]
    total = 0.0
    for ref in pieces:
        value = ref[...].astype(F32)
        total += jnp.sum(value * value, axis=-1, keepdims=True)
    scale = lax.rsqrt(total / model + 1e-06)
    for j, ref in enumerate(pieces):
        cols = pl.ds(pl.multiple_of((scalars[0] ^ j) * width, width), width)
        hidden_ref[:, cols] = ref[...]
        out_ref[:, cols] = (ref[...].astype(F32) * scale * gain_ref[:, cols]).astype(BF16)
    out_ref[:, model:] = pack_ref[...]


def load_kernel(lead, scalars, source, after_ref, target, done_ref, sems):
    done_ref[...] = jnp.zeros_like(done_ref)
    pieces = sems.shape[0]
    step = target.shape[0] // pieces
    cuts = [pl.ds(i * step, step) for i in range(pieces)]
    run_copies([(source.at[lead, cut], target.at[cut]) for cut in cuts], sems)


def load_near(scalars, source, lead, after):
    return call(
        functools.partial(load_kernel, lead),
        [shape(source.shape[1:], source.dtype), shape((8, HEAD), F32)],
        [scalars, source, after], far=(1,), scratch=[pltpu.SemaphoreType.DMA((8,))],
    )


def expert_kernel(blocks, scalars, gate_ref, up_ref, down_ref, *refs):
    x_refs, out_refs = refs[:blocks], refs[blocks:2 * blocks]
    rows_ref, act_ref, made_ref = refs[2 * blocks:]
    model, units = gate_ref.shape
    spans, packs = [], []
    first = 0
    for ref in x_refs:
        spans.append(slice(first, first + ref.shape[0]))
        rows_ref[spans[-1], :] = ref[:, :model]
        packs.append(ref[:, model:].astype(F32))
        first += ref.shape[0]
    pack = jnp.concatenate(packs)
    lane = lax.broadcasted_iota(jnp.int32, pack.shape, 1)
    chosen = (lane == scalars[3]) | (lane == scalars[3] + scalars[2])
    weight = jnp.sum(jnp.where(chosen, pack, 0.0), axis=-1, keepdims=True)
    chunk = min(units, 512)

    for step in range(units // chunk):
        cut = slice(step * chunk, (step + 1) * chunk)
        gate = jnp.dot(rows_ref[...], gate_ref[:, cut], preferred_element_type=F32)
        up = jnp.dot(rows_ref[...], up_ref[:, cut], preferred_element_type=F32)
        act_ref[:, cut] = (gate / (1.0 + jnp.exp(-gate)) * up).astype(BF16)

    wide = min(model, 1024)

    for step in range(model // wide):
        cut = slice(step * wide, (step + 1) * wide)
        produced = jnp.dot(act_ref[...], down_ref[:, cut], preferred_element_type=F32)
        made_ref[:, cut] = (produced.astype(BF16).astype(F32) * weight).astype(BF16)

    for out_ref, span in zip(out_refs, spans):
        out_ref[...] = made_ref[span, :]


def run_expert(scalars, blocks, weights_gate, weights_up, weights_out):
    units, model = weights_out.shape
    total = sum(b.shape[0] for b in blocks)
    return call(
        functools.partial(expert_kernel, len(blocks)),
        [shape((b.shape[0], model), BF16) for b in blocks],
        [scalars, weights_gate, weights_up, weights_out, *blocks],
        scratch=[
            pltpu.VMEM((total, model), BF16),
            pltpu.VMEM((total, units), BF16),
            pltpu.VMEM((total, model), BF16),
        ],
        flops=6 * total * model * units,
        limit=24 << 20,
    )


def ring_order(count):
    return list(range(0, count, 2)) + list(range(1, count, 2))[::-1]


def dense_experts(block, scalars, weights_gate, weights_up, expert_out):
    count, parts = lax.axis_size("seq"), lax.axis_size("exp")
    order = ring_order(count)
    far = count // 2

    def hop(rows, steps):
        pairs = []
        for e in range(parts):
            for p in range(count):
                target = order[(p + (steps if e % 2 == 0 else -steps)) % count]
                pairs.append((order[p] * parts + e, target * parts + e))
        return lax.ppermute(rows, ("seq", "exp"), pairs)

    first, second = [block], [block]
    for distance in range(1, far):
        first.append(hop(first[-1], 1))
        second.append(hop(second[-1], -1))
        if distance == 1:
            weights_out, _ = load_near(scalars, expert_out, 0, first[-1])
    farthest = hop(first[-2], 2)
    own, *made, farthest = run_expert(
        scalars, first + second[1:] + [farthest], weights_gate, weights_up, weights_out
    )
    made_first, made_second = made[:far - 1], made[far - 1:]
    back_first, back_second = hop(made_first[-1], -1), hop(made_second[-1], 1)
    early = [hop(farthest, -2)]
    for distance in range(far - 2, 0, -1):
        back_first = add_rows(back_first, made_first[distance - 1], *early)
        back_second = add_rows(back_second, made_second[distance - 1])
        back_first, back_second = hop(back_first, -1), hop(back_second, 1)
        early = []
    return own, back_first, back_second


def slot_ids(block_routes, expert_count, capacity):
    row_count, top_count = block_routes.shape
    expert_ids = jnp.arange(expert_count, dtype=jnp.int32)
    onehot = (
        (block_routes[:, :, None] == expert_ids[None, None, :])
        .astype(jnp.int32)
        .reshape(row_count * top_count, expert_count)
    )
    earlier = jnp.cumsum(onehot, axis=0) - onehot
    ranking = jnp.sum(earlier * onehot, axis=1).reshape(row_count, top_count)
    return block_routes * capacity + ranking


def routed_experts(normed, my_routes, my_gates, expert_in, expert_out):
    sub_count, model_width = normed.shape
    expert_count = lax.axis_size("seq") * expert_in.shape[0]
    top_count = my_routes.shape[1]
    capacity = min(sub_count, max(2, 3 * sub_count * top_count // (2 * expert_count)))
    slot_count = expert_count * capacity
    my_slots = slot_ids(my_routes, expert_count, capacity)
    columns = jnp.arange(slot_count, dtype=jnp.int32)
    placer = jnp.sum(
        (my_slots[None, :, :] == columns[:, None, None]).astype(jnp.int32), axis=2
    ).astype(BF16)
    outgoing = (
        jnp.dot(placer, normed, preferred_element_type=F32)
        .astype(BF16)
        .reshape(expert_count, capacity, model_width)
    )
    arrived = lax.all_to_all(outgoing, "seq", split_axis=0, concat_axis=0, tiled=True)
    flat_rows = arrived.reshape(-1, model_width)
    gate_up = jnp.einsum("nd,gdf->gnf", flat_rows, expert_in[0], preferred_element_type=F32)
    activated = (jax.nn.silu(gate_up[0]) * gate_up[1]).astype(BF16)
    produced = jnp.dot(activated, expert_out[0], preferred_element_type=F32).astype(BF16)
    answered = produced.reshape(arrived.shape)
    returned = lax.all_to_all(answered, "seq", split_axis=0, concat_axis=0, tiled=True)
    picked = returned.reshape(slot_count, model_width)[my_slots.reshape(-1)].reshape(
        sub_count, top_count, model_width
    )
    return jnp.sum(picked.astype(F32) * my_gates[:, :, None], axis=1)


def swap_pairs(rows, distance):
    count = lax.axis_size("seq")
    return lax.ppermute(rows, "seq", [(i, i ^ (2 * distance)) for i in range(count)])


def pair_steps(pairs):
    bits = pairs.bit_length() - 1
    direct = pairs <= 4
    steps = range(1, pairs) if direct else [1 << b for b in range(bits)]
    return direct, [(d, d.bit_length() - 1) for d in steps]


def prior_states(total):
    count = lax.axis_size("seq")
    direct, steps = pair_steps(count // 2)
    terms = []
    for distance, _ in steps:
        terms.append(
            lax.ppermute(total, "seq", [(i, i ^ (2 * distance)) for i in range(count)])
        )
        if not direct:
            total = add_rows(total, terms[-1])
    return terms


def exchange(pieces):
    parts = len(pieces)
    return [pieces[0]] + [
        lax.ppermute(pieces[j], "exp", [(i, i ^ j) for i in range(parts)])
        for j in range(1, parts)
    ]


def turn_order(items, turns):
    for b, turn in enumerate(turns):
        items = [jnp.where(turn, items[i ^ (1 << b)], items[i]) for i in range(len(items))]
    return items


def per_device(
    residual,
    queries,
    key_vectors,
    value_vectors,
    head_gain,
    norm_gain,
    routes,
    route_gates,
    expert_in,
    expert_out,
):
    rows, width = residual.shape
    seq, parts = lax.axis_size("seq"), lax.axis_size("exp")
    count, half, model = rows // parts, width // 2, width * parts
    experts = seq * expert_in.shape[0]
    position = lax.axis_index("seq")
    my_index = lax.axis_index("exp")
    place = position % 2
    _, steps = pair_steps(seq // 2)
    scalars = jnp.stack(
        [my_index, place, experts, position] + [(position >> (bit + 1)) & 1 for _, bit in steps]
    ).astype(jnp.int32)
    swap = [(i, i ^ 1) for i in range(seq)]
    turns = [
        ((my_index >> b) & 1 != 0).reshape(1, 1) for b in range(parts.bit_length() - 1)
    ]
    my_rows = (my_index * count).astype(jnp.uint32)
    scalars, turns, my_rows = lax.optimization_barrier((scalars, turns, my_rows))
    state, heads = shape((HEAD, half), BF16), shape((rows, width), BF16)
    kept, given, keys, values, query, rest, my_gain, my_norm = call(
        open_kernel,
        [state] * 2 + [heads] * 4 + [shape((1, width), F32), shape((1, model), F32)],
        [
            scalars, key_vectors, value_vectors, queries, residual, head_gain[None, :],
            norm_gain[None, :],
        ],
        far=(1, 2, 3, 4, 5, 6),
        scratch=[pltpu.SemaphoreType.DMA((6,))],
        flops=2 * rows * width * HEAD,
    )
    partner = lax.ppermute(given, "seq", swap)
    [within] = call(
        within_kernel, [shape((rows, width), F32)], [scalars, keys, values, query],
        flops=6 * rows * rows * width,
    )
    dense = routes.shape[1] == experts
    total, within = lax.optimization_barrier((add_rows(kept, partner), within))
    sign = jnp.zeros((8, HEAD), F32)
    if dense:
        weights_gate, sign = load_near(scalars, expert_in[0], 0, total)
    before = prior_states(total)
    mine, lacked = call(
        functools.partial(back_kernel, len(before)), [shape(state.shape, F32), state],
        [scalars, sign, kept, partner, *before],
    )
    other = lax.ppermute(lacked, "seq", swap)
    if dense:
        weights_up, sign = load_near(scalars, expert_in[0], 1, lacked)
    pieces = call(
        functools.partial(attend_kernel, parts),
        [shape((count, width), BF16)] * parts,
        [scalars, sign, within, query, rest, my_gain, mine, other],
        scratch=[pltpu.VMEM((rows, width), BF16)],
        flops=4 * rows * width * HEAD,
    )
    gathered = exchange(pieces)

    my_routes = lax.dynamic_slice_in_dim(routes, my_rows, count, 0)
    my_gates = lax.dynamic_slice_in_dim(route_gates, my_rows, count, 0)
    mixing = jnp.sum(
        jnp.where(
            my_routes[:, :, None] == jnp.arange(experts, dtype=jnp.int32),
            my_gates[:, :, None],
            0.0,
        ),
        axis=1,
    )
    high = lax.reduce_precision(mixing, 8, 7)
    lanes = -(-2 * experts // HEAD) * HEAD
    pack = jnp.pad(
        jnp.concatenate([high, mixing - high], axis=1), ((0, 0), (0, lanes - 2 * experts))
    ).astype(BF16)
    hidden, block = call(
        norm_kernel,
        [shape((count, model), BF16), shape((count, model + lanes), BF16)],
        [scalars, my_norm, pack] + gathered,
    )
    if dense:
        terms = dense_experts(
            block, scalars, weights_gate, weights_up, expert_out
        )
    else:
        mixed = routed_experts(block[:, :model], my_routes, my_gates, expert_in, expert_out)
        terms = [mixed]
    own, *others = terms
    mixed = own.astype(F32) + sum(t.astype(F32) for t in others)
    ready = (hidden.astype(F32) + mixed).astype(BF16)
    columns = [ready[:, i * width:(i + 1) * width] for i in range(parts)]
    return jnp.concatenate(turn_order(exchange(turn_order(columns, turns)), turns))


def solution(mesh):
    placed = (
        P("seq", "exp"),
        P("seq", "exp"),
        P("seq", "exp"),
        P("seq", "exp"),
        P("exp"),
        P(),
        P("seq", None),
        P("seq", None),
        P("seq", None, None, None),
        P("seq", None, None),
    )
    return jax.shard_map(
        per_device, mesh=mesh, in_specs=placed, out_specs=P("seq", "exp"), check_vma=False
    )
```

```python
import functools

import jax
import jax.numpy as jnp
from jax import lax
from jax.experimental import pallas as pl
from jax.experimental.pallas import tpu as pltpu
from jax.sharding import PartitionSpec as P

HEAD = 128
F32 = jnp.float32
BF16 = jnp.bfloat16
WHOLE = pl.BlockSpec(memory_space=pltpu.VMEM)
FAR = pl.BlockSpec(memory_space=pltpu.HBM)
SCALAR = pl.BlockSpec(memory_space=pltpu.SMEM)


def call(kernel, outs, inputs, far=(), small=(), scratch=(), out_specs=None, flops=0, limit=16 << 20):
    moved = sum(a.size * a.dtype.itemsize for a in [*inputs, *outs])
    inputs = [
        pltpu.with_memory_space_constraint(a, pltpu.HBM) if i in far else a
        for i, a in enumerate(inputs)
    ]
    return pl.pallas_call(
        kernel,
        out_shape=outs,
        in_specs=[
            SCALAR if i == 0 or i in small else FAR if i in far else WHOLE
            for i in range(len(inputs))
        ],
        out_specs=out_specs or [WHOLE] * len(outs),
        scratch_shapes=scratch,
        compiler_params=pltpu.CompilerParams(vmem_limit_bytes=limit),
        cost_estimate=pl.CostEstimate(flops=flops, bytes_accessed=moved, transcendentals=0),
    )(*inputs)


def shape(dims, dtype):
    return jax.ShapeDtypeStruct(dims, dtype)


def split(value):
    high = value.astype(BF16)
    return high, (value - high.astype(F32)).astype(BF16)


def add_rows(*terms):
    return sum(t.astype(F32) for t in terms).astype(BF16)


def run_copies(pairs, sems):
    copies = [pltpu.make_async_copy(a, b, sems.at[i]) for i, (a, b) in enumerate(pairs)]
    for copy in copies:
        copy.start()
    for copy in copies:
        copy.wait()


def open_kernel(
    scalars, key_ref, value_ref, query_ref, residual_ref, gain_ref,
    kept_ref, given_ref, keys, values, query, residual, gain, flags_ref, sems
):
    pairs = [
        (key_ref, keys), (value_ref, values), (query_ref, query), (residual_ref, residual),
        (gain_ref, gain),
    ]
    copies = [pltpu.make_async_copy(a, b, sems.at[i]) for i, (a, b) in enumerate(pairs)]
    for copy in copies:
        copy.start()
    for i in range(flags_ref.shape[0]):
        value = 1 - scalars[1] if i == 1 else scalars[1 if i == 0 else 2 + i]
        flags_ref[i:i + 1, :] = jnp.full((1, flags_ref.shape[1]), value, jnp.int32).astype(F32)
    for copy in copies[:2]:
        copy.wait()
    width = keys.shape[1] // 2
    place = scalars[1]
    sides = []
    for side in range(2):
        cols = slice(side * width, (side + 1) * width)
        square = lax.dot_general(
            keys[:, cols], values[:, cols], (((0,), (0,)), ((), ())), preferred_element_type=F32
        )
        sides.append(
            jnp.concatenate(
                [square[h:h + HEAD, h:h + HEAD] for h in range(0, width, HEAD)], axis=1
            ).astype(BF16)
        )
    kept_ref[...] = jnp.where(place == 0, sides[0], sides[1])
    given_ref[...] = jnp.where(place == 0, sides[1], sides[0])
    for copy in copies[2:]:
        copy.wait()


def within_kernel(scalars, keys, values, queries, out_ref):
    rows, width = out_ref.shape
    causal = lax.broadcasted_iota(jnp.int32, (rows, rows), 0) >= lax.broadcasted_iota(
        jnp.int32, (rows, rows), 1
    )
    for start in range(0, width, HEAD):
        cols = slice(start, start + HEAD)
        scores = lax.dot_general(
            queries[:, cols], keys[:, cols], (((1,), (1,)), ((), ())), preferred_element_type=F32
        )
        high, low = split(jnp.where(causal, scores, 0.0))
        out_ref[:, cols] = jnp.dot(
            high, values[:, cols], preferred_element_type=F32
        ) + jnp.dot(low, values[:, cols], preferred_element_type=F32)


def attend_kernel(
    parts, scalars, within_ref, queries, residuals, gain_ref, mine_ref, other_ref, *refs
):
    piece_refs, hidden = refs[-1 - parts:-1], refs[-1]
    rows, full = hidden.shape
    width = full // 2
    first = scalars[1] == 0
    mine, other = mine_ref[...], other_ref[...].astype(F32)
    halves = [jnp.where(first, mine, other), jnp.where(first, other, mine)]
    for start in range(0, full, HEAD):
        cols = slice(start, start + HEAD)
        half, inner = divmod(start, width)
        high, low = split(halves[half][:, inner:inner + HEAD])
        raw = (
            jnp.dot(queries[:, cols], high, preferred_element_type=F32)
            + jnp.dot(queries[:, cols], low, preferred_element_type=F32)
            + within_ref[:, cols]
        )
        scaled = raw * lax.rsqrt(jnp.mean(raw * raw, axis=-1, keepdims=True) + 1e-06)
        hidden[:, cols] = (residuals[:, cols].astype(F32) + scaled * gain_ref[:, cols]).astype(BF16)
    count = rows // parts
    for j, piece in enumerate(piece_refs):
        piece[...] = hidden[pl.ds(pl.multiple_of((scalars[0] ^ j) * count, count), count), :]


def load_kernel(lead, scalars, source, after_ref, target, done_ref, sems):
    done_ref[...] = jnp.zeros_like(done_ref)
    pieces = sems.shape[0]
    step = target.shape[0] // pieces
    cuts = [pl.ds(i * step, step) for i in range(pieces)]
    run_copies([(source.at[lead, cut], target.at[cut]) for cut in cuts], sems)


def load_near(scalars, source, lead, after):
    return call(
        functools.partial(load_kernel, lead),
        [shape(source.shape[1:], source.dtype), shape((8, HEAD), F32)],
        [scalars, source, after], far=(1,), scratch=[pltpu.SemaphoreType.DMA((8,))],
    )


def expert_kernel(blocks, scalars, gate_ref, up_ref, down_ref, *refs):
    x_refs, out_refs = refs[:blocks], refs[blocks:2 * blocks]
    rows_ref, act_ref, made_ref = refs[2 * blocks:]
    model, units = gate_ref.shape
    spans, packs = [], []
    first = 0
    for ref in x_refs:
        spans.append(slice(first, first + ref.shape[0]))
        rows_ref[spans[-1], :] = ref[:, :model]
        packs.append(ref[:, model:].astype(F32))
        first += ref.shape[0]
    pack = jnp.concatenate(packs)
    lane = lax.broadcasted_iota(jnp.int32, pack.shape, 1)
    chosen = (lane == scalars[3]) | (lane == scalars[3] + scalars[2])
    weight = jnp.sum(jnp.where(chosen, pack, 0.0), axis=-1, keepdims=True)
    chunk = min(units, 512)

    for step in range(units // chunk):
        cut = slice(step * chunk, (step + 1) * chunk)
        gate = jnp.dot(rows_ref[...], gate_ref[:, cut], preferred_element_type=F32)
        up = jnp.dot(rows_ref[...], up_ref[:, cut], preferred_element_type=F32)
        act_ref[:, cut] = (gate / (1.0 + jnp.exp(-gate)) * up).astype(BF16)

    wide = min(model, 1024)

    for step in range(model // wide):
        cut = slice(step * wide, (step + 1) * wide)
        produced = jnp.dot(act_ref[...], down_ref[:, cut], preferred_element_type=F32)
        made_ref[:, cut] = (produced.astype(BF16).astype(F32) * weight).astype(BF16)

    for out_ref, span in zip(out_refs, spans):
        out_ref[...] = made_ref[span, :]


def run_expert(scalars, blocks, weights_gate, weights_up, weights_out):
    units, model = weights_out.shape
    total = sum(b.shape[0] for b in blocks)
    return call(
        functools.partial(expert_kernel, len(blocks)),
        [shape((b.shape[0], model), BF16) for b in blocks],
        [scalars, weights_gate, weights_up, weights_out, *blocks],
        scratch=[
            pltpu.VMEM((total, model), BF16),
            pltpu.VMEM((total, units), BF16),
            pltpu.VMEM((total, model), BF16),
        ],
        flops=6 * total * model * units,
        limit=24 << 20,
    )


def ring_order(count):
    return list(range(0, count, 2)) + list(range(1, count, 2))[::-1]


def dense_experts(block, scalars, turns, weights_gate, weights_up, expert_out):
    count = lax.axis_size("seq")
    order = ring_order(count)
    far = count // 2
    parts = lax.axis_size("exp")

    def hop(rows, steps):
        return lax.ppermute(
            rows, "seq", [(order[p], order[(p + steps) % count]) for p in range(count)]
        )

    def far_hop(rows):
        pairs = []
        for p in range(count):
            for e in range(parts):
                target = order[(p + (2 if e % 2 == 0 else -2)) % count]
                pairs.append((order[p] * parts + e, target * parts + e))
        return lax.ppermute(rows, ("seq", "exp"), pairs)

    ahead, behind = [block], [block]
    for distance in range(1, far):
        came, went = hop(ahead[-1], 1), hop(behind[-1], -1)
        if distance == 1:
            weights_out, _ = load_near(scalars, expert_out, 0, came)
        ahead.append(came)
        behind.append(went)
    turned = turns[0]
    farthest = far_hop(jnp.where(turned, behind[-2], ahead[-2]))
    made = run_expert(
        scalars, ahead + behind[1:] + [farthest], weights_gate, weights_up, weights_out
    )
    own, to_back, to_front, farthest = made[0], made[1:far], made[far:-1], made[-1]
    going, coming = hop(to_front[-1], 1), hop(to_back[-1], -1)
    early = far_hop(farthest)
    for distance in range(far - 2, 0, -1):
        front, back = to_front[distance - 1], to_back[distance - 1]
        if distance == far - 2:
            nothing = jnp.zeros_like(early)
            going = add_rows(going, front, jnp.where(turned, nothing, early))
            coming = add_rows(coming, back, jnp.where(turned, early, nothing))
        else:
            going = add_rows(going, front)
            coming = add_rows(coming, back)
        going, coming = hop(going, 1), hop(coming, -1)
    return own, going, coming


def slot_ids(block_routes, expert_count, capacity):
    row_count, top_count = block_routes.shape
    expert_ids = jnp.arange(expert_count, dtype=jnp.int32)
    onehot = (
        (block_routes[:, :, None] == expert_ids[None, None, :])
        .astype(jnp.int32)
        .reshape(row_count * top_count, expert_count)
    )
    earlier = jnp.cumsum(onehot, axis=0) - onehot
    ranking = jnp.sum(earlier * onehot, axis=1).reshape(row_count, top_count)
    return block_routes * capacity + ranking


def routed_experts(normed, my_routes, my_gates, expert_in, expert_out):
    sub_count, model_width = normed.shape
    expert_count = lax.axis_size("seq") * expert_in.shape[0]
    top_count = my_routes.shape[1]
    capacity = min(sub_count, max(2, 3 * sub_count * top_count // (2 * expert_count)))
    slot_count = expert_count * capacity
    my_slots = slot_ids(my_routes, expert_count, capacity)
    columns = jnp.arange(slot_count, dtype=jnp.int32)
    placer = jnp.sum(
        (my_slots[None, :, :] == columns[:, None, None]).astype(jnp.int32), axis=2
    ).astype(BF16)
    outgoing = (
        jnp.dot(placer, normed, preferred_element_type=F32)
        .astype(BF16)
        .reshape(expert_count, capacity, model_width)
    )
    arrived = lax.all_to_all(outgoing, "seq", split_axis=0, concat_axis=0, tiled=True)
    flat_rows = arrived.reshape(-1, model_width)
    gate_up = jnp.einsum("nd,gdf->gnf", flat_rows, expert_in[0], preferred_element_type=F32)
    activated = (jax.nn.silu(gate_up[0]) * gate_up[1]).astype(BF16)
    produced = jnp.dot(activated, expert_out[0], preferred_element_type=F32).astype(BF16)
    answered = produced.reshape(arrived.shape)
    returned = lax.all_to_all(answered, "seq", split_axis=0, concat_axis=0, tiled=True)
    picked = returned.reshape(slot_count, model_width)[my_slots.reshape(-1)].reshape(
        sub_count, top_count, model_width
    )
    return jnp.sum(picked.astype(F32) * my_gates[:, :, None], axis=1)


def swap_pairs(rows, distance):
    count = lax.axis_size("seq")
    return lax.ppermute(rows, "seq", [(i, i ^ (2 * distance)) for i in range(count)])


def pair_steps(pairs):
    bits = pairs.bit_length() - 1
    direct = pairs <= 4
    steps = range(1, pairs) if direct else [1 << b for b in range(bits)]
    return direct, [(d, d.bit_length() - 1) for d in steps]


def prior_states(total):
    count = lax.axis_size("seq")
    direct, steps = pair_steps(count // 2)
    terms = []
    for distance, _ in steps:
        terms.append(
            lax.ppermute(total, "seq", [(i, i ^ (2 * distance)) for i in range(count)])
        )
        if not direct:
            total = add_rows(total, terms[-1])
    return terms


def exchange(pieces):
    parts = len(pieces)
    return [pieces[0]] + [
        lax.ppermute(pieces[j], "exp", [(i, i ^ j) for i in range(parts)])
        for j in range(1, parts)
    ]


def turn_order(items, turns):
    for b, turn in enumerate(turns):
        items = [jnp.where(turn, items[i ^ (1 << b)], items[i]) for i in range(len(items))]
    return items


def per_device(
    residual,
    queries,
    key_vectors,
    value_vectors,
    head_gain,
    norm_gain,
    routes,
    route_gates,
    expert_in,
    expert_out,
):
    rows, width = residual.shape
    seq, parts = lax.axis_size("seq"), lax.axis_size("exp")
    count, half, model = rows // parts, width // 2, width * parts
    experts = seq * expert_in.shape[0]
    position = lax.axis_index("seq")
    my_index = lax.axis_index("exp")
    place = position % 2
    _, steps = pair_steps(seq // 2)
    scalars = jnp.stack(
        [my_index, place, experts, position] + [(position >> (bit + 1)) & 1 for _, bit in steps]
    ).astype(jnp.int32)
    swap = [(i, i ^ 1) for i in range(seq)]
    turns = [
        ((my_index >> b) & 1 != 0).reshape(1, 1) for b in range(parts.bit_length() - 1)
    ]
    my_rows = (my_index * count).astype(jnp.uint32)
    scalars, turns, my_rows = lax.optimization_barrier((scalars, turns, my_rows))
    state, heads = shape((HEAD, half), BF16), shape((rows, width), BF16)
    kept, given, keys, values, query, rest, my_gain, flags = call(
        open_kernel,
        [state] * 2 + [heads] * 4
        + [shape((1, width), F32), shape((2 + len(steps), half), F32)],
        [scalars, key_vectors, value_vectors, queries, residual, head_gain[None, :]],
        far=(1, 2, 3, 4, 5),
        scratch=[pltpu.SemaphoreType.DMA((5,))],
        flops=2 * rows * width * HEAD,
    )
    partner = lax.ppermute(given, "seq", swap)
    [within] = call(
        within_kernel, [shape((rows, width), F32)], [scalars, keys, values, query],
        flops=6 * rows * rows * width,
    )
    dense = routes.shape[1] == experts
    total, within = lax.optimization_barrier((add_rows(kept, partner), within))
    sign = jnp.zeros((8, HEAD), F32)
    if dense:
        weights_gate, sign = load_near(scalars, expert_in[0], 0, total)
    before = sum(
        came.astype(F32) * flags[2 + i:3 + i] for i, came in enumerate(prior_states(total))
    )
    mine = before + partner.astype(F32) * flags[:1]
    lacked = (before + kept.astype(F32) * flags[1:2]).astype(BF16)
    lacked, sign = lax.optimization_barrier((lacked, sign))
    other = lax.ppermute(lacked, "seq", swap)
    signs = [sign]
    if dense:
        weights_up, sign = load_near(scalars, expert_in[0], 1, lacked)
        signs.append(sign)
    pieces = call(
        functools.partial(attend_kernel, parts),
        [shape((count, width), BF16)] * parts,
        [scalars, within, query, rest, my_gain, mine, other, *signs],
        scratch=[pltpu.VMEM((rows, width), BF16)],
        flops=4 * rows * width * HEAD,
    )
    gathered = exchange(pieces)

    my_routes = lax.dynamic_slice_in_dim(routes, my_rows, count, 0)
    my_gates = lax.dynamic_slice_in_dim(route_gates, my_rows, count, 0)
    mixing = jnp.sum(
        jnp.where(
            my_routes[:, :, None] == jnp.arange(experts, dtype=jnp.int32),
            my_gates[:, :, None],
            0.0,
        ),
        axis=1,
    )
    high = lax.reduce_precision(mixing, 8, 7)
    lanes = -(-2 * experts // HEAD) * HEAD
    pack = jnp.pad(
        jnp.concatenate([high, mixing - high], axis=1), ((0, 0), (0, lanes - 2 * experts))
    ).astype(BF16)
    hidden = jnp.concatenate(turn_order(gathered, turns), axis=1)
    widened = hidden.astype(F32)
    normed = (
        widened
        * lax.rsqrt(jnp.mean(widened * widened, axis=-1, keepdims=True) + 1e-06)
        * norm_gain
    ).astype(BF16)
    if dense:
        block = jnp.concatenate([normed, pack], axis=1)
        terms = dense_experts(
            block, scalars, turns, weights_gate, weights_up, expert_out
        )
    else:
        mixed = routed_experts(normed, my_routes, my_gates, expert_in, expert_out)
        terms = [mixed]
    own, *others = terms
    mixed = own.astype(F32) + sum(t.astype(F32) for t in others)
    ready = (hidden.astype(F32) + mixed).astype(BF16)
    columns = [ready[:, i * width:(i + 1) * width] for i in range(parts)]
    return jnp.concatenate(turn_order(exchange(turn_order(columns, turns)), turns))


def solution(mesh):
    placed = (
        P("seq", "exp"),
        P("seq", "exp"),
        P("seq", "exp"),
        P("seq", "exp"),
        P("exp"),
        P(),
        P("seq", None),
        P("seq", None),
        P("seq", None, None, None),
        P("seq", None, None),
    )
    return jax.shard_map(
        per_device, mesh=mesh, in_specs=placed, out_specs=P("seq", "exp"), check_vma=False
    )
```

```python
import functools

import jax
import jax.numpy as jnp
from jax import lax
from jax.experimental import pallas as pl
from jax.experimental.pallas import tpu as pltpu
from jax.sharding import PartitionSpec as P

HEAD = 128
F32 = jnp.float32
BF16 = jnp.bfloat16
WHOLE = pl.BlockSpec(memory_space=pltpu.VMEM)
FAR = pl.BlockSpec(memory_space=pltpu.HBM)
SCALAR = pl.BlockSpec(memory_space=pltpu.SMEM)


def call(kernel, outs, inputs, far=(), small=(), scratch=(), out_specs=None, flops=0, limit=16 << 20):
    moved = sum(a.size * a.dtype.itemsize for a in [*inputs, *outs])
    inputs = [
        pltpu.with_memory_space_constraint(a, pltpu.HBM) if i in far else a
        for i, a in enumerate(inputs)
    ]
    return pl.pallas_call(
        kernel,
        out_shape=outs,
        in_specs=[
            SCALAR if i == 0 or i in small else FAR if i in far else WHOLE
            for i in range(len(inputs))
        ],
        out_specs=out_specs or [WHOLE] * len(outs),
        scratch_shapes=scratch,
        compiler_params=pltpu.CompilerParams(vmem_limit_bytes=limit),
        cost_estimate=pl.CostEstimate(flops=flops, bytes_accessed=moved, transcendentals=0),
    )(*inputs)


def shape(dims, dtype):
    return jax.ShapeDtypeStruct(dims, dtype)


def split(value):
    high = value.astype(BF16)
    return high, (value - high.astype(F32)).astype(BF16)


def add_rows(*terms):
    return sum(t.astype(F32) for t in terms).astype(BF16)


def run_copies(pairs, sems):
    copies = [pltpu.make_async_copy(a, b, sems.at[i]) for i, (a, b) in enumerate(pairs)]
    for copy in copies:
        copy.start()
    for copy in copies:
        copy.wait()


def open_kernel(
    scalars, key_ref, value_ref, query_ref, residual_ref, gain_ref,
    kept_ref, given_ref, keys, values, query, residual, gain, flags_ref, sems
):
    pairs = [
        (key_ref, keys), (value_ref, values), (query_ref, query), (residual_ref, residual),
        (gain_ref, gain),
    ]
    copies = [pltpu.make_async_copy(a, b, sems.at[i]) for i, (a, b) in enumerate(pairs)]
    for copy in copies:
        copy.start()
    for i in range(flags_ref.shape[0]):
        value = 1 - scalars[1] if i == 1 else scalars[1 if i == 0 else 2 + i]
        flags_ref[i:i + 1, :] = jnp.full((1, flags_ref.shape[1]), value, jnp.int32).astype(F32)
    for copy in copies[:2]:
        copy.wait()
    width = keys.shape[1] // 2
    place = scalars[1]
    sides = []
    for side in range(2):
        cols = slice(side * width, (side + 1) * width)
        square = lax.dot_general(
            keys[:, cols], values[:, cols], (((0,), (0,)), ((), ())), preferred_element_type=F32
        )
        sides.append(
            jnp.concatenate(
                [square[h:h + HEAD, h:h + HEAD] for h in range(0, width, HEAD)], axis=1
            ).astype(BF16)
        )
    kept_ref[...] = jnp.where(place == 0, sides[0], sides[1])
    given_ref[...] = jnp.where(place == 0, sides[1], sides[0])
    for copy in copies[2:]:
        copy.wait()


def within_kernel(scalars, keys, values, queries, out_ref):
    rows, width = out_ref.shape
    causal = lax.broadcasted_iota(jnp.int32, (rows, rows), 0) >= lax.broadcasted_iota(
        jnp.int32, (rows, rows), 1
    )
    for start in range(0, width, HEAD):
        cols = slice(start, start + HEAD)
        scores = lax.dot_general(
            queries[:, cols], keys[:, cols], (((1,), (1,)), ((), ())), preferred_element_type=F32
        )
        high, low = split(jnp.where(causal, scores, 0.0))
        out_ref[:, cols] = jnp.dot(
            high, values[:, cols], preferred_element_type=F32
        ) + jnp.dot(low, values[:, cols], preferred_element_type=F32)


def attend_kernel(
    parts, scalars, within_ref, queries, residuals, gain_ref, mine_ref, other_ref, *refs
):
    piece_refs, hidden = refs[-1 - parts:-1], refs[-1]
    rows, full = hidden.shape
    width = full // 2
    first = scalars[1] == 0
    mine, other = mine_ref[...], other_ref[...].astype(F32)
    halves = [jnp.where(first, mine, other), jnp.where(first, other, mine)]
    for start in range(0, full, HEAD):
        cols = slice(start, start + HEAD)
        half, inner = divmod(start, width)
        high, low = split(halves[half][:, inner:inner + HEAD])
        raw = (
            jnp.dot(queries[:, cols], high, preferred_element_type=F32)
            + jnp.dot(queries[:, cols], low, preferred_element_type=F32)
            + within_ref[:, cols]
        )
        scaled = raw * lax.rsqrt(jnp.mean(raw * raw, axis=-1, keepdims=True) + 1e-06)
        hidden[:, cols] = (residuals[:, cols].astype(F32) + scaled * gain_ref[:, cols]).astype(BF16)
    count = rows // parts
    for j, piece in enumerate(piece_refs):
        piece[...] = hidden[pl.ds(pl.multiple_of((scalars[0] ^ j) * count, count), count), :]


def load_kernel(lead, scalars, source, after_ref, target, done_ref, sems):
    done_ref[...] = jnp.zeros_like(done_ref)
    pieces = sems.shape[0]
    step = target.shape[0] // pieces
    cuts = [pl.ds(i * step, step) for i in range(pieces)]
    run_copies([(source.at[lead, cut], target.at[cut]) for cut in cuts], sems)


def load_near(scalars, source, lead, after):
    return call(
        functools.partial(load_kernel, lead),
        [shape(source.shape[1:], source.dtype), shape((8, HEAD), F32)],
        [scalars, source, after], far=(1,), scratch=[pltpu.SemaphoreType.DMA((8,))],
    )


def expert_kernel(blocks, scalars, gate_ref, up_ref, down_ref, *refs):
    x_refs, out_refs = refs[:blocks], refs[blocks:2 * blocks]
    rows_ref, act_ref, made_ref = refs[2 * blocks:]
    model, units = gate_ref.shape
    spans, packs = [], []
    first = 0
    for ref in x_refs:
        spans.append(slice(first, first + ref.shape[0]))
        rows_ref[spans[-1], :] = ref[:, :model]
        packs.append(ref[:, model:].astype(F32))
        first += ref.shape[0]
    pack = jnp.concatenate(packs)
    lane = lax.broadcasted_iota(jnp.int32, pack.shape, 1)
    chosen = (lane == scalars[3]) | (lane == scalars[3] + scalars[2])
    weight = jnp.sum(jnp.where(chosen, pack, 0.0), axis=-1, keepdims=True)
    chunk = min(units, 512)

    for step in range(units // chunk):
        cut = slice(step * chunk, (step + 1) * chunk)
        gate = jnp.dot(rows_ref[...], gate_ref[:, cut], preferred_element_type=F32)
        up = jnp.dot(rows_ref[...], up_ref[:, cut], preferred_element_type=F32)
        act_ref[:, cut] = (gate / (1.0 + jnp.exp(-gate)) * up).astype(BF16)

    wide = min(model, 1024)

    for step in range(model // wide):
        cut = slice(step * wide, (step + 1) * wide)
        produced = jnp.dot(act_ref[...], down_ref[:, cut], preferred_element_type=F32)
        made_ref[:, cut] = (produced.astype(BF16).astype(F32) * weight).astype(BF16)

    for out_ref, span in zip(out_refs, spans):
        out_ref[...] = made_ref[span, :]


def run_expert(scalars, blocks, weights_gate, weights_up, weights_out):
    units, model = weights_out.shape
    total = sum(b.shape[0] for b in blocks)
    return call(
        functools.partial(expert_kernel, len(blocks)),
        [shape((b.shape[0], model), BF16) for b in blocks],
        [scalars, weights_gate, weights_up, weights_out, *blocks],
        scratch=[
            pltpu.VMEM((total, model), BF16),
            pltpu.VMEM((total, units), BF16),
            pltpu.VMEM((total, model), BF16),
        ],
        flops=6 * total * model * units,
        limit=24 << 20,
    )


def ring_order(count):
    return list(range(0, count, 2)) + list(range(1, count, 2))[::-1]


def dense_experts(block, scalars, turns, weights_gate, weights_up, expert_out):
    count, parts = lax.axis_size("seq"), lax.axis_size("exp")
    order = ring_order(count)
    far = count // 2
    turned = turns[0]

    def hop(rows, steps):
        return lax.ppermute(
            rows, "seq", [(order[p], order[(p + steps) % count]) for p in range(count)]
        )

    def far_hop(rows):
        pairs = []
        for p in range(count):
            for e in range(parts):
                target = order[(p + (2 if e % 2 == 0 else -2)) % count]
                pairs.append((order[p] * parts + e, target * parts + e))
        return lax.ppermute(rows, ("seq", "exp"), pairs)

    def gather(rows):
        ahead, behind = [rows], [rows]
        for distance in range(1, far):
            ahead.append(hop(ahead[-1], 1))
            behind.append(hop(behind[-1], -1))
        return ahead + behind[1:] + [far_hop(jnp.where(turned, behind[-2], ahead[-2]))]

    def scatter(made):
        own, to_back, to_front, farthest = made[0], made[1:far], made[far:-1], made[-1]
        going, coming = hop(to_front[-1], 1), hop(to_back[-1], -1)
        early = far_hop(farthest)
        nothing = jnp.zeros_like(early)
        for distance in range(far - 2, 0, -1):
            front, back = [to_front[distance - 1]], [to_back[distance - 1]]
            if distance == far - 2:
                front.append(jnp.where(turned, nothing, early))
                back.append(jnp.where(turned, early, nothing))
            going, coming = add_rows(going, *front), add_rows(coming, *back)
            going, coming = hop(going, 1), hop(coming, -1)
        return own, going, coming

    half = block.shape[0] // 2
    streams = [gather(rows) for rows in (block[:half], block[half:])]
    weights_out, _ = load_near(scalars, expert_out, 0, streams[0][1])
    terms = [
        scatter(run_expert(scalars, blocks, weights_gate, weights_up, weights_out))
        for blocks in streams
    ]
    return [jnp.concatenate(pair) for pair in zip(*terms)]


def slot_ids(block_routes, expert_count, capacity):
    row_count, top_count = block_routes.shape
    expert_ids = jnp.arange(expert_count, dtype=jnp.int32)
    onehot = (
        (block_routes[:, :, None] == expert_ids[None, None, :])
        .astype(jnp.int32)
        .reshape(row_count * top_count, expert_count)
    )
    earlier = jnp.cumsum(onehot, axis=0) - onehot
    ranking = jnp.sum(earlier * onehot, axis=1).reshape(row_count, top_count)
    return block_routes * capacity + ranking


def routed_experts(normed, my_routes, my_gates, expert_in, expert_out):
    sub_count, model_width = normed.shape
    expert_count = lax.axis_size("seq") * expert_in.shape[0]
    top_count = my_routes.shape[1]
    capacity = min(sub_count, max(2, 3 * sub_count * top_count // (2 * expert_count)))
    slot_count = expert_count * capacity
    my_slots = slot_ids(my_routes, expert_count, capacity)
    columns = jnp.arange(slot_count, dtype=jnp.int32)
    placer = jnp.sum(
        (my_slots[None, :, :] == columns[:, None, None]).astype(jnp.int32), axis=2
    ).astype(BF16)
    outgoing = (
        jnp.dot(placer, normed, preferred_element_type=F32)
        .astype(BF16)
        .reshape(expert_count, capacity, model_width)
    )
    arrived = lax.all_to_all(outgoing, "seq", split_axis=0, concat_axis=0, tiled=True)
    flat_rows = arrived.reshape(-1, model_width)
    gate_up = jnp.einsum("nd,gdf->gnf", flat_rows, expert_in[0], preferred_element_type=F32)
    activated = (jax.nn.silu(gate_up[0]) * gate_up[1]).astype(BF16)
    produced = jnp.dot(activated, expert_out[0], preferred_element_type=F32).astype(BF16)
    answered = produced.reshape(arrived.shape)
    returned = lax.all_to_all(answered, "seq", split_axis=0, concat_axis=0, tiled=True)
    picked = returned.reshape(slot_count, model_width)[my_slots.reshape(-1)].reshape(
        sub_count, top_count, model_width
    )
    return jnp.sum(picked.astype(F32) * my_gates[:, :, None], axis=1)


def swap_pairs(rows, distance):
    count = lax.axis_size("seq")
    return lax.ppermute(rows, "seq", [(i, i ^ (2 * distance)) for i in range(count)])


def pair_steps(pairs):
    bits = pairs.bit_length() - 1
    direct = pairs <= 4
    steps = range(1, pairs) if direct else [1 << b for b in range(bits)]
    return direct, [(d, d.bit_length() - 1) for d in steps]


def prior_states(total):
    count = lax.axis_size("seq")
    direct, steps = pair_steps(count // 2)
    terms = []
    for distance, _ in steps:
        terms.append(
            lax.ppermute(total, "seq", [(i, i ^ (2 * distance)) for i in range(count)])
        )
        if not direct:
            total = add_rows(total, terms[-1])
    return terms


def exchange(pieces):
    parts = len(pieces)
    return [pieces[0]] + [
        lax.ppermute(pieces[j], "exp", [(i, i ^ j) for i in range(parts)])
        for j in range(1, parts)
    ]


def turn_order(items, turns):
    for b, turn in enumerate(turns):
        items = [jnp.where(turn, items[i ^ (1 << b)], items[i]) for i in range(len(items))]
    return items


def per_device(
    residual,
    queries,
    key_vectors,
    value_vectors,
    head_gain,
    norm_gain,
    routes,
    route_gates,
    expert_in,
    expert_out,
):
    rows, width = residual.shape
    seq, parts = lax.axis_size("seq"), lax.axis_size("exp")
    count, half, model = rows // parts, width // 2, width * parts
    experts = seq * expert_in.shape[0]
    position = lax.axis_index("seq")
    my_index = lax.axis_index("exp")
    place = position % 2
    _, steps = pair_steps(seq // 2)
    scalars = jnp.stack(
        [my_index, place, experts, position] + [(position >> (bit + 1)) & 1 for _, bit in steps]
    ).astype(jnp.int32)
    swap = [(i, i ^ 1) for i in range(seq)]
    turns = [
        ((my_index >> b) & 1 != 0).reshape(1, 1) for b in range(parts.bit_length() - 1)
    ]
    my_rows = (my_index * count).astype(jnp.uint32)
    scalars, turns, my_rows = lax.optimization_barrier((scalars, turns, my_rows))
    state, heads = shape((HEAD, half), BF16), shape((rows, width), BF16)
    kept, given, keys, values, query, rest, my_gain, flags = call(
        open_kernel,
        [state] * 2 + [heads] * 4
        + [shape((1, width), F32), shape((2 + len(steps), half), F32)],
        [scalars, key_vectors, value_vectors, queries, residual, head_gain[None, :]],
        far=(1, 2, 3, 4, 5),
        scratch=[pltpu.SemaphoreType.DMA((5,))],
        flops=2 * rows * width * HEAD,
    )
    partner = lax.ppermute(given, "seq", swap)
    [within] = call(
        within_kernel, [shape((rows, width), F32)], [scalars, keys, values, query],
        flops=6 * rows * rows * width,
    )
    dense = routes.shape[1] == experts
    total, within = lax.optimization_barrier((add_rows(kept, partner), within))
    sign = jnp.zeros((8, HEAD), F32)
    if dense:
        weights_gate, sign = load_near(scalars, expert_in[0], 0, total)
    before = sum(
        came.astype(F32) * flags[2 + i:3 + i] for i, came in enumerate(prior_states(total))
    )
    mine = before + partner.astype(F32) * flags[:1]
    lacked = (before + kept.astype(F32) * flags[1:2]).astype(BF16)
    lacked, sign = lax.optimization_barrier((lacked, sign))
    other = lax.ppermute(lacked, "seq", swap)
    signs = [sign]
    if dense:
        weights_up, sign = load_near(scalars, expert_in[0], 1, lacked)
        signs.append(sign)
    pieces = call(
        functools.partial(attend_kernel, parts),
        [shape((count, width), BF16)] * parts,
        [scalars, within, query, rest, my_gain, mine, other, *signs],
        scratch=[pltpu.VMEM((rows, width), BF16)],
        flops=4 * rows * width * HEAD,
    )
    gathered = exchange(pieces)

    my_routes = lax.dynamic_slice_in_dim(routes, my_rows, count, 0)
    my_gates = lax.dynamic_slice_in_dim(route_gates, my_rows, count, 0)
    mixing = jnp.sum(
        jnp.where(
            my_routes[:, :, None] == jnp.arange(experts, dtype=jnp.int32),
            my_gates[:, :, None],
            0.0,
        ),
        axis=1,
    )
    high = lax.reduce_precision(mixing, 8, 7)
    lanes = -(-2 * experts // HEAD) * HEAD
    pack = jnp.pad(
        jnp.concatenate([high, mixing - high], axis=1), ((0, 0), (0, lanes - 2 * experts))
    ).astype(BF16)
    hidden = jnp.concatenate(turn_order(gathered, turns), axis=1)
    widened = hidden.astype(F32)
    normed = (
        widened
        * lax.rsqrt(jnp.mean(widened * widened, axis=-1, keepdims=True) + 1e-06)
        * norm_gain
    ).astype(BF16)
    if dense:
        block = jnp.concatenate([normed, pack], axis=1)
        terms = dense_experts(
            block, scalars, turns, weights_gate, weights_up, expert_out
        )
    else:
        mixed = routed_experts(normed, my_routes, my_gates, expert_in, expert_out)
        terms = [mixed]
    own, *others = terms
    mixed = own.astype(F32) + sum(t.astype(F32) for t in others)
    ready = (hidden.astype(F32) + mixed).astype(BF16)
    columns = [ready[:, i * width:(i + 1) * width] for i in range(parts)]
    return jnp.concatenate(turn_order(exchange(turn_order(columns, turns)), turns))


def solution(mesh):
    placed = (
        P("seq", "exp"),
        P("seq", "exp"),
        P("seq", "exp"),
        P("seq", "exp"),
        P("exp"),
        P(),
        P("seq", None),
        P("seq", None),
        P("seq", None, None, None),
        P("seq", None, None),
    )
    return jax.shard_map(
        per_device, mesh=mesh, in_specs=placed, out_specs=P("seq", "exp"), check_vma=False
    )
```

```python
import functools

import jax
import jax.numpy as jnp
from jax import lax
from jax.experimental import pallas as pl
from jax.experimental.pallas import tpu as pltpu
from jax.sharding import PartitionSpec as P

HEAD = 128
F32 = jnp.float32
BF16 = jnp.bfloat16
WHOLE = pl.BlockSpec(memory_space=pltpu.VMEM)
FAR = pl.BlockSpec(memory_space=pltpu.HBM)
SCALAR = pl.BlockSpec(memory_space=pltpu.SMEM)


def call(kernel, outs, inputs, far=(), small=(), scratch=(), out_specs=None, flops=0, limit=16 << 20):
    moved = sum(a.size * a.dtype.itemsize for a in [*inputs, *outs])
    inputs = [
        pltpu.with_memory_space_constraint(a, pltpu.HBM) if i in far else a
        for i, a in enumerate(inputs)
    ]
    return pl.pallas_call(
        kernel,
        out_shape=outs,
        in_specs=[
            SCALAR if i == 0 or i in small else FAR if i in far else WHOLE
            for i in range(len(inputs))
        ],
        out_specs=out_specs or [WHOLE] * len(outs),
        scratch_shapes=scratch,
        compiler_params=pltpu.CompilerParams(vmem_limit_bytes=limit),
        cost_estimate=pl.CostEstimate(flops=flops, bytes_accessed=moved, transcendentals=0),
    )(*inputs)


def shape(dims, dtype):
    return jax.ShapeDtypeStruct(dims, dtype)


def split(value):
    high = value.astype(BF16)
    return high, (value - high.astype(F32)).astype(BF16)


def add_rows(*terms):
    return sum(t.astype(F32) for t in terms).astype(BF16)


def run_copies(pairs, sems):
    copies = [pltpu.make_async_copy(a, b, sems.at[i]) for i, (a, b) in enumerate(pairs)]
    for copy in copies:
        copy.start()
    for copy in copies:
        copy.wait()


def open_kernel(
    scalars, key_ref, value_ref, query_ref, residual_ref, gain_ref,
    kept_ref, given_ref, keys, values, query, residual, gain, flags_ref, sems
):
    pairs = [
        (key_ref, keys), (value_ref, values), (query_ref, query), (residual_ref, residual),
        (gain_ref, gain),
    ]
    copies = [pltpu.make_async_copy(a, b, sems.at[i]) for i, (a, b) in enumerate(pairs)]
    for copy in copies:
        copy.start()
    for i in range(flags_ref.shape[0]):
        value = 1 - scalars[1] if i == 1 else scalars[1 if i == 0 else 2 + i]
        flags_ref[i:i + 1, :] = jnp.full((1, flags_ref.shape[1]), value, jnp.int32).astype(F32)
    for copy in copies[:2]:
        copy.wait()
    width = keys.shape[1] // 2
    place = scalars[1]
    sides = []
    for side in range(2):
        cols = slice(side * width, (side + 1) * width)
        square = lax.dot_general(
            keys[:, cols], values[:, cols], (((0,), (0,)), ((), ())), preferred_element_type=F32
        )
        sides.append(
            jnp.concatenate(
                [square[h:h + HEAD, h:h + HEAD] for h in range(0, width, HEAD)], axis=1
            ).astype(BF16)
        )
    kept_ref[...] = jnp.where(place == 0, sides[0], sides[1])
    given_ref[...] = jnp.where(place == 0, sides[1], sides[0])
    for copy in copies[2:]:
        copy.wait()


def within_kernel(scalars, keys, values, queries, out_ref):
    rows, width = out_ref.shape
    causal = lax.broadcasted_iota(jnp.int32, (rows, rows), 0) >= lax.broadcasted_iota(
        jnp.int32, (rows, rows), 1
    )
    for start in range(0, width, HEAD):
        cols = slice(start, start + HEAD)
        scores = lax.dot_general(
            queries[:, cols], keys[:, cols], (((1,), (1,)), ((), ())), preferred_element_type=F32
        )
        high, low = split(jnp.where(causal, scores, 0.0))
        out_ref[:, cols] = jnp.dot(
            high, values[:, cols], preferred_element_type=F32
        ) + jnp.dot(low, values[:, cols], preferred_element_type=F32)


def attend_kernel(
    parts, scalars, within_ref, queries, residuals, gain_ref, mine_ref, other_ref, *refs
):
    piece_refs, hidden = refs[-1 - parts:-1], refs[-1]
    rows, full = hidden.shape
    width = full // 2
    first = scalars[1] == 0
    mine, other = mine_ref[...], other_ref[...].astype(F32)
    halves = [jnp.where(first, mine, other), jnp.where(first, other, mine)]
    for start in range(0, full, HEAD):
        cols = slice(start, start + HEAD)
        half, inner = divmod(start, width)
        high, low = split(halves[half][:, inner:inner + HEAD])
        raw = (
            jnp.dot(queries[:, cols], high, preferred_element_type=F32)
            + jnp.dot(queries[:, cols], low, preferred_element_type=F32)
            + within_ref[:, cols]
        )
        scaled = raw * lax.rsqrt(jnp.mean(raw * raw, axis=-1, keepdims=True) + 1e-06)
        hidden[:, cols] = (residuals[:, cols].astype(F32) + scaled * gain_ref[:, cols]).astype(BF16)
    count = rows // parts
    for j, piece in enumerate(piece_refs):
        piece[...] = hidden[pl.ds(pl.multiple_of((scalars[0] ^ j) * count, count), count), :]


def load_kernel(lead, scalars, source, after_ref, target, done_ref, sems):
    done_ref[...] = jnp.zeros_like(done_ref)
    pieces = sems.shape[0]
    step = target.shape[0] // pieces
    cuts = [pl.ds(i * step, step) for i in range(pieces)]
    run_copies([(source.at[lead, cut], target.at[cut]) for cut in cuts], sems)


def load_near(scalars, source, lead, after):
    return call(
        functools.partial(load_kernel, lead),
        [shape(source.shape[1:], source.dtype), shape((8, HEAD), F32)],
        [scalars, source, after], far=(1,), scratch=[pltpu.SemaphoreType.DMA((8,))],
    )


def expert_kernel(blocks, scalars, sign_ref, gate_ref, up_ref, down_ref, *refs):
    x_refs, out_refs, done_ref = refs[:blocks], refs[blocks:2 * blocks], refs[2 * blocks]
    rows_ref, act_ref, made_ref = refs[2 * blocks + 1:]
    done_ref[...] = jnp.zeros_like(done_ref)
    model, units = gate_ref.shape
    spans, packs = [], []
    first = 0
    for ref in x_refs:
        spans.append(slice(first, first + ref.shape[0]))
        rows_ref[spans[-1], :] = ref[:, :model]
        packs.append(ref[:, model:].astype(F32))
        first += ref.shape[0]
    pack = jnp.concatenate(packs)
    lane = lax.broadcasted_iota(jnp.int32, pack.shape, 1)
    chosen = (lane == scalars[3]) | (lane == scalars[3] + scalars[2])
    weight = jnp.sum(jnp.where(chosen, pack, 0.0), axis=-1, keepdims=True)
    chunk = min(units, 512)

    for step in range(units // chunk):
        cut = slice(step * chunk, (step + 1) * chunk)
        gate = jnp.dot(rows_ref[...], gate_ref[:, cut], preferred_element_type=F32)
        up = jnp.dot(rows_ref[...], up_ref[:, cut], preferred_element_type=F32)
        act_ref[:, cut] = (gate / (1.0 + jnp.exp(-gate)) * up).astype(BF16)

    wide = min(model, 1024)

    for step in range(model // wide):
        cut = slice(step * wide, (step + 1) * wide)
        produced = jnp.dot(act_ref[...], down_ref[:, cut], preferred_element_type=F32)
        made_ref[:, cut] = (produced.astype(BF16).astype(F32) * weight).astype(BF16)

    for out_ref, span in zip(out_refs, spans):
        out_ref[...] = made_ref[span, :]


def run_expert(scalars, sign, blocks, weights_gate, weights_up, weights_out):
    units, model = weights_out.shape
    total = sum(b.shape[0] for b in blocks)
    *made, sign = call(
        functools.partial(expert_kernel, len(blocks)),
        [shape((b.shape[0], model), BF16) for b in blocks] + [shape((8, HEAD), F32)],
        [scalars, sign, weights_gate, weights_up, weights_out, *blocks],
        scratch=[
            pltpu.VMEM((total, model), BF16),
            pltpu.VMEM((total, units), BF16),
            pltpu.VMEM((total, model), BF16),
        ],
        flops=6 * total * model * units,
        limit=24 << 20,
    )
    return made, sign


def ring_order(count):
    return list(range(0, count, 2)) + list(range(1, count, 2))[::-1]


def dense_experts(block, scalars, turns, weights_gate, weights_up, expert_out):
    count = lax.axis_size("seq")
    order = ring_order(count)
    far = count // 2
    parts = lax.axis_size("exp")

    def hop(rows, steps):
        return lax.ppermute(
            rows, "seq", [(order[p], order[(p + steps) % count]) for p in range(count)]
        )

    def far_hop(rows):
        pairs = []
        for p in range(count):
            for e in range(parts):
                target = order[(p + (2 if e % 2 == 0 else -2)) % count]
                pairs.append((order[p] * parts + e, target * parts + e))
        return lax.ppermute(rows, ("seq", "exp"), pairs)

    ahead, behind = [block], [block]
    for distance in range(1, far - 1):
        came, went = hop(ahead[-1], 1), hop(behind[-1], -1)
        if distance == far - 2:
            weights_out, sign = load_near(scalars, expert_out, 0, ahead[-1])
            came, went, sign = lax.optimization_barrier((came, went, sign))
        ahead.append(came)
        behind.append(went)
    last = hop(ahead[-1], 1), hop(behind[-1], -1)
    turned = turns[0]
    farthest = far_hop(jnp.where(turned, behind[-1], ahead[-1]))
    weights = weights_gate, weights_up, weights_out
    (own, *near), sign = run_expert(scalars, sign, ahead + behind[1:], *weights)
    *last, farthest, sign = lax.optimization_barrier((*last, farthest, sign))
    (back, front, farthest), _ = run_expert(scalars, sign, [*last, farthest], *weights)
    to_back, to_front = near[:far - 2] + [back], near[far - 2:] + [front]
    going, coming = hop(to_front[-1], 1), hop(to_back[-1], -1)
    early = far_hop(farthest)
    for distance in range(far - 2, 0, -1):
        front, back = to_front[distance - 1], to_back[distance - 1]
        if distance == far - 2:
            nothing = jnp.zeros_like(early)
            going = add_rows(going, front, jnp.where(turned, nothing, early))
            coming = add_rows(coming, back, jnp.where(turned, early, nothing))
        else:
            going = add_rows(going, front)
            coming = add_rows(coming, back)
        going, coming = hop(going, 1), hop(coming, -1)
    return own, going, coming


def slot_ids(block_routes, expert_count, capacity):
    row_count, top_count = block_routes.shape
    expert_ids = jnp.arange(expert_count, dtype=jnp.int32)
    onehot = (
        (block_routes[:, :, None] == expert_ids[None, None, :])
        .astype(jnp.int32)
        .reshape(row_count * top_count, expert_count)
    )
    earlier = jnp.cumsum(onehot, axis=0) - onehot
    ranking = jnp.sum(earlier * onehot, axis=1).reshape(row_count, top_count)
    return block_routes * capacity + ranking


def routed_experts(normed, my_routes, my_gates, expert_in, expert_out):
    sub_count, model_width = normed.shape
    expert_count = lax.axis_size("seq") * expert_in.shape[0]
    top_count = my_routes.shape[1]
    capacity = min(sub_count, max(2, 3 * sub_count * top_count // (2 * expert_count)))
    slot_count = expert_count * capacity
    my_slots = slot_ids(my_routes, expert_count, capacity)
    columns = jnp.arange(slot_count, dtype=jnp.int32)
    placer = jnp.sum(
        (my_slots[None, :, :] == columns[:, None, None]).astype(jnp.int32), axis=2
    ).astype(BF16)
    outgoing = (
        jnp.dot(placer, normed, preferred_element_type=F32)
        .astype(BF16)
        .reshape(expert_count, capacity, model_width)
    )
    arrived = lax.all_to_all(outgoing, "seq", split_axis=0, concat_axis=0, tiled=True)
    flat_rows = arrived.reshape(-1, model_width)
    gate_up = jnp.einsum("nd,gdf->gnf", flat_rows, expert_in[0], preferred_element_type=F32)
    activated = (jax.nn.silu(gate_up[0]) * gate_up[1]).astype(BF16)
    produced = jnp.dot(activated, expert_out[0], preferred_element_type=F32).astype(BF16)
    answered = produced.reshape(arrived.shape)
    returned = lax.all_to_all(answered, "seq", split_axis=0, concat_axis=0, tiled=True)
    picked = returned.reshape(slot_count, model_width)[my_slots.reshape(-1)].reshape(
        sub_count, top_count, model_width
    )
    return jnp.sum(picked.astype(F32) * my_gates[:, :, None], axis=1)


def swap_pairs(rows, distance):
    count = lax.axis_size("seq")
    return lax.ppermute(rows, "seq", [(i, i ^ (2 * distance)) for i in range(count)])


def pair_steps(pairs):
    bits = pairs.bit_length() - 1
    direct = pairs <= 4
    steps = range(1, pairs) if direct else [1 << b for b in range(bits)]
    return direct, [(d, d.bit_length() - 1) for d in steps]


def prior_states(total):
    count = lax.axis_size("seq")
    direct, steps = pair_steps(count // 2)
    terms = []
    for distance, _ in steps:
        terms.append(
            lax.ppermute(total, "seq", [(i, i ^ (2 * distance)) for i in range(count)])
        )
        if not direct:
            total = add_rows(total, terms[-1])
    return terms


def exchange(pieces):
    parts = len(pieces)
    return [pieces[0]] + [
        lax.ppermute(pieces[j], "exp", [(i, i ^ j) for i in range(parts)])
        for j in range(1, parts)
    ]


def turn_order(items, turns):
    for b, turn in enumerate(turns):
        items = [jnp.where(turn, items[i ^ (1 << b)], items[i]) for i in range(len(items))]
    return items


def per_device(
    residual,
    queries,
    key_vectors,
    value_vectors,
    head_gain,
    norm_gain,
    routes,
    route_gates,
    expert_in,
    expert_out,
):
    rows, width = residual.shape
    seq, parts = lax.axis_size("seq"), lax.axis_size("exp")
    count, half, model = rows // parts, width // 2, width * parts
    experts = seq * expert_in.shape[0]
    position = lax.axis_index("seq")
    my_index = lax.axis_index("exp")
    place = position % 2
    _, steps = pair_steps(seq // 2)
    scalars = jnp.stack(
        [my_index, place, experts, position] + [(position >> (bit + 1)) & 1 for _, bit in steps]
    ).astype(jnp.int32)
    swap = [(i, i ^ 1) for i in range(seq)]
    turns = [
        ((my_index >> b) & 1 != 0).reshape(1, 1) for b in range(parts.bit_length() - 1)
    ]
    my_rows = (my_index * count).astype(jnp.uint32)
    scalars, turns, my_rows = lax.optimization_barrier((scalars, turns, my_rows))
    state, heads = shape((HEAD, half), BF16), shape((rows, width), BF16)
    kept, given, keys, values, query, rest, my_gain, flags = call(
        open_kernel,
        [state] * 2 + [heads] * 4
        + [shape((1, width), F32), shape((2 + len(steps), half), F32)],
        [scalars, key_vectors, value_vectors, queries, residual, head_gain[None, :]],
        far=(1, 2, 3, 4, 5),
        scratch=[pltpu.SemaphoreType.DMA((5,))],
        flops=2 * rows * width * HEAD,
    )
    partner = lax.ppermute(given, "seq", swap)
    [within] = call(
        within_kernel, [shape((rows, width), F32)], [scalars, keys, values, query],
        flops=6 * rows * rows * width,
    )
    dense = routes.shape[1] == experts
    total, within = lax.optimization_barrier((add_rows(kept, partner), within))
    sign = jnp.zeros((8, HEAD), F32)
    if dense:
        weights_gate, sign = load_near(scalars, expert_in[0], 0, total)
    before = sum(
        came.astype(F32) * flags[2 + i:3 + i] for i, came in enumerate(prior_states(total))
    )
    mine = before + partner.astype(F32) * flags[:1]
    lacked = (before + kept.astype(F32) * flags[1:2]).astype(BF16)
    lacked, sign = lax.optimization_barrier((lacked, sign))
    other = lax.ppermute(lacked, "seq", swap)
    signs = [sign]
    if dense:
        weights_up, sign = load_near(scalars, expert_in[0], 1, lacked)
        signs.append(sign)
    pieces = call(
        functools.partial(attend_kernel, parts),
        [shape((count, width), BF16)] * parts,
        [scalars, within, query, rest, my_gain, mine, other, *signs],
        scratch=[pltpu.VMEM((rows, width), BF16)],
        flops=4 * rows * width * HEAD,
    )
    gathered = exchange(pieces)

    my_routes = lax.dynamic_slice_in_dim(routes, my_rows, count, 0)
    my_gates = lax.dynamic_slice_in_dim(route_gates, my_rows, count, 0)
    mixing = jnp.sum(
        jnp.where(
            my_routes[:, :, None] == jnp.arange(experts, dtype=jnp.int32),
            my_gates[:, :, None],
            0.0,
        ),
        axis=1,
    )
    high = lax.reduce_precision(mixing, 8, 7)
    lanes = -(-2 * experts // HEAD) * HEAD
    pack = jnp.pad(
        jnp.concatenate([high, mixing - high], axis=1), ((0, 0), (0, lanes - 2 * experts))
    ).astype(BF16)
    hidden = jnp.concatenate(turn_order(gathered, turns), axis=1)
    widened = hidden.astype(F32)
    normed = (
        widened
        * lax.rsqrt(jnp.mean(widened * widened, axis=-1, keepdims=True) + 1e-06)
        * norm_gain
    ).astype(BF16)
    if dense:
        block = jnp.concatenate([normed, pack], axis=1)
        terms = dense_experts(
            block, scalars, turns, weights_gate, weights_up, expert_out
        )
    else:
        mixed = routed_experts(normed, my_routes, my_gates, expert_in, expert_out)
        terms = [mixed]
    own, *others = terms
    mixed = own.astype(F32) + sum(t.astype(F32) for t in others)
    ready = (hidden.astype(F32) + mixed).astype(BF16)
    columns = [ready[:, i * width:(i + 1) * width] for i in range(parts)]
    return jnp.concatenate(turn_order(exchange(turn_order(columns, turns)), turns))


def solution(mesh):
    placed = (
        P("seq", "exp"),
        P("seq", "exp"),
        P("seq", "exp"),
        P("seq", "exp"),
        P("exp"),
        P(),
        P("seq", None),
        P("seq", None),
        P("seq", None, None, None),
        P("seq", None, None),
    )
    return jax.shard_map(
        per_device, mesh=mesh, in_specs=placed, out_specs=P("seq", "exp"), check_vma=False
    )
```

```python
import functools

import jax
import jax.numpy as jnp
from jax import lax
from jax.experimental import pallas as pl
from jax.experimental.pallas import tpu as pltpu
from jax.sharding import PartitionSpec as P

HEAD = 128
F32 = jnp.float32
BF16 = jnp.bfloat16
WHOLE = pl.BlockSpec(memory_space=pltpu.VMEM)
FAR = pl.BlockSpec(memory_space=pltpu.HBM)
SCALAR = pl.BlockSpec(memory_space=pltpu.SMEM)


def call(kernel, outs, inputs, far=(), small=(), scratch=(), out_specs=None, flops=0, limit=16 << 20):
    moved = sum(a.size * a.dtype.itemsize for a in [*inputs, *outs])
    inputs = [
        pltpu.with_memory_space_constraint(a, pltpu.HBM) if i in far else a
        for i, a in enumerate(inputs)
    ]
    return pl.pallas_call(
        kernel,
        out_shape=outs,
        in_specs=[
            SCALAR if i == 0 or i in small else FAR if i in far else WHOLE
            for i in range(len(inputs))
        ],
        out_specs=out_specs or [WHOLE] * len(outs),
        scratch_shapes=scratch,
        compiler_params=pltpu.CompilerParams(vmem_limit_bytes=limit),
        cost_estimate=pl.CostEstimate(flops=flops, bytes_accessed=moved, transcendentals=0),
    )(*inputs)


def shape(dims, dtype):
    return jax.ShapeDtypeStruct(dims, dtype)


def split(value):
    high = value.astype(BF16)
    return high, (value - high.astype(F32)).astype(BF16)


def add_rows(*terms):
    return sum(t.astype(F32) for t in terms).astype(BF16)


def run_copies(pairs, sems):
    copies = [pltpu.make_async_copy(a, b, sems.at[i]) for i, (a, b) in enumerate(pairs)]
    for copy in copies:
        copy.start()
    for copy in copies:
        copy.wait()


def open_kernel(
    scalars, key_ref, value_ref, query_ref, residual_ref, gain_ref,
    kept_ref, given_ref, keys, values, query, residual, gain, flags_ref, sems
):
    pairs = [
        (key_ref, keys), (value_ref, values), (query_ref, query), (residual_ref, residual),
        (gain_ref, gain),
    ]
    copies = [pltpu.make_async_copy(a, b, sems.at[i]) for i, (a, b) in enumerate(pairs)]
    for copy in copies:
        copy.start()
    for i in range(flags_ref.shape[0]):
        value = 1 - scalars[1] if i == 1 else scalars[1 if i == 0 else 2 + i]
        flags_ref[i:i + 1, :] = jnp.full((1, flags_ref.shape[1]), value, jnp.int32).astype(F32)
    for copy in copies[:2]:
        copy.wait()
    width = keys.shape[1] // 2
    place = scalars[1]
    sides = []
    for side in range(2):
        cols = slice(side * width, (side + 1) * width)
        square = lax.dot_general(
            keys[:, cols], values[:, cols], (((0,), (0,)), ((), ())), preferred_element_type=F32
        )
        sides.append(
            jnp.concatenate(
                [square[h:h + HEAD, h:h + HEAD] for h in range(0, width, HEAD)], axis=1
            ).astype(BF16)
        )
    kept_ref[...] = jnp.where(place == 0, sides[0], sides[1])
    given_ref[...] = jnp.where(place == 0, sides[1], sides[0])
    for copy in copies[2:]:
        copy.wait()


def within_kernel(scalars, keys, values, queries, out_ref):
    rows, width = out_ref.shape
    causal = lax.broadcasted_iota(jnp.int32, (rows, rows), 0) >= lax.broadcasted_iota(
        jnp.int32, (rows, rows), 1
    )
    for start in range(0, width, HEAD):
        cols = slice(start, start + HEAD)
        scores = lax.dot_general(
            queries[:, cols], keys[:, cols], (((1,), (1,)), ((), ())), preferred_element_type=F32
        )
        high, low = split(jnp.where(causal, scores, 0.0))
        out_ref[:, cols] = jnp.dot(
            high, values[:, cols], preferred_element_type=F32
        ) + jnp.dot(low, values[:, cols], preferred_element_type=F32)


def attend_kernel(
    parts, scalars, within_ref, queries, residuals, gain_ref, mine_ref, other_ref, *refs
):
    piece_refs, hidden = refs[-1 - parts:-1], refs[-1]
    rows, full = hidden.shape
    width = full // 2
    first = scalars[1] == 0
    mine, other = mine_ref[...], other_ref[...].astype(F32)
    halves = [jnp.where(first, mine, other), jnp.where(first, other, mine)]
    for start in range(0, full, HEAD):
        cols = slice(start, start + HEAD)
        half, inner = divmod(start, width)
        high, low = split(halves[half][:, inner:inner + HEAD])
        raw = (
            jnp.dot(queries[:, cols], high, preferred_element_type=F32)
            + jnp.dot(queries[:, cols], low, preferred_element_type=F32)
            + within_ref[:, cols]
        )
        scaled = raw * lax.rsqrt(jnp.mean(raw * raw, axis=-1, keepdims=True) + 1e-06)
        hidden[:, cols] = (residuals[:, cols].astype(F32) + scaled * gain_ref[:, cols]).astype(BF16)
    count = rows // parts
    for j, piece in enumerate(piece_refs):
        piece[...] = hidden[pl.ds(pl.multiple_of((scalars[0] ^ j) * count, count), count), :]


def load_kernel(lead, scalars, source, after_ref, target, done_ref, sems):
    done_ref[...] = jnp.zeros_like(done_ref)
    pieces = sems.shape[0]
    step = target.shape[0] // pieces
    cuts = [pl.ds(i * step, step) for i in range(pieces)]
    run_copies([(source.at[lead, cut], target.at[cut]) for cut in cuts], sems)


def load_near(scalars, source, lead, after):
    return call(
        functools.partial(load_kernel, lead),
        [shape(source.shape[1:], source.dtype), shape((8, HEAD), F32)],
        [scalars, source, after], far=(1,), scratch=[pltpu.SemaphoreType.DMA((8,))],
    )


def expert_kernel(blocks, scalars, sign_ref, gate_ref, up_ref, down_ref, *refs):
    x_refs, out_refs, done_ref = refs[:blocks], refs[blocks:2 * blocks], refs[2 * blocks]
    rows_ref, act_ref, made_ref = refs[2 * blocks + 1:]
    done_ref[...] = jnp.zeros_like(done_ref)
    model, units = gate_ref.shape
    spans, packs = [], []
    first = 0
    for ref in x_refs:
        spans.append(slice(first, first + ref.shape[0]))
        rows_ref[spans[-1], :] = ref[:, :model]
        packs.append(ref[:, model:].astype(F32))
        first += ref.shape[0]
    spare = rows_ref.shape[0] - first
    if spare:
        rows_ref[first:, :] = jnp.zeros((spare, model), BF16)
        packs.append(jnp.zeros((spare, packs[0].shape[1]), F32))
    pack = jnp.concatenate(packs)
    lane = lax.broadcasted_iota(jnp.int32, pack.shape, 1)
    chosen = (lane == scalars[3]) | (lane == scalars[3] + scalars[2])
    weight = jnp.sum(jnp.where(chosen, pack, 0.0), axis=-1, keepdims=True)
    chunk = min(units, 512)

    for step in range(units // chunk):
        cut = slice(step * chunk, (step + 1) * chunk)
        gate = jnp.dot(rows_ref[...], gate_ref[:, cut], preferred_element_type=F32)
        up = jnp.dot(rows_ref[...], up_ref[:, cut], preferred_element_type=F32)
        act_ref[:, cut] = (gate / (1.0 + jnp.exp(-gate)) * up).astype(BF16)

    wide = min(model, 1024)

    for step in range(model // wide):
        cut = slice(step * wide, (step + 1) * wide)
        produced = jnp.dot(act_ref[...], down_ref[:, cut], preferred_element_type=F32)
        made_ref[:, cut] = (produced.astype(BF16).astype(F32) * weight).astype(BF16)

    for out_ref, span in zip(out_refs, spans):
        out_ref[...] = made_ref[span, :]


def run_expert(scalars, sign, blocks, weights_gate, weights_up, weights_out):
    units, model = weights_out.shape
    total = -(-sum(b.shape[0] for b in blocks) // HEAD) * HEAD
    *made, sign = call(
        functools.partial(expert_kernel, len(blocks)),
        [shape((b.shape[0], model), BF16) for b in blocks] + [shape((8, HEAD), F32)],
        [scalars, sign, weights_gate, weights_up, weights_out, *blocks],
        scratch=[
            pltpu.VMEM((total, model), BF16),
            pltpu.VMEM((total, units), BF16),
            pltpu.VMEM((total, model), BF16),
        ],
        flops=6 * total * model * units,
        limit=24 << 20,
    )
    return made, sign


def ring_order(count):
    return list(range(0, count, 2)) + list(range(1, count, 2))[::-1]


def dense_experts(block, scalars, weights_gate, weights_up, expert_out):
    count = lax.axis_size("seq")
    order = ring_order(count)
    far = count // 2

    def hop(rows, steps):
        return lax.ppermute(
            rows, "seq", [(order[p], order[(p + steps) % count]) for p in range(count)]
        )

    ahead, behind = [block], [block]
    farthest = hop(block, far)
    for distance in range(1, far - 1):
        came, went = hop(ahead[-1], 1), hop(behind[-1], -1)
        if distance == far - 2:
            weights_out, sign = load_near(scalars, expert_out, 0, ahead[-1])
            came, went, sign = lax.optimization_barrier((came, went, sign))
        ahead.append(came)
        behind.append(went)
    last = hop(ahead[-1], 1), hop(behind[-1], -1)
    weights = weights_gate, weights_up, weights_out
    (own, *near), sign = run_expert(scalars, sign, ahead + behind[1:], *weights)
    *last, farthest, sign = lax.optimization_barrier((*last, farthest, sign))
    (back, front, farthest), _ = run_expert(scalars, sign, [*last, farthest], *weights)
    to_back, to_front = near[:far - 2] + [back], near[far - 2:] + [front]
    going, coming = hop(to_front[-1], 1), hop(to_back[-1], -1)
    straight = hop(farthest, far)
    for distance in range(far - 2, -1, -1):
        if distance == 0:
            return own, going, coming, straight
        going = hop(add_rows(going, to_front[distance - 1]), 1)
        coming = hop(add_rows(coming, to_back[distance - 1]), -1)


def slot_ids(block_routes, expert_count, capacity):
    row_count, top_count = block_routes.shape
    expert_ids = jnp.arange(expert_count, dtype=jnp.int32)
    onehot = (
        (block_routes[:, :, None] == expert_ids[None, None, :])
        .astype(jnp.int32)
        .reshape(row_count * top_count, expert_count)
    )
    earlier = jnp.cumsum(onehot, axis=0) - onehot
    ranking = jnp.sum(earlier * onehot, axis=1).reshape(row_count, top_count)
    return block_routes * capacity + ranking


def routed_experts(normed, my_routes, my_gates, expert_in, expert_out):
    sub_count, model_width = normed.shape
    expert_count = lax.axis_size("seq") * expert_in.shape[0]
    top_count = my_routes.shape[1]
    capacity = min(sub_count, max(2, 3 * sub_count * top_count // (2 * expert_count)))
    slot_count = expert_count * capacity
    my_slots = slot_ids(my_routes, expert_count, capacity)
    columns = jnp.arange(slot_count, dtype=jnp.int32)
    placer = jnp.sum(
        (my_slots[None, :, :] == columns[:, None, None]).astype(jnp.int32), axis=2
    ).astype(BF16)
    outgoing = (
        jnp.dot(placer, normed, preferred_element_type=F32)
        .astype(BF16)
        .reshape(expert_count, capacity, model_width)
    )
    arrived = lax.all_to_all(outgoing, "seq", split_axis=0, concat_axis=0, tiled=True)
    flat_rows = arrived.reshape(-1, model_width)
    gate_up = jnp.einsum("nd,gdf->gnf", flat_rows, expert_in[0], preferred_element_type=F32)
    activated = (jax.nn.silu(gate_up[0]) * gate_up[1]).astype(BF16)
    produced = jnp.dot(activated, expert_out[0], preferred_element_type=F32).astype(BF16)
    answered = produced.reshape(arrived.shape)
    returned = lax.all_to_all(answered, "seq", split_axis=0, concat_axis=0, tiled=True)
    picked = returned.reshape(slot_count, model_width)[my_slots.reshape(-1)].reshape(
        sub_count, top_count, model_width
    )
    return jnp.sum(picked.astype(F32) * my_gates[:, :, None], axis=1)


def swap_pairs(rows, distance):
    count = lax.axis_size("seq")
    return lax.ppermute(rows, "seq", [(i, i ^ (2 * distance)) for i in range(count)])


def pair_steps(pairs):
    bits = pairs.bit_length() - 1
    direct = pairs <= 4
    steps = range(1, pairs) if direct else [1 << b for b in range(bits)]
    return direct, [(d, d.bit_length() - 1) for d in steps]


def prior_states(total):
    count = lax.axis_size("seq")
    direct, steps = pair_steps(count // 2)
    terms = []
    for distance, _ in steps:
        terms.append(
            lax.ppermute(total, "seq", [(i, i ^ (2 * distance)) for i in range(count)])
        )
        if not direct:
            total = add_rows(total, terms[-1])
    return terms


def exchange(pieces):
    parts = len(pieces)
    return [pieces[0]] + [
        lax.ppermute(pieces[j], "exp", [(i, i ^ j) for i in range(parts)])
        for j in range(1, parts)
    ]


def turn_order(items, turns):
    for b, turn in enumerate(turns):
        items = [jnp.where(turn, items[i ^ (1 << b)], items[i]) for i in range(len(items))]
    return items


def per_device(
    residual,
    queries,
    key_vectors,
    value_vectors,
    head_gain,
    norm_gain,
    routes,
    route_gates,
    expert_in,
    expert_out,
):
    rows, width = residual.shape
    seq, parts = lax.axis_size("seq"), lax.axis_size("exp")
    count, half, model = rows // parts, width // 2, width * parts
    experts = seq * expert_in.shape[0]
    position = lax.axis_index("seq")
    my_index = lax.axis_index("exp")
    place = position % 2
    _, steps = pair_steps(seq // 2)
    scalars = jnp.stack(
        [my_index, place, experts, position] + [(position >> (bit + 1)) & 1 for _, bit in steps]
    ).astype(jnp.int32)
    swap = [(i, i ^ 1) for i in range(seq)]
    turns = [
        ((my_index >> b) & 1 != 0).reshape(1, 1) for b in range(parts.bit_length() - 1)
    ]
    my_rows = (my_index * count).astype(jnp.uint32)
    scalars, turns, my_rows = lax.optimization_barrier((scalars, turns, my_rows))
    state, heads = shape((HEAD, half), BF16), shape((rows, width), BF16)
    kept, given, keys, values, query, rest, my_gain, flags = call(
        open_kernel,
        [state] * 2 + [heads] * 4
        + [shape((1, width), F32), shape((2 + len(steps), half), F32)],
        [scalars, key_vectors, value_vectors, queries, residual, head_gain[None, :]],
        far=(1, 2, 3, 4, 5),
        scratch=[pltpu.SemaphoreType.DMA((5,))],
        flops=2 * rows * width * HEAD,
    )
    partner = lax.ppermute(given, "seq", swap)
    [within] = call(
        within_kernel, [shape((rows, width), F32)], [scalars, keys, values, query],
        flops=6 * rows * rows * width,
    )
    dense = routes.shape[1] == experts
    total, within = lax.optimization_barrier((add_rows(kept, partner), within))
    sign = jnp.zeros((8, HEAD), F32)
    if dense:
        weights_gate, sign = load_near(scalars, expert_in[0], 0, total)
    before = sum(
        came.astype(F32) * flags[2 + i:3 + i] for i, came in enumerate(prior_states(total))
    )
    mine = before + partner.astype(F32) * flags[:1]
    lacked = (before + kept.astype(F32) * flags[1:2]).astype(BF16)
    lacked, sign = lax.optimization_barrier((lacked, sign))
    other = lax.ppermute(lacked, "seq", swap)
    signs = [sign]
    if dense:
        weights_up, sign = load_near(scalars, expert_in[0], 1, lacked)
        signs.append(sign)
    pieces = call(
        functools.partial(attend_kernel, parts),
        [shape((count, width), BF16)] * parts,
        [scalars, within, query, rest, my_gain, mine, other, *signs],
        scratch=[pltpu.VMEM((rows, width), BF16)],
        flops=4 * rows * width * HEAD,
    )
    gathered = exchange(pieces)

    my_routes = lax.dynamic_slice_in_dim(routes, my_rows, count, 0)
    my_gates = lax.dynamic_slice_in_dim(route_gates, my_rows, count, 0)
    mixing = jnp.sum(
        jnp.where(
            my_routes[:, :, None] == jnp.arange(experts, dtype=jnp.int32),
            my_gates[:, :, None],
            0.0,
        ),
        axis=1,
    )
    high = lax.reduce_precision(mixing, 8, 7)
    lanes = -(-2 * experts // HEAD) * HEAD
    pack = jnp.pad(
        jnp.concatenate([high, mixing - high], axis=1), ((0, 0), (0, lanes - 2 * experts))
    ).astype(BF16)
    hidden = jnp.concatenate(turn_order(gathered, turns), axis=1)
    widened = hidden.astype(F32)
    normed = (
        widened
        * lax.rsqrt(jnp.mean(widened * widened, axis=-1, keepdims=True) + 1e-06)
        * norm_gain
    ).astype(BF16)
    if dense:
        block = jnp.concatenate([normed, pack], axis=1)
        terms = dense_experts(
            block, scalars, weights_gate, weights_up, expert_out
        )
    else:
        mixed = routed_experts(normed, my_routes, my_gates, expert_in, expert_out)
        terms = [mixed]
    own, *others = terms
    mixed = own.astype(F32) + sum(t.astype(F32) for t in others)
    ready = (hidden.astype(F32) + mixed).astype(BF16)
    columns = [ready[:, i * width:(i + 1) * width] for i in range(parts)]
    return jnp.concatenate(turn_order(exchange(turn_order(columns, turns)), turns))


def solution(mesh):
    placed = (
        P("seq", "exp"),
        P("seq", "exp"),
        P("seq", "exp"),
        P("seq", "exp"),
        P("exp"),
        P(),
        P("seq", None),
        P("seq", None),
        P("seq", None, None, None),
        P("seq", None, None),
    )
    return jax.shard_map(
        per_device, mesh=mesh, in_specs=placed, out_specs=P("seq", "exp"), check_vma=False
    )
```

```python
import functools

import jax
import jax.numpy as jnp
from jax import lax
from jax.experimental import pallas as pl
from jax.experimental.pallas import tpu as pltpu
from jax.sharding import PartitionSpec as P

HEAD = 128
F32 = jnp.float32
BF16 = jnp.bfloat16
WHOLE = pl.BlockSpec(memory_space=pltpu.VMEM)
FAR = pl.BlockSpec(memory_space=pltpu.HBM)
SCALAR = pl.BlockSpec(memory_space=pltpu.SMEM)


def call(kernel, outs, inputs, far=(), small=(), scratch=(), out_specs=None, flops=0, limit=16 << 20):
    moved = sum(a.size * a.dtype.itemsize for a in [*inputs, *outs])
    inputs = [
        pltpu.with_memory_space_constraint(a, pltpu.HBM) if i in far else a
        for i, a in enumerate(inputs)
    ]
    return pl.pallas_call(
        kernel,
        out_shape=outs,
        in_specs=[
            SCALAR if i == 0 or i in small else FAR if i in far else WHOLE
            for i in range(len(inputs))
        ],
        out_specs=out_specs or [WHOLE] * len(outs),
        scratch_shapes=scratch,
        compiler_params=pltpu.CompilerParams(vmem_limit_bytes=limit),
        cost_estimate=pl.CostEstimate(flops=flops, bytes_accessed=moved, transcendentals=0),
    )(*inputs)


def shape(dims, dtype):
    return jax.ShapeDtypeStruct(dims, dtype)


def split(value):
    high = value.astype(BF16)
    return high, (value - high.astype(F32)).astype(BF16)


def add_rows(*terms):
    return sum(t.astype(F32) for t in terms).astype(BF16)


def run_copies(pairs, sems):
    copies = [pltpu.make_async_copy(a, b, sems.at[i]) for i, (a, b) in enumerate(pairs)]
    for copy in copies:
        copy.start()
    for copy in copies:
        copy.wait()


def open_kernel(
    scalars, key_ref, value_ref, query_ref, residual_ref, gain_ref,
    kept_ref, given_ref, keys, values, query, residual, gain, flags_ref, sems
):
    pairs = [
        (key_ref, keys), (value_ref, values), (query_ref, query), (residual_ref, residual),
        (gain_ref, gain),
    ]
    copies = [pltpu.make_async_copy(a, b, sems.at[i]) for i, (a, b) in enumerate(pairs)]
    for copy in copies:
        copy.start()
    for i in range(flags_ref.shape[0]):
        value = 1 - scalars[1] if i == 1 else scalars[1 if i == 0 else 2 + i]
        flags_ref[i:i + 1, :] = jnp.full((1, flags_ref.shape[1]), value, jnp.int32).astype(F32)
    for copy in copies[:2]:
        copy.wait()
    width = keys.shape[1] // 2
    place = scalars[1]
    sides = []
    for side in range(2):
        cols = slice(side * width, (side + 1) * width)
        square = lax.dot_general(
            keys[:, cols], values[:, cols], (((0,), (0,)), ((), ())), preferred_element_type=F32
        )
        sides.append(
            jnp.concatenate(
                [square[h:h + HEAD, h:h + HEAD] for h in range(0, width, HEAD)], axis=1
            ).astype(BF16)
        )
    kept_ref[...] = jnp.where(place == 0, sides[0], sides[1])
    given_ref[...] = jnp.where(place == 0, sides[1], sides[0])
    for copy in copies[2:]:
        copy.wait()


def within_kernel(scalars, keys, values, queries, out_ref):
    rows, width = out_ref.shape
    causal = lax.broadcasted_iota(jnp.int32, (rows, rows), 0) >= lax.broadcasted_iota(
        jnp.int32, (rows, rows), 1
    )
    for start in range(0, width, HEAD):
        cols = slice(start, start + HEAD)
        scores = lax.dot_general(
            queries[:, cols], keys[:, cols], (((1,), (1,)), ((), ())), preferred_element_type=F32
        )
        high, low = split(jnp.where(causal, scores, 0.0))
        out_ref[:, cols] = jnp.dot(
            high, values[:, cols], preferred_element_type=F32
        ) + jnp.dot(low, values[:, cols], preferred_element_type=F32)


def attend_kernel(
    parts, scalars, within_ref, queries, residuals, gain_ref, mine_ref, other_ref, *refs
):
    piece_refs, hidden = refs[-1 - parts:-1], refs[-1]
    rows, full = hidden.shape
    width = full // 2
    first = scalars[1] == 0
    mine, other = mine_ref[...], other_ref[...].astype(F32)
    halves = [jnp.where(first, mine, other), jnp.where(first, other, mine)]
    for start in range(0, full, HEAD):
        cols = slice(start, start + HEAD)
        half, inner = divmod(start, width)
        high, low = split(halves[half][:, inner:inner + HEAD])
        raw = (
            jnp.dot(queries[:, cols], high, preferred_element_type=F32)
            + jnp.dot(queries[:, cols], low, preferred_element_type=F32)
            + within_ref[:, cols]
        )
        scaled = raw * lax.rsqrt(jnp.mean(raw * raw, axis=-1, keepdims=True) + 1e-06)
        hidden[:, cols] = (residuals[:, cols].astype(F32) + scaled * gain_ref[:, cols]).astype(BF16)
    count = rows // parts
    for j, piece in enumerate(piece_refs):
        piece[...] = hidden[pl.ds(pl.multiple_of((scalars[0] ^ j) * count, count), count), :]


def load_kernel(lead, scalars, source, after_ref, target, done_ref, sems):
    done_ref[...] = jnp.zeros_like(done_ref)
    pieces = sems.shape[0]
    step = target.shape[0] // pieces
    cuts = [pl.ds(i * step, step) for i in range(pieces)]
    run_copies([(source.at[lead, cut], target.at[cut]) for cut in cuts], sems)


def load_near(scalars, source, lead, after):
    return call(
        functools.partial(load_kernel, lead),
        [shape(source.shape[1:], source.dtype), shape((8, HEAD), F32)],
        [scalars, source, after], far=(1,), scratch=[pltpu.SemaphoreType.DMA((8,))],
    )


def expert_kernel(blocks, scalars, sign_ref, gate_ref, up_ref, down_ref, *refs):
    x_refs, out_refs, done_ref = refs[:blocks], refs[blocks:2 * blocks], refs[2 * blocks]
    rows_ref, act_ref, made_ref = refs[2 * blocks + 1:]
    done_ref[...] = jnp.zeros_like(done_ref)
    model, units = gate_ref.shape
    spans, packs = [], []
    first = 0
    for ref in x_refs:
        spans.append(slice(first, first + ref.shape[0]))
        rows_ref[spans[-1], :] = ref[:, :model]
        packs.append(ref[:, model:].astype(F32))
        first += ref.shape[0]
    spare = rows_ref.shape[0] - first
    if spare:
        rows_ref[first:, :] = jnp.zeros((spare, model), BF16)
        packs.append(jnp.zeros((spare, packs[0].shape[1]), F32))
    pack = jnp.concatenate(packs)
    lane = lax.broadcasted_iota(jnp.int32, pack.shape, 1)
    chosen = (lane == scalars[3]) | (lane == scalars[3] + scalars[2])
    weight = jnp.sum(jnp.where(chosen, pack, 0.0), axis=-1, keepdims=True)
    chunk = min(units, 512)

    for step in range(units // chunk):
        cut = slice(step * chunk, (step + 1) * chunk)
        gate = jnp.dot(rows_ref[...], gate_ref[:, cut], preferred_element_type=F32)
        up = jnp.dot(rows_ref[...], up_ref[:, cut], preferred_element_type=F32)
        act_ref[:, cut] = (gate / (1.0 + jnp.exp(-gate)) * up).astype(BF16)

    wide = min(model, 1024)

    for step in range(model // wide):
        cut = slice(step * wide, (step + 1) * wide)
        produced = jnp.dot(act_ref[...], down_ref[:, cut], preferred_element_type=F32)
        made_ref[:, cut] = (produced.astype(BF16).astype(F32) * weight).astype(BF16)

    for out_ref, span in zip(out_refs, spans):
        out_ref[...] = made_ref[span, :]


def run_expert(scalars, sign, blocks, weights_gate, weights_up, weights_out):
    units, model = weights_out.shape
    total = max(HEAD, sum(b.shape[0] for b in blocks))
    *made, sign = call(
        functools.partial(expert_kernel, len(blocks)),
        [shape((b.shape[0], model), BF16) for b in blocks] + [shape((8, HEAD), F32)],
        [scalars, sign, weights_gate, weights_up, weights_out, *blocks],
        scratch=[
            pltpu.VMEM((total, model), BF16),
            pltpu.VMEM((total, units), BF16),
            pltpu.VMEM((total, model), BF16),
        ],
        flops=6 * total * model * units,
        limit=24 << 20,
    )
    return made, sign


def ring_order(count):
    return list(range(0, count, 2)) + list(range(1, count, 2))[::-1]


def dense_experts(block, scalars, weights_gate, weights_up, expert_out):
    count = lax.axis_size("seq")
    order = ring_order(count)
    far = count // 2

    def hop(rows, steps):
        return lax.ppermute(
            rows, "seq", [(order[p], order[(p + steps) % count]) for p in range(count)]
        )

    ahead, behind = [block], [block]
    farthest = hop(block, far)
    for distance in range(1, far - 1):
        came, went = hop(ahead[-1], 1), hop(behind[-1], -1)
        if distance == far - 2:
            weights_out, sign = load_near(scalars, expert_out, 0, ahead[-1])
            came, went, sign, farthest = lax.optimization_barrier((came, went, sign, farthest))
        ahead.append(came)
        behind.append(went)
    last = hop(ahead[-1], 1), hop(behind[-1], -1)
    weights = weights_gate, weights_up, weights_out
    (own, *near), sign = run_expert(scalars, sign, ahead + behind[1:], *weights)
    *last, farthest, sign = lax.optimization_barrier((*last, farthest, sign))
    (back, front, farthest), _ = run_expert(scalars, sign, [*last, farthest], *weights)
    to_back, to_front = near[:far - 2] + [back], near[far - 2:] + [front]
    going, coming = hop(to_front[-1], 1), hop(to_back[-1], -1)
    straight = hop(farthest, far)
    for distance in range(far - 2, -1, -1):
        if distance == 0:
            return own, going, coming, straight
        going = hop(add_rows(going, to_front[distance - 1]), 1)
        coming = hop(add_rows(coming, to_back[distance - 1]), -1)


def slot_ids(block_routes, expert_count, capacity):
    row_count, top_count = block_routes.shape
    expert_ids = jnp.arange(expert_count, dtype=jnp.int32)
    onehot = (
        (block_routes[:, :, None] == expert_ids[None, None, :])
        .astype(jnp.int32)
        .reshape(row_count * top_count, expert_count)
    )
    earlier = jnp.cumsum(onehot, axis=0) - onehot
    ranking = jnp.sum(earlier * onehot, axis=1).reshape(row_count, top_count)
    return block_routes * capacity + ranking


def routed_experts(normed, my_routes, my_gates, expert_in, expert_out):
    sub_count, model_width = normed.shape
    expert_count = lax.axis_size("seq") * expert_in.shape[0]
    top_count = my_routes.shape[1]
    capacity = min(sub_count, max(2, 3 * sub_count * top_count // (2 * expert_count)))
    slot_count = expert_count * capacity
    my_slots = slot_ids(my_routes, expert_count, capacity)
    columns = jnp.arange(slot_count, dtype=jnp.int32)
    placer = jnp.sum(
        (my_slots[None, :, :] == columns[:, None, None]).astype(jnp.int32), axis=2
    ).astype(BF16)
    outgoing = (
        jnp.dot(placer, normed, preferred_element_type=F32)
        .astype(BF16)
        .reshape(expert_count, capacity, model_width)
    )
    arrived = lax.all_to_all(outgoing, "seq", split_axis=0, concat_axis=0, tiled=True)
    flat_rows = arrived.reshape(-1, model_width)
    gate_up = jnp.einsum("nd,gdf->gnf", flat_rows, expert_in[0], preferred_element_type=F32)
    activated = (jax.nn.silu(gate_up[0]) * gate_up[1]).astype(BF16)
    produced = jnp.dot(activated, expert_out[0], preferred_element_type=F32).astype(BF16)
    answered = produced.reshape(arrived.shape)
    returned = lax.all_to_all(answered, "seq", split_axis=0, concat_axis=0, tiled=True)
    picked = returned.reshape(slot_count, model_width)[my_slots.reshape(-1)].reshape(
        sub_count, top_count, model_width
    )
    return jnp.sum(picked.astype(F32) * my_gates[:, :, None], axis=1)


def swap_pairs(rows, distance):
    count = lax.axis_size("seq")
    return lax.ppermute(rows, "seq", [(i, i ^ (2 * distance)) for i in range(count)])


def pair_steps(pairs):
    bits = pairs.bit_length() - 1
    direct = pairs <= 4
    steps = range(1, pairs) if direct else [1 << b for b in range(bits)]
    return direct, [(d, d.bit_length() - 1) for d in steps]


def prior_states(total):
    count = lax.axis_size("seq")
    direct, steps = pair_steps(count // 2)
    terms = []
    for distance, _ in steps:
        terms.append(
            lax.ppermute(total, "seq", [(i, i ^ (2 * distance)) for i in range(count)])
        )
        if not direct:
            total = add_rows(total, terms[-1])
    return terms


def exchange(pieces):
    parts = len(pieces)
    return [pieces[0]] + [
        lax.ppermute(pieces[j], "exp", [(i, i ^ j) for i in range(parts)])
        for j in range(1, parts)
    ]


def turn_order(items, turns):
    for b, turn in enumerate(turns):
        items = [jnp.where(turn, items[i ^ (1 << b)], items[i]) for i in range(len(items))]
    return items


def per_device(
    residual,
    queries,
    key_vectors,
    value_vectors,
    head_gain,
    norm_gain,
    routes,
    route_gates,
    expert_in,
    expert_out,
):
    rows, width = residual.shape
    seq, parts = lax.axis_size("seq"), lax.axis_size("exp")
    count, half, model = rows // parts, width // 2, width * parts
    experts = seq * expert_in.shape[0]
    position = lax.axis_index("seq")
    my_index = lax.axis_index("exp")
    place = position % 2
    _, steps = pair_steps(seq // 2)
    scalars = jnp.stack(
        [my_index, place, experts, position] + [(position >> (bit + 1)) & 1 for _, bit in steps]
    ).astype(jnp.int32)
    swap = [(i, i ^ 1) for i in range(seq)]
    turns = [
        ((my_index >> b) & 1 != 0).reshape(1, 1) for b in range(parts.bit_length() - 1)
    ]
    my_rows = (my_index * count).astype(jnp.uint32)
    scalars, turns, my_rows = lax.optimization_barrier((scalars, turns, my_rows))
    state, heads = shape((HEAD, half), BF16), shape((rows, width), BF16)
    kept, given, keys, values, query, rest, my_gain, flags = call(
        open_kernel,
        [state] * 2 + [heads] * 4
        + [shape((1, width), F32), shape((2 + len(steps), half), F32)],
        [scalars, key_vectors, value_vectors, queries, residual, head_gain[None, :]],
        far=(1, 2, 3, 4, 5),
        scratch=[pltpu.SemaphoreType.DMA((5,))],
        flops=2 * rows * width * HEAD,
    )
    partner = lax.ppermute(given, "seq", swap)
    [within] = call(
        within_kernel, [shape((rows, width), F32)], [scalars, keys, values, query],
        flops=6 * rows * rows * width,
    )
    dense = routes.shape[1] == experts
    total, within = lax.optimization_barrier((add_rows(kept, partner), within))
    sign = jnp.zeros((8, HEAD), F32)
    if dense:
        weights_gate, sign = load_near(scalars, expert_in[0], 0, total)
    before = sum(
        came.astype(F32) * flags[2 + i:3 + i] for i, came in enumerate(prior_states(total))
    )
    mine = before + partner.astype(F32) * flags[:1]
    lacked = (before + kept.astype(F32) * flags[1:2]).astype(BF16)
    lacked, sign = lax.optimization_barrier((lacked, sign))
    other = lax.ppermute(lacked, "seq", swap)
    signs = [sign]
    if dense:
        weights_up, sign = load_near(scalars, expert_in[0], 1, lacked)
        signs.append(sign)
    pieces = call(
        functools.partial(attend_kernel, parts),
        [shape((count, width), BF16)] * parts,
        [scalars, within, query, rest, my_gain, mine, other, *signs],
        scratch=[pltpu.VMEM((rows, width), BF16)],
        flops=4 * rows * width * HEAD,
    )
    gathered = exchange(pieces)

    my_routes = lax.dynamic_slice_in_dim(routes, my_rows, count, 0)
    my_gates = lax.dynamic_slice_in_dim(route_gates, my_rows, count, 0)
    mixing = jnp.sum(
        jnp.where(
            my_routes[:, :, None] == jnp.arange(experts, dtype=jnp.int32),
            my_gates[:, :, None],
            0.0,
        ),
        axis=1,
    )
    high = lax.reduce_precision(mixing, 8, 7)
    lanes = -(-2 * experts // HEAD) * HEAD
    pack = jnp.pad(
        jnp.concatenate([high, mixing - high], axis=1), ((0, 0), (0, lanes - 2 * experts))
    ).astype(BF16)
    hidden = jnp.concatenate(turn_order(gathered, turns), axis=1)
    widened = hidden.astype(F32)
    normed = (
        widened
        * lax.rsqrt(jnp.mean(widened * widened, axis=-1, keepdims=True) + 1e-06)
        * norm_gain
    ).astype(BF16)
    if dense:
        block = jnp.concatenate([normed, pack], axis=1)
        terms = dense_experts(
            block, scalars, weights_gate, weights_up, expert_out
        )
    else:
        mixed = routed_experts(normed, my_routes, my_gates, expert_in, expert_out)
        terms = [mixed]
    own, *others = terms
    mixed = own.astype(F32) + sum(t.astype(F32) for t in others)
    ready = (hidden.astype(F32) + mixed).astype(BF16)
    columns = [ready[:, i * width:(i + 1) * width] for i in range(parts)]
    return jnp.concatenate(turn_order(exchange(turn_order(columns, turns)), turns))


def solution(mesh):
    placed = (
        P("seq", "exp"),
        P("seq", "exp"),
        P("seq", "exp"),
        P("seq", "exp"),
        P("exp"),
        P(),
        P("seq", None),
        P("seq", None),
        P("seq", None, None, None),
        P("seq", None, None),
    )
    return jax.shard_map(
        per_device, mesh=mesh, in_specs=placed, out_specs=P("seq", "exp"), check_vma=False
    )
```

```python
import functools

import jax
import jax.numpy as jnp
from jax import lax
from jax.experimental import pallas as pl
from jax.experimental.pallas import tpu as pltpu
from jax.sharding import PartitionSpec as P

HEAD = 128
F32 = jnp.float32
BF16 = jnp.bfloat16
WHOLE = pl.BlockSpec(memory_space=pltpu.VMEM)
FAR = pl.BlockSpec(memory_space=pltpu.HBM)
SCALAR = pl.BlockSpec(memory_space=pltpu.SMEM)


def call(kernel, outs, inputs, far=(), small=(), scratch=(), out_specs=None, flops=0, limit=16 << 20):
    moved = sum(a.size * a.dtype.itemsize for a in [*inputs, *outs])
    inputs = [
        pltpu.with_memory_space_constraint(a, pltpu.HBM) if i in far else a
        for i, a in enumerate(inputs)
    ]
    return pl.pallas_call(
        kernel,
        out_shape=outs,
        in_specs=[
            SCALAR if i == 0 or i in small else FAR if i in far else WHOLE
            for i in range(len(inputs))
        ],
        out_specs=out_specs or [WHOLE] * len(outs),
        scratch_shapes=scratch,
        compiler_params=pltpu.CompilerParams(vmem_limit_bytes=limit),
        cost_estimate=pl.CostEstimate(flops=flops, bytes_accessed=moved, transcendentals=0),
    )(*inputs)


def shape(dims, dtype):
    return jax.ShapeDtypeStruct(dims, dtype)


def split(value):
    high = value.astype(BF16)
    return high, (value - high.astype(F32)).astype(BF16)


def add_rows(*terms):
    return sum(t.astype(F32) for t in terms).astype(BF16)


def run_copies(pairs, sems):
    copies = [pltpu.make_async_copy(a, b, sems.at[i]) for i, (a, b) in enumerate(pairs)]
    for copy in copies:
        copy.start()
    for copy in copies:
        copy.wait()


def open_kernel(
    scalars, key_ref, value_ref, query_ref, residual_ref, gain_ref,
    kept_ref, given_ref, keys, values, query, residual, gain, flags_ref, sems
):
    pairs = [
        (key_ref, keys), (value_ref, values), (query_ref, query), (residual_ref, residual),
        (gain_ref, gain),
    ]
    copies = [pltpu.make_async_copy(a, b, sems.at[i]) for i, (a, b) in enumerate(pairs)]
    for copy in copies:
        copy.start()
    for i in range(flags_ref.shape[0]):
        value = 1 - scalars[1] if i == 1 else scalars[1 if i == 0 else 2 + i]
        flags_ref[i:i + 1, :] = jnp.full((1, flags_ref.shape[1]), value, jnp.int32).astype(F32)
    for copy in copies[:2]:
        copy.wait()
    width = keys.shape[1] // 2
    place = scalars[1]
    sides = []
    for side in range(2):
        cols = slice(side * width, (side + 1) * width)
        square = lax.dot_general(
            keys[:, cols], values[:, cols], (((0,), (0,)), ((), ())), preferred_element_type=F32
        )
        sides.append(
            jnp.concatenate(
                [square[h:h + HEAD, h:h + HEAD] for h in range(0, width, HEAD)], axis=1
            ).astype(BF16)
        )
    kept_ref[...] = jnp.where(place == 0, sides[0], sides[1])
    given_ref[...] = jnp.where(place == 0, sides[1], sides[0])
    for copy in copies[2:]:
        copy.wait()


def within_kernel(scalars, keys, values, queries, out_ref):
    rows, width = out_ref.shape
    causal = lax.broadcasted_iota(jnp.int32, (rows, rows), 0) >= lax.broadcasted_iota(
        jnp.int32, (rows, rows), 1
    )
    for start in range(0, width, HEAD):
        cols = slice(start, start + HEAD)
        scores = lax.dot_general(
            queries[:, cols], keys[:, cols], (((1,), (1,)), ((), ())), preferred_element_type=F32
        )
        high, low = split(jnp.where(causal, scores, 0.0))
        out_ref[:, cols] = jnp.dot(
            high, values[:, cols], preferred_element_type=F32
        ) + jnp.dot(low, values[:, cols], preferred_element_type=F32)


def attend_kernel(
    parts, scalars, within_ref, queries, residuals, gain_ref, mine_ref, other_ref, *refs
):
    piece_refs, hidden = refs[-1 - parts:-1], refs[-1]
    rows, full = hidden.shape
    width = full // 2
    first = scalars[1] == 0
    mine, other = mine_ref[...], other_ref[...].astype(F32)
    halves = [jnp.where(first, mine, other), jnp.where(first, other, mine)]
    for start in range(0, full, HEAD):
        cols = slice(start, start + HEAD)
        half, inner = divmod(start, width)
        high, low = split(halves[half][:, inner:inner + HEAD])
        raw = (
            jnp.dot(queries[:, cols], high, preferred_element_type=F32)
            + jnp.dot(queries[:, cols], low, preferred_element_type=F32)
            + within_ref[:, cols]
        )
        scaled = raw * lax.rsqrt(jnp.mean(raw * raw, axis=-1, keepdims=True) + 1e-06)
        hidden[:, cols] = (residuals[:, cols].astype(F32) + scaled * gain_ref[:, cols]).astype(BF16)
    count = rows // parts
    for j, piece in enumerate(piece_refs):
        piece[...] = hidden[pl.ds(pl.multiple_of((scalars[0] ^ j) * count, count), count), :]


def load_kernel(lead, scalars, source, after_ref, target, done_ref, sems):
    done_ref[...] = jnp.zeros_like(done_ref)
    pieces = sems.shape[0]
    step = target.shape[0] // pieces
    cuts = [pl.ds(i * step, step) for i in range(pieces)]
    run_copies([(source.at[lead, cut], target.at[cut]) for cut in cuts], sems)


def load_near(scalars, source, lead, after):
    return call(
        functools.partial(load_kernel, lead),
        [shape(source.shape[1:], source.dtype), shape((8, HEAD), F32)],
        [scalars, source, after], far=(1,), scratch=[pltpu.SemaphoreType.DMA((8,))],
    )


def expert_kernel(blocks, scalars, sign_ref, gate_ref, up_ref, down_ref, *refs):
    x_refs, out_refs, done_ref = refs[:blocks], refs[blocks:2 * blocks], refs[2 * blocks]
    rows_ref, act_ref, made_ref = refs[2 * blocks + 1:]
    done_ref[...] = jnp.zeros_like(done_ref)
    model, units = gate_ref.shape
    spans, packs = [], []
    first = 0
    for ref in x_refs:
        spans.append(slice(first, first + ref.shape[0]))
        rows_ref[spans[-1], :] = ref[:, :model]
        packs.append(ref[:, model:].astype(F32))
        first += ref.shape[0]
    spare = rows_ref.shape[0] - first
    if spare:
        rows_ref[first:, :] = jnp.zeros((spare, model), BF16)
        packs.append(jnp.zeros((spare, packs[0].shape[1]), F32))
    pack = jnp.concatenate(packs)
    lane = lax.broadcasted_iota(jnp.int32, pack.shape, 1)
    chosen = (lane == scalars[3]) | (lane == scalars[3] + scalars[2])
    weight = jnp.sum(jnp.where(chosen, pack, 0.0), axis=-1, keepdims=True)
    chunk = min(units, 512)

    for step in range(units // chunk):
        cut = slice(step * chunk, (step + 1) * chunk)
        gate = jnp.dot(rows_ref[...], gate_ref[:, cut], preferred_element_type=F32)
        up = jnp.dot(rows_ref[...], up_ref[:, cut], preferred_element_type=F32)
        act_ref[:, cut] = (gate / (1.0 + jnp.exp(-gate)) * up).astype(BF16)

    wide = min(model, 1024)

    for step in range(model // wide):
        cut = slice(step * wide, (step + 1) * wide)
        produced = jnp.dot(act_ref[...], down_ref[:, cut], preferred_element_type=F32)
        made_ref[:, cut] = (produced.astype(BF16).astype(F32) * weight).astype(BF16)

    for out_ref, span in zip(out_refs, spans):
        out_ref[...] = made_ref[span, :]


def run_expert(scalars, sign, blocks, weights_gate, weights_up, weights_out):
    units, model = weights_out.shape
    total = max(HEAD, sum(b.shape[0] for b in blocks))
    *made, sign = call(
        functools.partial(expert_kernel, len(blocks)),
        [shape((b.shape[0], model), BF16) for b in blocks] + [shape((8, HEAD), F32)],
        [scalars, sign, weights_gate, weights_up, weights_out, *blocks],
        scratch=[
            pltpu.VMEM((total, model), BF16),
            pltpu.VMEM((total, units), BF16),
            pltpu.VMEM((total, model), BF16),
        ],
        flops=6 * total * model * units,
        limit=24 << 20,
    )
    return made, sign


def ring_order(count):
    return list(range(0, count, 2)) + list(range(1, count, 2))[::-1]


def dense_experts(block, scalars, weights_gate, weights_up, expert_out):
    count = lax.axis_size("seq")
    order = ring_order(count)
    far = count // 2

    def hop(rows, steps):
        return lax.ppermute(
            rows, "seq", [(order[p], order[(p + steps) % count]) for p in range(count)]
        )

    ahead, behind = [block], [block]
    farthest = hop(block, far)
    for distance in range(1, far - 1):
        came, went = hop(ahead[-1], 1), hop(behind[-1], -1)
        if distance == far - 2:
            weights_out, sign = load_near(scalars, expert_out, 0, ahead[-1])
            came, went, sign, farthest = lax.optimization_barrier((came, went, sign, farthest))
        ahead.append(came)
        behind.append(went)
    last = hop(ahead[-1], 1), hop(behind[-1], -1)
    weights = weights_gate, weights_up, weights_out
    (own, *near), sign = run_expert(scalars, sign, ahead + behind[1:], *weights)
    *last, farthest, sign = lax.optimization_barrier((*last, farthest, sign))
    (back, front, farthest), _ = run_expert(scalars, sign, [*last, farthest], *weights)
    to_back, to_front = near[:far - 2] + [back], near[far - 2:] + [front]
    going, coming = hop(to_front[-1], 1), hop(to_back[-1], -1)
    straight = hop(farthest, far)
    for distance in range(far - 2, -1, -1):
        if distance == 0:
            return own, going, coming, straight
        going = hop(add_rows(going, to_front[distance - 1]), 1)
        coming = hop(add_rows(coming, to_back[distance - 1]), -1)


def slot_ids(block_routes, expert_count, capacity):
    row_count, top_count = block_routes.shape
    expert_ids = jnp.arange(expert_count, dtype=jnp.int32)
    onehot = (
        (block_routes[:, :, None] == expert_ids[None, None, :])
        .astype(jnp.int32)
        .reshape(row_count * top_count, expert_count)
    )
    earlier = jnp.cumsum(onehot, axis=0) - onehot
    ranking = jnp.sum(earlier * onehot, axis=1).reshape(row_count, top_count)
    return block_routes * capacity + ranking


def routed_experts(normed, my_routes, my_gates, expert_in, expert_out):
    sub_count, model_width = normed.shape
    expert_count = lax.axis_size("seq") * expert_in.shape[0]
    top_count = my_routes.shape[1]
    capacity = min(sub_count, max(2, 3 * sub_count * top_count // (2 * expert_count)))
    slot_count = expert_count * capacity
    my_slots = slot_ids(my_routes, expert_count, capacity)
    columns = jnp.arange(slot_count, dtype=jnp.int32)
    placer = jnp.sum(
        (my_slots[None, :, :] == columns[:, None, None]).astype(jnp.int32), axis=2
    ).astype(BF16)
    outgoing = (
        jnp.dot(placer, normed, preferred_element_type=F32)
        .astype(BF16)
        .reshape(expert_count, capacity, model_width)
    )
    arrived = lax.all_to_all(outgoing, "seq", split_axis=0, concat_axis=0, tiled=True)
    flat_rows = arrived.reshape(-1, model_width)
    gate_up = jnp.einsum("nd,gdf->gnf", flat_rows, expert_in[0], preferred_element_type=F32)
    activated = (jax.nn.silu(gate_up[0]) * gate_up[1]).astype(BF16)
    produced = jnp.dot(activated, expert_out[0], preferred_element_type=F32).astype(BF16)
    answered = produced.reshape(arrived.shape)
    returned = lax.all_to_all(answered, "seq", split_axis=0, concat_axis=0, tiled=True)
    picked = returned.reshape(slot_count, model_width)[my_slots.reshape(-1)].reshape(
        sub_count, top_count, model_width
    )
    return jnp.sum(picked.astype(F32) * my_gates[:, :, None], axis=1)


def swap_pairs(rows, distance):
    count = lax.axis_size("seq")
    return lax.ppermute(rows, "seq", [(i, i ^ (2 * distance)) for i in range(count)])


def pair_steps(pairs):
    bits = pairs.bit_length() - 1
    direct = pairs <= 4
    steps = range(pairs - 1, 0, -1) if direct else [1 << b for b in range(bits)]
    return direct, [(d, d.bit_length() - 1) for d in steps]


def prior_states(total):
    count = lax.axis_size("seq")
    direct, steps = pair_steps(count // 2)
    terms = []
    for distance, _ in steps:
        terms.append(
            lax.ppermute(total, "seq", [(i, i ^ (2 * distance)) for i in range(count)])
        )
        if not direct:
            total = add_rows(total, terms[-1])
    return terms


def exchange(pieces):
    parts = len(pieces)
    return [pieces[0]] + [
        lax.ppermute(pieces[j], "exp", [(i, i ^ j) for i in range(parts)])
        for j in range(1, parts)
    ]


def turn_order(items, turns):
    for b, turn in enumerate(turns):
        items = [jnp.where(turn, items[i ^ (1 << b)], items[i]) for i in range(len(items))]
    return items


def per_device(
    residual,
    queries,
    key_vectors,
    value_vectors,
    head_gain,
    norm_gain,
    routes,
    route_gates,
    expert_in,
    expert_out,
):
    rows, width = residual.shape
    seq, parts = lax.axis_size("seq"), lax.axis_size("exp")
    count, half, model = rows // parts, width // 2, width * parts
    experts = seq * expert_in.shape[0]
    position = lax.axis_index("seq")
    my_index = lax.axis_index("exp")
    place = position % 2
    _, steps = pair_steps(seq // 2)
    scalars = jnp.stack(
        [my_index, place, experts, position] + [(position >> (bit + 1)) & 1 for _, bit in steps]
    ).astype(jnp.int32)
    swap = [(i, i ^ 1) for i in range(seq)]
    turns = [
        ((my_index >> b) & 1 != 0).reshape(1, 1) for b in range(parts.bit_length() - 1)
    ]
    my_rows = (my_index * count).astype(jnp.uint32)
    scalars, turns, my_rows = lax.optimization_barrier((scalars, turns, my_rows))
    state, heads = shape((HEAD, half), BF16), shape((rows, width), BF16)
    kept, given, keys, values, query, rest, my_gain, flags = call(
        open_kernel,
        [state] * 2 + [heads] * 4
        + [shape((1, width), F32), shape((2 + len(steps), half), F32)],
        [scalars, key_vectors, value_vectors, queries, residual, head_gain[None, :]],
        far=(1, 2, 3, 4, 5),
        scratch=[pltpu.SemaphoreType.DMA((5,))],
        flops=2 * rows * width * HEAD,
    )
    partner = lax.ppermute(given, "seq", swap)
    [within] = call(
        within_kernel, [shape((rows, width), F32)], [scalars, keys, values, query],
        flops=6 * rows * rows * width,
    )
    dense = routes.shape[1] == experts
    total, within = lax.optimization_barrier((add_rows(kept, partner), within))
    sign = jnp.zeros((8, HEAD), F32)
    if dense:
        weights_gate, sign = load_near(scalars, expert_in[0], 0, total)
    before = sum(
        came.astype(F32) * flags[2 + i:3 + i] for i, came in enumerate(prior_states(total))
    )
    mine = before + partner.astype(F32) * flags[:1]
    lacked = (before + kept.astype(F32) * flags[1:2]).astype(BF16)
    lacked, sign = lax.optimization_barrier((lacked, sign))
    other = lax.ppermute(lacked, "seq", swap)
    signs = [sign]
    if dense:
        weights_up, sign = load_near(scalars, expert_in[0], 1, lacked)
        signs.append(sign)
    pieces = call(
        functools.partial(attend_kernel, parts),
        [shape((count, width), BF16)] * parts,
        [scalars, within, query, rest, my_gain, mine, other, *signs],
        scratch=[pltpu.VMEM((rows, width), BF16)],
        flops=4 * rows * width * HEAD,
    )
    gathered = exchange(pieces)

    my_routes = lax.dynamic_slice_in_dim(routes, my_rows, count, 0)
    my_gates = lax.dynamic_slice_in_dim(route_gates, my_rows, count, 0)
    mixing = jnp.sum(
        jnp.where(
            my_routes[:, :, None] == jnp.arange(experts, dtype=jnp.int32),
            my_gates[:, :, None],
            0.0,
        ),
        axis=1,
    )
    high = lax.reduce_precision(mixing, 8, 7)
    lanes = -(-2 * experts // HEAD) * HEAD
    pack = jnp.pad(
        jnp.concatenate([high, mixing - high], axis=1), ((0, 0), (0, lanes - 2 * experts))
    ).astype(BF16)
    hidden = jnp.concatenate(turn_order(gathered, turns), axis=1)
    widened = hidden.astype(F32)
    normed = (
        widened
        * lax.rsqrt(jnp.mean(widened * widened, axis=-1, keepdims=True) + 1e-06)
        * norm_gain
    ).astype(BF16)
    if dense:
        block = jnp.concatenate([normed, pack], axis=1)
        terms = dense_experts(
            block, scalars, weights_gate, weights_up, expert_out
        )
    else:
        mixed = routed_experts(normed, my_routes, my_gates, expert_in, expert_out)
        terms = [mixed]
    own, *others = terms
    mixed = own.astype(F32) + sum(t.astype(F32) for t in others)
    ready = (hidden.astype(F32) + mixed).astype(BF16)
    columns = [ready[:, i * width:(i + 1) * width] for i in range(parts)]
    return jnp.concatenate(turn_order(exchange(turn_order(columns, turns)), turns))


def solution(mesh):
    placed = (
        P("seq", "exp"),
        P("seq", "exp"),
        P("seq", "exp"),
        P("seq", "exp"),
        P("exp"),
        P(),
        P("seq", None),
        P("seq", None),
        P("seq", None, None, None),
        P("seq", None, None),
    )
    return jax.shard_map(
        per_device, mesh=mesh, in_specs=placed, out_specs=P("seq", "exp"), check_vma=False
    )
```

```python
import functools

import jax
import jax.numpy as jnp
from jax import lax
from jax.experimental import pallas as pl
from jax.experimental.pallas import tpu as pltpu
from jax.sharding import PartitionSpec as P

HEAD = 128
F32 = jnp.float32
BF16 = jnp.bfloat16
WHOLE = pl.BlockSpec(memory_space=pltpu.VMEM)
FAR = pl.BlockSpec(memory_space=pltpu.HBM)
SCALAR = pl.BlockSpec(memory_space=pltpu.SMEM)


def call(kernel, outs, inputs, far=(), small=(), scratch=(), out_specs=None, flops=0, limit=16 << 20):
    moved = sum(a.size * a.dtype.itemsize for a in [*inputs, *outs])
    inputs = [
        pltpu.with_memory_space_constraint(a, pltpu.HBM) if i in far else a
        for i, a in enumerate(inputs)
    ]
    return pl.pallas_call(
        kernel,
        out_shape=outs,
        in_specs=[
            SCALAR if i == 0 or i in small else FAR if i in far else WHOLE
            for i in range(len(inputs))
        ],
        out_specs=out_specs or [WHOLE] * len(outs),
        scratch_shapes=scratch,
        compiler_params=pltpu.CompilerParams(vmem_limit_bytes=limit),
        cost_estimate=pl.CostEstimate(flops=flops, bytes_accessed=moved, transcendentals=0),
    )(*inputs)


def shape(dims, dtype):
    return jax.ShapeDtypeStruct(dims, dtype)


def split(value):
    high = value.astype(BF16)
    return high, (value - high.astype(F32)).astype(BF16)


def add_rows(*terms):
    return sum(t.astype(F32) for t in terms).astype(BF16)


def run_copies(pairs, sems):
    copies = [pltpu.make_async_copy(a, b, sems.at[i]) for i, (a, b) in enumerate(pairs)]
    for copy in copies:
        copy.start()
    for copy in copies:
        copy.wait()


def open_kernel(
    scalars, key_ref, value_ref, query_ref, residual_ref, gain_ref,
    kept_ref, given_ref, keys, values, query, residual, gain, flags_ref, sems
):
    pairs = [
        (key_ref, keys), (value_ref, values), (query_ref, query), (residual_ref, residual),
        (gain_ref, gain),
    ]
    copies = [pltpu.make_async_copy(a, b, sems.at[i]) for i, (a, b) in enumerate(pairs)]
    for copy in copies:
        copy.start()
    for i in range(flags_ref.shape[0]):
        value = 1 - scalars[1] if i == 1 else scalars[1 if i == 0 else 2 + i]
        flags_ref[i:i + 1, :] = jnp.full((1, flags_ref.shape[1]), value, jnp.int32).astype(F32)
    for copy in copies[:2]:
        copy.wait()
    width = keys.shape[1] // 2
    place = scalars[1]
    sides = []
    for side in range(2):
        cols = slice(side * width, (side + 1) * width)
        square = lax.dot_general(
            keys[:, cols], values[:, cols], (((0,), (0,)), ((), ())), preferred_element_type=F32
        )
        sides.append(
            jnp.concatenate(
                [square[h:h + HEAD, h:h + HEAD] for h in range(0, width, HEAD)], axis=1
            ).astype(BF16)
        )
    kept_ref[...] = jnp.where(place == 0, sides[0], sides[1])
    given_ref[...] = jnp.where(place == 0, sides[1], sides[0])
    for copy in copies[2:]:
        copy.wait()


def within_kernel(scalars, keys, values, queries, out_ref):
    rows, width = out_ref.shape
    causal = lax.broadcasted_iota(jnp.int32, (rows, rows), 0) >= lax.broadcasted_iota(
        jnp.int32, (rows, rows), 1
    )
    for start in range(0, width, HEAD):
        cols = slice(start, start + HEAD)
        scores = lax.dot_general(
            queries[:, cols], keys[:, cols], (((1,), (1,)), ((), ())), preferred_element_type=F32
        )
        high, low = split(jnp.where(causal, scores, 0.0))
        out_ref[:, cols] = jnp.dot(
            high, values[:, cols], preferred_element_type=F32
        ) + jnp.dot(low, values[:, cols], preferred_element_type=F32)


def attend_kernel(
    parts, scalars, within_ref, queries, residuals, gain_ref, mine_ref, other_ref, *refs
):
    piece_refs, hidden = refs[-1 - parts:-1], refs[-1]
    rows, full = hidden.shape
    width = full // 2
    first = scalars[1] == 0
    mine, other = mine_ref[...], other_ref[...].astype(F32)
    halves = [jnp.where(first, mine, other), jnp.where(first, other, mine)]
    for start in range(0, full, HEAD):
        cols = slice(start, start + HEAD)
        half, inner = divmod(start, width)
        high, low = split(halves[half][:, inner:inner + HEAD])
        raw = (
            jnp.dot(queries[:, cols], high, preferred_element_type=F32)
            + jnp.dot(queries[:, cols], low, preferred_element_type=F32)
            + within_ref[:, cols]
        )
        scaled = raw * lax.rsqrt(jnp.mean(raw * raw, axis=-1, keepdims=True) + 1e-06)
        hidden[:, cols] = (residuals[:, cols].astype(F32) + scaled * gain_ref[:, cols]).astype(BF16)
    count = rows // parts
    for j, piece in enumerate(piece_refs):
        piece[...] = hidden[pl.ds(pl.multiple_of((scalars[0] ^ j) * count, count), count), :]


def load_kernel(lead, scalars, source, after_ref, target, done_ref, sems):
    done_ref[...] = jnp.zeros_like(done_ref)
    pieces = sems.shape[0]
    step = target.shape[0] // pieces
    cuts = [pl.ds(i * step, step) for i in range(pieces)]
    run_copies([(source.at[lead, cut], target.at[cut]) for cut in cuts], sems)


def load_near(scalars, source, lead, after):
    return call(
        functools.partial(load_kernel, lead),
        [shape(source.shape[1:], source.dtype), shape((8, HEAD), F32)],
        [scalars, source, after], far=(1,), scratch=[pltpu.SemaphoreType.DMA((8,))],
    )


def expert_kernel(blocks, scalars, sign_ref, gate_ref, up_ref, down_ref, *refs):
    x_refs, out_refs, done_ref = refs[:blocks], refs[blocks:2 * blocks], refs[2 * blocks]
    rows_ref, act_ref, made_ref = refs[2 * blocks + 1:]
    done_ref[...] = jnp.zeros_like(done_ref)
    model, units = gate_ref.shape
    spans, packs = [], []
    first = 0
    for ref in x_refs:
        spans.append(slice(first, first + ref.shape[0]))
        rows_ref[spans[-1], :] = ref[:, :model]
        packs.append(ref[:, model:].astype(F32))
        first += ref.shape[0]
    spare = rows_ref.shape[0] - first
    if spare:
        rows_ref[first:, :] = jnp.zeros((spare, model), BF16)
        packs.append(jnp.zeros((spare, packs[0].shape[1]), F32))
    pack = jnp.concatenate(packs)
    lane = lax.broadcasted_iota(jnp.int32, pack.shape, 1)
    chosen = (lane == scalars[3]) | (lane == scalars[3] + scalars[2])
    weight = jnp.sum(jnp.where(chosen, pack, 0.0), axis=-1, keepdims=True)
    chunk = min(units, 512)

    for step in range(units // chunk):
        cut = slice(step * chunk, (step + 1) * chunk)
        gate = jnp.dot(rows_ref[...], gate_ref[:, cut], preferred_element_type=F32)
        up = jnp.dot(rows_ref[...], up_ref[:, cut], preferred_element_type=F32)
        act_ref[:, cut] = (gate / (1.0 + jnp.exp(-gate)) * up).astype(BF16)

    wide = min(model, 1024)

    for step in range(model // wide):
        cut = slice(step * wide, (step + 1) * wide)
        produced = jnp.dot(act_ref[...], down_ref[:, cut], preferred_element_type=F32)
        made_ref[:, cut] = (produced.astype(BF16).astype(F32) * weight).astype(BF16)

    for out_ref, span in zip(out_refs, spans):
        out_ref[...] = made_ref[span, :]


def run_expert(scalars, sign, blocks, weights_gate, weights_up, weights_out):
    units, model = weights_out.shape
    total = max(HEAD, sum(b.shape[0] for b in blocks))
    *made, sign = call(
        functools.partial(expert_kernel, len(blocks)),
        [shape((b.shape[0], model), BF16) for b in blocks] + [shape((8, HEAD), F32)],
        [scalars, sign, weights_gate, weights_up, weights_out, *blocks],
        scratch=[
            pltpu.VMEM((total, model), BF16),
            pltpu.VMEM((total, units), BF16),
            pltpu.VMEM((total, model), BF16),
        ],
        flops=6 * total * model * units,
        limit=24 << 20,
    )
    return made, sign


def ring_order(count):
    return list(range(0, count, 2)) + list(range(1, count, 2))[::-1]


def dense_experts(block, scalars, weights_gate, weights_up, expert_out):
    count = lax.axis_size("seq")
    order = ring_order(count)
    far = count // 2

    def hop(rows, steps):
        return lax.ppermute(
            rows, "seq", [(order[p], order[(p + steps) % count]) for p in range(count)]
        )

    ahead, behind = [block], [block]
    farthest = hop(block, far)
    for distance in range(1, far - 1):
        came, went = hop(ahead[-1], 1), hop(behind[-1], -1)
        if distance == far - 2:
            weights_out, sign = load_near(scalars, expert_out, 0, ahead[-1])
            came, went, sign = lax.optimization_barrier((came, went, sign))
        ahead.append(came)
        behind.append(went)
    last = hop(ahead[-1], 1), hop(behind[-1], -1)
    weights = weights_gate, weights_up, weights_out
    (own, *near), sign = run_expert(scalars, sign, ahead + behind[1:], *weights)
    *last, farthest, sign = lax.optimization_barrier((*last, farthest, sign))
    (back, front, farthest), _ = run_expert(scalars, sign, [*last, farthest], *weights)
    to_back, to_front = near[:far - 2] + [back], near[far - 2:] + [front]
    going, coming = hop(to_front[-1], 1), hop(to_back[-1], -1)
    straight = hop(farthest, far)
    for distance in range(far - 2, -1, -1):
        if distance == 0:
            return own, going, coming, straight
        going = hop(add_rows(going, to_front[distance - 1]), 1)
        coming = hop(add_rows(coming, to_back[distance - 1]), -1)


def slot_ids(block_routes, expert_count, capacity):
    row_count, top_count = block_routes.shape
    expert_ids = jnp.arange(expert_count, dtype=jnp.int32)
    onehot = (
        (block_routes[:, :, None] == expert_ids[None, None, :])
        .astype(jnp.int32)
        .reshape(row_count * top_count, expert_count)
    )
    earlier = jnp.cumsum(onehot, axis=0) - onehot
    ranking = jnp.sum(earlier * onehot, axis=1).reshape(row_count, top_count)
    return block_routes * capacity + ranking


def routed_experts(normed, my_routes, my_gates, expert_in, expert_out):
    sub_count, model_width = normed.shape
    expert_count = lax.axis_size("seq") * expert_in.shape[0]
    top_count = my_routes.shape[1]
    capacity = min(sub_count, max(2, 3 * sub_count * top_count // (2 * expert_count)))
    slot_count = expert_count * capacity
    my_slots = slot_ids(my_routes, expert_count, capacity)
    columns = jnp.arange(slot_count, dtype=jnp.int32)
    placer = jnp.sum(
        (my_slots[None, :, :] == columns[:, None, None]).astype(jnp.int32), axis=2
    ).astype(BF16)
    outgoing = (
        jnp.dot(placer, normed, preferred_element_type=F32)
        .astype(BF16)
        .reshape(expert_count, capacity, model_width)
    )
    arrived = lax.all_to_all(outgoing, "seq", split_axis=0, concat_axis=0, tiled=True)
    flat_rows = arrived.reshape(-1, model_width)
    gate_up = jnp.einsum("nd,gdf->gnf", flat_rows, expert_in[0], preferred_element_type=F32)
    activated = (jax.nn.silu(gate_up[0]) * gate_up[1]).astype(BF16)
    produced = jnp.dot(activated, expert_out[0], preferred_element_type=F32).astype(BF16)
    answered = produced.reshape(arrived.shape)
    returned = lax.all_to_all(answered, "seq", split_axis=0, concat_axis=0, tiled=True)
    picked = returned.reshape(slot_count, model_width)[my_slots.reshape(-1)].reshape(
        sub_count, top_count, model_width
    )
    return jnp.sum(picked.astype(F32) * my_gates[:, :, None], axis=1)


def swap_pairs(rows, distance):
    count = lax.axis_size("seq")
    return lax.ppermute(rows, "seq", [(i, i ^ (2 * distance)) for i in range(count)])


def pair_steps(pairs):
    bits = pairs.bit_length() - 1
    direct = pairs <= 4
    steps = range(pairs - 1, 0, -1) if direct else [1 << b for b in range(bits)]
    return direct, [(d, d.bit_length() - 1) for d in steps]


def prior_states(total):
    count = lax.axis_size("seq")
    direct, steps = pair_steps(count // 2)
    terms = []
    for distance, _ in steps:
        terms.append(
            lax.ppermute(total, "seq", [(i, i ^ (2 * distance)) for i in range(count)])
        )
        if not direct:
            total = add_rows(total, terms[-1])
    return terms


def exchange(pieces):
    parts = len(pieces)
    return [pieces[0]] + [
        lax.ppermute(pieces[j], "exp", [(i, i ^ j) for i in range(parts)])
        for j in range(1, parts)
    ]


def turn_order(items, turns):
    for b, turn in enumerate(turns):
        items = [jnp.where(turn, items[i ^ (1 << b)], items[i]) for i in range(len(items))]
    return items


def per_device(
    residual,
    queries,
    key_vectors,
    value_vectors,
    head_gain,
    norm_gain,
    routes,
    route_gates,
    expert_in,
    expert_out,
):
    rows, width = residual.shape
    seq, parts = lax.axis_size("seq"), lax.axis_size("exp")
    count, half, model = rows // parts, width // 2, width * parts
    experts = seq * expert_in.shape[0]
    position = lax.axis_index("seq")
    my_index = lax.axis_index("exp")
    place = position % 2
    _, steps = pair_steps(seq // 2)
    scalars = jnp.stack(
        [my_index, place, experts, position] + [(position >> (bit + 1)) & 1 for _, bit in steps]
    ).astype(jnp.int32)
    swap = [(i, i ^ 1) for i in range(seq)]
    turns = [
        ((my_index >> b) & 1 != 0).reshape(1, 1) for b in range(parts.bit_length() - 1)
    ]
    my_rows = (my_index * count).astype(jnp.uint32)
    scalars, turns, my_rows = lax.optimization_barrier((scalars, turns, my_rows))
    state, heads = shape((HEAD, half), BF16), shape((rows, width), BF16)
    kept, given, keys, values, query, rest, my_gain, flags = call(
        open_kernel,
        [state] * 2 + [heads] * 4
        + [shape((1, width), F32), shape((2 + len(steps), half), F32)],
        [scalars, key_vectors, value_vectors, queries, residual, head_gain[None, :]],
        far=(1, 2, 3, 4, 5),
        scratch=[pltpu.SemaphoreType.DMA((5,))],
        flops=2 * rows * width * HEAD,
    )
    partner = lax.ppermute(given, "seq", swap)
    [within] = call(
        within_kernel, [shape((rows, width), F32)], [scalars, keys, values, query],
        flops=6 * rows * rows * width,
    )
    dense = routes.shape[1] == experts
    total, within = lax.optimization_barrier((add_rows(kept, partner), within))
    sign = jnp.zeros((8, HEAD), F32)
    if dense:
        weights_gate, sign = load_near(scalars, expert_in[0], 0, total)
    before = sum(
        came.astype(F32) * flags[2 + i:3 + i] for i, came in enumerate(prior_states(total))
    )
    mine = before + partner.astype(F32) * flags[:1]
    lacked = (before + kept.astype(F32) * flags[1:2]).astype(BF16)
    lacked, sign = lax.optimization_barrier((lacked, sign))
    other = lax.ppermute(lacked, "seq", swap)
    signs = [sign]
    if dense:
        weights_up, sign = load_near(scalars, expert_in[0], 1, lacked)
        signs.append(sign)
    pieces = call(
        functools.partial(attend_kernel, parts),
        [shape((count, width), BF16)] * parts,
        [scalars, within, query, rest, my_gain, mine, other, *signs],
        scratch=[pltpu.VMEM((rows, width), BF16)],
        flops=4 * rows * width * HEAD,
    )
    gathered = exchange(pieces)

    my_routes = lax.dynamic_slice_in_dim(routes, my_rows, count, 0)
    my_gates = lax.dynamic_slice_in_dim(route_gates, my_rows, count, 0)
    mixing = jnp.sum(
        jnp.where(
            my_routes[:, :, None] == jnp.arange(experts, dtype=jnp.int32),
            my_gates[:, :, None],
            0.0,
        ),
        axis=1,
    )
    high = lax.reduce_precision(mixing, 8, 7)
    lanes = -(-2 * experts // HEAD) * HEAD
    pack = jnp.pad(
        jnp.concatenate([high, mixing - high], axis=1), ((0, 0), (0, lanes - 2 * experts))
    ).astype(BF16)
    hidden = jnp.concatenate(turn_order(gathered, turns), axis=1)
    widened = hidden.astype(F32)
    normed = (
        widened
        * lax.rsqrt(jnp.mean(widened * widened, axis=-1, keepdims=True) + 1e-06)
        * norm_gain
    ).astype(BF16)
    if dense:
        block = jnp.concatenate([normed, pack], axis=1)
        terms = dense_experts(
            block, scalars, weights_gate, weights_up, expert_out
        )
    else:
        mixed = routed_experts(normed, my_routes, my_gates, expert_in, expert_out)
        terms = [mixed]
    own, *others = terms
    mixed = own.astype(F32) + sum(t.astype(F32) for t in others)
    ready = (hidden.astype(F32) + mixed).astype(BF16)
    columns = [ready[:, i * width:(i + 1) * width] for i in range(parts)]
    return jnp.concatenate(turn_order(exchange(turn_order(columns, turns)), turns))


def solution(mesh):
    placed = (
        P("seq", "exp"),
        P("seq", "exp"),
        P("seq", "exp"),
        P("seq", "exp"),
        P("exp"),
        P(),
        P("seq", None),
        P("seq", None),
        P("seq", None, None, None),
        P("seq", None, None),
    )
    return jax.shard_map(
        per_device, mesh=mesh, in_specs=placed, out_specs=P("seq", "exp"), check_vma=False
    )
```

```python
import functools

import jax
import jax.numpy as jnp
from jax import lax
from jax.experimental import pallas as pl
from jax.experimental.pallas import tpu as pltpu
from jax.sharding import PartitionSpec as P

HEAD = 128
F32 = jnp.float32
BF16 = jnp.bfloat16
WHOLE = pl.BlockSpec(memory_space=pltpu.VMEM)
FAR = pl.BlockSpec(memory_space=pltpu.HBM)
SCALAR = pl.BlockSpec(memory_space=pltpu.SMEM)


def call(kernel, outs, inputs, far=(), small=(), scratch=(), out_specs=None, flops=0, limit=16 << 20):
    moved = sum(a.size * a.dtype.itemsize for a in [*inputs, *outs])
    inputs = [
        pltpu.with_memory_space_constraint(a, pltpu.HBM) if i in far else a
        for i, a in enumerate(inputs)
    ]
    return pl.pallas_call(
        kernel,
        out_shape=outs,
        in_specs=[
            SCALAR if i == 0 or i in small else FAR if i in far else WHOLE
            for i in range(len(inputs))
        ],
        out_specs=out_specs or [WHOLE] * len(outs),
        scratch_shapes=scratch,
        compiler_params=pltpu.CompilerParams(vmem_limit_bytes=limit),
        cost_estimate=pl.CostEstimate(flops=flops, bytes_accessed=moved, transcendentals=0),
    )(*inputs)


def shape(dims, dtype):
    return jax.ShapeDtypeStruct(dims, dtype)


def split(value):
    high = value.astype(BF16)
    return high, (value - high.astype(F32)).astype(BF16)


def add_rows(*terms):
    return sum(t.astype(F32) for t in terms).astype(BF16)


def run_copies(pairs, sems):
    copies = [pltpu.make_async_copy(a, b, sems.at[i]) for i, (a, b) in enumerate(pairs)]
    for copy in copies:
        copy.start()
    for copy in copies:
        copy.wait()


def open_kernel(
    scalars, key_ref, value_ref, query_ref, residual_ref, gain_ref,
    kept_ref, given_ref, keys, values, query, residual, gain, flags_ref, sems
):
    pairs = [
        (key_ref, keys), (value_ref, values), (query_ref, query), (residual_ref, residual),
        (gain_ref, gain),
    ]
    copies = [pltpu.make_async_copy(a, b, sems.at[i]) for i, (a, b) in enumerate(pairs)]
    for copy in copies:
        copy.start()
    for i in range(flags_ref.shape[0]):
        value = 1 - scalars[1] if i == 1 else scalars[1 if i == 0 else 2 + i]
        flags_ref[i:i + 1, :] = jnp.full((1, flags_ref.shape[1]), value, jnp.int32).astype(F32)
    for copy in copies[:2]:
        copy.wait()
    width = keys.shape[1] // 2
    place = scalars[1]
    sides = []
    for side in range(2):
        cols = slice(side * width, (side + 1) * width)
        square = lax.dot_general(
            keys[:, cols], values[:, cols], (((0,), (0,)), ((), ())), preferred_element_type=F32
        )
        sides.append(
            jnp.concatenate(
                [square[h:h + HEAD, h:h + HEAD] for h in range(0, width, HEAD)], axis=1
            ).astype(BF16)
        )
    kept_ref[...] = jnp.where(place == 0, sides[0], sides[1])
    given_ref[...] = jnp.where(place == 0, sides[1], sides[0])
    for copy in copies[2:]:
        copy.wait()


def within_kernel(scalars, keys, values, queries, out_ref):
    rows, width = out_ref.shape
    causal = lax.broadcasted_iota(jnp.int32, (rows, rows), 0) >= lax.broadcasted_iota(
        jnp.int32, (rows, rows), 1
    )
    for start in range(0, width, HEAD):
        cols = slice(start, start + HEAD)
        scores = lax.dot_general(
            queries[:, cols], keys[:, cols], (((1,), (1,)), ((), ())), preferred_element_type=F32
        )
        high, low = split(jnp.where(causal, scores, 0.0))
        out_ref[:, cols] = jnp.dot(
            high, values[:, cols], preferred_element_type=F32
        ) + jnp.dot(low, values[:, cols], preferred_element_type=F32)


def attend_kernel(
    parts, scalars, within_ref, queries, residuals, gain_ref, mine_ref, other_ref, *refs
):
    piece_refs, hidden = refs[-1 - parts:-1], refs[-1]
    rows, full = hidden.shape
    width = full // 2
    first = scalars[1] == 0
    mine, other = mine_ref[...], other_ref[...].astype(F32)
    halves = [jnp.where(first, mine, other), jnp.where(first, other, mine)]
    for start in range(0, full, HEAD):
        cols = slice(start, start + HEAD)
        half, inner = divmod(start, width)
        high, low = split(halves[half][:, inner:inner + HEAD])
        raw = (
            jnp.dot(queries[:, cols], high, preferred_element_type=F32)
            + jnp.dot(queries[:, cols], low, preferred_element_type=F32)
            + within_ref[:, cols]
        )
        scaled = raw * lax.rsqrt(jnp.mean(raw * raw, axis=-1, keepdims=True) + 1e-06)
        hidden[:, cols] = (residuals[:, cols].astype(F32) + scaled * gain_ref[:, cols]).astype(BF16)
    count = rows // parts
    for j, piece in enumerate(piece_refs):
        piece[...] = hidden[pl.ds(pl.multiple_of((scalars[0] ^ j) * count, count), count), :]


def load_kernel(lead, scalars, source, after_ref, target, done_ref, sems):
    done_ref[...] = jnp.zeros_like(done_ref)
    pieces = sems.shape[0]
    step = target.shape[0] // pieces
    cuts = [pl.ds(i * step, step) for i in range(pieces)]
    run_copies([(source.at[lead, cut], target.at[cut]) for cut in cuts], sems)


def load_near(scalars, source, lead, after):
    return call(
        functools.partial(load_kernel, lead),
        [shape(source.shape[1:], source.dtype), shape((8, HEAD), F32)],
        [scalars, source, after], far=(1,), scratch=[pltpu.SemaphoreType.DMA((8,))],
    )


def expert_kernel(blocks, scalars, sign_ref, gate_ref, up_ref, down_ref, *refs):
    x_refs, out_refs, done_ref = refs[:blocks], refs[blocks:2 * blocks], refs[2 * blocks]
    rows_ref, act_ref, made_ref = refs[2 * blocks + 1:]
    done_ref[...] = jnp.zeros_like(done_ref)
    model, units = gate_ref.shape
    spans, packs = [], []
    first = 0
    for ref in x_refs:
        spans.append(slice(first, first + ref.shape[0]))
        rows_ref[spans[-1], :] = ref[:, :model]
        packs.append(ref[:, model:].astype(F32))
        first += ref.shape[0]
    spare = rows_ref.shape[0] - first
    if spare:
        rows_ref[first:, :] = jnp.zeros((spare, model), BF16)
        packs.append(jnp.zeros((spare, packs[0].shape[1]), F32))
    pack = jnp.concatenate(packs)
    lane = lax.broadcasted_iota(jnp.int32, pack.shape, 1)
    chosen = (lane == scalars[3]) | (lane == scalars[3] + scalars[2])
    weight = jnp.sum(jnp.where(chosen, pack, 0.0), axis=-1, keepdims=True)
    chunk = min(units, 512)

    for step in range(units // chunk):
        cut = slice(step * chunk, (step + 1) * chunk)
        gate = jnp.dot(rows_ref[...], gate_ref[:, cut], preferred_element_type=F32)
        up = jnp.dot(rows_ref[...], up_ref[:, cut], preferred_element_type=F32)
        act_ref[:, cut] = (gate / (1.0 + jnp.exp(-gate)) * up).astype(BF16)

    wide = min(model, 1024)

    for step in range(model // wide):
        cut = slice(step * wide, (step + 1) * wide)
        produced = jnp.dot(act_ref[...], down_ref[:, cut], preferred_element_type=F32)
        made_ref[:, cut] = (produced.astype(BF16).astype(F32) * weight).astype(BF16)

    for out_ref, span in zip(out_refs, spans):
        out_ref[...] = made_ref[span, :]


def run_expert(scalars, sign, blocks, weights_gate, weights_up, weights_out):
    units, model = weights_out.shape
    total = max(HEAD, sum(b.shape[0] for b in blocks))
    *made, sign = call(
        functools.partial(expert_kernel, len(blocks)),
        [shape((b.shape[0], model), BF16) for b in blocks] + [shape((8, HEAD), F32)],
        [scalars, sign, weights_gate, weights_up, weights_out, *blocks],
        scratch=[
            pltpu.VMEM((total, model), BF16),
            pltpu.VMEM((total, units), BF16),
            pltpu.VMEM((total, model), BF16),
        ],
        flops=6 * total * model * units,
        limit=24 << 20,
    )
    return made, sign


def ring_order(count):
    return list(range(0, count, 2)) + list(range(1, count, 2))[::-1]


def dense_experts(block, scalars, turns, weights_gate, weights_up, expert_out):
    count, parts = lax.axis_size("seq"), lax.axis_size("exp")
    order = ring_order(count)
    far = count // 2

    def hop(rows, steps):
        return lax.ppermute(
            rows, "seq", [(order[p], order[(p + steps) % count]) for p in range(count)]
        )

    def far_hop(rows):
        pairs = []
        for p in range(count):
            for e in range(parts):
                target = order[(p + (2 if e % 2 == 0 else -2)) % count]
                pairs.append((order[p] * parts + e, target * parts + e))
        return lax.ppermute(rows, ("seq", "exp"), pairs)

    ahead, behind = [block], [block]
    for distance in range(1, far - 1):
        came, went = hop(ahead[-1], 1), hop(behind[-1], -1)
        if distance == far - 2:
            weights_out, sign = load_near(scalars, expert_out, 0, ahead[-1])
            came, went, sign = lax.optimization_barrier((came, went, sign))
        ahead.append(came)
        behind.append(went)
    last = hop(ahead[-1], 1), hop(behind[-1], -1)
    farthest = far_hop(jnp.where(turns[0], behind[-1], ahead[-1]))
    weights = weights_gate, weights_up, weights_out
    (own, *near), sign = run_expert(scalars, sign, ahead + behind[1:], *weights)
    *last, farthest, sign = lax.optimization_barrier((*last, farthest, sign))
    (back, front, farthest), _ = run_expert(scalars, sign, [*last, farthest], *weights)
    to_back, to_front = near[:far - 2] + [back], near[far - 2:] + [front]
    going, coming = hop(to_front[-1], 1), hop(to_back[-1], -1)
    straight = hop(farthest, far)
    for distance in range(far - 2, -1, -1):
        if distance == 0:
            return own, going, coming, straight
        going = hop(add_rows(going, to_front[distance - 1]), 1)
        coming = hop(add_rows(coming, to_back[distance - 1]), -1)


def slot_ids(block_routes, expert_count, capacity):
    row_count, top_count = block_routes.shape
    expert_ids = jnp.arange(expert_count, dtype=jnp.int32)
    onehot = (
        (block_routes[:, :, None] == expert_ids[None, None, :])
        .astype(jnp.int32)
        .reshape(row_count * top_count, expert_count)
    )
    earlier = jnp.cumsum(onehot, axis=0) - onehot
    ranking = jnp.sum(earlier * onehot, axis=1).reshape(row_count, top_count)
    return block_routes * capacity + ranking


def routed_experts(normed, my_routes, my_gates, expert_in, expert_out):
    sub_count, model_width = normed.shape
    expert_count = lax.axis_size("seq") * expert_in.shape[0]
    top_count = my_routes.shape[1]
    capacity = min(sub_count, max(2, 3 * sub_count * top_count // (2 * expert_count)))
    slot_count = expert_count * capacity
    my_slots = slot_ids(my_routes, expert_count, capacity)
    columns = jnp.arange(slot_count, dtype=jnp.int32)
    placer = jnp.sum(
        (my_slots[None, :, :] == columns[:, None, None]).astype(jnp.int32), axis=2
    ).astype(BF16)
    outgoing = (
        jnp.dot(placer, normed, preferred_element_type=F32)
        .astype(BF16)
        .reshape(expert_count, capacity, model_width)
    )
    arrived = lax.all_to_all(outgoing, "seq", split_axis=0, concat_axis=0, tiled=True)
    flat_rows = arrived.reshape(-1, model_width)
    gate_up = jnp.einsum("nd,gdf->gnf", flat_rows, expert_in[0], preferred_element_type=F32)
    activated = (jax.nn.silu(gate_up[0]) * gate_up[1]).astype(BF16)
    produced = jnp.dot(activated, expert_out[0], preferred_element_type=F32).astype(BF16)
    answered = produced.reshape(arrived.shape)
    returned = lax.all_to_all(answered, "seq", split_axis=0, concat_axis=0, tiled=True)
    picked = returned.reshape(slot_count, model_width)[my_slots.reshape(-1)].reshape(
        sub_count, top_count, model_width
    )
    return jnp.sum(picked.astype(F32) * my_gates[:, :, None], axis=1)


def swap_pairs(rows, distance):
    count = lax.axis_size("seq")
    return lax.ppermute(rows, "seq", [(i, i ^ (2 * distance)) for i in range(count)])


def pair_steps(pairs):
    bits = pairs.bit_length() - 1
    direct = pairs <= 4
    steps = range(pairs - 1, 0, -1) if direct else [1 << b for b in range(bits)]
    return direct, [(d, d.bit_length() - 1) for d in steps]


def prior_states(total):
    count = lax.axis_size("seq")
    direct, steps = pair_steps(count // 2)
    terms = []
    for distance, _ in steps:
        terms.append(
            lax.ppermute(total, "seq", [(i, i ^ (2 * distance)) for i in range(count)])
        )
        if not direct:
            total = add_rows(total, terms[-1])
    return terms


def exchange(pieces):
    parts = len(pieces)
    return [pieces[0]] + [
        lax.ppermute(pieces[j], "exp", [(i, i ^ j) for i in range(parts)])
        for j in range(1, parts)
    ]


def turn_order(items, turns):
    for b, turn in enumerate(turns):
        items = [jnp.where(turn, items[i ^ (1 << b)], items[i]) for i in range(len(items))]
    return items


def per_device(
    residual,
    queries,
    key_vectors,
    value_vectors,
    head_gain,
    norm_gain,
    routes,
    route_gates,
    expert_in,
    expert_out,
):
    rows, width = residual.shape
    seq, parts = lax.axis_size("seq"), lax.axis_size("exp")
    count, half, model = rows // parts, width // 2, width * parts
    experts = seq * expert_in.shape[0]
    position = lax.axis_index("seq")
    my_index = lax.axis_index("exp")
    place = position % 2
    _, steps = pair_steps(seq // 2)
    scalars = jnp.stack(
        [my_index, place, experts, position] + [(position >> (bit + 1)) & 1 for _, bit in steps]
    ).astype(jnp.int32)
    swap = [(i, i ^ 1) for i in range(seq)]
    turns = [
        ((my_index >> b) & 1 != 0).reshape(1, 1) for b in range(parts.bit_length() - 1)
    ]
    my_rows = (my_index * count).astype(jnp.uint32)
    scalars, turns, my_rows = lax.optimization_barrier((scalars, turns, my_rows))
    state, heads = shape((HEAD, half), BF16), shape((rows, width), BF16)
    kept, given, keys, values, query, rest, my_gain, flags = call(
        open_kernel,
        [state] * 2 + [heads] * 4
        + [shape((1, width), F32), shape((2 + len(steps), half), F32)],
        [scalars, key_vectors, value_vectors, queries, residual, head_gain[None, :]],
        far=(1, 2, 3, 4, 5),
        scratch=[pltpu.SemaphoreType.DMA((5,))],
        flops=2 * rows * width * HEAD,
    )
    partner = lax.ppermute(given, "seq", swap)
    [within] = call(
        within_kernel, [shape((rows, width), F32)], [scalars, keys, values, query],
        flops=6 * rows * rows * width,
    )
    dense = routes.shape[1] == experts
    total, within = lax.optimization_barrier((add_rows(kept, partner), within))
    sign = jnp.zeros((8, HEAD), F32)
    if dense:
        weights_gate, sign = load_near(scalars, expert_in[0], 0, total)
    before = sum(
        came.astype(F32) * flags[2 + i:3 + i] for i, came in enumerate(prior_states(total))
    )
    mine = before + partner.astype(F32) * flags[:1]
    lacked = (before + kept.astype(F32) * flags[1:2]).astype(BF16)
    lacked, sign = lax.optimization_barrier((lacked, sign))
    other = lax.ppermute(lacked, "seq", swap)
    signs = [sign]
    if dense:
        weights_up, sign = load_near(scalars, expert_in[0], 1, lacked)
        signs.append(sign)
    pieces = call(
        functools.partial(attend_kernel, parts),
        [shape((count, width), BF16)] * parts,
        [scalars, within, query, rest, my_gain, mine, other, *signs],
        scratch=[pltpu.VMEM((rows, width), BF16)],
        flops=4 * rows * width * HEAD,
    )
    gathered = exchange(pieces)

    my_routes = lax.dynamic_slice_in_dim(routes, my_rows, count, 0)
    my_gates = lax.dynamic_slice_in_dim(route_gates, my_rows, count, 0)
    mixing = jnp.sum(
        jnp.where(
            my_routes[:, :, None] == jnp.arange(experts, dtype=jnp.int32),
            my_gates[:, :, None],
            0.0,
        ),
        axis=1,
    )
    high = lax.reduce_precision(mixing, 8, 7)
    lanes = -(-2 * experts // HEAD) * HEAD
    pack = jnp.pad(
        jnp.concatenate([high, mixing - high], axis=1), ((0, 0), (0, lanes - 2 * experts))
    ).astype(BF16)
    hidden = jnp.concatenate(turn_order(gathered, turns), axis=1)
    widened = hidden.astype(F32)
    normed = (
        widened
        * lax.rsqrt(jnp.mean(widened * widened, axis=-1, keepdims=True) + 1e-06)
        * norm_gain
    ).astype(BF16)
    if dense:
        block = jnp.concatenate([normed, pack], axis=1)
        terms = dense_experts(
            block, scalars, turns, weights_gate, weights_up, expert_out
        )
    else:
        mixed = routed_experts(normed, my_routes, my_gates, expert_in, expert_out)
        terms = [mixed]
    own, *others = terms
    mixed = own.astype(F32) + sum(t.astype(F32) for t in others)
    ready = (hidden.astype(F32) + mixed).astype(BF16)
    columns = [ready[:, i * width:(i + 1) * width] for i in range(parts)]
    return jnp.concatenate(turn_order(exchange(turn_order(columns, turns)), turns))


def solution(mesh):
    placed = (
        P("seq", "exp"),
        P("seq", "exp"),
        P("seq", "exp"),
        P("seq", "exp"),
        P("exp"),
        P(),
        P("seq", None),
        P("seq", None),
        P("seq", None, None, None),
        P("seq", None, None),
    )
    return jax.shard_map(
        per_device, mesh=mesh, in_specs=placed, out_specs=P("seq", "exp"), check_vma=False
    )
```

```python
import functools

import jax
import jax.numpy as jnp
from jax import lax
from jax.experimental import pallas as pl
from jax.experimental.pallas import tpu as pltpu
from jax.sharding import PartitionSpec as P

HEAD = 128
F32 = jnp.float32
BF16 = jnp.bfloat16
WHOLE = pl.BlockSpec(memory_space=pltpu.VMEM)
FAR = pl.BlockSpec(memory_space=pltpu.HBM)
SCALAR = pl.BlockSpec(memory_space=pltpu.SMEM)


def call(kernel, outs, inputs, far=(), small=(), scratch=(), out_specs=None, flops=0, limit=16 << 20):
    moved = sum(a.size * a.dtype.itemsize for a in [*inputs, *outs])
    inputs = [
        pltpu.with_memory_space_constraint(a, pltpu.HBM) if i in far else a
        for i, a in enumerate(inputs)
    ]
    return pl.pallas_call(
        kernel,
        out_shape=outs,
        in_specs=[
            SCALAR if i == 0 or i in small else FAR if i in far else WHOLE
            for i in range(len(inputs))
        ],
        out_specs=out_specs or [WHOLE] * len(outs),
        scratch_shapes=scratch,
        compiler_params=pltpu.CompilerParams(vmem_limit_bytes=limit),
        cost_estimate=pl.CostEstimate(flops=flops, bytes_accessed=moved, transcendentals=0),
    )(*inputs)


def shape(dims, dtype):
    return jax.ShapeDtypeStruct(dims, dtype)


def split(value):
    high = value.astype(BF16)
    return high, (value - high.astype(F32)).astype(BF16)


def add_rows(*terms):
    return sum(t.astype(F32) for t in terms).astype(BF16)


def run_copies(pairs, sems):
    copies = [pltpu.make_async_copy(a, b, sems.at[i]) for i, (a, b) in enumerate(pairs)]
    for copy in copies:
        copy.start()
    for copy in copies:
        copy.wait()


def open_kernel(
    scalars, key_ref, value_ref, query_ref, residual_ref, gain_ref,
    kept_ref, given_ref, keys, values, query, residual, gain, flags_ref, sems
):
    pairs = [
        (key_ref, keys), (value_ref, values), (query_ref, query), (residual_ref, residual),
        (gain_ref, gain),
    ]
    copies = [pltpu.make_async_copy(a, b, sems.at[i]) for i, (a, b) in enumerate(pairs)]
    for copy in copies:
        copy.start()
    for i in range(flags_ref.shape[0]):
        value = 1 - scalars[1] if i == 1 else scalars[1 if i == 0 else 2 + i]
        flags_ref[i:i + 1, :] = jnp.full((1, flags_ref.shape[1]), value, jnp.int32).astype(F32)
    for copy in copies[:2]:
        copy.wait()
    width = keys.shape[1] // 2
    place = scalars[1]
    sides = []
    for side in range(2):
        cols = slice(side * width, (side + 1) * width)
        square = lax.dot_general(
            keys[:, cols], values[:, cols], (((0,), (0,)), ((), ())), preferred_element_type=F32
        )
        sides.append(
            jnp.concatenate(
                [square[h:h + HEAD, h:h + HEAD] for h in range(0, width, HEAD)], axis=1
            ).astype(BF16)
        )
    kept_ref[...] = jnp.where(place == 0, sides[0], sides[1])
    given_ref[...] = jnp.where(place == 0, sides[1], sides[0])
    for copy in copies[2:]:
        copy.wait()


def within_kernel(scalars, keys, values, queries, out_ref):
    rows, width = out_ref.shape
    causal = lax.broadcasted_iota(jnp.int32, (rows, rows), 0) >= lax.broadcasted_iota(
        jnp.int32, (rows, rows), 1
    )
    for start in range(0, width, HEAD):
        cols = slice(start, start + HEAD)
        scores = lax.dot_general(
            queries[:, cols], keys[:, cols], (((1,), (1,)), ((), ())), preferred_element_type=F32
        )
        high, low = split(jnp.where(causal, scores, 0.0))
        out_ref[:, cols] = jnp.dot(
            high, values[:, cols], preferred_element_type=F32
        ) + jnp.dot(low, values[:, cols], preferred_element_type=F32)


def attend_kernel(
    parts, scalars, within_ref, queries, residuals, gain_ref, mine_ref, other_ref, *refs
):
    piece_refs, hidden = refs[-1 - parts:-1], refs[-1]
    rows, full = hidden.shape
    width = full // 2
    first = scalars[1] == 0
    mine, other = mine_ref[...], other_ref[...].astype(F32)
    halves = [jnp.where(first, mine, other), jnp.where(first, other, mine)]
    for start in range(0, full, HEAD):
        cols = slice(start, start + HEAD)
        half, inner = divmod(start, width)
        high, low = split(halves[half][:, inner:inner + HEAD])
        raw = (
            jnp.dot(queries[:, cols], high, preferred_element_type=F32)
            + jnp.dot(queries[:, cols], low, preferred_element_type=F32)
            + within_ref[:, cols]
        )
        scaled = raw * lax.rsqrt(jnp.mean(raw * raw, axis=-1, keepdims=True) + 1e-06)
        hidden[:, cols] = (residuals[:, cols].astype(F32) + scaled * gain_ref[:, cols]).astype(BF16)
    count = rows // parts
    for j, piece in enumerate(piece_refs):
        piece[...] = hidden[pl.ds(pl.multiple_of((scalars[0] ^ j) * count, count), count), :]


def load_kernel(lead, scalars, source, after_ref, target, done_ref, sems):
    done_ref[...] = jnp.zeros_like(done_ref)
    pieces = sems.shape[0]
    step = target.shape[0] // pieces
    cuts = [pl.ds(i * step, step) for i in range(pieces)]
    run_copies([(source.at[lead, cut], target.at[cut]) for cut in cuts], sems)


def load_near(scalars, source, lead, after):
    return call(
        functools.partial(load_kernel, lead),
        [shape(source.shape[1:], source.dtype), shape((8, HEAD), F32)],
        [scalars, source, after], far=(1,), scratch=[pltpu.SemaphoreType.DMA((8,))],
    )


def expert_kernel(blocks, scalars, sign_ref, gate_ref, up_ref, down_ref, *refs):
    x_refs, out_refs, done_ref = refs[:blocks], refs[blocks:2 * blocks], refs[2 * blocks]
    rows_ref, act_ref = refs[2 * blocks + 1:]
    done_ref[...] = jnp.zeros_like(done_ref)
    model, units = gate_ref.shape
    spans, packs = [], []
    first = 0
    for ref in x_refs:
        spans.append(slice(first, first + ref.shape[0]))
        rows_ref[spans[-1], :] = ref[:, :model]
        packs.append(ref[:, model:].astype(F32))
        first += ref.shape[0]
    spare = rows_ref.shape[0] - first
    if spare:
        rows_ref[first:, :] = jnp.zeros((spare, model), BF16)
        packs.append(jnp.zeros((spare, packs[0].shape[1]), F32))
    pack = jnp.concatenate(packs)
    lane = lax.broadcasted_iota(jnp.int32, pack.shape, 1)
    chosen = (lane == scalars[3]) | (lane == scalars[3] + scalars[2])
    weight = jnp.sum(jnp.where(chosen, pack, 0.0), axis=-1, keepdims=True)
    chunk = min(units, 512)

    for step in range(units // chunk):
        cut = slice(step * chunk, (step + 1) * chunk)
        gate = jnp.dot(rows_ref[...], gate_ref[:, cut], preferred_element_type=F32)
        up = jnp.dot(rows_ref[...], up_ref[:, cut], preferred_element_type=F32)
        act_ref[:, cut] = (gate / (1.0 + jnp.exp(-gate)) * up).astype(BF16)

    wide = min(model, 1024)

    for step in range(model // wide):
        cut = slice(step * wide, (step + 1) * wide)
        produced = jnp.dot(act_ref[...], down_ref[:, cut], preferred_element_type=F32)
        made = (produced.astype(BF16).astype(F32) * weight).astype(BF16)
        for out_ref, span in zip(out_refs, spans):
            out_ref[:, cut] = made[span, :]


def run_expert(scalars, sign, blocks, weights_gate, weights_up, weights_out):
    units, model = weights_out.shape
    total = max(HEAD, sum(b.shape[0] for b in blocks))
    *made, sign = call(
        functools.partial(expert_kernel, len(blocks)),
        [shape((b.shape[0], model), BF16) for b in blocks] + [shape((8, HEAD), F32)],
        [scalars, sign, weights_gate, weights_up, weights_out, *blocks],
        scratch=[
            pltpu.VMEM((total, model), BF16),
            pltpu.VMEM((total, units), BF16),
        ],
        flops=6 * total * model * units,
        limit=24 << 20,
    )
    return made, sign


def ring_order(count):
    return list(range(0, count, 2)) + list(range(1, count, 2))[::-1]


def dense_experts(block, scalars, weights_gate, weights_up, expert_out):
    count = lax.axis_size("seq")
    order = ring_order(count)
    far = count // 2

    def hop(rows, steps):
        return lax.ppermute(
            rows, "seq", [(order[p], order[(p + steps) % count]) for p in range(count)]
        )

    ahead, behind = [block], [block]
    farthest = hop(block, far)
    for distance in range(1, far - 1):
        came, went = hop(ahead[-1], 1), hop(behind[-1], -1)
        if distance == far - 2:
            weights_out, sign = load_near(scalars, expert_out, 0, ahead[-1])
            came, went, sign, farthest = lax.optimization_barrier((came, went, sign, farthest))
        ahead.append(came)
        behind.append(went)
    last = hop(ahead[-1], 1), hop(behind[-1], -1)
    weights = weights_gate, weights_up, weights_out
    (own, *near), sign = run_expert(scalars, sign, ahead + behind[1:], *weights)
    *last, farthest, sign = lax.optimization_barrier((*last, farthest, sign))
    (back, front, farthest), _ = run_expert(scalars, sign, [*last, farthest], *weights)
    to_back, to_front = near[:far - 2] + [back], near[far - 2:] + [front]
    going, coming = hop(to_front[-1], 1), hop(to_back[-1], -1)
    straight = hop(farthest, far)
    for distance in range(far - 2, -1, -1):
        if distance == 0:
            return own, going, coming, straight
        going = hop(add_rows(going, to_front[distance - 1]), 1)
        coming = hop(add_rows(coming, to_back[distance - 1]), -1)


def slot_ids(block_routes, expert_count, capacity):
    row_count, top_count = block_routes.shape
    expert_ids = jnp.arange(expert_count, dtype=jnp.int32)
    onehot = (
        (block_routes[:, :, None] == expert_ids[None, None, :])
        .astype(jnp.int32)
        .reshape(row_count * top_count, expert_count)
    )
    earlier = jnp.cumsum(onehot, axis=0) - onehot
    ranking = jnp.sum(earlier * onehot, axis=1).reshape(row_count, top_count)
    return block_routes * capacity + ranking


def routed_experts(normed, my_routes, my_gates, expert_in, expert_out):
    sub_count, model_width = normed.shape
    expert_count = lax.axis_size("seq") * expert_in.shape[0]
    top_count = my_routes.shape[1]
    capacity = min(sub_count, max(2, 3 * sub_count * top_count // (2 * expert_count)))
    slot_count = expert_count * capacity
    my_slots = slot_ids(my_routes, expert_count, capacity)
    columns = jnp.arange(slot_count, dtype=jnp.int32)
    placer = jnp.sum(
        (my_slots[None, :, :] == columns[:, None, None]).astype(jnp.int32), axis=2
    ).astype(BF16)
    outgoing = (
        jnp.dot(placer, normed, preferred_element_type=F32)
        .astype(BF16)
        .reshape(expert_count, capacity, model_width)
    )
    arrived = lax.all_to_all(outgoing, "seq", split_axis=0, concat_axis=0, tiled=True)
    flat_rows = arrived.reshape(-1, model_width)
    gate_up = jnp.einsum("nd,gdf->gnf", flat_rows, expert_in[0], preferred_element_type=F32)
    activated = (jax.nn.silu(gate_up[0]) * gate_up[1]).astype(BF16)
    produced = jnp.dot(activated, expert_out[0], preferred_element_type=F32).astype(BF16)
    answered = produced.reshape(arrived.shape)
    returned = lax.all_to_all(answered, "seq", split_axis=0, concat_axis=0, tiled=True)
    picked = returned.reshape(slot_count, model_width)[my_slots.reshape(-1)].reshape(
        sub_count, top_count, model_width
    )
    return jnp.sum(picked.astype(F32) * my_gates[:, :, None], axis=1)


def swap_pairs(rows, distance):
    count = lax.axis_size("seq")
    return lax.ppermute(rows, "seq", [(i, i ^ (2 * distance)) for i in range(count)])


def pair_steps(pairs):
    bits = pairs.bit_length() - 1
    direct = pairs <= 4
    steps = range(pairs - 1, 0, -1) if direct else [1 << b for b in range(bits)]
    return direct, [(d, d.bit_length() - 1) for d in steps]


def prior_states(total):
    count = lax.axis_size("seq")
    direct, steps = pair_steps(count // 2)
    terms = []
    for distance, _ in steps:
        terms.append(
            lax.ppermute(total, "seq", [(i, i ^ (2 * distance)) for i in range(count)])
        )
        if not direct:
            total = add_rows(total, terms[-1])
    return terms


def exchange(pieces):
    parts = len(pieces)
    return [pieces[0]] + [
        lax.ppermute(pieces[j], "exp", [(i, i ^ j) for i in range(parts)])
        for j in range(1, parts)
    ]


def turn_order(items, turns):
    for b, turn in enumerate(turns):
        items = [jnp.where(turn, items[i ^ (1 << b)], items[i]) for i in range(len(items))]
    return items


def per_device(
    residual,
    queries,
    key_vectors,
    value_vectors,
    head_gain,
    norm_gain,
    routes,
    route_gates,
    expert_in,
    expert_out,
):
    rows, width = residual.shape
    seq, parts = lax.axis_size("seq"), lax.axis_size("exp")
    count, half, model = rows // parts, width // 2, width * parts
    experts = seq * expert_in.shape[0]
    position = lax.axis_index("seq")
    my_index = lax.axis_index("exp")
    place = position % 2
    _, steps = pair_steps(seq // 2)
    scalars = jnp.stack(
        [my_index, place, experts, position] + [(position >> (bit + 1)) & 1 for _, bit in steps]
    ).astype(jnp.int32)
    swap = [(i, i ^ 1) for i in range(seq)]
    turns = [
        ((my_index >> b) & 1 != 0).reshape(1, 1) for b in range(parts.bit_length() - 1)
    ]
    my_rows = (my_index * count).astype(jnp.uint32)
    scalars, turns, my_rows = lax.optimization_barrier((scalars, turns, my_rows))
    state, heads = shape((HEAD, half), BF16), shape((rows, width), BF16)
    kept, given, keys, values, query, rest, my_gain, flags = call(
        open_kernel,
        [state] * 2 + [heads] * 4
        + [shape((1, width), F32), shape((2 + len(steps), half), F32)],
        [scalars, key_vectors, value_vectors, queries, residual, head_gain[None, :]],
        far=(1, 2, 3, 4, 5),
        scratch=[pltpu.SemaphoreType.DMA((5,))],
        flops=2 * rows * width * HEAD,
    )
    partner = lax.ppermute(given, "seq", swap)
    [within] = call(
        within_kernel, [shape((rows, width), F32)], [scalars, keys, values, query],
        flops=6 * rows * rows * width,
    )
    dense = routes.shape[1] == experts
    total, within = lax.optimization_barrier((add_rows(kept, partner), within))
    sign = jnp.zeros((8, HEAD), F32)
    if dense:
        weights_gate, sign = load_near(scalars, expert_in[0], 0, total)
    before = sum(
        came.astype(F32) * flags[2 + i:3 + i] for i, came in enumerate(prior_states(total))
    )
    mine = before + partner.astype(F32) * flags[:1]
    lacked = (before + kept.astype(F32) * flags[1:2]).astype(BF16)
    lacked, sign = lax.optimization_barrier((lacked, sign))
    other = lax.ppermute(lacked, "seq", swap)
    signs = [sign]
    if dense:
        weights_up, sign = load_near(scalars, expert_in[0], 1, lacked)
        signs.append(sign)
    pieces = call(
        functools.partial(attend_kernel, parts),
        [shape((count, width), BF16)] * parts,
        [scalars, within, query, rest, my_gain, mine, other, *signs],
        scratch=[pltpu.VMEM((rows, width), BF16)],
        flops=4 * rows * width * HEAD,
    )
    gathered = exchange(pieces)

    my_routes = lax.dynamic_slice_in_dim(routes, my_rows, count, 0)
    my_gates = lax.dynamic_slice_in_dim(route_gates, my_rows, count, 0)
    mixing = jnp.sum(
        jnp.where(
            my_routes[:, :, None] == jnp.arange(experts, dtype=jnp.int32),
            my_gates[:, :, None],
            0.0,
        ),
        axis=1,
    )
    high = lax.reduce_precision(mixing, 8, 7)
    lanes = -(-2 * experts // HEAD) * HEAD
    pack = jnp.pad(
        jnp.concatenate([high, mixing - high], axis=1), ((0, 0), (0, lanes - 2 * experts))
    ).astype(BF16)
    hidden = jnp.concatenate(turn_order(gathered, turns), axis=1)
    widened = hidden.astype(F32)
    normed = (
        widened
        * lax.rsqrt(jnp.mean(widened * widened, axis=-1, keepdims=True) + 1e-06)
        * norm_gain
    ).astype(BF16)
    if dense:
        block = jnp.concatenate([normed, pack], axis=1)
        terms = dense_experts(
            block, scalars, weights_gate, weights_up, expert_out
        )
    else:
        mixed = routed_experts(normed, my_routes, my_gates, expert_in, expert_out)
        terms = [mixed]
    own, *others = terms
    mixed = own.astype(F32) + sum(t.astype(F32) for t in others)
    ready = (hidden.astype(F32) + mixed).astype(BF16)
    columns = [ready[:, i * width:(i + 1) * width] for i in range(parts)]
    return jnp.concatenate(turn_order(exchange(turn_order(columns, turns)), turns))


def solution(mesh):
    placed = (
        P("seq", "exp"),
        P("seq", "exp"),
        P("seq", "exp"),
        P("seq", "exp"),
        P("exp"),
        P(),
        P("seq", None),
        P("seq", None),
        P("seq", None, None, None),
        P("seq", None, None),
    )
    return jax.shard_map(
        per_device, mesh=mesh, in_specs=placed, out_specs=P("seq", "exp"), check_vma=False
    )
```

```python
import functools

import jax
import jax.numpy as jnp
from jax import lax
from jax.experimental import pallas as pl
from jax.experimental.pallas import tpu as pltpu
from jax.sharding import PartitionSpec as P

HEAD = 128
F32 = jnp.float32
BF16 = jnp.bfloat16
WHOLE = pl.BlockSpec(memory_space=pltpu.VMEM)
FAR = pl.BlockSpec(memory_space=pltpu.HBM)
SCALAR = pl.BlockSpec(memory_space=pltpu.SMEM)


def call(kernel, outs, inputs, far=(), small=(), scratch=(), out_specs=None, flops=0, limit=16 << 20):
    moved = sum(a.size * a.dtype.itemsize for a in [*inputs, *outs])
    inputs = [
        pltpu.with_memory_space_constraint(a, pltpu.HBM) if i in far else a
        for i, a in enumerate(inputs)
    ]
    return pl.pallas_call(
        kernel,
        out_shape=outs,
        in_specs=[
            SCALAR if i == 0 or i in small else FAR if i in far else WHOLE
            for i in range(len(inputs))
        ],
        out_specs=out_specs or [WHOLE] * len(outs),
        scratch_shapes=scratch,
        compiler_params=pltpu.CompilerParams(vmem_limit_bytes=limit),
        cost_estimate=pl.CostEstimate(flops=flops, bytes_accessed=moved, transcendentals=0),
    )(*inputs)


def shape(dims, dtype):
    return jax.ShapeDtypeStruct(dims, dtype)


def split(value):
    high = value.astype(BF16)
    return high, (value - high.astype(F32)).astype(BF16)


def add_rows(*terms):
    return sum(t.astype(F32) for t in terms).astype(BF16)


def run_copies(pairs, sems):
    copies = [pltpu.make_async_copy(a, b, sems.at[i]) for i, (a, b) in enumerate(pairs)]
    for copy in copies:
        copy.start()
    for copy in copies:
        copy.wait()


def open_kernel(
    scalars, key_ref, value_ref, query_ref, residual_ref, gain_ref,
    kept_ref, given_ref, keys, values, query, residual, gain, flags_ref, sems
):
    pairs = [
        (key_ref, keys), (value_ref, values), (query_ref, query), (residual_ref, residual),
        (gain_ref, gain),
    ]
    copies = [pltpu.make_async_copy(a, b, sems.at[i]) for i, (a, b) in enumerate(pairs)]
    for copy in copies:
        copy.start()
    for i in range(flags_ref.shape[0]):
        value = 1 - scalars[1] if i == 1 else scalars[1 if i == 0 else 2 + i]
        flags_ref[i:i + 1, :] = jnp.full((1, flags_ref.shape[1]), value, jnp.int32).astype(F32)
    for copy in copies[:2]:
        copy.wait()
    width = keys.shape[1] // 2
    place = scalars[1]
    sides = []
    for side in range(2):
        cols = slice(side * width, (side + 1) * width)
        square = lax.dot_general(
            keys[:, cols], values[:, cols], (((0,), (0,)), ((), ())), preferred_element_type=F32
        )
        sides.append(
            jnp.concatenate(
                [square[h:h + HEAD, h:h + HEAD] for h in range(0, width, HEAD)], axis=1
            ).astype(BF16)
        )
    kept_ref[...] = jnp.where(place == 0, sides[0], sides[1])
    given_ref[...] = jnp.where(place == 0, sides[1], sides[0])
    for copy in copies[2:]:
        copy.wait()


def within_kernel(scalars, keys, values, queries, out_ref):
    rows, width = out_ref.shape
    causal = lax.broadcasted_iota(jnp.int32, (rows, rows), 0) >= lax.broadcasted_iota(
        jnp.int32, (rows, rows), 1
    )
    for start in range(0, width, HEAD):
        cols = slice(start, start + HEAD)
        scores = lax.dot_general(
            queries[:, cols], keys[:, cols], (((1,), (1,)), ((), ())), preferred_element_type=F32
        )
        high, low = split(jnp.where(causal, scores, 0.0))
        out_ref[:, cols] = jnp.dot(
            high, values[:, cols], preferred_element_type=F32
        ) + jnp.dot(low, values[:, cols], preferred_element_type=F32)


def attend_kernel(
    parts, scalars, within_ref, queries, residuals, gain_ref, mine_ref, other_ref, *refs
):
    piece_refs, hidden = refs[-1 - parts:-1], refs[-1]
    rows, full = hidden.shape
    width = full // 2
    first = scalars[1] == 0
    mine, other = mine_ref[...], other_ref[...].astype(F32)
    halves = [jnp.where(first, mine, other), jnp.where(first, other, mine)]
    for start in range(0, full, HEAD):
        cols = slice(start, start + HEAD)
        half, inner = divmod(start, width)
        high, low = split(halves[half][:, inner:inner + HEAD])
        raw = (
            jnp.dot(queries[:, cols], high, preferred_element_type=F32)
            + jnp.dot(queries[:, cols], low, preferred_element_type=F32)
            + within_ref[:, cols]
        )
        scaled = raw * lax.rsqrt(jnp.mean(raw * raw, axis=-1, keepdims=True) + 1e-06)
        hidden[:, cols] = (residuals[:, cols].astype(F32) + scaled * gain_ref[:, cols]).astype(BF16)
    count = rows // parts
    for j, piece in enumerate(piece_refs):
        piece[...] = hidden[pl.ds(pl.multiple_of((scalars[0] ^ j) * count, count), count), :]


def load_kernel(lead, scalars, pair_ref, down_ref, after_ref, near_ref, part_ref, done_ref, sems):
    done_ref[...] = jnp.zeros_like(done_ref)
    pieces = sems.shape[0] // 2
    pairs = []
    for source, target, first in (
        (pair_ref.at[lead], near_ref, 0),
        (down_ref, part_ref, lead * part_ref.shape[0]),
    ):
        step = target.shape[0] // pieces
        for i in range(pieces):
            pairs.append(
                (source.at[pl.ds(first + i * step, step)], target.at[pl.ds(i * step, step)])
            )
    run_copies(pairs, sems)


def load_near(scalars, expert_in, expert_out, lead, after):
    units, model = expert_out.shape
    return call(
        functools.partial(load_kernel, lead),
        [
            shape(expert_in.shape[1:], BF16), shape((units // 2, model), BF16),
            shape((8, HEAD), F32),
        ],
        [scalars, expert_in, expert_out, after], far=(1, 2),
        scratch=[pltpu.SemaphoreType.DMA((16,))],
    )


def expert_kernel(blocks, scalars, sign_ref, gate_ref, up_ref, top_ref, low_ref, *refs):
    x_refs, out_refs, done_ref = refs[:blocks], refs[blocks:2 * blocks], refs[2 * blocks]
    rows_ref, act_ref, made_ref = refs[2 * blocks + 1:]
    done_ref[...] = jnp.zeros_like(done_ref)
    model, units = gate_ref.shape
    spans, packs = [], []
    first = 0
    for ref in x_refs:
        spans.append(slice(first, first + ref.shape[0]))
        rows_ref[spans[-1], :] = ref[:, :model]
        packs.append(ref[:, model:].astype(F32))
        first += ref.shape[0]
    spare = rows_ref.shape[0] - first
    if spare:
        rows_ref[first:, :] = jnp.zeros((spare, model), BF16)
        packs.append(jnp.zeros((spare, packs[0].shape[1]), F32))
    pack = jnp.concatenate(packs)
    lane = lax.broadcasted_iota(jnp.int32, pack.shape, 1)
    chosen = (lane == scalars[3]) | (lane == scalars[3] + scalars[2])
    weight = jnp.sum(jnp.where(chosen, pack, 0.0), axis=-1, keepdims=True)
    chunk = min(units, 512)

    for step in range(units // chunk):
        cut = slice(step * chunk, (step + 1) * chunk)
        gate = jnp.dot(rows_ref[...], gate_ref[:, cut], preferred_element_type=F32)
        up = jnp.dot(rows_ref[...], up_ref[:, cut], preferred_element_type=F32)
        act_ref[:, cut] = (gate / (1.0 + jnp.exp(-gate)) * up).astype(BF16)

    wide = min(model, 1024)

    for step in range(model // wide):
        cut = slice(step * wide, (step + 1) * wide)
        produced = jnp.dot(
            act_ref[:, :units // 2], top_ref[:, cut], preferred_element_type=F32
        ) + jnp.dot(act_ref[:, units // 2:], low_ref[:, cut], preferred_element_type=F32)
        made_ref[:, cut] = (produced.astype(BF16).astype(F32) * weight).astype(BF16)

    for out_ref, span in zip(out_refs, spans):
        out_ref[...] = made_ref[span, :]


def run_expert(scalars, sign, blocks, weights):
    model, units = weights[0].shape
    total = max(HEAD, sum(b.shape[0] for b in blocks))
    *made, sign = call(
        functools.partial(expert_kernel, len(blocks)),
        [shape((b.shape[0], model), BF16) for b in blocks] + [shape((8, HEAD), F32)],
        [scalars, sign, *weights, *blocks],
        scratch=[
            pltpu.VMEM((total, model), BF16),
            pltpu.VMEM((total, units), BF16),
            pltpu.VMEM((total, model), BF16),
        ],
        flops=6 * total * model * units,
        limit=24 << 20,
    )
    return made, sign


def ring_order(count):
    return list(range(0, count, 2)) + list(range(1, count, 2))[::-1]


def dense_experts(block, scalars, sign, weights):
    count = lax.axis_size("seq")
    order = ring_order(count)
    far = count // 2

    def hop(rows, steps):
        return lax.ppermute(
            rows, "seq", [(order[p], order[(p + steps) % count]) for p in range(count)]
        )

    ahead, behind = [block], [block]
    farthest = hop(block, far)
    for distance in range(1, far - 1):
        came, went = hop(ahead[-1], 1), hop(behind[-1], -1)
        if distance == far - 2:
            came, went, farthest = lax.optimization_barrier((came, went, farthest))
        ahead.append(came)
        behind.append(went)
    last = hop(ahead[-1], 1), hop(behind[-1], -1)
    (own, *near), sign = run_expert(scalars, sign, ahead + behind[1:], weights)
    *last, farthest, sign = lax.optimization_barrier((*last, farthest, sign))
    (back, front, farthest), _ = run_expert(scalars, sign, [*last, farthest], weights)
    to_back, to_front = near[:far - 2] + [back], near[far - 2:] + [front]
    going, coming = hop(to_front[-1], 1), hop(to_back[-1], -1)
    straight = hop(farthest, far)
    for distance in range(far - 2, -1, -1):
        if distance == 0:
            return own, going, coming, straight
        going = hop(add_rows(going, to_front[distance - 1]), 1)
        coming = hop(add_rows(coming, to_back[distance - 1]), -1)


def slot_ids(block_routes, expert_count, capacity):
    row_count, top_count = block_routes.shape
    expert_ids = jnp.arange(expert_count, dtype=jnp.int32)
    onehot = (
        (block_routes[:, :, None] == expert_ids[None, None, :])
        .astype(jnp.int32)
        .reshape(row_count * top_count, expert_count)
    )
    earlier = jnp.cumsum(onehot, axis=0) - onehot
    ranking = jnp.sum(earlier * onehot, axis=1).reshape(row_count, top_count)
    return block_routes * capacity + ranking


def routed_experts(normed, my_routes, my_gates, expert_in, expert_out):
    sub_count, model_width = normed.shape
    expert_count = lax.axis_size("seq") * expert_in.shape[0]
    top_count = my_routes.shape[1]
    capacity = min(sub_count, max(2, 3 * sub_count * top_count // (2 * expert_count)))
    slot_count = expert_count * capacity
    my_slots = slot_ids(my_routes, expert_count, capacity)
    columns = jnp.arange(slot_count, dtype=jnp.int32)
    placer = jnp.sum(
        (my_slots[None, :, :] == columns[:, None, None]).astype(jnp.int32), axis=2
    ).astype(BF16)
    outgoing = (
        jnp.dot(placer, normed, preferred_element_type=F32)
        .astype(BF16)
        .reshape(expert_count, capacity, model_width)
    )
    arrived = lax.all_to_all(outgoing, "seq", split_axis=0, concat_axis=0, tiled=True)
    flat_rows = arrived.reshape(-1, model_width)
    gate_up = jnp.einsum("nd,gdf->gnf", flat_rows, expert_in[0], preferred_element_type=F32)
    activated = (jax.nn.silu(gate_up[0]) * gate_up[1]).astype(BF16)
    produced = jnp.dot(activated, expert_out[0], preferred_element_type=F32).astype(BF16)
    answered = produced.reshape(arrived.shape)
    returned = lax.all_to_all(answered, "seq", split_axis=0, concat_axis=0, tiled=True)
    picked = returned.reshape(slot_count, model_width)[my_slots.reshape(-1)].reshape(
        sub_count, top_count, model_width
    )
    return jnp.sum(picked.astype(F32) * my_gates[:, :, None], axis=1)


def swap_pairs(rows, distance):
    count = lax.axis_size("seq")
    return lax.ppermute(rows, "seq", [(i, i ^ (2 * distance)) for i in range(count)])


def pair_steps(pairs):
    bits = pairs.bit_length() - 1
    direct = pairs <= 4
    steps = range(pairs - 1, 0, -1) if direct else [1 << b for b in range(bits)]
    return direct, [(d, d.bit_length() - 1) for d in steps]


def prior_states(total):
    count = lax.axis_size("seq")
    direct, steps = pair_steps(count // 2)
    terms = []
    for distance, _ in steps:
        terms.append(
            lax.ppermute(total, "seq", [(i, i ^ (2 * distance)) for i in range(count)])
        )
        if not direct:
            total = add_rows(total, terms[-1])
    return terms


def exchange(pieces):
    parts = len(pieces)
    return [pieces[0]] + [
        lax.ppermute(pieces[j], "exp", [(i, i ^ j) for i in range(parts)])
        for j in range(1, parts)
    ]


def turn_order(items, turns):
    for b, turn in enumerate(turns):
        items = [jnp.where(turn, items[i ^ (1 << b)], items[i]) for i in range(len(items))]
    return items


def per_device(
    residual,
    queries,
    key_vectors,
    value_vectors,
    head_gain,
    norm_gain,
    routes,
    route_gates,
    expert_in,
    expert_out,
):
    rows, width = residual.shape
    seq, parts = lax.axis_size("seq"), lax.axis_size("exp")
    count, half, model = rows // parts, width // 2, width * parts
    experts = seq * expert_in.shape[0]
    position = lax.axis_index("seq")
    my_index = lax.axis_index("exp")
    place = position % 2
    _, steps = pair_steps(seq // 2)
    scalars = jnp.stack(
        [my_index, place, experts, position] + [(position >> (bit + 1)) & 1 for _, bit in steps]
    ).astype(jnp.int32)
    swap = [(i, i ^ 1) for i in range(seq)]
    turns = [
        ((my_index >> b) & 1 != 0).reshape(1, 1) for b in range(parts.bit_length() - 1)
    ]
    my_rows = (my_index * count).astype(jnp.uint32)
    scalars, turns, my_rows = lax.optimization_barrier((scalars, turns, my_rows))
    state, heads = shape((HEAD, half), BF16), shape((rows, width), BF16)
    kept, given, keys, values, query, rest, my_gain, flags = call(
        open_kernel,
        [state] * 2 + [heads] * 4
        + [shape((1, width), F32), shape((2 + len(steps), half), F32)],
        [scalars, key_vectors, value_vectors, queries, residual, head_gain[None, :]],
        far=(1, 2, 3, 4, 5),
        scratch=[pltpu.SemaphoreType.DMA((5,))],
        flops=2 * rows * width * HEAD,
    )
    partner = lax.ppermute(given, "seq", swap)
    [within] = call(
        within_kernel, [shape((rows, width), F32)], [scalars, keys, values, query],
        flops=6 * rows * rows * width,
    )
    dense = routes.shape[1] == experts
    total, within = lax.optimization_barrier((add_rows(kept, partner), within))
    sign = jnp.zeros((8, HEAD), F32)
    if dense:
        gate, top, sign = load_near(scalars, expert_in[0], expert_out[0], 0, total)
    before = sum(
        came.astype(F32) * flags[2 + i:3 + i] for i, came in enumerate(prior_states(total))
    )
    mine = before + partner.astype(F32) * flags[:1]
    lacked = (before + kept.astype(F32) * flags[1:2]).astype(BF16)
    lacked, sign = lax.optimization_barrier((lacked, sign))
    other = lax.ppermute(lacked, "seq", swap)
    signs = [sign]
    if dense:
        up, low, sign = load_near(scalars, expert_in[0], expert_out[0], 1, lacked)
        signs.append(sign)
    pieces = call(
        functools.partial(attend_kernel, parts),
        [shape((count, width), BF16)] * parts,
        [scalars, within, query, rest, my_gain, mine, other, *signs],
        scratch=[pltpu.VMEM((rows, width), BF16)],
        flops=4 * rows * width * HEAD,
    )
    gathered = exchange(pieces)

    my_routes = lax.dynamic_slice_in_dim(routes, my_rows, count, 0)
    my_gates = lax.dynamic_slice_in_dim(route_gates, my_rows, count, 0)
    mixing = jnp.sum(
        jnp.where(
            my_routes[:, :, None] == jnp.arange(experts, dtype=jnp.int32),
            my_gates[:, :, None],
            0.0,
        ),
        axis=1,
    )
    high = lax.reduce_precision(mixing, 8, 7)
    lanes = -(-2 * experts // HEAD) * HEAD
    pack = jnp.pad(
        jnp.concatenate([high, mixing - high], axis=1), ((0, 0), (0, lanes - 2 * experts))
    ).astype(BF16)
    hidden = jnp.concatenate(turn_order(gathered, turns), axis=1)
    widened = hidden.astype(F32)
    normed = (
        widened
        * lax.rsqrt(jnp.mean(widened * widened, axis=-1, keepdims=True) + 1e-06)
        * norm_gain
    ).astype(BF16)
    if dense:
        block = jnp.concatenate([normed, pack], axis=1)
        terms = dense_experts(block, scalars, sign, [gate, up, top, low])
    else:
        mixed = routed_experts(normed, my_routes, my_gates, expert_in, expert_out)
        terms = [mixed]
    own, *others = terms
    mixed = own.astype(F32) + sum(t.astype(F32) for t in others)
    ready = (hidden.astype(F32) + mixed).astype(BF16)
    columns = [ready[:, i * width:(i + 1) * width] for i in range(parts)]
    return jnp.concatenate(turn_order(exchange(turn_order(columns, turns)), turns))


def solution(mesh):
    placed = (
        P("seq", "exp"),
        P("seq", "exp"),
        P("seq", "exp"),
        P("seq", "exp"),
        P("exp"),
        P(),
        P("seq", None),
        P("seq", None),
        P("seq", None, None, None),
        P("seq", None, None),
    )
    return jax.shard_map(
        per_device, mesh=mesh, in_specs=placed, out_specs=P("seq", "exp"), check_vma=False
    )
```

```python
import functools

import jax
import jax.numpy as jnp
from jax import lax
from jax.experimental import pallas as pl
from jax.experimental.pallas import tpu as pltpu
from jax.sharding import PartitionSpec as P

HEAD = 128
F32 = jnp.float32
BF16 = jnp.bfloat16
WHOLE = pl.BlockSpec(memory_space=pltpu.VMEM)
FAR = pl.BlockSpec(memory_space=pltpu.HBM)
SCALAR = pl.BlockSpec(memory_space=pltpu.SMEM)


def call(kernel, outs, inputs, far=(), small=(), scratch=(), out_specs=None, flops=0, limit=16 << 20):
    moved = sum(a.size * a.dtype.itemsize for a in [*inputs, *outs])
    inputs = [
        pltpu.with_memory_space_constraint(a, pltpu.HBM) if i in far else a
        for i, a in enumerate(inputs)
    ]
    return pl.pallas_call(
        kernel,
        out_shape=outs,
        in_specs=[
            SCALAR if i == 0 or i in small else FAR if i in far else WHOLE
            for i in range(len(inputs))
        ],
        out_specs=out_specs or [WHOLE] * len(outs),
        scratch_shapes=scratch,
        compiler_params=pltpu.CompilerParams(vmem_limit_bytes=limit),
        cost_estimate=pl.CostEstimate(flops=flops, bytes_accessed=moved, transcendentals=0),
    )(*inputs)


def shape(dims, dtype):
    return jax.ShapeDtypeStruct(dims, dtype)


def split(value):
    high = value.astype(BF16)
    return high, (value - high.astype(F32)).astype(BF16)


def add_rows(*terms):
    return sum(t.astype(F32) for t in terms).astype(BF16)


def run_copies(pairs, sems):
    copies = [pltpu.make_async_copy(a, b, sems.at[i]) for i, (a, b) in enumerate(pairs)]
    for copy in copies:
        copy.start()
    for copy in copies:
        copy.wait()


def open_kernel(
    scalars, key_ref, value_ref, query_ref, residual_ref, gain_ref,
    kept_ref, given_ref, keys, values, query, residual, gain, flags_ref, sems
):
    pairs = [
        (key_ref, keys), (value_ref, values), (query_ref, query), (residual_ref, residual),
        (gain_ref, gain),
    ]
    copies = [pltpu.make_async_copy(a, b, sems.at[i]) for i, (a, b) in enumerate(pairs)]
    for copy in copies:
        copy.start()
    for i in range(flags_ref.shape[0]):
        value = 1 - scalars[1] if i == 1 else scalars[1 if i == 0 else 2 + i]
        flags_ref[i:i + 1, :] = jnp.full((1, flags_ref.shape[1]), value, jnp.int32).astype(F32)
    for copy in copies[:2]:
        copy.wait()
    width = keys.shape[1] // 2
    place = scalars[1]
    sides = []
    for side in range(2):
        cols = slice(side * width, (side + 1) * width)
        square = lax.dot_general(
            keys[:, cols], values[:, cols], (((0,), (0,)), ((), ())), preferred_element_type=F32
        )
        sides.append(
            jnp.concatenate(
                [square[h:h + HEAD, h:h + HEAD] for h in range(0, width, HEAD)], axis=1
            ).astype(BF16)
        )
    kept_ref[...] = jnp.where(place == 0, sides[0], sides[1])
    given_ref[...] = jnp.where(place == 0, sides[1], sides[0])
    for copy in copies[2:]:
        copy.wait()


def within_kernel(scalars, keys, values, queries, out_ref):
    rows, width = out_ref.shape
    causal = lax.broadcasted_iota(jnp.int32, (rows, rows), 0) >= lax.broadcasted_iota(
        jnp.int32, (rows, rows), 1
    )
    for start in range(0, width, HEAD):
        cols = slice(start, start + HEAD)
        scores = lax.dot_general(
            queries[:, cols], keys[:, cols], (((1,), (1,)), ((), ())), preferred_element_type=F32
        )
        high, low = split(jnp.where(causal, scores, 0.0))
        out_ref[:, cols] = jnp.dot(
            high, values[:, cols], preferred_element_type=F32
        ) + jnp.dot(low, values[:, cols], preferred_element_type=F32)


def attend_kernel(
    parts, scalars, within_ref, queries, residuals, gain_ref, mine_ref, other_ref, *refs
):
    piece_refs, hidden = refs[-1 - parts:-1], refs[-1]
    rows, full = hidden.shape
    width = full // 2
    first = scalars[1] == 0
    mine, other = mine_ref[...], other_ref[...].astype(F32)
    halves = [jnp.where(first, mine, other), jnp.where(first, other, mine)]
    for start in range(0, full, HEAD):
        cols = slice(start, start + HEAD)
        half, inner = divmod(start, width)
        high, low = split(halves[half][:, inner:inner + HEAD])
        raw = (
            jnp.dot(queries[:, cols], high, preferred_element_type=F32)
            + jnp.dot(queries[:, cols], low, preferred_element_type=F32)
            + within_ref[:, cols]
        )
        scaled = raw * lax.rsqrt(jnp.mean(raw * raw, axis=-1, keepdims=True) + 1e-06)
        hidden[:, cols] = (residuals[:, cols].astype(F32) + scaled * gain_ref[:, cols]).astype(BF16)
    count = rows // parts
    for j, piece in enumerate(piece_refs):
        piece[...] = hidden[pl.ds(pl.multiple_of((scalars[0] ^ j) * count, count), count), :]


def load_kernel(lead, scalars, source, after_ref, target, done_ref, sems):
    done_ref[...] = jnp.zeros_like(done_ref)
    pieces = sems.shape[0]
    step = target.shape[0] // pieces
    cuts = [pl.ds(i * step, step) for i in range(pieces)]
    run_copies([(source.at[lead, cut], target.at[cut]) for cut in cuts], sems)


def load_near(scalars, source, lead, after):
    return call(
        functools.partial(load_kernel, lead),
        [shape(source.shape[1:], source.dtype), shape((8, HEAD), F32)],
        [scalars, source, after], far=(1,), scratch=[pltpu.SemaphoreType.DMA((8,))],
    )


def expert_kernel(blocks, scalars, sign_ref, gate_ref, up_ref, down_ref, *refs):
    x_refs, out_refs, done_ref = refs[:blocks], refs[blocks:2 * blocks], refs[2 * blocks]
    rows_ref, act_ref, made_ref = refs[2 * blocks + 1:]
    done_ref[...] = jnp.zeros_like(done_ref)
    model, units = gate_ref.shape
    spans, packs = [], []
    first = 0
    for ref in x_refs:
        spans.append(slice(first, first + ref.shape[0]))
        rows_ref[spans[-1], :] = ref[:, :model]
        packs.append(ref[:, model:].astype(F32))
        first += ref.shape[0]
    spare = rows_ref.shape[0] - first
    if spare:
        rows_ref[first:, :] = jnp.zeros((spare, model), BF16)
        packs.append(jnp.zeros((spare, packs[0].shape[1]), F32))
    pack = jnp.concatenate(packs)
    lane = lax.broadcasted_iota(jnp.int32, pack.shape, 1)
    chosen = (lane == scalars[3]) | (lane == scalars[3] + scalars[2])
    weight = jnp.sum(jnp.where(chosen, pack, 0.0), axis=-1, keepdims=True)
    chunk = min(units, 512)

    for step in range(units // chunk):
        cut = slice(step * chunk, (step + 1) * chunk)
        gate = jnp.dot(rows_ref[...], gate_ref[:, cut], preferred_element_type=F32)
        up = jnp.dot(rows_ref[...], up_ref[:, cut], preferred_element_type=F32)
        act_ref[:, cut] = (gate / (1.0 + jnp.exp(-gate)) * up).astype(BF16)

    wide = min(model, 1024)

    for step in range(model // wide):
        cut = slice(step * wide, (step + 1) * wide)
        produced = jnp.dot(act_ref[...], down_ref[:, cut], preferred_element_type=F32)
        made_ref[:, cut] = (produced.astype(BF16).astype(F32) * weight).astype(BF16)

    for out_ref, span in zip(out_refs, spans):
        out_ref[...] = made_ref[span, :]


def run_expert(scalars, sign, blocks, weights_gate, weights_up, weights_out):
    units, model = weights_out.shape
    total = max(HEAD, sum(b.shape[0] for b in blocks))
    *made, sign = call(
        functools.partial(expert_kernel, len(blocks)),
        [shape((b.shape[0], model), BF16) for b in blocks] + [shape((8, HEAD), F32)],
        [scalars, sign, weights_gate, weights_up, weights_out, *blocks],
        scratch=[
            pltpu.VMEM((total, model), BF16),
            pltpu.VMEM((total, units), BF16),
            pltpu.VMEM((total, model), BF16),
        ],
        flops=6 * total * model * units,
        limit=24 << 20,
    )
    return made, sign


def ring_order(count):
    return list(range(0, count, 2)) + list(range(1, count, 2))[::-1]


def dense_experts(block, scalars, weights_gate, weights_up, expert_out):
    count = lax.axis_size("seq")
    order = ring_order(count)
    far = count // 2

    def hop(rows, steps):
        return lax.ppermute(
            rows, "seq", [(order[p], order[(p + steps) % count]) for p in range(count)]
        )

    ahead, behind = [block], [block]
    farthest = hop(block, far)
    for distance in range(1, far - 1):
        came, went = hop(ahead[-1], 1), hop(behind[-1], -1)
        if distance == far - 2:
            weights_out, sign = load_near(scalars, expert_out, 0, ahead[-1])
            came, went, sign, farthest = lax.optimization_barrier((came, went, sign, farthest))
        ahead.append(came)
        behind.append(went)
    last = hop(ahead[-1], 1), hop(behind[-1], -1)
    weights = weights_gate, weights_up, weights_out
    (own, *near), sign = run_expert(scalars, sign, ahead + behind[1:], *weights)
    *last, farthest, sign = lax.optimization_barrier((*last, farthest, sign))
    (back, front, farthest), _ = run_expert(scalars, sign, [*last, farthest], *weights)
    to_back, to_front = near[:far - 2] + [back], near[far - 2:] + [front]
    going, coming = hop(to_front[-1], 1), hop(to_back[-1], -1)
    for distance in range(far - 2, -1, -1):
        if distance == 0:
            return own, going, coming, straight
        going = add_rows(going, to_front[distance - 1])
        if distance == far - 2:
            going, farthest = lax.optimization_barrier((going, farthest))
            straight = hop(farthest, far)
        going = hop(going, 1)
        coming = hop(add_rows(coming, to_back[distance - 1]), -1)


def slot_ids(block_routes, expert_count, capacity):
    row_count, top_count = block_routes.shape
    expert_ids = jnp.arange(expert_count, dtype=jnp.int32)
    onehot = (
        (block_routes[:, :, None] == expert_ids[None, None, :])
        .astype(jnp.int32)
        .reshape(row_count * top_count, expert_count)
    )
    earlier = jnp.cumsum(onehot, axis=0) - onehot
    ranking = jnp.sum(earlier * onehot, axis=1).reshape(row_count, top_count)
    return block_routes * capacity + ranking


def routed_experts(normed, my_routes, my_gates, expert_in, expert_out):
    sub_count, model_width = normed.shape
    expert_count = lax.axis_size("seq") * expert_in.shape[0]
    top_count = my_routes.shape[1]
    capacity = min(sub_count, max(2, 3 * sub_count * top_count // (2 * expert_count)))
    slot_count = expert_count * capacity
    my_slots = slot_ids(my_routes, expert_count, capacity)
    columns = jnp.arange(slot_count, dtype=jnp.int32)
    placer = jnp.sum(
        (my_slots[None, :, :] == columns[:, None, None]).astype(jnp.int32), axis=2
    ).astype(BF16)
    outgoing = (
        jnp.dot(placer, normed, preferred_element_type=F32)
        .astype(BF16)
        .reshape(expert_count, capacity, model_width)
    )
    arrived = lax.all_to_all(outgoing, "seq", split_axis=0, concat_axis=0, tiled=True)
    flat_rows = arrived.reshape(-1, model_width)
    gate_up = jnp.einsum("nd,gdf->gnf", flat_rows, expert_in[0], preferred_element_type=F32)
    activated = (jax.nn.silu(gate_up[0]) * gate_up[1]).astype(BF16)
    produced = jnp.dot(activated, expert_out[0], preferred_element_type=F32).astype(BF16)
    answered = produced.reshape(arrived.shape)
    returned = lax.all_to_all(answered, "seq", split_axis=0, concat_axis=0, tiled=True)
    picked = returned.reshape(slot_count, model_width)[my_slots.reshape(-1)].reshape(
        sub_count, top_count, model_width
    )
    return jnp.sum(picked.astype(F32) * my_gates[:, :, None], axis=1)


def swap_pairs(rows, distance):
    count = lax.axis_size("seq")
    return lax.ppermute(rows, "seq", [(i, i ^ (2 * distance)) for i in range(count)])


def pair_steps(pairs):
    bits = pairs.bit_length() - 1
    direct = pairs <= 4
    steps = range(pairs - 1, 0, -1) if direct else [1 << b for b in range(bits)]
    return direct, [(d, d.bit_length() - 1) for d in steps]


def prior_states(total):
    count = lax.axis_size("seq")
    direct, steps = pair_steps(count // 2)
    terms = []
    for distance, _ in steps:
        terms.append(
            lax.ppermute(total, "seq", [(i, i ^ (2 * distance)) for i in range(count)])
        )
        if not direct:
            total = add_rows(total, terms[-1])
    return terms


def exchange(pieces):
    parts = len(pieces)
    return [pieces[0]] + [
        lax.ppermute(pieces[j], "exp", [(i, i ^ j) for i in range(parts)])
        for j in range(1, parts)
    ]


def turn_order(items, turns):
    for b, turn in enumerate(turns):
        items = [jnp.where(turn, items[i ^ (1 << b)], items[i]) for i in range(len(items))]
    return items


def per_device(
    residual,
    queries,
    key_vectors,
    value_vectors,
    head_gain,
    norm_gain,
    routes,
    route_gates,
    expert_in,
    expert_out,
):
    rows, width = residual.shape
    seq, parts = lax.axis_size("seq"), lax.axis_size("exp")
    count, half, model = rows // parts, width // 2, width * parts
    experts = seq * expert_in.shape[0]
    position = lax.axis_index("seq")
    my_index = lax.axis_index("exp")
    place = position % 2
    _, steps = pair_steps(seq // 2)
    scalars = jnp.stack(
        [my_index, place, experts, position] + [(position >> (bit + 1)) & 1 for _, bit in steps]
    ).astype(jnp.int32)
    swap = [(i, i ^ 1) for i in range(seq)]
    turns = [
        ((my_index >> b) & 1 != 0).reshape(1, 1) for b in range(parts.bit_length() - 1)
    ]
    my_rows = (my_index * count).astype(jnp.uint32)
    scalars, turns, my_rows = lax.optimization_barrier((scalars, turns, my_rows))
    state, heads = shape((HEAD, half), BF16), shape((rows, width), BF16)
    kept, given, keys, values, query, rest, my_gain, flags = call(
        open_kernel,
        [state] * 2 + [heads] * 4
        + [shape((1, width), F32), shape((2 + len(steps), half), F32)],
        [scalars, key_vectors, value_vectors, queries, residual, head_gain[None, :]],
        far=(1, 2, 3, 4, 5),
        scratch=[pltpu.SemaphoreType.DMA((5,))],
        flops=2 * rows * width * HEAD,
    )
    partner = lax.ppermute(given, "seq", swap)
    [within] = call(
        within_kernel, [shape((rows, width), F32)], [scalars, keys, values, query],
        flops=6 * rows * rows * width,
    )
    dense = routes.shape[1] == experts
    total, within = lax.optimization_barrier((add_rows(kept, partner), within))
    sign = jnp.zeros((8, HEAD), F32)
    if dense:
        weights_gate, sign = load_near(scalars, expert_in[0], 0, total)
    before = sum(
        came.astype(F32) * flags[2 + i:3 + i] for i, came in enumerate(prior_states(total))
    )
    mine = before + partner.astype(F32) * flags[:1]
    lacked = (before + kept.astype(F32) * flags[1:2]).astype(BF16)
    lacked, sign = lax.optimization_barrier((lacked, sign))
    other = lax.ppermute(lacked, "seq", swap)
    signs = [sign]
    if dense:
        weights_up, sign = load_near(scalars, expert_in[0], 1, lacked)
        signs.append(sign)
    pieces = call(
        functools.partial(attend_kernel, parts),
        [shape((count, width), BF16)] * parts,
        [scalars, within, query, rest, my_gain, mine, other, *signs],
        scratch=[pltpu.VMEM((rows, width), BF16)],
        flops=4 * rows * width * HEAD,
    )
    gathered = exchange(pieces)

    my_routes = lax.dynamic_slice_in_dim(routes, my_rows, count, 0)
    my_gates = lax.dynamic_slice_in_dim(route_gates, my_rows, count, 0)
    mixing = jnp.sum(
        jnp.where(
            my_routes[:, :, None] == jnp.arange(experts, dtype=jnp.int32),
            my_gates[:, :, None],
            0.0,
        ),
        axis=1,
    )
    high = lax.reduce_precision(mixing, 8, 7)
    lanes = -(-2 * experts // HEAD) * HEAD
    pack = jnp.pad(
        jnp.concatenate([high, mixing - high], axis=1), ((0, 0), (0, lanes - 2 * experts))
    ).astype(BF16)
    hidden = jnp.concatenate(turn_order(gathered, turns), axis=1)
    widened = hidden.astype(F32)
    normed = (
        widened
        * lax.rsqrt(jnp.mean(widened * widened, axis=-1, keepdims=True) + 1e-06)
        * norm_gain
    ).astype(BF16)
    if dense:
        block = jnp.concatenate([normed, pack], axis=1)
        terms = dense_experts(
            block, scalars, weights_gate, weights_up, expert_out
        )
    else:
        mixed = routed_experts(normed, my_routes, my_gates, expert_in, expert_out)
        terms = [mixed]
    own, *others = terms
    mixed = own.astype(F32) + sum(t.astype(F32) for t in others)
    ready = (hidden.astype(F32) + mixed).astype(BF16)
    columns = [ready[:, i * width:(i + 1) * width] for i in range(parts)]
    return jnp.concatenate(turn_order(exchange(turn_order(columns, turns)), turns))


def solution(mesh):
    placed = (
        P("seq", "exp"),
        P("seq", "exp"),
        P("seq", "exp"),
        P("seq", "exp"),
        P("exp"),
        P(),
        P("seq", None),
        P("seq", None),
        P("seq", None, None, None),
        P("seq", None, None),
    )
    return jax.shard_map(
        per_device, mesh=mesh, in_specs=placed, out_specs=P("seq", "exp"), check_vma=False
    )
```

```python
import functools

import jax
import jax.numpy as jnp
from jax import lax
from jax.experimental import pallas as pl
from jax.experimental.pallas import tpu as pltpu
from jax.sharding import PartitionSpec as P

HEAD = 128
F32 = jnp.float32
BF16 = jnp.bfloat16
WHOLE = pl.BlockSpec(memory_space=pltpu.VMEM)
FAR = pl.BlockSpec(memory_space=pltpu.HBM)
SCALAR = pl.BlockSpec(memory_space=pltpu.SMEM)


def call(kernel, outs, inputs, far=(), small=(), scratch=(), out_specs=None, flops=0, limit=16 << 20):
    moved = sum(a.size * a.dtype.itemsize for a in [*inputs, *outs])
    inputs = [
        pltpu.with_memory_space_constraint(a, pltpu.HBM) if i in far else a
        for i, a in enumerate(inputs)
    ]
    return pl.pallas_call(
        kernel,
        out_shape=outs,
        in_specs=[
            SCALAR if i == 0 or i in small else FAR if i in far else WHOLE
            for i in range(len(inputs))
        ],
        out_specs=out_specs or [WHOLE] * len(outs),
        scratch_shapes=scratch,
        compiler_params=pltpu.CompilerParams(vmem_limit_bytes=limit),
        cost_estimate=pl.CostEstimate(flops=flops, bytes_accessed=moved, transcendentals=0),
    )(*inputs)


def shape(dims, dtype):
    return jax.ShapeDtypeStruct(dims, dtype)


def split(value):
    high = value.astype(BF16)
    return high, (value - high.astype(F32)).astype(BF16)


def add_rows(*terms):
    return sum(t.astype(F32) for t in terms).astype(BF16)


def run_copies(pairs, sems):
    copies = [pltpu.make_async_copy(a, b, sems.at[i]) for i, (a, b) in enumerate(pairs)]
    for copy in copies:
        copy.start()
    for copy in copies:
        copy.wait()


def open_kernel(
    scalars, key_ref, value_ref, query_ref, residual_ref, gain_ref,
    kept_ref, given_ref, keys, values, query, residual, gain, flags_ref, sems
):
    pairs = [
        (key_ref, keys), (value_ref, values), (query_ref, query), (residual_ref, residual),
        (gain_ref, gain),
    ]
    copies = [pltpu.make_async_copy(a, b, sems.at[i]) for i, (a, b) in enumerate(pairs)]
    for copy in copies:
        copy.start()
    for i in range(flags_ref.shape[0]):
        value = 1 - scalars[1] if i == 1 else scalars[1 if i == 0 else 2 + i]
        flags_ref[i:i + 1, :] = jnp.full((1, flags_ref.shape[1]), value, jnp.int32).astype(F32)
    for copy in copies[:2]:
        copy.wait()
    width = keys.shape[1] // 2
    place = scalars[1]
    sides = []
    for side in range(2):
        cols = slice(side * width, (side + 1) * width)
        square = lax.dot_general(
            keys[:, cols], values[:, cols], (((0,), (0,)), ((), ())), preferred_element_type=F32
        )
        sides.append(
            jnp.concatenate(
                [square[h:h + HEAD, h:h + HEAD] for h in range(0, width, HEAD)], axis=1
            ).astype(BF16)
        )
    kept_ref[...] = jnp.where(place == 0, sides[0], sides[1])
    given_ref[...] = jnp.where(place == 0, sides[1], sides[0])
    for copy in copies[2:]:
        copy.wait()


def within_kernel(scalars, keys, values, queries, out_ref):
    rows, width = out_ref.shape
    causal = lax.broadcasted_iota(jnp.int32, (rows, rows), 0) >= lax.broadcasted_iota(
        jnp.int32, (rows, rows), 1
    )
    for start in range(0, width, HEAD):
        cols = slice(start, start + HEAD)
        scores = lax.dot_general(
            queries[:, cols], keys[:, cols], (((1,), (1,)), ((), ())), preferred_element_type=F32
        )
        high, low = split(jnp.where(causal, scores, 0.0))
        out_ref[:, cols] = jnp.dot(
            high, values[:, cols], preferred_element_type=F32
        ) + jnp.dot(low, values[:, cols], preferred_element_type=F32)


def attend_kernel(
    parts, scalars, within_ref, queries, residuals, gain_ref, mine_ref, other_ref, *refs
):
    piece_refs, hidden = refs[-1 - parts:-1], refs[-1]
    rows, full = hidden.shape
    width = full // 2
    first = scalars[1] == 0
    mine, other = mine_ref[...], other_ref[...].astype(F32)
    halves = [jnp.where(first, mine, other), jnp.where(first, other, mine)]
    for start in range(0, full, HEAD):
        cols = slice(start, start + HEAD)
        half, inner = divmod(start, width)
        high, low = split(halves[half][:, inner:inner + HEAD])
        raw = (
            jnp.dot(queries[:, cols], high, preferred_element_type=F32)
            + jnp.dot(queries[:, cols], low, preferred_element_type=F32)
            + within_ref[:, cols]
        )
        scaled = raw * lax.rsqrt(jnp.mean(raw * raw, axis=-1, keepdims=True) + 1e-06)
        hidden[:, cols] = (residuals[:, cols].astype(F32) + scaled * gain_ref[:, cols]).astype(BF16)
    count = rows // parts
    for j, piece in enumerate(piece_refs):
        piece[...] = hidden[pl.ds(pl.multiple_of((scalars[0] ^ j) * count, count), count), :]


def load_kernel(lead, scalars, source, after_ref, target, done_ref, sems):
    done_ref[...] = jnp.zeros_like(done_ref)
    pieces = sems.shape[0]
    step = target.shape[0] // pieces
    cuts = [pl.ds(i * step, step) for i in range(pieces)]
    run_copies([(source.at[lead, cut], target.at[cut]) for cut in cuts], sems)


def load_near(scalars, source, lead, after):
    return call(
        functools.partial(load_kernel, lead),
        [shape(source.shape[1:], source.dtype), shape((8, HEAD), F32)],
        [scalars, source, after], far=(1,), scratch=[pltpu.SemaphoreType.DMA((8,))],
    )


def expert_kernel(blocks, scalars, sign_ref, gate_ref, up_ref, down_ref, *refs):
    x_refs, out_refs, done_ref = refs[:blocks], refs[blocks:2 * blocks], refs[2 * blocks]
    rows_ref, act_ref, made_ref = refs[2 * blocks + 1:]
    done_ref[...] = jnp.zeros_like(done_ref)
    model, units = gate_ref.shape
    spans, packs = [], []
    first = 0
    for ref in x_refs:
        spans.append(slice(first, first + ref.shape[0]))
        rows_ref[spans[-1], :] = ref[:, :model]
        packs.append(ref[:, model:].astype(F32))
        first += ref.shape[0]
    spare = rows_ref.shape[0] - first
    if spare:
        rows_ref[first:, :] = jnp.zeros((spare, model), BF16)
        packs.append(jnp.zeros((spare, packs[0].shape[1]), F32))
    pack = jnp.concatenate(packs)
    lane = lax.broadcasted_iota(jnp.int32, pack.shape, 1)
    chosen = (lane == scalars[3]) | (lane == scalars[3] + scalars[2])
    weight = jnp.sum(jnp.where(chosen, pack, 0.0), axis=-1, keepdims=True)
    chunk = min(units, 256)

    for step in range(units // chunk):
        cut = slice(step * chunk, (step + 1) * chunk)
        gate = jnp.dot(rows_ref[...], gate_ref[:, cut], preferred_element_type=F32)
        up = jnp.dot(rows_ref[...], up_ref[:, cut], preferred_element_type=F32)
        act_ref[:, cut] = (gate / (1.0 + jnp.exp(-gate)) * up).astype(BF16)

    wide = min(model, 512)

    for step in range(model // wide):
        cut = slice(step * wide, (step + 1) * wide)
        produced = jnp.dot(act_ref[...], down_ref[:, cut], preferred_element_type=F32)
        made_ref[:, cut] = (produced.astype(BF16).astype(F32) * weight).astype(BF16)

    for out_ref, span in zip(out_refs, spans):
        out_ref[...] = made_ref[span, :]


def run_expert(scalars, sign, blocks, weights_gate, weights_up, weights_out):
    units, model = weights_out.shape
    total = max(HEAD, sum(b.shape[0] for b in blocks))
    *made, sign = call(
        functools.partial(expert_kernel, len(blocks)),
        [shape((b.shape[0], model), BF16) for b in blocks] + [shape((8, HEAD), F32)],
        [scalars, sign, weights_gate, weights_up, weights_out, *blocks],
        scratch=[
            pltpu.VMEM((total, model), BF16),
            pltpu.VMEM((total, units), BF16),
            pltpu.VMEM((total, model), BF16),
        ],
        flops=6 * total * model * units,
        limit=24 << 20,
    )
    return made, sign


def ring_order(count):
    return list(range(0, count, 2)) + list(range(1, count, 2))[::-1]


def dense_experts(block, scalars, weights_gate, weights_up, expert_out):
    count = lax.axis_size("seq")
    order = ring_order(count)
    far = count // 2

    def hop(rows, steps):
        return lax.ppermute(
            rows, "seq", [(order[p], order[(p + steps) % count]) for p in range(count)]
        )

    ahead, behind = [block], [block]
    farthest = hop(block, far)
    for distance in range(1, far - 1):
        came, went = hop(ahead[-1], 1), hop(behind[-1], -1)
        if distance == far - 2:
            weights_out, sign = load_near(scalars, expert_out, 0, ahead[-1])
            came, went, sign, farthest = lax.optimization_barrier((came, went, sign, farthest))
        ahead.append(came)
        behind.append(went)
    last = hop(ahead[-1], 1), hop(behind[-1], -1)
    weights = weights_gate, weights_up, weights_out
    (own, *near), sign = run_expert(scalars, sign, ahead + behind[1:], *weights)
    *last, farthest, sign = lax.optimization_barrier((*last, farthest, sign))
    (back, front, farthest), _ = run_expert(scalars, sign, [*last, farthest], *weights)
    to_back, to_front = near[:far - 2] + [back], near[far - 2:] + [front]
    going, coming = hop(to_front[-1], 1), hop(to_back[-1], -1)
    straight = hop(farthest, far)
    for distance in range(far - 2, -1, -1):
        if distance == 0:
            return own, going, coming, straight
        going = hop(add_rows(going, to_front[distance - 1]), 1)
        coming = hop(add_rows(coming, to_back[distance - 1]), -1)


def slot_ids(block_routes, expert_count, capacity):
    row_count, top_count = block_routes.shape
    expert_ids = jnp.arange(expert_count, dtype=jnp.int32)
    onehot = (
        (block_routes[:, :, None] == expert_ids[None, None, :])
        .astype(jnp.int32)
        .reshape(row_count * top_count, expert_count)
    )
    earlier = jnp.cumsum(onehot, axis=0) - onehot
    ranking = jnp.sum(earlier * onehot, axis=1).reshape(row_count, top_count)
    return block_routes * capacity + ranking


def routed_experts(normed, my_routes, my_gates, expert_in, expert_out):
    sub_count, model_width = normed.shape
    expert_count = lax.axis_size("seq") * expert_in.shape[0]
    top_count = my_routes.shape[1]
    capacity = min(sub_count, max(2, 3 * sub_count * top_count // (2 * expert_count)))
    slot_count = expert_count * capacity
    my_slots = slot_ids(my_routes, expert_count, capacity)
    columns = jnp.arange(slot_count, dtype=jnp.int32)
    placer = jnp.sum(
        (my_slots[None, :, :] == columns[:, None, None]).astype(jnp.int32), axis=2
    ).astype(BF16)
    outgoing = (
        jnp.dot(placer, normed, preferred_element_type=F32)
        .astype(BF16)
        .reshape(expert_count, capacity, model_width)
    )
    arrived = lax.all_to_all(outgoing, "seq", split_axis=0, concat_axis=0, tiled=True)
    flat_rows = arrived.reshape(-1, model_width)
    gate_up = jnp.einsum("nd,gdf->gnf", flat_rows, expert_in[0], preferred_element_type=F32)
    activated = (jax.nn.silu(gate_up[0]) * gate_up[1]).astype(BF16)
    produced = jnp.dot(activated, expert_out[0], preferred_element_type=F32).astype(BF16)
    answered = produced.reshape(arrived.shape)
    returned = lax.all_to_all(answered, "seq", split_axis=0, concat_axis=0, tiled=True)
    picked = returned.reshape(slot_count, model_width)[my_slots.reshape(-1)].reshape(
        sub_count, top_count, model_width
    )
    return jnp.sum(picked.astype(F32) * my_gates[:, :, None], axis=1)


def swap_pairs(rows, distance):
    count = lax.axis_size("seq")
    return lax.ppermute(rows, "seq", [(i, i ^ (2 * distance)) for i in range(count)])


def pair_steps(pairs):
    bits = pairs.bit_length() - 1
    direct = pairs <= 4
    steps = range(pairs - 1, 0, -1) if direct else [1 << b for b in range(bits)]
    return direct, [(d, d.bit_length() - 1) for d in steps]


def prior_states(total):
    count = lax.axis_size("seq")
    direct, steps = pair_steps(count // 2)
    terms = []
    for distance, _ in steps:
        terms.append(
            lax.ppermute(total, "seq", [(i, i ^ (2 * distance)) for i in range(count)])
        )
        if not direct:
            total = add_rows(total, terms[-1])
    return terms


def exchange(pieces):
    parts = len(pieces)
    return [pieces[0]] + [
        lax.ppermute(pieces[j], "exp", [(i, i ^ j) for i in range(parts)])
        for j in range(1, parts)
    ]


def turn_order(items, turns):
    for b, turn in enumerate(turns):
        items = [jnp.where(turn, items[i ^ (1 << b)], items[i]) for i in range(len(items))]
    return items


def per_device(
    residual,
    queries,
    key_vectors,
    value_vectors,
    head_gain,
    norm_gain,
    routes,
    route_gates,
    expert_in,
    expert_out,
):
    rows, width = residual.shape
    seq, parts = lax.axis_size("seq"), lax.axis_size("exp")
    count, half, model = rows // parts, width // 2, width * parts
    experts = seq * expert_in.shape[0]
    position = lax.axis_index("seq")
    my_index = lax.axis_index("exp")
    place = position % 2
    _, steps = pair_steps(seq // 2)
    scalars = jnp.stack(
        [my_index, place, experts, position] + [(position >> (bit + 1)) & 1 for _, bit in steps]
    ).astype(jnp.int32)
    swap = [(i, i ^ 1) for i in range(seq)]
    turns = [
        ((my_index >> b) & 1 != 0).reshape(1, 1) for b in range(parts.bit_length() - 1)
    ]
    my_rows = (my_index * count).astype(jnp.uint32)
    scalars, turns, my_rows = lax.optimization_barrier((scalars, turns, my_rows))
    state, heads = shape((HEAD, half), BF16), shape((rows, width), BF16)
    kept, given, keys, values, query, rest, my_gain, flags = call(
        open_kernel,
        [state] * 2 + [heads] * 4
        + [shape((1, width), F32), shape((2 + len(steps), half), F32)],
        [scalars, key_vectors, value_vectors, queries, residual, head_gain[None, :]],
        far=(1, 2, 3, 4, 5),
        scratch=[pltpu.SemaphoreType.DMA((5,))],
        flops=2 * rows * width * HEAD,
    )
    partner = lax.ppermute(given, "seq", swap)
    [within] = call(
        within_kernel, [shape((rows, width), F32)], [scalars, keys, values, query],
        flops=6 * rows * rows * width,
    )
    dense = routes.shape[1] == experts
    total, within = lax.optimization_barrier((add_rows(kept, partner), within))
    sign = jnp.zeros((8, HEAD), F32)
    if dense:
        weights_gate, sign = load_near(scalars, expert_in[0], 0, total)
    before = sum(
        came.astype(F32) * flags[2 + i:3 + i] for i, came in enumerate(prior_states(total))
    )
    mine = before + partner.astype(F32) * flags[:1]
    lacked = (before + kept.astype(F32) * flags[1:2]).astype(BF16)
    lacked, sign = lax.optimization_barrier((lacked, sign))
    other = lax.ppermute(lacked, "seq", swap)
    signs = [sign]
    if dense:
        weights_up, sign = load_near(scalars, expert_in[0], 1, lacked)
        signs.append(sign)
    pieces = call(
        functools.partial(attend_kernel, parts),
        [shape((count, width), BF16)] * parts,
        [scalars, within, query, rest, my_gain, mine, other, *signs],
        scratch=[pltpu.VMEM((rows, width), BF16)],
        flops=4 * rows * width * HEAD,
    )
    gathered = exchange(pieces)

    my_routes = lax.dynamic_slice_in_dim(routes, my_rows, count, 0)
    my_gates = lax.dynamic_slice_in_dim(route_gates, my_rows, count, 0)
    mixing = jnp.sum(
        jnp.where(
            my_routes[:, :, None] == jnp.arange(experts, dtype=jnp.int32),
            my_gates[:, :, None],
            0.0,
        ),
        axis=1,
    )
    high = lax.reduce_precision(mixing, 8, 7)
    lanes = -(-2 * experts // HEAD) * HEAD
    pack = jnp.pad(
        jnp.concatenate([high, mixing - high], axis=1), ((0, 0), (0, lanes - 2 * experts))
    ).astype(BF16)
    hidden = jnp.concatenate(turn_order(gathered, turns), axis=1)
    widened = hidden.astype(F32)
    normed = (
        widened
        * lax.rsqrt(jnp.mean(widened * widened, axis=-1, keepdims=True) + 1e-06)
        * norm_gain
    ).astype(BF16)
    if dense:
        block = jnp.concatenate([normed, pack], axis=1)
        terms = dense_experts(
            block, scalars, weights_gate, weights_up, expert_out
        )
    else:
        mixed = routed_experts(normed, my_routes, my_gates, expert_in, expert_out)
        terms = [mixed]
    own, *others = terms
    mixed = own.astype(F32) + sum(t.astype(F32) for t in others)
    ready = (hidden.astype(F32) + mixed).astype(BF16)
    columns = [ready[:, i * width:(i + 1) * width] for i in range(parts)]
    return jnp.concatenate(turn_order(exchange(turn_order(columns, turns)), turns))


def solution(mesh):
    placed = (
        P("seq", "exp"),
        P("seq", "exp"),
        P("seq", "exp"),
        P("seq", "exp"),
        P("exp"),
        P(),
        P("seq", None),
        P("seq", None),
        P("seq", None, None, None),
        P("seq", None, None),
    )
    return jax.shard_map(
        per_device, mesh=mesh, in_specs=placed, out_specs=P("seq", "exp"), check_vma=False
    )
```
